32 devices in a mesh: dp: 8 (over z, x), seq: 4 (over y, core).
Axes of the slice: x: 2, y: 2, z: 4, core: 2. Of those that a mesh axis runs over, the one named last changes fastest.
Arguments:
- tokens: float32 [8192, 384], P(('dp', 'seq')), may hold values from -6 to 6
- class_tokens: float32 [32, 384], P('dp'), may hold values from -6 to 6
- cot_patch: float32 [8192, 384], P(('dp', 'seq')), may hold values from -6 to 6
- cot_class: float32 [32, 384], P('dp'), may hold values from -6 to 6
- lengths: int32 [8, 4], P('dp'), may hold values from 64 to 832, as said below
- matrices: float32 [2, 3, 384, 1536], replicated, may hold values from -0.3125 to 0.3125
- matrices_moment1: float32 [2, 3, 384, 1536], P(None, None, 'dp'), may hold values from -0.00035029993 to 0.00035029993
- matrices_moment2: float32 [2, 3, 384, 1536], P(None, None, 'dp'), may hold values from 2.8170347e-10 to 1.1268139e-09
- matrices_ema: float32 [2, 3, 384, 1536], P(None, None, 'dp'), may hold values from -0.3125 to 0.3125
- vectors: float32 [28, 384], replicated, may hold values from -1 to 3
- vectors_moment1: float32 [28, 384], P(None, 'dp'), may hold values from -0.0014011997 to 0.0014011997
- vectors_moment2: float32 [28, 384], P(None, 'dp'), may hold values from 4.5072555e-09 to 1.8029022e-08
- vectors_ema: float32 [28, 384], P(None, 'dp'), may hold values from 0.5 to 1.5
- talking: float32 [8, 17], replicated, may hold values from -1 to 2
- talking_moment1: float32 [8, 17], replicated, may hold values from -0.0035029992 to 0.0035029992
- talking_moment2: float32 [8, 17], replicated, may hold values from 2.8170348e-08 to 1.1268139e-07
- talking_ema: float32 [8, 17], replicated, may hold values from -3 to 3
Outputs:
- patch_out: float32 [8192, 384], P(('dp', 'seq'))
- class_out: float32 [32, 384], P('dp')
- grad_tokens: float32 [8192, 384], P(('dp', 'seq'))
- grad_class: float32 [32, 384], P('dp')
- clip_norm: float32 [], replicated
- matrices_new: float32 [2, 3, 384, 1536], P(None, None, 'dp')
- matrices_first: float32 [2, 3, 384, 1536], P(None, None, 'dp')
- matrices_second: float32 [2, 3, 384, 1536], P(None, None, 'dp')
- matrices_average: float32 [2, 3, 384, 1536], P(None, None, 'dp')
- vectors_new: float32 [28, 384], P(None, 'dp')
- vectors_first: float32 [28, 384], P(None, 'dp')
- vectors_second: float32 [28, 384], P(None, 'dp')
- vectors_average: float32 [28, 384], P(None, 'dp')
- talking_new: float32 [8, 17], replicated
- talking_first: float32 [8, 17], replicated
- talking_second: float32 [8, 17], replicated
- talking_average: float32 [8, 17], replicated
The draws below stay inside these ranges and needn't reach their ends.
Inputs may be any that keep to these rules, and one draw needn't show every extreme that they name: In every data group the 4 lengths sum to 1024; one image of each group, neither the first nor the last and in a drawn place, begins within the first 256 positions of the group and ends within its last 256.
All inputs are finite; a program needn't handle non-finite values.
Results may differ from the reference program's by a relative error of at most 0.0003.
Values sent between devices are 32-bit elements; how exact they have to be, the bound alone decides.
No kernel may reach another device: no remote copies, remote signals or barrier semaphores. Data moves between devices by JAX's collectives and lax.ppermute only.
A program may use at most 256 MiB of HBM per device.

```python
import math
import jax
import jax.numpy as jnp
from jax import lax

D = 384
FF = 1536
HEADS = 8
TOK_DEV = 256
IMGS = 4
MIN_LEN = 64
STEP = 10
NVEC = 28
SEQ_TOK = 1024
TOKENS = 8192
GROUPS = 8
IMAGES = 32
TALK_COLS = 17
NPARAM = 3549832


def draw_lengths(key, part):
    key = jax.random.fold_in(key, 11)
    short_key, place_key, group_key = jax.random.split(key, 3)
    short_most = (TOK_DEV - 1) // (IMGS - 2)
    short_rows = jax.random.randint(short_key, (GROUPS, IMGS), MIN_LEN, short_most + 1)
    long_slot = jax.random.randint(place_key, (GROUPS, 1), 1, IMGS - 1)
    tight_group = jax.random.randint(group_key, (1, 1), 0, GROUPS)
    slots = jnp.arange(IMGS)[None, :]
    group_rows = jnp.arange(GROUPS)[:, None]
    short_rows = jnp.where(group_rows == tight_group, MIN_LEN, short_rows)
    others = jnp.sum(jnp.where(slots == long_slot, 0, short_rows), axis=1, keepdims=True)
    return jnp.where(slots == long_slot, SEQ_TOK - others, short_rows).astype(jnp.int32)


def draw_vectors(key, part):
    key = jax.random.fold_in(key, 12)
    jitter_key, shift_key = jax.random.split(key)
    column = jnp.arange(D).astype(jnp.float32) / (D - 1)
    ramp = 0.6 * jnp.exp(jnp.log(3.0) * column)
    jitter = 1.0 + 0.05 * jnp.clip(jax.random.normal(jitter_key, (NVEC, D), jnp.float32), -3.0, 3.0)
    shifts = 0.3 * jnp.clip(jax.random.normal(shift_key, (NVEC, D), jnp.float32), -3.0, 3.0)
    row_kind = jnp.arange(NVEC)[:, None] % 14
    scaled_rows = (row_kind == 0) | (row_kind == 5) | (row_kind == 6) | (row_kind == 13)
    return jnp.where(scaled_rows, ramp[None, :] * jitter, shifts)


def draw_talking(key, part):
    key = jax.random.fold_in(key, 13)
    noise = 0.3 * jnp.clip(jax.random.normal(key, (HEADS, TALK_COLS), jnp.float32), -3.0, 3.0)
    column = jnp.arange(TALK_COLS)[None, :]
    row_index = jnp.arange(HEADS)[:, None]
    identity = ((column == row_index) | (column == row_index + HEADS)).astype(jnp.float32)
    damping = jnp.where(column == 2 * HEADS, 1.0 / SEQ_TOK, 1.0)
    return identity + noise * damping


def level_of(key, extent, cuts, smallest, largest):
    def one(axis_at, shards_of):
        draws = jax.random.uniform(jax.random.fold_in(jax.random.fold_in(key, 6), axis_at), (shards_of,), jnp.float32, smallest / len(cuts), largest / len(cuts))
        return jnp.repeat(jnp.exp(draws), extent[axis_at] // shards_of).reshape((-1,) + (1,) * (len(extent) - axis_at - 1))

    factor_of = one(*cuts[0])
    for cut in cuts[1:]:
        factor_of = factor_of * one(*cut)
    return factor_of


def bell_draw(stream_key, shape, scale, bound, shards=(), kind=jnp.bfloat16):
    entries = scale * jax.random.normal(stream_key, shape, jnp.float32)
    if shards:
        entries = entries * level_of(stream_key, shape, shards, -0.22, 0.18)
    return jnp.clip(entries, -bound, bound).astype(kind)


def setup_inputs(seed: int = 0) -> dict:
    streams_of = jax.random.split(jax.random.key(seed), 18)
    return {
        "tokens": bell_draw(streams_of[0], (TOKENS, D), 1.0, 6.0, ((0, 32),), jnp.float32),
        "class_tokens": bell_draw(streams_of[1], (IMAGES, D), 1.0, 6.0, ((0, 8),), jnp.float32),
        "cot_patch": bell_draw(streams_of[2], (TOKENS, D), 1.0, 6.0, ((0, 32),), jnp.float32),
        "cot_class": bell_draw(streams_of[3], (IMAGES, D), 1.0, 6.0, ((0, 8),), jnp.float32),
        "lengths": draw_lengths(jax.random.fold_in(streams_of[17], 71), 0),
        "matrices": bell_draw(streams_of[5], (2, 3, D, FF), D ** -0.5, 0.3125, (), jnp.float32),
        "matrices_moment1": bell_draw(streams_of[6], (2, 3, D, FF), (0.11 / NPARAM ** 0.5), 0.00035029993, ((2, 8),), jnp.float32),
        "matrices_moment2": jnp.clip(jnp.exp(math.log(1.1268138644382475e-09) - 1.3862944 * jax.random.uniform(streams_of[7], (2, 3, D, FF), jnp.float32) ** level_of(streams_of[7], (2, 3, D, FF), ((2, 8),), -0.2, 0.2)), 2.8170346610956187e-10, 1.1268138644382475e-09),
        "matrices_ema": bell_draw(streams_of[8], (2, 3, D, FF), D ** -0.5, 0.3125, ((2, 8),), jnp.float32),
        "vectors": draw_vectors(jax.random.fold_in(streams_of[17], 71), 0),
        "vectors_moment1": bell_draw(streams_of[10], (NVEC, D), (0.44 / NPARAM ** 0.5), 0.0014011997, ((1, 8),), jnp.float32),
        "vectors_moment2": jnp.clip(jnp.exp(math.log(1.802902183101196e-08) - 1.3862944 * jax.random.uniform(streams_of[11], (NVEC, D), jnp.float32) ** level_of(streams_of[11], (NVEC, D), ((1, 8),), -0.2, 0.2)), 4.50725545775299e-09, 1.802902183101196e-08),
        "vectors_ema": jnp.clip(1.0 + 0.1 * jax.random.normal(streams_of[12], (NVEC, D), jnp.float32), 0.5, 1.5),
        "talking": draw_talking(jax.random.fold_in(streams_of[17], 71), 0),
        "talking_moment1": bell_draw(streams_of[14], (HEADS, TALK_COLS), (1.1 / NPARAM ** 0.5), 0.0035029992, (), jnp.float32),
        "talking_moment2": jnp.clip(jnp.exp(jax.random.uniform(streams_of[15], (HEADS, TALK_COLS), jnp.float32, math.log(2.8170347832201514e-08), math.log(1.1268139132880606e-07))), 2.8170347832201514e-08, 1.1268139132880606e-07),
        "talking_ema": bell_draw(streams_of[16], (HEADS, TALK_COLS), 0.5, 3.0, (), jnp.float32),
    }


EPS_NORM = 1e-06
MASKED = -1e+30
LR_MATRIX = 0.05
LR_VECTOR = 0.1
LR_TALKING = 0.2
BETA_ONE = 0.9
BETA_TWO = 0.999
ADAM_EPS = 1e-08
WEIGHT_DECAY = 0.05
EMA_RATE = 0.9
CLIP_NORM = 1.0
HIGHEST = lax.Precision.HIGHEST

@jax.custom_vjp
def low(v):
    return lax.optimization_barrier(v.astype(jnp.bfloat16)).astype(jnp.float32)

@jax.custom_vjp
def low_back(v):
    return v

def low_keep(v):
    return (low(v), None)

def low_pass(kept, grad):
    return (grad,)

def back_keep(v):
    return (v, None)

def back_low(kept, grad):
    return (low(grad),)
low.defvjp(low_keep, low_pass)
low_back.defvjp(back_keep, back_low)

def matmul(left, right):
    return jnp.dot(left, right, precision=HIGHEST, preferred_element_type=jnp.float32)

def layer_norm(values, gain_row, shift_row):
    average = lax.optimization_barrier(jnp.mean(values, axis=-1, keepdims=True))
    centered = values - average
    variance = lax.optimization_barrier(jnp.mean(centered * centered, axis=-1, keepdims=True))
    return centered * lax.rsqrt(variance + EPS_NORM) * gain_row + shift_row

def project_all(inputs, mats, vecs):
    model_width = inputs.shape[1]
    normed = layer_norm(inputs, vecs[0], vecs[1])
    query = matmul(normed, mats[0][:, :model_width]) + vecs[2]
    keys = matmul(normed, mats[0][:, model_width:2 * model_width])
    values = matmul(normed, mats[0][:, 2 * model_width:3 * model_width]) + vecs[3]
    return (query, keys, values)

def project_keys(inputs, mats, vecs):
    model_width = inputs.shape[1]
    normed = layer_norm(inputs, vecs[0], vecs[1])
    keys = matmul(normed, mats[0][:, model_width:2 * model_width])
    values = matmul(normed, mats[0][:, 2 * model_width:3 * model_width]) + vecs[3]
    return (keys, values)

def block_tail(inputs, attended, mats, vecs):
    model_width = inputs.shape[1]
    mixed_rows = inputs + vecs[5] * (matmul(attended, mats[0][:, 3 * model_width:]) + vecs[4])
    normed = layer_norm(mixed_rows, vecs[6], vecs[7])
    hidden = jax.nn.gelu(matmul(normed, mats[1]) + vecs[8:12].reshape(-1), approximate=False)
    output_rows = jnp.einsum('nf,df->nd', hidden, mats[2], precision=HIGHEST)
    return mixed_rows + vecs[13] * (output_rows + vecs[12])

def segment_ids(positions, image_lengths):
    image_ends = jnp.cumsum(image_lengths).astype(jnp.int32)
    return lax.optimization_barrier(jnp.sum((positions[:, None] >= image_ends[None, :]).astype(jnp.int32), axis=1))

def self_attention(query, keys, values, segment, talking):
    head_count = talking.shape[0]
    row_count, model_width = query.shape
    head_size = model_width // head_count
    query_split = query.reshape(row_count, head_count, head_size)
    keys_split = keys.reshape(row_count, head_count, head_size)
    values_split = values.reshape(row_count, head_count, head_size)
    raw_scores = jnp.einsum('ihe,jhe->hij', query_split, keys_split, precision=HIGHEST) * head_size ** (-0.5)
    mixed_scores = jnp.einsum('hg,gij->hij', talking[:, :head_count], raw_scores, precision=HIGHEST)
    inside = (segment[:, None] == segment[None, :])[None]
    masked_scores = jnp.where(inside, mixed_scores, MASKED)
    row_top = lax.optimization_barrier(jnp.max(masked_scores, axis=2, keepdims=True))
    exponentials = jnp.exp(masked_scores - row_top) * inside
    probabilities = exponentials / lax.optimization_barrier(jnp.sum(exponentials, axis=2, keepdims=True))
    weights = jnp.einsum('hg,gij->hij', talking[:, head_count:2 * head_count], probabilities, precision=HIGHEST)
    weights = weights + talking[:, 2 * head_count][:, None, None] * inside
    attended = jnp.einsum('hij,jhe->ihe', weights, values_split, precision=HIGHEST)
    return attended.reshape(row_count, model_width)

def class_attention(query_cls, keys_cls, values_cls, patch_keys, patch_values, segment):
    image_count, model_width = query_cls.shape
    head_size = model_width // HEADS
    score_scale = head_size ** (-0.5)
    query_split = query_cls.reshape(image_count, HEADS, head_size)
    own_keys = keys_cls.reshape(image_count, HEADS, head_size)
    own_values = values_cls.reshape(image_count, HEADS, head_size)
    keys_split = patch_keys.reshape(-1, HEADS, head_size)
    values_split = patch_values.reshape(-1, HEADS, head_size)
    image_ids = jnp.arange(image_count).astype(jnp.int32)
    belong = (segment[None, :] == image_ids[:, None])[:, None, :]
    patch_scores = jnp.einsum('ahe,jhe->ahj', query_split, keys_split, precision=HIGHEST) * score_scale
    patch_scores = jnp.where(belong, patch_scores, MASKED)
    own_score = lax.optimization_barrier(jnp.sum(query_split * own_keys, axis=2)) * score_scale
    class_top = jnp.maximum(lax.optimization_barrier(jnp.max(patch_scores, axis=2)), own_score)
    patch_weights = jnp.exp(patch_scores - class_top[..., None]) * belong
    own_weight = jnp.exp(own_score - class_top)
    class_sum = lax.optimization_barrier(jnp.sum(patch_weights, axis=2)) + own_weight
    gathered_values = jnp.einsum('ahj,jhe->ahe', patch_weights, values_split, precision=HIGHEST)
    result = (gathered_values + own_weight[..., None] * own_values) / class_sum[..., None]
    return result.reshape(image_count, model_width)

def group_forward(inputs, class_rows, image_lengths, matrices, vectors, talking):
    positions = jnp.arange(inputs.shape[0]).astype(jnp.int32)
    segment = segment_ids(positions, image_lengths)
    query, keys, values = project_all(inputs, matrices[0], vectors[:14])
    attended = self_attention(query, keys, values, segment, talking)
    patch_out = block_tail(inputs, attended, matrices[0], vectors[:14])
    query_cls, keys_cls, values_cls = project_all(class_rows, matrices[1], vectors[14:])
    patch_keys, patch_values = project_keys(patch_out, matrices[1], vectors[14:])
    class_attended = class_attention(query_cls, keys_cls, values_cls, patch_keys, patch_values, segment)
    class_out = block_tail(class_rows, class_attended, matrices[1], vectors[14:])
    return (patch_out, class_out)

def adam_step(weight, gradient, moment1, moment2, rate, decay):
    first = BETA_ONE * moment1 + (1.0 - BETA_ONE) * gradient
    second = BETA_TWO * moment2 + (1.0 - BETA_TWO) * gradient * gradient
    first_hat = first / (1.0 - BETA_ONE ** STEP)
    second_hat = second / (1.0 - BETA_TWO ** STEP)
    updated = weight - rate * (first_hat / (jnp.sqrt(second_hat) + ADAM_EPS) + decay * weight)
    return (updated, first, second)

def reference(tokens, class_tokens, cot_patch, cot_class, lengths, matrices, matrices_moment1, matrices_moment2, matrices_ema, vectors, vectors_moment1, vectors_moment2, vectors_ema, talking, talking_moment1, talking_moment2, talking_ema):
    group_count = lengths.shape[0]

    def forward(tokens_all, class_all, mats, vecs, talk):

        def one_group(element):
            return group_forward(element[0], element[1], element[2], mats, vecs, talk)
        stacked = (tokens_all.reshape(group_count, -1, tokens_all.shape[1]), class_all.reshape(group_count, -1, class_all.shape[1]), lengths)
        patch_rows, class_rows = lax.map(jax.checkpoint(one_group), stacked)
        return (patch_rows.reshape(tokens_all.shape), class_rows.reshape(class_all.shape))
    (patch_out, class_out), pullback = jax.vjp(forward, tokens, class_tokens, matrices, vectors, talking)
    grad_tokens, grad_class, grad_mats, grad_vecs, grad_talk = pullback((cot_patch, cot_class))
    squares = jnp.sum(grad_mats * grad_mats) + jnp.sum(grad_vecs * grad_vecs) + jnp.sum(grad_talk * grad_talk)
    clip_norm = jnp.sqrt(squares)
    factor = jnp.minimum(1.0, CLIP_NORM / clip_norm)
    matrices_new, matrices_first, matrices_second = adam_step(matrices, grad_mats * factor, matrices_moment1, matrices_moment2, LR_MATRIX, WEIGHT_DECAY)
    vectors_new, vectors_first, vectors_second = adam_step(vectors, grad_vecs * factor, vectors_moment1, vectors_moment2, LR_VECTOR, 0.0)
    talking_new, talking_first, talking_second = adam_step(talking, grad_talk * factor, talking_moment1, talking_moment2, LR_TALKING, 0.0)
    matrices_average = EMA_RATE * matrices_ema + (1.0 - EMA_RATE) * matrices_new
    vectors_average = EMA_RATE * vectors_ema + (1.0 - EMA_RATE) * vectors_new
    talking_average = EMA_RATE * talking_ema + (1.0 - EMA_RATE) * talking_new
    return (patch_out, class_out, grad_tokens, grad_class, clip_norm, matrices_new, matrices_first, matrices_second, matrices_average, vectors_new, vectors_first, vectors_second, vectors_average, talking_new, talking_first, talking_second, talking_average)
```

```python
import functools

import jax
import jax.numpy as jnp
from jax import lax
from jax.experimental import pallas as pl
from jax.experimental.pallas import tpu as pltpu
from jax.sharding import PartitionSpec as P

STEP = 10
EPS_NORM = 1e-06
MASKED = -1e30
LR_MATRIX = 0.05
LR_VECTOR = 0.1
LR_TALKING = 0.2
BETA_ONE = 0.9
BETA_TWO = 0.999
ADAM_EPS = 1e-08
WEIGHT_DECAY = 0.05
EMA_RATE = 0.9
CLIP_NORM = 1.0
F32 = jnp.float32
BF16 = jnp.bfloat16
NN = (((1,), (0,)), ((), ()))
NT = (((1,), (1,)), ((), ()))
TN = (((0,), (0,)), ((), ()))
VMEM_BYTES = 56 << 20


def split(value):
    high = value.astype(BF16)
    return high, (value - high.astype(F32)).astype(BF16)


def mm(left, right, dims=NN):
    return lax.dot_general(left, right, dims, preferred_element_type=F32)


def mm3(left, right, dims=NN):
    return mm(left[0], right[0], dims) + (mm(left[0], right[1], dims) + mm(left[1], right[0], dims))


def dot_kernel(left, right, dims=NN):
    return mm3(split(left), split(right), dims)


def dot_plain(left, right, dims=NN):
    return lax.dot_general(
        left, right, dims, precision=lax.Precision.HIGH, preferred_element_type=F32
    )


def norm_rows(values):
    average = jnp.mean(values, axis=-1, keepdims=True)
    centered = values - average
    variance = jnp.mean(centered * centered, axis=-1, keepdims=True)
    scale = lax.rsqrt(variance + EPS_NORM)
    return centered * scale, scale


def norm_back(grad, unit, scale):
    inner = jnp.mean(grad * unit, axis=-1, keepdims=True)
    return scale * (grad - jnp.mean(grad, axis=-1, keepdims=True) - unit * inner)


def gelu_both(values):
    half = 0.5 * (1.0 + lax.erf(values * 0.7071067811865476))
    slope = half + values * (0.3989422804014327 * jnp.exp(-0.5 * values * values))
    return values * half, slope


def row_sum(values):
    return jnp.sum(values, axis=0, keepdims=True)


def tail_forward(dot, inputs, attended, w_out, w_up, w_down, vecs, up_bias):
    projected = dot(attended, w_out) + vecs[4:5]
    mixed = inputs + vecs[5:6] * projected
    unit, scale = norm_rows(mixed)
    normed = unit * vecs[6:7] + vecs[7:8]
    hidden, slope = gelu_both(dot(normed, w_up) + up_bias)
    lowered = dot(hidden, w_down, NT) + vecs[12:13]
    out = mixed + vecs[13:14] * lowered
    return out, (projected, unit, scale, normed, hidden, slope, lowered)


def tail_backward(dot, cot, kept, w_out, w_up, w_down, vecs):
    projected, unit, scale, normed, hidden, slope, lowered = kept
    d_lowered = cot * vecs[13:14]
    d_hidden = dot(d_lowered, w_down) * slope
    d_normed = dot(d_hidden, w_up, NT)
    d_mixed = cot + norm_back(d_normed * vecs[6:7], unit, scale)
    d_projected = d_mixed * vecs[5:6]
    d_attended = dot(d_projected, w_out, NT)
    rows = {
        4: row_sum(d_projected),
        5: row_sum(d_mixed * projected),
        6: row_sum(d_normed * unit),
        7: row_sum(d_normed),
        12: row_sum(d_lowered),
        13: row_sum(cot * lowered),
    }
    return d_mixed, d_attended, d_projected, d_hidden, d_lowered, rows, row_sum(d_hidden)


def image_of(lengths_ref, images, positions):
    end = lengths_ref[0, 0]
    inside = (positions >= end).astype(jnp.int32)
    for image in range(1, images):
        end = end + lengths_ref[0, image]
        inside = inside + (positions >= end).astype(jnp.int32)
    return inside


def same_image(lengths_ref, images, place, slots, rows):
    queries = place * rows + lax.broadcasted_iota(jnp.int32, (1, rows), 1)
    query_image = image_of(lengths_ref, images, queries)
    parts = []
    for slot in range(slots):
        keys = jnp.bitwise_xor(place, slot) * rows + lax.broadcasted_iota(jnp.int32, (rows, 1), 0)
        parts.append(image_of(lengths_ref, images, keys) == query_image)
    return parts


def column_of(table, number):
    lanes = lax.broadcasted_iota(jnp.int32, (1, table.shape[1]), 1)
    return jnp.sum(jnp.where(lanes == number, table, 0.0), axis=1, keepdims=True)


def forward_kernel(slots, images, *refs):
    place_ref, lengths_ref = refs[:2]
    token_refs = refs[2 : 2 + slots]
    w_ref, vecs_ref, t1_ref, t2_ref = refs[2 + slots : 6 + slots]
    (
        p_high_ref, p_low_ref, pv_ref, pv_bias_ref, attended_ref, normed_ref,
        kt_high_ref, kt_low_ref, v_high_ref, v_low_ref, query_ref,
        k_high, k_low, vt_high, vt_low, qt, bias, attended_t,
    ) = refs[6 + slots :]
    rows, width = token_refs[0].shape
    head = pl.program_id(0)
    heads = pl.num_programs(0)
    head_size = width // 8

    @pl.when(head == 0)
    def _():
        place = place_ref[0]
        w_kv = split(w_ref[:, width : 3 * width])
        shift = vecs_ref[3:4, :]
        inside = same_image(lengths_ref, images, place, slots, rows)
        for slot in range(slots):
            unit, _ = norm_rows(token_refs[slot][...])
            normed = unit * vecs_ref[0:1, :] + vecs_ref[1:2, :]
            here = pl.ds(slot * rows, rows)
            normed_ref[here, :] = normed
            normed = split(normed)
            both = mm3(normed, w_kv)
            keys, values = both[:, :width], both[:, width:] + shift
            k_high[here, :], k_low[here, :] = split(keys)
            v_high_ref[here, :], v_low_ref[here, :] = split(values)
            kt_high_ref[:, here], kt_low_ref[:, here] = split(keys.T)
            vt_high[:, here], vt_low[:, here] = split(values.T)
            bias[here, :] = jnp.where(inside[slot], 0.0, MASKED)
            if slot == 0:
                query = mm3(normed, split(w_ref[:, :width])) + vecs_ref[2:3, :]
                query = query * head_size ** (-0.5)
                query_ref[...] = query
                qt[...] = query.T

    mixed = mm3((k_high[...], k_low[...]), split(qt[...] * column_of(t1_ref[...], head)))
    mixed = mixed + bias[...]
    exponentials = jnp.exp(mixed - jnp.max(mixed, axis=0, keepdims=True))
    probs = split(exponentials * (1.0 / jnp.sum(exponentials, axis=0, keepdims=True)))
    p_high_ref[0], p_low_ref[0] = probs
    values = mm3((vt_high[...], vt_low[...]), probs)
    pv_ref[0] = values
    term = values * column_of(t2_ref[...], head)

    @pl.when(head == 0)
    def _():
        attended_t[...] = term

    @pl.when(head > 0)
    def _():
        attended_t[...] += term

    @pl.when(head == heads - 1)
    def _():
        inside = jnp.where(bias[...] < 0.0, 0.0, 1.0).astype(BF16)
        summed = mm(vt_high[...], inside) + mm(vt_low[...], inside)
        pv_bias_ref[...] = summed
        attended_ref[...] = (attended_t[...] + summed * t2_ref[:, 8:9]).T


def whole(shape):
    return pl.BlockSpec(shape, lambda *_: (0,) * len(shape))


def struct(shape, dtype=F32):
    return jax.ShapeDtypeStruct(shape, dtype)


def attention_forward(place, lengths, token_slots, w_first, vecs, t1, t2):
    slots, (rows, width) = len(token_slots), token_slots[0].shape
    total, heads = slots * rows, 8
    smem = pl.BlockSpec(memory_space=pltpu.SMEM)
    by_head = lambda *shape: pl.BlockSpec((1,) + shape, lambda g: (g, 0, 0))
    outs = [
        (by_head(total, rows), struct((heads, total, rows), BF16)),
        (by_head(total, rows), struct((heads, total, rows), BF16)),
        (by_head(width, rows), struct((heads, width, rows))),
        (whole((width, rows)), struct((width, rows))),
        (whole((rows, width)), struct((rows, width))),
        (whole((total, width)), struct((total, width))),
        (whole((width, total)), struct((width, total), BF16)),
        (whole((width, total)), struct((width, total), BF16)),
        (whole((total, width)), struct((total, width), BF16)),
        (whole((total, width)), struct((total, width), BF16)),
        (whole((rows, width)), struct((rows, width))),
    ]
    operands = [*token_slots, w_first, vecs, t1, t2]
    flops = 2 * 3 * (2 * heads + 3) * total * rows * width
    return pl.pallas_call(
        functools.partial(forward_kernel, slots, lengths.shape[1]),
        grid=(heads,),
        in_specs=[smem, smem] + [whole(operand.shape) for operand in operands],
        out_specs=[spec for spec, _ in outs],
        out_shape=[shape for _, shape in outs],
        scratch_shapes=[
            pltpu.VMEM((total, width), BF16),
            pltpu.VMEM((total, width), BF16),
            pltpu.VMEM((width, total), BF16),
            pltpu.VMEM((width, total), BF16),
            pltpu.VMEM((width, rows), F32),
            pltpu.VMEM((total, rows), F32),
            pltpu.VMEM((width, rows), F32),
        ],
        compiler_params=pltpu.CompilerParams(vmem_limit_bytes=VMEM_BYTES),
        cost_estimate=pl.CostEstimate(
            flops=flops, bytes_accessed=20 << 20, transcendentals=heads * total * rows
        ),
        name="attention_forward",
    )(place, lengths, *operands)


def backward_kernel(slots, images, *refs):
    (
        place_ref, lengths_ref, p_high_ref, p_low_ref, pv_ref, pv_bias_ref, cot_ref,
        kt_high, kt_low, v_high, v_low, query_ref, t1_ref, t2_ref, t1_rows, t2_rows,
        d_keys_ref, d_values_ref, d_query_ref, c1_ref, c2_ref,
        cot_t, qt, d_qt,
    ) = refs
    rows, width = cot_ref.shape
    head = pl.program_id(0)
    heads = pl.num_programs(0)
    head_size = width // 8
    lanes = lax.broadcasted_iota(jnp.int32, (1, 128), 1)

    @pl.when(head == 0)
    def _():
        cot_t[...] = cot_ref[...].T
        qt[...] = query_ref[...].T
        d_qt[...] = jnp.zeros_like(d_qt)
        d_keys_ref[...] = jnp.zeros_like(d_keys_ref)
        c1_ref[...] = jnp.zeros_like(c1_ref)
        c2_ref[...] = jnp.where(
            lanes == 8, jnp.sum(cot_t[...] * pv_bias_ref[...], axis=1, keepdims=True), 0.0
        )
        inside = jnp.concatenate(same_image(lengths_ref, images, place_ref[0], slots, rows), axis=0)
        inside = jnp.where(inside, 1.0, 0.0).astype(BF16)
        high, low = split(cot_ref[...] * t2_rows[8:9, :])
        d_values_ref[...] = mm(inside, high) + mm(inside, low)

    t1_column = column_of(t1_ref[...], head)
    t2_column = column_of(t2_ref[...], head)
    crossed = cot_t[...] * pv_ref[0]
    c2_ref[...] += jnp.where(lanes == head, jnp.sum(crossed, axis=1, keepdims=True), 0.0)
    delta = jnp.sum(crossed * t2_column, axis=0, keepdims=True)
    d_probs = mm3((v_high[...], v_low[...]), split(cot_t[...] * t2_column))
    probs = (p_high_ref[0], p_low_ref[0])
    d_values_ref[...] += mm3(probs, split(cot_ref[...] * t2_rows[pl.ds(head, 1), :]))
    d_mixed = (probs[0].astype(F32) + probs[1].astype(F32)) * (d_probs - delta)
    d_mixed = split(d_mixed)
    d_keys_ref[...] += mm3(d_mixed, split(query_ref[...] * t1_rows[pl.ds(head, 1), :]))
    back = mm3((kt_high[...], kt_low[...]), d_mixed)
    d_qt[...] += back * t1_column
    c1_ref[...] += jnp.where(
        lanes == head, jnp.sum(back * qt[...], axis=1, keepdims=True), 0.0
    )

    @pl.when(head == heads - 1)
    def _():
        d_query_ref[...] = d_qt[...].T * head_size ** (-0.5)


def attention_backward(place, lengths, p_high, p_low, pv, pv_bias, cot, keys_t, values, query, tables):
    rows, width = cot.shape
    heads, total, _ = p_high.shape
    smem = pl.BlockSpec(memory_space=pltpu.SMEM)
    by_head = lambda shape: pl.BlockSpec((1,) + shape[1:], lambda g: (g, 0, 0))
    operands = [p_high, p_low, pv, pv_bias, cot, *keys_t, *values, query, *tables]
    outs = [struct((total, width)), struct((total, width)), struct((rows, width)),
            struct((width, 128)), struct((width, 128))]
    flops = 2 * 3 * (4 * heads + 1) * total * rows * width
    return pl.pallas_call(
        functools.partial(backward_kernel, total // rows, lengths.shape[1]),
        grid=(heads,),
        in_specs=[smem, smem]
        + [by_head(operand.shape) for operand in operands[:3]]
        + [whole(operand.shape) for operand in operands[3:]],
        out_specs=[whole(out.shape) for out in outs],
        out_shape=outs,
        scratch_shapes=[pltpu.VMEM((width, rows), F32)] * 3,
        compiler_params=pltpu.CompilerParams(vmem_limit_bytes=VMEM_BYTES),
        cost_estimate=pl.CostEstimate(flops=flops, bytes_accessed=20 << 20, transcendentals=0),
        name="attention_backward",
    )(place, lengths, *operands)


def swap(value, axis, size, bit):
    return lax.ppermute(value, axis, [(place, place ^ bit) for place in range(size)])


def gather_slots(own, axis, size):
    found = {0: own}
    bit = size // 2
    while bit:
        for slot in sorted(found):
            found[slot | bit] = swap(found[slot], axis, size, bit)
        bit //= 2
    return [found[slot] for slot in range(size)]


def scatter_slots(parts, axis, size):
    parts = list(parts)
    bit = 1
    while bit < size:
        step = 2 * bit
        for slot in range(0, size, step):
            parts[slot] = parts[slot] + swap(parts[slot + bit], axis, size, bit)
        bit *= 2
    return parts[0]


def reduce_rows(value, dp_size, seq_size):
    dp_index, seq_index = lax.axis_index("dp"), lax.axis_index("seq")
    core = seq_index % 2
    kept = lax.dynamic_index_in_dim(value, core, 1, keepdims=False)
    sent = lax.dynamic_index_in_dim(value, 1 - core, 1, keepdims=False)
    value = kept + swap(sent, "seq", seq_size, 1)
    bit = 1
    while bit < dp_size:
        mine = (dp_index // bit) % 2
        pairs = value.reshape((-1, 2) + value.shape[1:])
        kept = lax.dynamic_index_in_dim(pairs, mine, 1, keepdims=False)
        sent = lax.dynamic_index_in_dim(pairs, 1 - mine, 1, keepdims=False)
        value = kept + swap(sent, "dp", dp_size, bit)
        bit *= 2
    value = value[0]
    bit = 2
    while bit < seq_size:
        value = value + swap(value, "seq", seq_size, bit)
        bit *= 2
    return value


def both_cores(value, seq_size):
    core = lax.axis_index("seq") % 2
    other = swap(value, "seq", seq_size, 1)
    first = jnp.where(core == 0, value, other)
    second = jnp.where(core == 0, other, value)
    return jnp.concatenate([first, second], axis=0)


def adam_step(weight, gradient, moment1, moment2, rate, decay):
    first = BETA_ONE * moment1 + (1.0 - BETA_ONE) * gradient
    second = BETA_TWO * moment2 + (1.0 - BETA_TWO) * gradient * gradient
    first_hat = first / (1.0 - BETA_ONE**STEP)
    second_hat = second / (1.0 - BETA_TWO**STEP)
    updated = weight - rate * (first_hat / (jnp.sqrt(second_hat) + ADAM_EPS) + decay * weight)
    return (updated, first, second)


def on_device(
    dp_size, seq_size,
    tokens, class_tokens, cot_patch, cot_class, lengths,
    matrices, matrices_moment1, matrices_moment2, matrices_ema,
    vectors, vectors_moment1, vectors_moment2, vectors_ema,
    talking, talking_moment1, talking_moment2, talking_ema,
):
    rows, width = tokens.shape
    images = class_tokens.shape[0]
    heads = talking.shape[0]
    head_size = width // heads
    score_scale = head_size ** (-0.5)
    seq_index = lax.axis_index("seq")
    dp_index = lax.axis_index("dp")
    place = seq_index.astype(jnp.int32).reshape(1)
    dot = dot_plain

    mats_self, mats_class = matrices[0], matrices[1]
    vecs_self, vecs_class = vectors[:14], vectors[14:]
    up_bias_self = vecs_self[8:12].reshape(1, -1)
    up_bias_class = vecs_class[8:12].reshape(1, -1)
    pre_mix, post_mix = talking[:, :heads], talking[:, heads:]
    t1 = jnp.repeat(pre_mix.T, head_size, axis=0)
    t2 = jnp.repeat(post_mix, head_size, axis=0)
    tables = (t1, t2, t1.T, t2.T)

    token_slots = gather_slots(tokens, "seq", seq_size)
    (
        p_high, p_low, pv, pv_bias, attended, normed_all,
        kt_high, kt_low, v_high, v_low, query,
    ) = attention_forward(place, lengths, token_slots, mats_self[0], vecs_self, t1, t2)
    self_tail = (mats_self[0][:, 3 * width :], mats_self[1], mats_self[2], vecs_self)
    patch_out, kept_self = tail_forward(dot, tokens, attended, *self_tail, up_bias_self)

    w_q, w_k, w_v, w_o = (mats_class[0][:, i * width : (i + 1) * width] for i in range(4))
    unit_c, scale_c = norm_rows(class_tokens)
    normed_c = unit_c * vecs_class[0:1] + vecs_class[1:2]
    query_c = dot(normed_c, w_q) + vecs_class[2:3]
    keys_c = dot(normed_c, w_k)
    values_c = dot(normed_c, w_v) + vecs_class[3:4]
    heads_of = jnp.arange(width) // head_size
    by_head = (heads_of[None, :] == jnp.arange(heads)[:, None]).astype(F32)

    def spread(value):
        return (value[:, None, :] * by_head[None]).reshape(images * heads, width)

    def gather_heads(value):
        return jnp.sum(value.reshape(images, heads, width) * by_head[None], axis=1)

    def head_sums(value):
        return jnp.sum(spread(value), axis=1, keepdims=True)

    key_rows = dot(spread(query_c), w_k, NT) * score_scale
    own_score = head_sums(query_c * keys_c) * score_scale
    unit_p, scale_p = norm_rows(patch_out)
    normed_p = unit_p * vecs_class[0:1] + vecs_class[1:2]
    ends = jnp.cumsum(lengths[0])
    positions = seq_index * rows + jnp.arange(rows)
    segment = jnp.sum((positions[:, None] >= ends[None, :]).astype(jnp.int32), axis=1)
    belong = jnp.repeat(jnp.arange(images), heads)[:, None] == segment[None, :]
    scores = jnp.where(belong, dot(key_rows, normed_p, NT), MASKED)
    local_top = jnp.max(scores, axis=1, keepdims=True)
    local_weights = jnp.exp(scores - local_top) * belong
    local_sum = jnp.sum(local_weights, axis=1, keepdims=True)
    local_values = dot(local_weights, normed_p)
    packed = jnp.concatenate(
        [local_values, jnp.broadcast_to(local_top, (images * heads, 64)),
         jnp.broadcast_to(local_sum, (images * heads, 64))], axis=1)
    parts = lax.all_gather(packed, "seq", axis=0)
    tops, sums = parts[:, :, width : width + 1], parts[:, :, width + 64 : width + 65]
    class_top = jnp.maximum(jnp.max(tops, axis=0), own_score)
    rescale = jnp.exp(tops - class_top[None])
    own_weight = jnp.exp(own_score - class_top)
    class_sum = jnp.sum(sums * rescale, axis=0) + own_weight
    own_prob = own_weight / class_sum
    normed_rep = jnp.repeat(normed_c, heads, axis=0)
    value_rows = jnp.sum(parts[:, :, :width] * rescale, axis=0) / class_sum + own_prob * normed_rep
    class_attended = gather_heads(dot(value_rows, w_v)) + vecs_class[3:4]
    class_tail = (w_o, mats_class[1], mats_class[2], vecs_class)
    class_out, kept_class = tail_forward(dot, class_tokens, class_attended, *class_tail, up_bias_class)

    grad_class, d_attended_c, d_projected_c, d_hidden_c, d_lowered_c, rows_c, up_c = tail_backward(
        dot, cot_class, kept_class, *class_tail
    )
    class_delta = head_sums(d_attended_c * class_attended)
    cot_rows = dot(spread(d_attended_c), w_v, NT)
    cot_const = head_sums(d_attended_c * vecs_class[3:4])
    probs = jnp.exp(scores - class_top) * belong / class_sum
    d_scores = probs * (dot(cot_rows, normed_p, NT) + cot_const - class_delta)
    d_own = own_prob * (head_sums(d_attended_c * values_c) - class_delta)
    d_normed_p = dot(d_scores, key_rows, TN) + dot(probs, cot_rows, TN)
    d_patch = cot_patch + norm_back(d_normed_p * vecs_class[0:1], unit_p, scale_p)
    rows_p = {0: row_sum(d_normed_p * unit_p), 1: row_sum(d_normed_p)}

    grad_tokens_tail, d_attended, d_projected, d_hidden, d_lowered, rows_s, up_s = tail_backward(
        dot, d_patch, kept_self, *self_tail
    )
    g_out = dot(attended, d_projected, TN)
    g_up = dot(kept_self[3], d_hidden, TN)
    g_down = dot(d_lowered, kept_self[4], TN)

    query_rows = lax.psum(dot(d_scores, normed_p), "seq") + d_own * normed_rep
    d_query_c = gather_heads(dot(query_rows, w_k)) * score_scale
    d_normed_c = dot(d_query_c, w_q, NT) + jnp.sum(
        (d_own * key_rows + own_prob * cot_rows).reshape(images, heads, width), axis=1
    )
    grad_class = grad_class + norm_back(d_normed_c * vecs_class[0:1], unit_c, scale_c)
    rows_c.update({
        0: row_sum(d_normed_c * unit_c), 1: row_sum(d_normed_c),
        2: row_sum(d_query_c), 3: row_sum(d_attended_c),
    })
    factors = jnp.concatenate(
        [normed_c, class_attended, kept_class[3], d_lowered_c, query_rows, value_rows,
         d_query_c, query_c * score_scale, d_attended_c, d_projected_c,
         d_hidden_c.reshape(-1, width), kept_class[4].reshape(-1, width)], axis=0)
    share = factors.shape[0] // seq_size
    factors = lax.dynamic_slice_in_dim(factors, seq_index * share, share, 0)
    factors = lax.all_gather(factors, ("dp", "seq"), axis=0, tiled=True)

    d_keys, d_values, d_query, c1, c2 = attention_backward(
        place, lengths, p_high, p_low, pv, pv_bias, d_attended,
        (kt_high, kt_low), (v_high, v_low), query, tables,
    )
    w_self = mats_self[0]
    d_normed = dot(d_keys, w_self[:, width : 2 * width], NT) + dot(
        d_values, w_self[:, 2 * width : 3 * width], NT
    )
    d_slots = [d_normed[slot * rows : (slot + 1) * rows] for slot in range(seq_size)]
    d_slots[0] = d_slots[0] + dot(d_query, w_self[:, :width], NT)
    d_normed = scatter_slots(d_slots, "seq", seq_size)
    unit_s, scale_s = norm_rows(tokens)
    grad_tokens = grad_tokens_tail + norm_back(d_normed * vecs_self[0:1], unit_s, scale_s)
    rows_s.update({
        0: row_sum(d_normed * unit_s), 1: row_sum(d_normed),
        2: row_sum(d_query), 3: row_sum(d_values),
    })
    g_q = dot(normed_all[:rows], d_query, TN)
    g_k = dot(normed_all, d_keys, TN)
    g_v = dot(normed_all, d_values, TN)

    is_first = (seq_index == 0).astype(F32)

    def vector_rows(found, up):
        named = [found[i] for i in range(8)] + [up.reshape(4, width)] + [found[12], found[13]]
        return jnp.concatenate(named, axis=0)

    found_c = {i: rows_c[i] * is_first for i in rows_c}
    for i in rows_p:
        found_c[i] = found_c[i] + rows_p[i]
    grad_vecs = jnp.concatenate(
        [vector_rows(rows_s, up_s), vector_rows(found_c, up_c * is_first)], axis=0
    )
    fold = lambda value: jnp.sum(value.reshape(heads, head_size, -1), axis=1)
    grad_talk = jnp.concatenate([fold(c1[:, :heads]).T, fold(c2[:, : heads + 1])], axis=1)

    share_rows = width // (2 * dp_size)
    talk_columns = -(-talking.size // share_rows)
    talk_flat = jnp.pad(grad_talk.reshape(-1), (0, talk_columns * share_rows - talking.size))
    talk_block = jnp.tile(talk_flat.reshape(share_rows, talk_columns), (2 * dp_size, 1))
    vec_count = vectors.shape[0]
    spare = 128 - vec_count - talk_columns
    late = jnp.concatenate(
        [g_q, g_k, g_v, grad_vecs.T, talk_block, jnp.zeros((width, spare), F32)], axis=1
    )
    early = jnp.concatenate([g_out, g_up, g_down], axis=1)
    early = reduce_rows(early.reshape(dp_size, 2, share_rows, -1), dp_size, seq_size)
    late = reduce_rows(late.reshape(dp_size, 2, share_rows, -1), dp_size, seq_size)
    grad_talk = late[:, 3 * width + vec_count : 3 * width + vec_count + talk_columns]
    grad_talk = grad_talk.reshape(-1)[: talking.size].reshape(talking.shape)
    late = late[:, : 3 * width + vec_count]

    row_share = width // dp_size
    factors = factors.reshape(dp_size, -1, width)
    mine = lax.dynamic_slice_in_dim(factors, dp_index * row_share, row_share, 2)
    four = lambda array, at, count=images: array[:, at : at + count].reshape(dp_size * count, -1)
    at = images * 4 + 2 * images * heads
    pairs = images * heads

    def headed(left_at, right_at):
        left = mine[:, left_at : left_at + pairs].reshape(-1, heads, row_share)
        right = factors[:, right_at : right_at + images].reshape(-1, heads, head_size)
        out = jnp.einsum("ahr,ahe->rhe", left, right, precision=lax.Precision.HIGH)
        return out.reshape(row_share, width)

    c_first = jnp.concatenate(
        [dot(four(mine, 0), four(factors, at), TN),
         headed(4 * images, at + images),
         headed(4 * images + pairs, at + 2 * images),
         dot(four(mine, images), four(factors, at + 3 * images), TN)], axis=1)
    wide = lambda begin: factors[:, begin : begin + 4 * images].reshape(dp_size * images, 4 * width)
    c_up = dot(four(mine, 2 * images), wide(at + 4 * images), TN)
    c_down = dot(four(mine, 3 * images), wide(at + 8 * images), TN)
    class_share = jnp.stack([c_first, c_up, c_down])

    squares = jnp.sum(early * early) + jnp.sum(late * late) + 0.5 * jnp.sum(class_share * class_share)
    squares = squares.reshape(1, 1)
    squares = squares + swap(squares, "seq", seq_size, 1)
    bit = 1
    while bit < dp_size:
        squares = squares + swap(squares, "dp", dp_size, bit)
        bit *= 2
    clip_norm = jnp.sqrt(squares[0, 0] + jnp.sum(grad_talk * grad_talk))
    factor = jnp.minimum(1.0, CLIP_NORM / clip_norm)
    early = both_cores(early, seq_size)
    late = both_cores(late, seq_size)
    self_share = jnp.stack(
        [jnp.concatenate([late[:, : 3 * width], early[:, :width]], axis=1),
         early[:, width : 5 * width], early[:, 5 * width :]])
    mats_share = jnp.stack([self_share, class_share])
    vecs_share = late[:, 3 * width :].T
    column_share = width // dp_size
    weight_rows = lax.dynamic_slice_in_dim(matrices, dp_index * row_share, row_share, 2)
    vector_columns = lax.dynamic_slice_in_dim(vectors, dp_index * column_share, column_share, 1)
    matrices_new, matrices_first, matrices_second = adam_step(
        weight_rows, mats_share * factor, matrices_moment1, matrices_moment2, LR_MATRIX, WEIGHT_DECAY
    )
    vectors_new, vectors_first, vectors_second = adam_step(
        vector_columns, vecs_share * factor, vectors_moment1, vectors_moment2, LR_VECTOR, 0.0
    )
    talking_new, talking_first, talking_second = adam_step(
        talking, grad_talk * factor, talking_moment1, talking_moment2, LR_TALKING, 0.0
    )
    matrices_average = EMA_RATE * matrices_ema + (1.0 - EMA_RATE) * matrices_new
    vectors_average = EMA_RATE * vectors_ema + (1.0 - EMA_RATE) * vectors_new
    talking_average = EMA_RATE * talking_ema + (1.0 - EMA_RATE) * talking_new
    return (
        patch_out, class_out, grad_tokens, grad_class, clip_norm,
        matrices_new, matrices_first, matrices_second, matrices_average,
        vectors_new, vectors_first, vectors_second, vectors_average,
        talking_new, talking_first, talking_second, talking_average,
    )


def solution(mesh):
    tokens = P(("dp", "seq"), None)
    by_group = P("dp", None)
    mats = P(None, None, "dp", None)
    vecs = P(None, "dp")
    body = functools.partial(on_device, mesh.shape["dp"], mesh.shape["seq"])
    return jax.shard_map(
        body,
        mesh=mesh,
        in_specs=(tokens, by_group, tokens, by_group, by_group, P(), mats, mats, mats,
                  P(), vecs, vecs, vecs, P(), P(), P(), P()),
        out_specs=(tokens, by_group, tokens, by_group, P(), mats, mats, mats, mats,
                   vecs, vecs, vecs, vecs, P(), P(), P(), P()),
        check_vma=False,
    )
```

```python
import functools

import jax
import jax.numpy as jnp
from jax import lax
from jax.experimental import pallas as pl
from jax.experimental.pallas import tpu as pltpu
from jax.sharding import PartitionSpec as P

STEP = 10
EPS_NORM = 1e-06
MASKED = -1e30
LR_MATRIX = 0.05
LR_VECTOR = 0.1
LR_TALKING = 0.2
BETA_ONE = 0.9
BETA_TWO = 0.999
ADAM_EPS = 1e-08
WEIGHT_DECAY = 0.05
EMA_RATE = 0.9
CLIP_NORM = 1.0
F32 = jnp.float32
BF16 = jnp.bfloat16
NN = (((1,), (0,)), ((), ()))
NT = (((1,), (1,)), ((), ()))
TN = (((0,), (0,)), ((), ()))
FORWARD_MIB, MIDDLE_MIB, BACKWARD_MIB = 56, 56, 56


def split(value):
    high = value.astype(BF16)
    return high, (value - high.astype(F32)).astype(BF16)


def mm(left, right, dims=NN):
    return lax.dot_general(left, right, dims, preferred_element_type=F32)


def mm3(left, right, dims=NN):
    return mm(left[0], right[0], dims) + (mm(left[0], right[1], dims) + mm(left[1], right[0], dims))


def dot3(left, right, dims=NN):
    return mm3(split(left), split(right), dims)


def norm_rows(values):
    average = jnp.mean(values, axis=-1, keepdims=True)
    centered = values - average
    variance = jnp.mean(centered * centered, axis=-1, keepdims=True)
    scale = lax.rsqrt(variance + EPS_NORM)
    return centered * scale, scale


def norm_back(grad, unit, scale):
    inner = jnp.mean(grad * unit, axis=-1, keepdims=True)
    return scale * (grad - jnp.mean(grad, axis=-1, keepdims=True) - unit * inner)


def gelu_both(values):
    half = 0.5 * (1.0 + lax.erf(values * 0.7071067811865476))
    slope = half + values * (0.3989422804014327 * jnp.exp(-0.5 * values * values))
    return values * half, slope


def row_sum(values):
    return jnp.sum(values, axis=0, keepdims=True)


def tail_forward(inputs, attended, w_out, w_up, w_down, vecs):
    projected = dot3(attended, w_out) + vecs[4:5]
    mixed = inputs + vecs[5:6] * projected
    unit, _ = norm_rows(mixed)
    normed = unit * vecs[6:7] + vecs[7:8]
    up_bias = jnp.concatenate([vecs[row : row + 1] for row in range(8, 12)], axis=1)
    hidden, slope = gelu_both(dot3(normed, w_up) + up_bias)
    lowered = dot3(hidden, w_down, NT) + vecs[12:13]
    return mixed + vecs[13:14] * lowered, (projected, mixed, hidden, slope, lowered)


def tail_backward(cot, kept, w_out, w_up, w_down, vecs):
    projected, mixed, hidden, slope, lowered = kept
    width = cot.shape[1]
    unit, scale = norm_rows(mixed)
    normed = unit * vecs[6:7] + vecs[7:8]
    d_lowered = cot * vecs[13:14]
    d_hidden = dot3(d_lowered, w_down) * slope
    d_normed = dot3(d_hidden, w_up, NT)
    d_mixed = cot + norm_back(d_normed * vecs[6:7], unit, scale)
    d_projected = d_mixed * vecs[5:6]
    d_attended = dot3(d_projected, w_out, NT)
    d_up = row_sum(d_hidden)
    rows = [
        row_sum(d_projected), row_sum(d_mixed * projected), row_sum(d_normed * unit), row_sum(d_normed),
        *[d_up[:, i * width : (i + 1) * width] for i in range(4)],
        row_sum(d_lowered), row_sum(cot * lowered),
    ]
    return d_mixed, d_attended, d_projected, d_hidden, d_lowered, normed, rows


def image_of(lengths_ref, images, positions):
    end = lengths_ref[0, 0]
    inside = (positions >= end).astype(jnp.int32)
    for image in range(1, images):
        end = end + lengths_ref[0, image]
        inside = inside + (positions >= end).astype(jnp.int32)
    return inside


def same_image(lengths_ref, images, place, slots, rows):
    queries = place * rows + lax.broadcasted_iota(jnp.int32, (1, rows), 1)
    query_image = image_of(lengths_ref, images, queries)
    parts = []
    for slot in range(slots):
        keys = jnp.bitwise_xor(place, slot) * rows + lax.broadcasted_iota(jnp.int32, (rows, 1), 0)
        parts.append(image_of(lengths_ref, images, keys) == query_image)
    return parts


def column_of(table, number):
    lanes = lax.broadcasted_iota(jnp.int32, (1, table.shape[1]), 1)
    return jnp.sum(jnp.where(lanes == number, table, 0.0), axis=1, keepdims=True)


def head_mask(heads, width):
    row = lax.broadcasted_iota(jnp.int32, (heads, width), 0)
    return jnp.where(lax.broadcasted_iota(jnp.int32, (heads, width), 1) // (width // heads) == row, 1.0, 0.0)


def spread(value, mask):
    return jnp.concatenate([value[i : i + 1] * mask for i in range(value.shape[0])], axis=0)


def repeat_rows(value, heads):
    shape = (heads, value.shape[1])
    return jnp.concatenate(
        [jnp.broadcast_to(value[i : i + 1], shape) for i in range(value.shape[0])], axis=0
    )


def fold_heads(value, mask):
    heads = mask.shape[0]
    return jnp.concatenate(
        [row_sum(value[i : i + heads] * mask) for i in range(0, value.shape[0], heads)], axis=0
    )


def head_sums(value, mask):
    return jnp.sum(spread(value, mask), axis=1, keepdims=True)


def rows_of(value, heads):
    return jnp.concatenate(
        [row_sum(value[i : i + heads]) for i in range(0, value.shape[0], heads)], axis=0
    )


def wide(column):
    return jnp.broadcast_to(column, (column.shape[0], 128))


def whole(shape):
    return pl.BlockSpec(shape, lambda *_: (0,) * len(shape))


def struct(shape, dtype=F32):
    return jax.ShapeDtypeStruct(shape, dtype)


def smem():
    return pl.BlockSpec(memory_space=pltpu.SMEM)


def anywhere():
    return pl.BlockSpec(memory_space=pl.ANY)


def weight_block(block, matrix, shape):
    return pl.BlockSpec((None, None) + shape[2:], lambda *_: (block, matrix, 0, 0))


def limit(mebibytes):
    return pltpu.CompilerParams(vmem_limit_bytes=mebibytes << 20)


def prepare_kernel(class_ref, w_ref, vecs_ref, talk_ref, talk_t_ref,
                   normed_ref, query_ref, value_ref, key_rows_ref, own_ref,
                   t1_ref, t2_ref, t1_rows_ref, t2_rows_ref):
    width = class_ref.shape[1]
    heads = talk_ref.shape[0]
    size = width // heads
    mask = head_mask(heads, width)
    unit, _ = norm_rows(class_ref[...])
    normed = unit * vecs_ref[14:15, :] + vecs_ref[15:16, :]
    both = dot3(normed, w_ref[:, : 3 * width])
    query = both[:, :width] + vecs_ref[16:17, :]
    normed_ref[...] = normed
    query_ref[...] = query
    value_ref[...] = both[:, 2 * width :] + vecs_ref[17:18, :]
    scale = size ** (-0.5)
    key_rows_ref[...] = dot3(spread(query, mask), w_ref[:, width : 2 * width], NT) * scale
    own_ref[...] = wide(head_sums(query * both[:, width : 2 * width], mask) * scale)
    head_of = lax.broadcasted_iota(jnp.int32, (width, 1), 0) // size
    talk, talk_t = talk_ref[...], talk_t_ref[...]
    t1 = t2 = t1_rows = t2_rows = 0.0
    for head in range(heads):
        here = head_of == head
        t1 = t1 + jnp.where(here, talk_t[head : head + 1, :], 0.0)
        t2 = t2 + jnp.where(here, talk[head : head + 1, heads:], 0.0)
        t1_rows = t1_rows + mask[head : head + 1] * talk[:, head : head + 1]
        t2_rows = t2_rows + mask[head : head + 1] * talk_t[heads:, head : head + 1]
    t1_ref[...], t2_ref[...], t1_rows_ref[...], t2_rows_ref[...] = t1, t2, t1_rows, t2_rows


def prepare(class_tokens, matrices, vectors, talking):
    images, width = class_tokens.shape
    heads = talking.shape[0]
    pairs = images * heads
    outs = [struct((images, width))] * 3 + [
        struct((pairs, width)), struct((pairs, 128)),
        struct((width, heads)), struct((width, heads + 1)),
        struct((heads, width)), struct((heads + 1, width)),
    ]
    operands = [class_tokens, matrices, vectors, talking, talking.T]
    specs = [whole(operand.shape) for operand in operands]
    specs[1] = weight_block(1, 0, matrices.shape)
    return pl.pallas_call(
        prepare_kernel,
        grid=(1,),
        in_specs=specs,
        out_specs=[whole(out.shape) for out in outs],
        out_shape=outs,
        compiler_params=limit(16),
        cost_estimate=pl.CostEstimate(flops=1 << 30, bytes_accessed=3 << 20, transcendentals=0),
        name="prepare",
    )(*operands)


def forward_kernel(slots, images, *refs):
    place_ref, lengths_ref = refs[:2]
    token_refs = refs[2 : 2 + slots]
    w_ref, vecs_ref, t1_ref, t2_ref, key_rows_ref, mats_ref = refs[2 + slots : 8 + slots]
    (
        p_high_ref, p_low_ref, pv_ref, pv_bias_ref, attended_ref, unit_ref,
        kt_high_ref, kt_low_ref, v_high_ref, v_low_ref, query_ref,
        patch_ref, projected_ref, mixed_ref, hidden_ref, slope_ref, lowered_ref, packed_ref, scores_ref,
        k_high, k_low, vt_high, vt_low, qt, bias, attended_t, w_up, w_down, arrived,
    ) = refs[8 + slots :]
    rows, width = token_refs[0].shape
    head = pl.program_id(0)
    heads = pl.num_programs(0)
    head_size = width // 8
    place = place_ref[0]
    fetch_up = pltpu.make_async_copy(mats_ref.at[0, 1], w_up, arrived.at[0])
    fetch_down = pltpu.make_async_copy(mats_ref.at[0, 2], w_down, arrived.at[1])

    @pl.when(head == 0)
    def _():
        fetch_up.start()
        fetch_down.start()
        w_kv = split(w_ref[:, width : 3 * width])
        shift = vecs_ref[3:4, :]
        inside = same_image(lengths_ref, images, place, slots, rows)
        for slot in range(slots):
            unit, _ = norm_rows(token_refs[slot][...])
            normed = unit * vecs_ref[0:1, :] + vecs_ref[1:2, :]
            here = pl.ds(slot * rows, rows)
            unit_ref[here, :] = unit
            normed = split(normed)
            both = mm3(normed, w_kv)
            keys, values = both[:, :width], both[:, width:] + shift
            k_high[here, :], k_low[here, :] = split(keys)
            v_high_ref[here, :], v_low_ref[here, :] = split(values)
            kt_high_ref[:, here], kt_low_ref[:, here] = split(keys.T)
            vt_high[:, here], vt_low[:, here] = split(values.T)
            bias[here, :] = jnp.where(inside[slot], 0.0, MASKED)
            if slot == 0:
                query = mm3(normed, split(w_ref[:, :width])) + vecs_ref[2:3, :]
                query = query * head_size ** (-0.5)
                query_ref[...] = query
                qt[...] = query.T

    mixed = mm3((k_high[...], k_low[...]), split(qt[...] * column_of(t1_ref[...], head)))
    mixed = mixed + bias[...]
    exponentials = jnp.exp(mixed - jnp.max(mixed, axis=0, keepdims=True))
    probs = split(exponentials * (1.0 / jnp.sum(exponentials, axis=0, keepdims=True)))
    p_high_ref[0], p_low_ref[0] = probs
    values = mm3((vt_high[...], vt_low[...]), probs)
    pv_ref[0] = values
    term = values * column_of(t2_ref[...], head)

    @pl.when(head == 0)
    def _():
        attended_t[...] = term

    @pl.when(head > 0)
    def _():
        attended_t[...] += term

    @pl.when(head == heads - 1)
    def _():
        inside = jnp.where(bias[...] < 0.0, 0.0, 1.0).astype(BF16)
        summed = mm(vt_high[...], inside) + mm(vt_low[...], inside)
        pv_bias_ref[...] = summed
        attended = (attended_t[...] + summed * t2_ref[:, 8:9]).T
        attended_ref[...] = attended
        fetch_up.wait()
        fetch_down.wait()
        vecs = vecs_ref[...]
        patch, kept = tail_forward(
            token_refs[0][...], attended, w_ref[:, 3 * width :], w_up[...], w_down[...], vecs
        )
        patch_ref[...] = patch
        for ref, value in zip((projected_ref, mixed_ref, hidden_ref, slope_ref, lowered_ref), kept):
            ref[...] = value
        unit, _ = norm_rows(patch)
        normed = split(unit * vecs[14:15] + vecs[15:16])
        pairs = images * 8
        image = lax.broadcasted_iota(jnp.int32, (pairs, 1), 0) // 8
        positions = place * rows + lax.broadcasted_iota(jnp.int32, (1, rows), 1)
        belong = image_of(lengths_ref, images, positions) == image
        scores = mm3(split(key_rows_ref[...]), normed, NT)
        scores = jnp.where(belong, scores, MASKED)
        scores_ref[...] = scores
        top = jnp.max(scores, axis=1, keepdims=True)
        weights = jnp.where(belong, jnp.exp(scores - top), 0.0)
        packed_ref[:, :width] = mm3(split(weights), normed)
        lane = lax.broadcasted_iota(jnp.int32, (1, 128), 1)
        total = jnp.sum(weights, axis=1, keepdims=True)
        packed_ref[:, width:] = jnp.where(lane < 64, top, total)


def forward(place, lengths, token_slots, matrices, vectors, t1, t2, key_rows):
    slots, (rows, width) = len(token_slots), token_slots[0].shape
    total, heads = slots * rows, 8
    hidden = matrices.shape[3]
    pairs = key_rows.shape[0]
    by_head = lambda *shape: pl.BlockSpec((1,) + shape, lambda g: (g, 0, 0))
    outs = [struct((heads, total, rows), BF16)] * 2 + [struct((heads, width, rows))]
    specs = [by_head(*out.shape[1:]) for out in outs]
    rest = [
        struct((width, rows)), struct((rows, width)), struct((total, width)),
        struct((width, total), BF16), struct((width, total), BF16),
        struct((total, width), BF16), struct((total, width), BF16), struct((rows, width)),
        struct((rows, width)), struct((rows, width)), struct((rows, width)),
        struct((rows, hidden)), struct((rows, hidden)), struct((rows, width)),
        struct((pairs, width + 128)), struct((pairs, rows)),
    ]
    operands = [*token_slots, matrices, vectors, t1, t2, key_rows, matrices]
    in_specs = [whole(operand.shape) for operand in operands]
    in_specs[slots] = weight_block(0, 0, matrices.shape)
    in_specs[-1] = anywhere()
    flops = 2 * 3 * ((2 * heads + 3) * total + 9 * width) * rows * width
    return pl.pallas_call(
        functools.partial(forward_kernel, slots, lengths.shape[1]),
        grid=(heads,),
        in_specs=[smem(), smem()] + in_specs,
        out_specs=specs + [whole(out.shape) for out in rest],
        out_shape=outs + rest,
        scratch_shapes=[
            pltpu.VMEM((total, width), BF16),
            pltpu.VMEM((total, width), BF16),
            pltpu.VMEM((width, total), BF16),
            pltpu.VMEM((width, total), BF16),
            pltpu.VMEM((width, rows), F32),
            pltpu.VMEM((total, rows), F32),
            pltpu.VMEM((width, rows), F32),
            pltpu.VMEM((width, hidden), F32),
            pltpu.VMEM((width, hidden), F32),
            pltpu.SemaphoreType.DMA((2,)),
        ],
        compiler_params=limit(FORWARD_MIB),
        cost_estimate=pl.CostEstimate(
            flops=flops, bytes_accessed=24 << 20, transcendentals=heads * total * rows
        ),
        name="forward",
    )(place, lengths, *operands)


def middle_kernel(images, *refs):
    (
        place_ref, parts_ref, vecs_ref, normed_c_ref, query_c_ref, value_c_ref, key_rows_ref, own_ref,
        class_ref, cot_class_ref, cot_patch_ref, patch_ref, scores_ref, attended_ref,
        projected_ref, mixed_ref, hidden_ref, slope_ref, lowered_ref, mats_ref,
        class_out_ref, d_attended_ref, d_mixed_ref, keep_ref, send_ref, partial_ref,
        factors_ref, vec_rows_ref, class_terms_ref,
        wc0, wc1, wc2, ws0, ws1, ws2, arrived,
    ) = refs
    width = class_ref.shape[1]
    heads = 8
    size = width // heads
    fetches = [
        pltpu.make_async_copy(source, target, arrived.at[number])
        for number, (source, target) in enumerate([
            (mats_ref.at[1, 0], wc0), (mats_ref.at[1, 1], wc1), (mats_ref.at[1, 2], wc2),
            (mats_ref.at[0, 2], ws2), (mats_ref.at[0, 1], ws1), (mats_ref.at[0, 0], ws0),
        ])
    ]
    for fetch in fetches:
        fetch.start()
    vecs = vecs_ref[...]
    vecs_s, vecs_c = vecs[:14], vecs[14:]
    mask = head_mask(heads, width)
    first = jnp.where(place_ref[0] == 0, 1.0, 0.0)
    slots = parts_ref.shape[0]
    parts = [parts_ref[slot] for slot in range(slots)]
    own_score = own_ref[:, :1]
    normed_c = normed_c_ref[...]
    normed_rep = repeat_rows(normed_c, heads)
    top = own_score
    for part in parts:
        top = jnp.maximum(top, part[:, width : width + 1])
    own_weight = jnp.exp(own_score - top)
    total, summed = own_weight, own_weight * normed_rep
    for part in parts:
        rescale = jnp.exp(part[:, width : width + 1] - top)
        total = total + part[:, width + 64 : width + 65] * rescale
        summed = summed + part[:, :width] * rescale
    value_rows = summed / total
    own_prob = own_weight / total
    fetches[0].wait()
    w_v = split(wc0[:, 2 * width : 3 * width])
    class_attended = fold_heads(mm3(split(value_rows), w_v), mask) + vecs_c[3:4]
    fetches[1].wait()
    fetches[2].wait()
    w_out_c = wc0[:, 3 * width :]
    class_out, kept_c = tail_forward(class_ref[...], class_attended, w_out_c, wc1[...], wc2[...], vecs_c)
    class_out_ref[...] = class_out
    d_mixed_c, d_attended_c, d_projected_c, d_hidden_c, d_lowered_c, normed2_c, tail_rows_c = (
        tail_backward(cot_class_ref[...], kept_c, w_out_c, wc1[...], wc2[...], vecs_c)
    )
    delta = head_sums(d_attended_c * class_attended, mask)
    cot_rows = mm3(split(spread(d_attended_c, mask)), w_v, NT)
    cot_const = head_sums(d_attended_c * vecs_c[3:4], mask)
    scores = scores_ref[...]
    probs = jnp.where(scores > 0.5 * MASKED, jnp.exp(scores - top) * (1.0 / total), 0.0)
    unit_p, scale_p = norm_rows(patch_ref[...])
    normed_p = split(unit_p * vecs_c[0:1] + vecs_c[1:2])
    cot_split = split(cot_rows)
    d_scores = probs * (mm3(cot_split, normed_p, NT) + cot_const - delta)
    d_own = own_prob * (head_sums(d_attended_c * value_c_ref[...], mask) - delta)
    key_rows = key_rows_ref[...]
    d_split = split(d_scores)
    d_normed_p = mm3(d_split, split(key_rows), TN) + mm3(split(probs), cot_split, TN)
    partial_ref[...] = mm3(d_split, normed_p)
    cot = cot_patch_ref[...] + norm_back(d_normed_p * vecs_c[0:1], unit_p, scale_p)
    class_terms_ref[...] = jnp.concatenate(
        [rows_of(d_own * key_rows + own_prob * cot_rows, heads), d_mixed_c], axis=0
    )
    query_c = query_c_ref[...]
    chunks = lambda value: [value[:, i * width : (i + 1) * width] for i in range(4)]
    factors_ref[...] = jnp.concatenate(
        [normed_c, class_attended, normed2_c, d_lowered_c, d_own * normed_rep, value_rows,
         jnp.zeros_like(query_c), query_c * size ** (-0.5), d_attended_c, d_projected_c,
         *chunks(d_hidden_c), *chunks(kept_c[2])], axis=0)
    for fetch in fetches[3:]:
        fetch.wait()
    kept = tuple(ref[...] for ref in (projected_ref, mixed_ref, hidden_ref, slope_ref, lowered_ref))
    d_mixed, d_attended, d_projected, d_hidden, d_lowered, normed, tail_rows = tail_backward(
        cot, kept, ws0[:, 3 * width :], ws1[...], ws2[...], vecs_s
    )
    d_mixed_ref[...] = d_mixed
    d_attended_ref[...] = d_attended
    zero = jnp.zeros((1, width), F32)
    vec_rows_ref[...] = jnp.concatenate(
        [zero] * 4 + tail_rows
        + [row_sum(d_normed_p * unit_p), row_sum(d_normed_p), zero, row_sum(d_attended_c) * first]
        + [row * first for row in tail_rows_c], axis=0)
    g_out = dot3(attended_ref[...], d_projected, TN)
    g_up = dot3(normed, d_hidden, TN)
    g_down = dot3(d_lowered, hidden_ref[...], TN)
    even = jnp.bitwise_and(place_ref[0], 1) == 0
    hidden = g_up.shape[1]
    keep_ref[:, :hidden] = jnp.where(even, g_up, g_down)
    send_ref[:, :hidden] = jnp.where(even, g_down, g_up)
    left = g_out[:, :256]
    right = jnp.concatenate([g_out[:, 256:], jnp.zeros((width, 512 - width), F32)], axis=1)
    keep_ref[:, hidden:] = jnp.where(even, left, right)
    send_ref[:, hidden:] = jnp.where(even, right, left)


def middle(place, parts, vectors, prepared, class_tokens, cot_class, cot_patch, forwarded, matrices):
    images, width = class_tokens.shape
    rows = cot_patch.shape[0]
    hidden = matrices.shape[3]
    pairs = parts.shape[1]
    operands = [parts, vectors, *prepared, class_tokens, cot_class, cot_patch, *forwarded, matrices]
    in_specs = [whole(operand.shape) for operand in operands]
    in_specs[-1] = anywhere()
    outs = [
        struct((images, width)), struct((rows, width)), struct((rows, width)),
        struct((width, hidden + 256)), struct((width, hidden + 256)), struct((pairs, width)),
        struct((16 * images + 2 * pairs, width)), struct((28, width)), struct((2 * images, width)),
    ]
    return pl.pallas_call(
        functools.partial(middle_kernel, images),
        grid=(1,),
        in_specs=[smem()] + in_specs,
        out_specs=[whole(out.shape) for out in outs],
        out_shape=outs,
        scratch_shapes=[pltpu.VMEM((width, hidden), F32)] * 6 + [pltpu.SemaphoreType.DMA((6,))],
        compiler_params=limit(MIDDLE_MIB),
        cost_estimate=pl.CostEstimate(flops=8 << 30, bytes_accessed=28 << 20, transcendentals=1 << 19),
        name="middle",
    )(place, *operands)


def class_kernel(place_ref, partial_ref, terms_ref, vec_rows_ref, class_ref, vecs_ref, w_ref, factors_ref,
                 grad_ref, vec_out_ref, factors_out_ref):
    images, width = class_ref.shape
    pairs = partial_ref.shape[0]
    heads = pairs // images
    mask = head_mask(heads, width)
    first = jnp.where(place_ref[0] == 0, 1.0, 0.0)
    at = 4 * images
    query_rows = partial_ref[...] + factors_ref[at : at + pairs, :]
    w_k, w_q = w_ref[:, width : 2 * width], w_ref[:, :width]
    d_query = fold_heads(dot3(query_rows, w_k), mask) * (width // heads) ** (-0.5)
    d_normed = dot3(d_query, w_q, NT) + terms_ref[:images, :]
    unit, scale = norm_rows(class_ref[...])
    grad_ref[...] = terms_ref[images:, :] + norm_back(d_normed * vecs_ref[14:15, :], unit, scale)
    added = [row_sum(d_normed * unit), row_sum(d_normed), row_sum(d_query)]
    zero = jnp.zeros((14, width), F32)
    vec_out_ref[...] = vec_rows_ref[...] + first * jnp.concatenate([zero, *added, zero[:11]], axis=0)
    factors_out_ref[...] = factors_ref[...]
    factors_out_ref[at : at + pairs, :] = query_rows
    at = at + 2 * pairs
    factors_out_ref[at : at + images, :] = d_query


def class_finish(place, partial, terms, vec_rows, class_tokens, vectors, matrices, factors):
    operands = [partial, terms, vec_rows, class_tokens, vectors, matrices, factors]
    specs = [whole(operand.shape) for operand in operands]
    specs[5] = weight_block(1, 0, matrices.shape)
    outs = [struct(class_tokens.shape), struct(vec_rows.shape), struct(factors.shape)]
    return pl.pallas_call(
        class_kernel,
        grid=(1,),
        in_specs=[smem()] + specs,
        out_specs=[whole(out.shape) for out in outs],
        out_shape=outs,
        compiler_params=limit(16),
        cost_estimate=pl.CostEstimate(flops=1 << 29, bytes_accessed=3 << 20, transcendentals=0),
        name="class_finish",
    )(place, *operands)


def class_weights_kernel(images, mine_ref, factors_ref, grads_ref, squares_ref):
    groups, _, width = factors_ref.shape
    heads = 8
    pairs = images * heads
    mask = head_mask(heads, width)
    at = 4 * images + 2 * pairs

    def rows(ref, begin, count=images):
        return jnp.concatenate([ref[g, begin : begin + count, :] for g in range(groups)], axis=0)

    def chunked(begin):
        return jnp.concatenate([rows(factors_ref, begin + i * images) for i in range(4)], axis=1)

    def headed(left, right):
        return dot3(rows(mine_ref, left, pairs), spread(rows(factors_ref, right), mask), TN)

    grads_ref[0, :, :width] = dot3(rows(mine_ref, 0), rows(factors_ref, at), TN)
    grads_ref[0, :, width : 2 * width] = headed(4 * images, at + images)
    grads_ref[0, :, 2 * width : 3 * width] = headed(4 * images + pairs, at + 2 * images)
    grads_ref[0, :, 3 * width :] = dot3(rows(mine_ref, images), rows(factors_ref, at + 3 * images), TN)
    grads_ref[1] = dot3(rows(mine_ref, 2 * images), chunked(at + 4 * images), TN)
    grads_ref[2] = dot3(rows(mine_ref, 3 * images), chunked(at + 8 * images), TN)
    grads = grads_ref[...]
    squares_ref[...] = jnp.broadcast_to(jnp.sum(grads * grads), squares_ref.shape)


def class_weights(images, mine, factors):
    outs = [struct((3, mine.shape[2], 4 * factors.shape[2])), struct((8, 128))]
    return pl.pallas_call(
        functools.partial(class_weights_kernel, images),
        grid=(1,),
        in_specs=[whole(mine.shape), whole(factors.shape)],
        out_specs=[whole(out.shape) for out in outs],
        out_shape=outs,
        compiler_params=limit(32),
        cost_estimate=pl.CostEstimate(flops=1 << 29, bytes_accessed=3 << 20, transcendentals=0),
        name="class_weights",
    )(mine, factors)


def backward_kernel(slots, images, dp_size, *refs):
    (
        place_ref, lengths_ref, p_high_ref, p_low_ref, pv_ref, pv_bias_ref, cot_ref,
        kt_high, kt_low, v_high, v_low, query_ref, t1_ref, t2_ref, t1_rows, t2_rows,
        unit_ref, vec_rows_ref, vecs_ref, w_ref,
    ) = refs[:20]
    d_normed_refs = refs[20 : 20 + slots]
    keep_ref, send_ref, d_keys, d_values, c1, c2, cot_t, qt, d_qt = refs[20 + slots :]
    rows, width = cot_ref.shape
    head = pl.program_id(0)
    heads = pl.num_programs(0)
    size = width // 8
    lanes = lax.broadcasted_iota(jnp.int32, (1, 128), 1)

    @pl.when(head == 0)
    def _():
        cot_t[...] = cot_ref[...].T
        qt[...] = query_ref[...].T
        d_qt[...] = jnp.zeros_like(d_qt)
        d_keys[...] = jnp.zeros_like(d_keys)
        c1[...] = jnp.zeros_like(c1)
        c2[...] = jnp.where(
            lanes == 8, jnp.sum(cot_t[...] * pv_bias_ref[...], axis=1, keepdims=True), 0.0
        )
        inside = jnp.concatenate(same_image(lengths_ref, images, place_ref[0], slots, rows), axis=0)
        inside = jnp.where(inside, 1.0, 0.0).astype(BF16)
        high, low = split(cot_ref[...] * t2_rows[8:9, :])
        d_values[...] = mm(inside, high) + mm(inside, low)

    t1_column = column_of(t1_ref[...], head)
    t2_column = column_of(t2_ref[...], head)
    crossed = cot_t[...] * pv_ref[0]
    c2[...] += jnp.where(lanes == head, jnp.sum(crossed, axis=1, keepdims=True), 0.0)
    delta = jnp.sum(crossed * t2_column, axis=0, keepdims=True)
    d_probs = mm3((v_high[...], v_low[...]), split(cot_t[...] * t2_column))
    probs = (p_high_ref[0], p_low_ref[0])
    d_values[...] += mm3(probs, split(cot_ref[...] * t2_rows[pl.ds(head, 1), :]))
    d_mixed = (probs[0].astype(F32) + probs[1].astype(F32)) * (d_probs - delta)
    d_mixed = split(d_mixed)
    d_keys[...] += mm3(d_mixed, split(query_ref[...] * t1_rows[pl.ds(head, 1), :]))
    back = mm3((kt_high[...], kt_low[...]), d_mixed)
    d_qt[...] += back * t1_column
    c1[...] += jnp.where(lanes == head, jnp.sum(back * qt[...], axis=1, keepdims=True), 0.0)

    @pl.when(head == heads - 1)
    def _():
        d_query = d_qt[...].T * size ** (-0.5)
        dq, dk, dv = split(d_query), split(d_keys[...]), split(d_values[...])
        w_q, w_k, w_v = (split(w_ref[:, i * width : (i + 1) * width]) for i in range(3))
        unit = unit_ref[...]
        normed = split(unit * vecs_ref[0:1, :] + vecs_ref[1:2, :])
        d_normed = mm3(dk, w_k, NT) + mm3(dv, w_v, NT)
        first = d_normed[:rows] + mm3(dq, w_q, NT)
        d_normed_refs[0][...] = first
        gain, shift = row_sum(first * unit[:rows]), row_sum(first)
        for slot in range(1, slots):
            piece = d_normed[slot * rows : (slot + 1) * rows]
            d_normed_refs[slot][...] = piece
            gain = gain + row_sum(piece * unit[slot * rows : (slot + 1) * rows])
            shift = shift + row_sum(piece)
        own = (normed[0][:rows], normed[1][:rows])
        g_q, g_k, g_v = mm3(own, dq, TN), mm3(normed, dk, TN), mm3(normed, dv, TN)
        added = jnp.concatenate(
            [gain, shift, row_sum(d_query), row_sum(d_values[...]), jnp.zeros((4, width), F32)], axis=0
        )
        vec_rows = jnp.concatenate([vec_rows_ref[0:8, :] + added, vec_rows_ref[8:28, :]], axis=0)
        fold = lambda value: jnp.concatenate(
            [row_sum(value[i * size : (i + 1) * size]) for i in range(8)], axis=0
        )
        pre, post = fold(c1[...]).T[:8, :], fold(c2[...])
        count = vec_rows.shape[0]
        talk = jnp.concatenate([pre, post[:, :9], jnp.zeros((8, 128 - count - 17), F32)], axis=1)
        block = width // dp_size
        talk = jnp.concatenate([talk, jnp.zeros((block - 8, 128 - count), F32)], axis=0)
        talk = jnp.concatenate([talk] * dp_size, axis=0)
        small = jnp.concatenate([vec_rows.T, talk], axis=1)
        even = jnp.bitwise_and(place_ref[0], 1) == 0
        left = jnp.concatenate([g_q, g_k[:, :256]], axis=1)
        right = jnp.concatenate([g_k[:, 256:], g_v, small], axis=1)
        keep_ref[...] = jnp.where(even, left, right)
        send_ref[...] = jnp.where(even, right, left)


def backward(dp_size, place, lengths, forwarded, cot, tables, vec_rows, vectors, matrices):
    p_high, p_low, pv, pv_bias, unit, kt_high, kt_low, v_high, v_low, query = forwarded
    rows, width = cot.shape
    heads, total, _ = p_high.shape
    slots = total // rows
    by_head = lambda shape: pl.BlockSpec((1,) + shape[1:], lambda g: (g, 0, 0))
    operands = [p_high, p_low, pv, pv_bias, cot, kt_high, kt_low, v_high, v_low, query, *tables,
                unit, vec_rows, vectors, matrices]
    specs = [by_head(operand.shape) for operand in operands[:3]]
    specs += [whole(operand.shape) for operand in operands[3:]]
    specs[-1] = weight_block(0, 0, matrices.shape)
    outs = [struct((rows, width))] * slots + [struct((width, 640))] * 2
    flops = 2 * 3 * (4 * heads + 6) * total * rows * width
    return pl.pallas_call(
        functools.partial(backward_kernel, slots, lengths.shape[1], dp_size),
        grid=(heads,),
        in_specs=[smem(), smem()] + specs,
        out_specs=[whole(out.shape) for out in outs],
        out_shape=outs,
        scratch_shapes=[pltpu.VMEM((total, width), F32)] * 2
        + [pltpu.VMEM((width, 128), F32)] * 2
        + [pltpu.VMEM((width, rows), F32)] * 3,
        compiler_params=limit(BACKWARD_MIB),
        cost_estimate=pl.CostEstimate(flops=flops, bytes_accessed=20 << 20, transcendentals=0),
        name="backward",
    )(place, lengths, *operands)


def token_grad_kernel(tokens_ref, vecs_ref, near_ref, far_ref, tail_ref, grad_ref):
    unit, scale = norm_rows(tokens_ref[...])
    d_normed = near_ref[...] + far_ref[...]
    grad_ref[...] = tail_ref[...] + norm_back(d_normed * vecs_ref[0:1, :], unit, scale)


def token_grad(*operands):
    tokens = operands[0]
    return pl.pallas_call(
        token_grad_kernel,
        out_shape=struct(tokens.shape),
        cost_estimate=pl.CostEstimate(flops=1 << 21, bytes_accessed=2 << 20, transcendentals=0),
        name="token_grad",
    )(*operands)


def squares_kernel(dp_size, place_ref, early_ref, late_ref, class_ref, out_ref):
    late = late_ref[...]
    lane = lax.broadcasted_iota(jnp.int32, late.shape, 1)
    talk = jnp.logical_and(jnp.bitwise_and(place_ref[0], 1) == 1, jnp.logical_and(lane >= 540, lane < 557))
    late = late * late * jnp.where(talk, 1.0 / dp_size, 1.0)
    early = early_ref[...]
    out_ref[...] = 0.5 * class_ref[...] + (jnp.sum(late) + jnp.sum(early * early))


def squares_of(dp_size, place, early, late, class_squares):
    vmem = pl.BlockSpec(memory_space=pltpu.VMEM)
    return pl.pallas_call(
        functools.partial(squares_kernel, dp_size),
        in_specs=[smem(), vmem, vmem, vmem],
        out_shape=struct((8, 128)),
        cost_estimate=pl.CostEstimate(flops=1 << 18, bytes_accessed=1 << 19, transcendentals=0),
        name="squares",
    )(place, early, late, class_squares)


def adam_step(weight, gradient, moment1, moment2, rate, decay):
    first = BETA_ONE * moment1 + (1.0 - BETA_ONE) * gradient
    second = BETA_TWO * moment2 + (1.0 - BETA_TWO) * gradient * gradient
    first_hat = first * (1.0 / (1.0 - BETA_ONE**STEP))
    second_hat = second * (1.0 / (1.0 - BETA_TWO**STEP))
    updated = weight - rate * (first_hat / (jnp.sqrt(second_hat) + ADAM_EPS) + decay * weight)
    return (updated, first, second)


def adam_kernel(*refs):
    (
        place_ref, squares_ref, early_own, early_other, late_own, late_other, class_ref,
        w_ref, m1_ref, m2_ref, ema_ref, v_ref, v1_ref, v2_ref, v_ema_ref, t_ref, t1_ref, t2_ref, t_ema_ref,
    ) = refs[:19]
    norm_ref, new_ref, first_ref, second_ref, average_ref = refs[19:24]
    v_outs, t_outs = refs[24:28], refs[28:32]
    grads = refs[32]
    step = pl.program_id(0)
    norm = jnp.sqrt(squares_ref[0:1, 0:1])
    factor = jnp.minimum(1.0, CLIP_NORM / norm)

    def store(outs, weight, gradient, moment1, moment2, ema, rate, decay):
        updated, first, second = adam_step(weight, gradient * factor, moment1, moment2, rate, decay)
        average = EMA_RATE * ema + (1.0 - EMA_RATE) * updated
        for out, value in zip(outs, (updated, first, second, average)):
            out[...] = value

    @pl.when(step == 0)
    def _():
        norm_ref[...] = jnp.broadcast_to(norm, norm_ref.shape)
        even = jnp.bitwise_and(place_ref[0], 1) == 0
        pair = lambda own, other: (jnp.where(even, own[...], other[...]), jnp.where(even, other[...], own[...]))
        early_left, early_right = pair(early_own, early_other)
        late_left, late_right = pair(late_own, late_other)
        hidden = grads.shape[2]
        grads[0] = jnp.concatenate(
            [late_left, late_right[:, :512], early_left[:, hidden:], early_right[:, hidden : hidden + 128]],
            axis=1,
        )
        grads[1] = early_left[:, :hidden]
        grads[2] = early_right[:, :hidden]
        small = late_right[:, 512:]
        rows, count = small.shape[0], v_ref.shape[0]
        store(v_outs, v_ref[...], small.T[:count, :], v1_ref[...], v2_ref[...], v_ema_ref[...], LR_VECTOR, 0.0)
        talk = small[:8, count : count + 17]
        store(t_outs, t_ref[...], talk, t1_ref[...], t2_ref[...], t_ema_ref[...], LR_TALKING, 0.0)

    self_grad = grads[jnp.minimum(step, 2)]
    grad = jnp.where(step < 3, self_grad, class_ref[jnp.maximum(step - 3, 0)])
    store((new_ref, first_ref, second_ref, average_ref), w_ref[...], grad, m1_ref[...], m2_ref[...],
          ema_ref[...], LR_MATRIX, WEIGHT_DECAY)


def optimizer(place, squares, early, late, class_share, mats, vecs, talks):
    shape = mats[1].shape
    block = pl.BlockSpec((None, None) + shape[2:], lambda i: (i // 3, i % 3, 0, 0))
    operands = [squares, *early, *late, class_share, *mats, *vecs, *talks]
    specs = [whole(operand.shape) for operand in operands]
    specs[6:10] = [block] * 4
    outs = [struct((8, 128))] + [struct(shape)] * 4
    outs += [struct(vecs[0].shape)] * 4 + [struct(talks[0].shape)] * 4
    out_specs = [whole(out.shape) for out in outs]
    out_specs[1:5] = [block] * 4
    return pl.pallas_call(
        adam_kernel,
        grid=(6,),
        in_specs=[smem()] + specs,
        out_specs=out_specs,
        out_shape=outs,
        scratch_shapes=[pltpu.VMEM((3,) + shape[2:], F32)],
        compiler_params=limit(24),
        cost_estimate=pl.CostEstimate(flops=1 << 23, bytes_accessed=14 << 20, transcendentals=0),
        name="optimizer",
    )(place, *operands)


def swap(value, axis, size, bit):
    return lax.ppermute(value, axis, [(place, place ^ bit) for place in range(size)])


def gather_slots(own, axis, size):
    found = {0: own}
    bit = size // 2
    while bit:
        for slot in sorted(found):
            found[slot | bit] = swap(found[slot], axis, size, bit)
        bit //= 2
    return [found[slot] for slot in range(size)]


def reduce_rows(keep, send, dp_size, seq_size):
    dp_index = lax.axis_index("dp")
    value = keep + swap(send, "seq", seq_size, 1)
    value = value.reshape(dp_size, -1, keep.shape[1])
    bit = 1
    while bit < dp_size:
        mine = (dp_index // bit) % 2
        pairs = value.reshape((-1, 2) + value.shape[1:])
        kept = lax.dynamic_index_in_dim(pairs, mine, 1, keepdims=False)
        sent = lax.dynamic_index_in_dim(pairs, 1 - mine, 1, keepdims=False)
        value = kept + swap(sent, "dp", dp_size, bit)
        bit *= 2
    value = value[0]
    bit = 2
    while bit < seq_size:
        value = value + swap(value, "seq", seq_size, bit)
        bit *= 2
    return value


def gather_rows(value, dp_size, seq_size):
    value = value[None]
    for axis, size in (("dp", dp_size), ("seq", seq_size)):
        if axis == "seq":
            value = value[None]
        bit = 1
        while bit < size:
            value = jnp.concatenate([value, swap(value, axis, size, bit)], axis=0)
            bit *= 2
    return value


def on_device(
    dp_size, seq_size,
    tokens, class_tokens, cot_patch, cot_class, lengths,
    matrices, matrices_moment1, matrices_moment2, matrices_ema,
    vectors, vectors_moment1, vectors_moment2, vectors_ema,
    talking, talking_moment1, talking_moment2, talking_ema,
):
    rows, width = tokens.shape
    images = class_tokens.shape[0]
    seq_index = lax.axis_index("seq")
    dp_index = lax.axis_index("dp")
    place = seq_index.astype(jnp.int32).reshape(1)
    row_share = width // dp_size

    token_slots = gather_slots(tokens, "seq", seq_size)
    *prepared, t1, t2, t1_rows, t2_rows = prepare(class_tokens, matrices, vectors, talking)
    (
        p_high, p_low, pv, pv_bias, attended, unit, kt_high, kt_low, v_high, v_low, query,
        patch_out, *kept, packed, scores,
    ) = forward(place, lengths, token_slots, matrices, vectors, t1, t2, prepared[3])
    parts = lax.all_gather(packed, "seq", axis=0)
    (
        class_out, d_attended, d_mixed, early_keep, early_send, partial, factors, vec_rows, class_terms,
    ) = middle(
        place, parts, vectors, prepared, class_tokens, cot_class, cot_patch,
        [patch_out, scores, attended, *kept], matrices,
    )

    bit = 1
    while bit < seq_size:
        partial = partial + swap(partial, "seq", seq_size, bit)
        bit *= 2
    grad_class, vec_rows, factors = class_finish(
        place, partial, class_terms, vec_rows, class_tokens, vectors, matrices, factors
    )
    share = factors.shape[0] // seq_size
    found = gather_rows(
        lax.dynamic_slice_in_dim(factors, seq_index * share, share, 0), dp_size, seq_size
    )
    bit = 1
    order = seq_index
    found = found.transpose(1, 0, 2, 3)
    pieces = [found[:, slot] for slot in range(seq_size)]
    while bit < seq_size:
        odd = (order // bit) % 2 == 1
        pieces = [jnp.where(odd, pieces[slot ^ bit], pieces[slot]) for slot in range(seq_size)]
        bit *= 2
    factors = jnp.concatenate(pieces, axis=1)
    mine = lax.dynamic_slice_in_dim(factors, dp_index * row_share, row_share, 2)
    class_share, class_squares = class_weights(images, mine, factors)

    early = reduce_rows(early_keep, early_send, dp_size, seq_size)
    *d_slots, late_keep, late_send = backward(
        dp_size, place, lengths,
        [p_high, p_low, pv, pv_bias, unit, kt_high, kt_low, v_high, v_low, query],
        d_attended, [t1, t2, t1_rows, t2_rows], vec_rows, vectors, matrices,
    )
    late = reduce_rows(late_keep, late_send, dp_size, seq_size)
    bit = 1
    while 2 * bit < seq_size:
        for slot in range(0, seq_size, 2 * bit):
            d_slots[slot] = d_slots[slot] + swap(d_slots[slot + bit], "seq", seq_size, bit)
        bit *= 2
    far = swap(d_slots[bit], "seq", seq_size, bit)
    grad_tokens = token_grad(tokens, vectors, d_slots[0], far, d_mixed)

    squares = squares_of(dp_size, place, early, late, class_squares)
    squares = squares + swap(squares, "seq", seq_size, 1)
    bit = 1
    while bit < dp_size:
        squares = squares + swap(squares, "dp", dp_size, bit)
        bit *= 2
    early_other = swap(early, "seq", seq_size, 1)
    late_other = swap(late, "seq", seq_size, 1)
    weight_rows = lax.dynamic_slice_in_dim(matrices, dp_index * row_share, row_share, 2)
    vector_columns = lax.dynamic_slice_in_dim(vectors, dp_index * row_share, row_share, 1)
    norm, *updated = optimizer(
        place, squares, [early, early_other], [late, late_other], class_share,
        [weight_rows, matrices_moment1, matrices_moment2, matrices_ema],
        [vector_columns, vectors_moment1, vectors_moment2, vectors_ema],
        [talking, talking_moment1, talking_moment2, talking_ema],
    )
    return (patch_out, class_out, grad_tokens, grad_class, norm[0, 0], *updated)


def solution(mesh):
    tokens = P(("dp", "seq"), None)
    by_group = P("dp", None)
    mats = P(None, None, "dp", None)
    vecs = P(None, "dp")
    body = functools.partial(on_device, mesh.shape["dp"], mesh.shape["seq"])
    return jax.shard_map(
        body,
        mesh=mesh,
        in_specs=(tokens, by_group, tokens, by_group, by_group, P(), mats, mats, mats,
                  P(), vecs, vecs, vecs, P(), P(), P(), P()),
        out_specs=(tokens, by_group, tokens, by_group, P(), mats, mats, mats, mats,
                   vecs, vecs, vecs, vecs, P(), P(), P(), P()),
        check_vma=False,
    )
```

```python
import functools

import jax
import jax.numpy as jnp
from jax import lax
from jax.experimental import pallas as pl
from jax.experimental.pallas import tpu as pltpu
from jax.sharding import PartitionSpec as P

STEP = 10
EPS_NORM = 1e-06
MASKED = -1e30
LR_MATRIX = 0.05
LR_VECTOR = 0.1
LR_TALKING = 0.2
BETA_ONE = 0.9
BETA_TWO = 0.999
ADAM_EPS = 1e-08
WEIGHT_DECAY = 0.05
EMA_RATE = 0.9
CLIP_NORM = 1.0
F32 = jnp.float32
BF16 = jnp.bfloat16
NN = (((1,), (0,)), ((), ()))
NT = (((1,), (1,)), ((), ()))
TN = (((0,), (0,)), ((), ()))
KERNEL_MIB = 58


def split(value):
    high = value.astype(BF16)
    return high, (value - high.astype(F32)).astype(BF16)


def mm(left, right, dims=NN):
    return lax.dot_general(left, right, dims, preferred_element_type=F32)


def mm3(left, right, dims=NN):
    return mm(left[0], right[0], dims) + (mm(left[0], right[1], dims) + mm(left[1], right[0], dims))


def dot3(left, right, dims=NN):
    return mm3(split(left), split(right), dims)


def norm_rows(values):
    average = jnp.mean(values, axis=-1, keepdims=True)
    centered = values - average
    variance = jnp.mean(centered * centered, axis=-1, keepdims=True)
    scale = lax.rsqrt(variance + EPS_NORM)
    return centered * scale, scale


def norm_back(grad, unit, scale):
    inner = jnp.mean(grad * unit, axis=-1, keepdims=True)
    return scale * (grad - jnp.mean(grad, axis=-1, keepdims=True) - unit * inner)


def gelu_both(values):
    half = 0.5 * (1.0 + lax.erf(values * 0.7071067811865476))
    slope = half + values * (0.3989422804014327 * jnp.exp(-0.5 * values * values))
    return values * half, slope


def row_sum(values):
    return jnp.sum(values, axis=0, keepdims=True)


def tail_forward(inputs, attended, w_out, w_up, w_down, vecs):
    projected = dot3(attended, w_out) + vecs[4:5]
    mixed = inputs + vecs[5:6] * projected
    unit, _ = norm_rows(mixed)
    normed = unit * vecs[6:7] + vecs[7:8]
    up_bias = jnp.concatenate([vecs[row : row + 1] for row in range(8, 12)], axis=1)
    hidden, slope = gelu_both(dot3(normed, w_up) + up_bias)
    lowered = dot3(hidden, w_down, NT) + vecs[12:13]
    return mixed + vecs[13:14] * lowered, (projected, mixed, hidden, slope, lowered)


def tail_backward(cot, kept, w_out, w_up, w_down, vecs):
    projected, mixed, hidden, slope, lowered = kept
    width = cot.shape[1]
    unit, scale = norm_rows(mixed)
    normed = unit * vecs[6:7] + vecs[7:8]
    d_lowered = cot * vecs[13:14]
    d_hidden = dot3(d_lowered, w_down) * slope
    d_normed = dot3(d_hidden, w_up, NT)
    d_mixed = cot + norm_back(d_normed * vecs[6:7], unit, scale)
    d_projected = d_mixed * vecs[5:6]
    d_attended = dot3(d_projected, w_out, NT)
    d_up = row_sum(d_hidden)
    rows = [
        row_sum(d_projected), row_sum(d_mixed * projected), row_sum(d_normed * unit), row_sum(d_normed),
        *[d_up[:, i * width : (i + 1) * width] for i in range(4)],
        row_sum(d_lowered), row_sum(cot * lowered),
    ]
    return d_mixed, d_attended, d_projected, d_hidden, d_lowered, normed, rows


def image_of(lengths_ref, images, positions):
    end = lengths_ref[0, 0]
    inside = (positions >= end).astype(jnp.int32)
    for image in range(1, images):
        end = end + lengths_ref[0, image]
        inside = inside + (positions >= end).astype(jnp.int32)
    return inside


def same_image(lengths_ref, images, place, slots, rows):
    queries = place * rows + lax.broadcasted_iota(jnp.int32, (1, rows), 1)
    query_image = image_of(lengths_ref, images, queries)
    parts = []
    for slot in range(slots):
        keys = jnp.bitwise_xor(place, slot) * rows + lax.broadcasted_iota(jnp.int32, (rows, 1), 0)
        parts.append(image_of(lengths_ref, images, keys) == query_image)
    return parts


def column_of(table, number):
    lanes = lax.broadcasted_iota(jnp.int32, (1, table.shape[1]), 1)
    return jnp.sum(jnp.where(lanes == number, table, 0.0), axis=1, keepdims=True)


def head_mask(heads, width):
    row = lax.broadcasted_iota(jnp.int32, (heads, width), 0)
    return jnp.where(lax.broadcasted_iota(jnp.int32, (heads, width), 1) // (width // heads) == row, 1.0, 0.0)


def spread(value, mask):
    return jnp.concatenate([value[i : i + 1] * mask for i in range(value.shape[0])], axis=0)


def repeat_rows(value, heads):
    shape = (heads, value.shape[1])
    return jnp.concatenate(
        [jnp.broadcast_to(value[i : i + 1], shape) for i in range(value.shape[0])], axis=0
    )


def fold_heads(value, mask):
    heads = mask.shape[0]
    return jnp.concatenate(
        [row_sum(value[i : i + heads] * mask) for i in range(0, value.shape[0], heads)], axis=0
    )


def head_sums(value, mask):
    return jnp.sum(spread(value, mask), axis=1, keepdims=True)


def rows_of(value, heads):
    return jnp.concatenate(
        [row_sum(value[i : i + heads]) for i in range(0, value.shape[0], heads)], axis=0
    )


def wide(column):
    return jnp.broadcast_to(column, (column.shape[0], 128))


def whole(shape):
    return pl.BlockSpec(shape, lambda *_: (0,) * len(shape))


def struct(shape, dtype=F32):
    return jax.ShapeDtypeStruct(shape, dtype)


def smem():
    return pl.BlockSpec(memory_space=pltpu.SMEM)


def anywhere():
    return pl.BlockSpec(memory_space=pl.ANY)


def weight_block(block, matrix, shape):
    return pl.BlockSpec((None, None) + shape[2:], lambda *_: (block, matrix, 0, 0))


def limit(mebibytes):
    return pltpu.CompilerParams(vmem_limit_bytes=mebibytes << 20)


def prepare_kernel(
    own_ref, near_ref, class_ref, w_self_ref, w_class_ref, vecs_ref, talk_ref,
    normed_ref, query_c_ref, value_c_ref, key_rows_ref, score_ref, t1_ref, t2_ref, t1_rows_ref, t2_rows_ref,
    query_ref, k_high, k_low, v_high, v_low, kt_high, kt_low, vt_high, vt_low,
):
    rows, width = own_ref.shape
    heads = talk_ref.shape[0]
    size = width // heads
    scale = size ** (-0.5)
    vecs = vecs_ref[...]
    w_q, w_k, w_v = (split(w_self_ref[:, i * width : (i + 1) * width]) for i in range(3))
    tokens = jnp.concatenate([own_ref[...], near_ref[...]], axis=0)
    unit, _ = norm_rows(tokens)
    normed = split(unit * vecs[0:1] + vecs[1:2])
    query_ref[...] = (mm3((normed[0][:rows], normed[1][:rows]), w_q) + vecs[2:3]) * scale
    keys, values = mm3(normed, w_k), mm3(normed, w_v) + vecs[3:4]
    k_high[...], k_low[...] = split(keys)
    v_high[...], v_low[...] = split(values)
    kt_high[...], kt_low[...] = split(keys.T)
    vt_high[...], vt_low[...] = split(values.T)
    mask = head_mask(heads, width)
    unit, _ = norm_rows(class_ref[...])
    normed = unit * vecs[14:15] + vecs[15:16]
    both = dot3(normed, w_class_ref[:, : 3 * width])
    query = both[:, :width] + vecs[16:17]
    normed_ref[...] = normed
    query_c_ref[...] = query
    value_c_ref[...] = both[:, 2 * width :] + vecs[17:18]
    key_rows_ref[...] = dot3(spread(query, mask), w_class_ref[:, width : 2 * width], NT) * scale
    score_ref[...] = wide(head_sums(query * both[:, width : 2 * width], mask) * scale)
    head_of = lax.broadcasted_iota(jnp.int32, (width, 1), 0) // size
    talk = talk_ref[...]
    talk_t = jnp.concatenate([talk, jnp.zeros((heads, 128 - talk.shape[1]), F32)], axis=1).T[: talk.shape[1], :]
    t1 = t2 = t1_rows = t2_rows = 0.0
    for head in range(heads):
        here = head_of == head
        t1 = t1 + jnp.where(here, talk_t[head : head + 1, :], 0.0)
        t2 = t2 + jnp.where(here, talk[head : head + 1, heads:], 0.0)
        t1_rows = t1_rows + mask[head : head + 1] * talk[:, head : head + 1]
        t2_rows = t2_rows + mask[head : head + 1] * talk_t[heads:, head : head + 1]
    t1_ref[...], t2_ref[...], t1_rows_ref[...], t2_rows_ref[...] = t1, t2, t1_rows, t2_rows


def prepare(own, near, class_tokens, matrices, vectors, talking):
    images, width = class_tokens.shape
    rows = own.shape[0]
    heads = talking.shape[0]
    pairs = images * heads
    outs = [struct((images, width))] * 3 + [
        struct((pairs, width)), struct((pairs, 128)),
        struct((width, heads)), struct((width, heads + 1)),
        struct((heads, width)), struct((heads + 1, width)),
        struct((rows, width)),
    ]
    outs += [struct((2 * rows, width), BF16)] * 4 + [struct((width, 2 * rows), BF16)] * 4
    operands = [own, near, class_tokens, matrices, matrices, vectors, talking]
    specs = [whole(operand.shape) for operand in operands]
    specs[3] = weight_block(0, 0, matrices.shape)
    specs[4] = weight_block(1, 0, matrices.shape)
    return pl.pallas_call(
        prepare_kernel,
        grid=(1,),
        in_specs=specs,
        out_specs=[whole(out.shape) for out in outs],
        out_shape=outs,
        compiler_params=limit(KERNEL_MIB),
        cost_estimate=pl.CostEstimate(flops=4 << 30, bytes_accessed=8 << 20, transcendentals=0),
        name="prepare",
    )(*operands)


def forward_kernel(slots, images, unroll, *refs):
    place_ref, lengths_ref = refs[:2]
    token_refs = refs[2 : 2 + slots]
    (
        w_ref, vecs_ref, t1_ref, t2_ref, key_rows_ref, query_ref,
        k_high0, k_low0, v_high0, v_low0, kt_high0, kt_low0, vt_high0, vt_low0, mats_ref,
        e_high_ref, e_low_ref, pv_ref, inverse_ref, pv_bias_ref, attended_ref,
        kt_high, kt_low, v_high, v_low,
        patch_ref, projected_ref, mixed_ref, hidden_ref, slope_ref, lowered_ref, packed_ref, scores_ref,
        k_high, k_low, vt_high, vt_low, qt, bias, attended_t, w_up, w_down, arrived,
    ) = refs[2 + slots :]
    rows, width = token_refs[0].shape
    step = pl.program_id(0)
    place = place_ref[0]
    fetch_up = pltpu.make_async_copy(mats_ref.at[0, 1], w_up, arrived.at[0])
    fetch_down = pltpu.make_async_copy(mats_ref.at[0, 2], w_down, arrived.at[1])

    @pl.when(step == 0)
    def _():
        fetch_up.start()
        fetch_down.start()
        ready = pl.ds(0, 2 * rows)
        for ref, found in ((k_high, k_high0), (k_low, k_low0), (v_high, v_high0), (v_low, v_low0)):
            ref[ready, :] = found[...]
        for ref, found in ((kt_high, kt_high0), (kt_low, kt_low0), (vt_high, vt_high0), (vt_low, vt_low0)):
            ref[:, ready] = found[...]
        w_k, w_v = (split(w_ref[:, i * width : (i + 1) * width]) for i in (1, 2))
        vecs = vecs_ref[...]
        inside = same_image(lengths_ref, images, place, slots, rows)
        for slot in range(slots):
            here = pl.ds(slot * rows, rows)
            bias[here, :] = jnp.where(inside[slot], 0.0, MASKED)
            if slot < 2:
                continue
            unit, _ = norm_rows(token_refs[slot][...])
            normed = split(unit * vecs[0:1] + vecs[1:2])
            keys, values = mm3(normed, w_k), mm3(normed, w_v) + vecs[3:4]
            k_high[here, :], k_low[here, :] = split(keys)
            v_high[here, :], v_low[here, :] = split(values)
            kt_high[:, here], kt_low[:, here] = split(keys.T)
            vt_high[:, here], vt_low[:, here] = split(values.T)
        qt[...] = query_ref[...].T
        attended_t[...] = jnp.zeros_like(attended_t)

    scores = []
    for u in range(unroll):
        query = split(qt[...] * column_of(t1_ref[...], step * unroll + u))
        scores.append(mm3((k_high[...], k_low[...]), query) + bias[...])
    for u in range(unroll):
        exponentials = jnp.exp(scores[u] - jnp.max(scores[u], axis=0, keepdims=True))
        inverse = 1.0 / jnp.sum(exponentials, axis=0, keepdims=True)
        pair = split(exponentials)
        e_high_ref[u], e_low_ref[u] = pair
        inverse_ref[u] = inverse
        values = mm3((vt_high[...], vt_low[...]), pair) * inverse
        pv_ref[u] = values
        attended_t[...] += values * column_of(t2_ref[...], step * unroll + u)

    @pl.when(step == pl.num_programs(0) - 1)
    def _():
        inside = jnp.where(bias[...] < 0.0, 0.0, 1.0).astype(BF16)
        summed = mm(vt_high[...], inside) + mm(vt_low[...], inside)
        pv_bias_ref[...] = summed
        attended = (attended_t[...] + summed * t2_ref[:, 8:9]).T
        attended_ref[...] = attended
        fetch_up.wait()
        fetch_down.wait()
        vecs = vecs_ref[...]
        patch, kept = tail_forward(
            token_refs[0][...], attended, w_ref[:, 3 * width :], w_up[...], w_down[...], vecs
        )
        patch_ref[...] = patch
        for ref, value in zip((projected_ref, mixed_ref, hidden_ref, slope_ref, lowered_ref), kept):
            ref[...] = value
        unit, _ = norm_rows(patch)
        normed = split(unit * vecs[14:15] + vecs[15:16])
        pairs = images * 8
        image = lax.broadcasted_iota(jnp.int32, (pairs, 1), 0) // 8
        positions = place * rows + lax.broadcasted_iota(jnp.int32, (1, rows), 1)
        belong = image_of(lengths_ref, images, positions) == image
        class_scores = mm3(split(key_rows_ref[...]), normed, NT)
        class_scores = jnp.where(belong, class_scores, MASKED)
        scores_ref[...] = class_scores
        top = jnp.max(class_scores, axis=1, keepdims=True)
        weights = jnp.where(belong, jnp.exp(class_scores - top), 0.0)
        packed_ref[:, :width] = mm3(split(weights), normed)
        lane = lax.broadcasted_iota(jnp.int32, (1, 128), 1)
        total = jnp.sum(weights, axis=1, keepdims=True)
        packed_ref[:, width:] = jnp.where(lane < 64, top, total)


def by_head(unroll, shape):
    return pl.BlockSpec((unroll,) + shape[1:], lambda g: (g, 0, 0))


def forward(place, lengths, token_slots, matrices, vectors, t1, t2, key_rows, projected):
    slots, (rows, width) = len(token_slots), token_slots[0].shape
    total, heads = slots * rows, 8
    unroll = 4 if total <= 1024 else 1
    hidden = matrices.shape[3]
    pairs = key_rows.shape[0]
    outs = [struct((heads, total, rows), BF16)] * 2 + [struct((heads, width, rows)), struct((heads, 1, rows))]
    specs = [by_head(unroll, out.shape) for out in outs]
    rest = [
        struct((width, rows)), struct((rows, width)),
        struct((width, total), BF16), struct((width, total), BF16),
        struct((total, width), BF16), struct((total, width), BF16),
        struct((rows, width)), struct((rows, width)), struct((rows, width)),
        struct((rows, hidden)), struct((rows, hidden)), struct((rows, width)),
        struct((pairs, width + 128)), struct((pairs, rows)),
    ]
    operands = [*token_slots, matrices, vectors, t1, t2, key_rows, *projected, matrices]
    in_specs = [whole(operand.shape) for operand in operands]
    in_specs[slots] = weight_block(0, 0, matrices.shape)
    in_specs[-1] = anywhere()
    flops = 2 * 3 * ((2 * heads + 1) * total + 9 * width) * rows * width
    return pl.pallas_call(
        functools.partial(forward_kernel, slots, lengths.shape[1], unroll),
        grid=(heads // unroll,),
        in_specs=[smem(), smem()] + in_specs,
        out_specs=specs + [whole(out.shape) for out in rest],
        out_shape=outs + rest,
        scratch_shapes=[
            pltpu.VMEM((total, width), BF16),
            pltpu.VMEM((total, width), BF16),
            pltpu.VMEM((width, total), BF16),
            pltpu.VMEM((width, total), BF16),
            pltpu.VMEM((width, rows), F32),
            pltpu.VMEM((total, rows), F32),
            pltpu.VMEM((width, rows), F32),
            pltpu.VMEM((width, hidden), F32),
            pltpu.VMEM((width, hidden), F32),
            pltpu.SemaphoreType.DMA((2,)),
        ],
        compiler_params=limit(KERNEL_MIB),
        cost_estimate=pl.CostEstimate(
            flops=flops, bytes_accessed=24 << 20, transcendentals=heads * total * rows
        ),
        name="forward",
    )(place, lengths, *operands)


def middle_kernel(images, slots, *refs):
    place_ref = refs[0]
    parts = [ref[...] for ref in refs[1 : 1 + slots]]
    (
        vecs_ref, normed_c_ref, query_c_ref, value_c_ref, key_rows_ref, own_ref,
        class_ref, cot_class_ref, cot_patch_ref, patch_ref, scores_ref, attended_ref,
        projected_ref, mixed_ref, hidden_ref, slope_ref, lowered_ref, mats_ref,
        class_out_ref, d_attended_ref, d_mixed_ref, keep_ref, send_ref, partial_ref,
        factors_ref, vec_rows_ref, class_terms_ref,
        wc0, wc1, wc2, ws0, ws1, ws2, arrived,
    ) = refs[1 + slots :]
    width = class_ref.shape[1]
    heads = 8
    size = width // heads
    fetches = [
        pltpu.make_async_copy(source, target, arrived.at[number])
        for number, (source, target) in enumerate([
            (mats_ref.at[1, 0], wc0), (mats_ref.at[1, 1], wc1), (mats_ref.at[1, 2], wc2),
            (mats_ref.at[0, 2], ws2), (mats_ref.at[0, 1], ws1), (mats_ref.at[0, 0], ws0),
        ])
    ]
    for fetch in fetches:
        fetch.start()
    vecs = vecs_ref[...]
    vecs_s, vecs_c = vecs[:14], vecs[14:]
    mask = head_mask(heads, width)
    first = jnp.where(place_ref[0] == 0, 1.0, 0.0)
    own_score = own_ref[:, :1]
    normed_c = normed_c_ref[...]
    normed_rep = repeat_rows(normed_c, heads)
    top = own_score
    for part in parts:
        top = jnp.maximum(top, part[:, width : width + 1])
    own_weight = jnp.exp(own_score - top)
    total, summed = own_weight, own_weight * normed_rep
    for part in parts:
        rescale = jnp.exp(part[:, width : width + 1] - top)
        total = total + part[:, width + 64 : width + 65] * rescale
        summed = summed + part[:, :width] * rescale
    value_rows = summed / total
    own_prob = own_weight / total
    fetches[0].wait()
    w_v = split(wc0[:, 2 * width : 3 * width])
    class_attended = fold_heads(mm3(split(value_rows), w_v), mask) + vecs_c[3:4]
    fetches[1].wait()
    fetches[2].wait()
    w_out_c = wc0[:, 3 * width :]
    class_out, kept_c = tail_forward(class_ref[...], class_attended, w_out_c, wc1[...], wc2[...], vecs_c)
    class_out_ref[...] = class_out
    d_mixed_c, d_attended_c, d_projected_c, d_hidden_c, d_lowered_c, normed2_c, tail_rows_c = (
        tail_backward(cot_class_ref[...], kept_c, w_out_c, wc1[...], wc2[...], vecs_c)
    )
    delta = head_sums(d_attended_c * class_attended, mask)
    cot_rows = mm3(split(spread(d_attended_c, mask)), w_v, NT)
    cot_const = head_sums(d_attended_c * vecs_c[3:4], mask)
    scores = scores_ref[...]
    probs = jnp.where(scores > 0.5 * MASKED, jnp.exp(scores - top) * (1.0 / total), 0.0)
    unit_p, scale_p = norm_rows(patch_ref[...])
    normed_p = split(unit_p * vecs_c[0:1] + vecs_c[1:2])
    cot_split = split(cot_rows)
    d_scores = probs * (mm3(cot_split, normed_p, NT) + cot_const - delta)
    d_own = own_prob * (head_sums(d_attended_c * value_c_ref[...], mask) - delta)
    key_rows = key_rows_ref[...]
    d_split = split(d_scores)
    d_normed_p = mm3(d_split, split(key_rows), TN) + mm3(split(probs), cot_split, TN)
    partial_ref[...] = mm3(d_split, normed_p)
    cot = cot_patch_ref[...] + norm_back(d_normed_p * vecs_c[0:1], unit_p, scale_p)
    class_terms_ref[...] = jnp.concatenate(
        [rows_of(d_own * key_rows + own_prob * cot_rows, heads), d_mixed_c], axis=0
    )
    query_c = query_c_ref[...]
    chunks = lambda value: [value[:, i * width : (i + 1) * width] for i in range(4)]
    factors_ref[...] = jnp.concatenate(
        [normed_c, class_attended, normed2_c, d_lowered_c, d_own * normed_rep, value_rows,
         jnp.zeros_like(query_c), query_c * size ** (-0.5), d_attended_c, d_projected_c,
         *chunks(d_hidden_c), *chunks(kept_c[2])], axis=0)
    for fetch in fetches[3:]:
        fetch.wait()
    kept = tuple(ref[...] for ref in (projected_ref, mixed_ref, hidden_ref, slope_ref, lowered_ref))
    d_mixed, d_attended, d_projected, d_hidden, d_lowered, normed, tail_rows = tail_backward(
        cot, kept, ws0[:, 3 * width :], ws1[...], ws2[...], vecs_s
    )
    d_mixed_ref[...] = d_mixed
    d_attended_ref[...] = d_attended
    zero = jnp.zeros((1, width), F32)
    vec_rows_ref[...] = jnp.concatenate(
        [zero] * 4 + tail_rows
        + [row_sum(d_normed_p * unit_p), row_sum(d_normed_p), zero, row_sum(d_attended_c) * first]
        + [row * first for row in tail_rows_c], axis=0)
    g_out = dot3(attended_ref[...], d_projected, TN)
    g_up = dot3(normed, d_hidden, TN)
    g_down = dot3(d_lowered, hidden_ref[...], TN)
    even = jnp.bitwise_and(place_ref[0], 1) == 0
    hidden = g_up.shape[1]
    keep_ref[:, :hidden] = jnp.where(even, g_up, g_down)
    send_ref[:, :hidden] = jnp.where(even, g_down, g_up)
    left = g_out[:, :256]
    right = jnp.concatenate([g_out[:, 256:], jnp.zeros((width, 512 - width), F32)], axis=1)
    keep_ref[:, hidden:] = jnp.where(even, left, right)
    send_ref[:, hidden:] = jnp.where(even, right, left)


def middle(place, parts, vectors, prepared, class_tokens, cot_class, cot_patch, forwarded, matrices):
    images, width = class_tokens.shape
    rows = cot_patch.shape[0]
    hidden = matrices.shape[3]
    pairs = parts[0].shape[0]
    operands = [*parts, vectors, *prepared, class_tokens, cot_class, cot_patch, *forwarded, matrices]
    in_specs = [whole(operand.shape) for operand in operands]
    in_specs[-1] = anywhere()
    outs = [
        struct((images, width)), struct((rows, width)), struct((rows, width)),
        struct((width, hidden + 256)), struct((width, hidden + 256)), struct((pairs, width)),
        struct((16 * images + 2 * pairs, width)), struct((28, width)), struct((2 * images, width)),
    ]
    return pl.pallas_call(
        functools.partial(middle_kernel, images, len(parts)),
        grid=(1,),
        in_specs=[smem()] + in_specs,
        out_specs=[whole(out.shape) for out in outs],
        out_shape=outs,
        scratch_shapes=[pltpu.VMEM((width, hidden), F32)] * 6 + [pltpu.SemaphoreType.DMA((6,))],
        compiler_params=limit(KERNEL_MIB),
        cost_estimate=pl.CostEstimate(flops=8 << 30, bytes_accessed=28 << 20, transcendentals=1 << 19),
        name="middle",
    )(place, *operands)


def class_kernel(slots, *refs):
    partial_refs = refs[:slots]
    terms_ref, class_ref, vecs_ref, w_ref, factors_ref, grad_ref, factors_out_ref = refs[slots:]
    images, width = class_ref.shape
    pairs = partial_refs[0].shape[0]
    heads = pairs // images
    mask = head_mask(heads, width)
    at = 4 * images
    query_rows = sum_of([factors_ref[at : at + pairs, :]] + [ref[...] for ref in partial_refs])
    w_k, w_q = w_ref[:, width : 2 * width], w_ref[:, :width]
    d_query = fold_heads(dot3(query_rows, w_k), mask) * (width // heads) ** (-0.5)
    d_normed = dot3(d_query, w_q, NT) + terms_ref[:images, :]
    unit, scale = norm_rows(class_ref[...])
    grad_ref[...] = terms_ref[images:, :] + norm_back(d_normed * vecs_ref[14:15, :], unit, scale)
    count = factors_ref.shape[0]
    factors_out_ref[:count, :] = factors_ref[...]
    factors_out_ref[at : at + pairs, :] = query_rows
    at = at + 2 * pairs
    factors_out_ref[at : at + images, :] = d_query
    added = [row_sum(d_normed * unit), row_sum(d_normed), row_sum(d_query), jnp.zeros((5, width), F32)]
    factors_out_ref[count:, :] = jnp.concatenate(added, axis=0)


def class_finish(partials, terms, class_tokens, vectors, matrices, factors):
    operands = [*partials, terms, class_tokens, vectors, matrices, factors]
    specs = [whole(operand.shape) for operand in operands]
    specs[-2] = weight_block(1, 0, matrices.shape)
    outs = [struct(class_tokens.shape), struct((factors.shape[0] + 8, factors.shape[1]))]
    return pl.pallas_call(
        functools.partial(class_kernel, len(partials)),
        grid=(1,),
        in_specs=specs,
        out_specs=[whole(out.shape) for out in outs],
        out_shape=outs,
        compiler_params=limit(KERNEL_MIB),
        cost_estimate=pl.CostEstimate(flops=1 << 29, bytes_accessed=3 << 20, transcendentals=0),
        name="class_finish",
    )(*operands)


def class_weights_kernel(images, mine_ref, factors_ref, grads_ref, squares_ref, small_ref):
    groups, count, width = factors_ref.shape
    heads = 8
    pairs = images * heads
    mask = head_mask(heads, width)
    at = 4 * images + 2 * pairs

    def rows(ref, begin, count=images):
        return jnp.concatenate([ref[g, begin : begin + count, :] for g in range(groups)], axis=0)

    def chunked(begin):
        return jnp.concatenate([rows(factors_ref, begin + i * images) for i in range(4)], axis=1)

    def headed(left, right):
        return dot3(rows(mine_ref, left, pairs), spread(rows(factors_ref, right), mask), TN)

    grads_ref[0, :, :width] = dot3(rows(mine_ref, 0), rows(factors_ref, at), TN)
    grads_ref[0, :, width : 2 * width] = headed(4 * images, at + images)
    grads_ref[0, :, 2 * width : 3 * width] = headed(4 * images + pairs, at + 2 * images)
    grads_ref[0, :, 3 * width :] = dot3(rows(mine_ref, images), rows(factors_ref, at + 3 * images), TN)
    grads_ref[1] = dot3(rows(mine_ref, 2 * images), chunked(at + 4 * images), TN)
    grads_ref[2] = dot3(rows(mine_ref, 3 * images), chunked(at + 8 * images), TN)
    grads = grads_ref[...]
    squares_ref[...] = jnp.broadcast_to(jnp.sum(grads * grads), squares_ref.shape)
    added = sum_of([mine_ref[g, count - 8 :, :] for g in range(groups)])
    lanes = 128 - 22
    share = added.shape[1]
    added = jnp.concatenate([jnp.zeros((14, share), F32), added, jnp.zeros((lanes, share), F32)], axis=0)
    small_ref[...] = added.T


def class_weights(images, mine, factors):
    share = mine.shape[2]
    outs = [struct((3, share, 4 * factors.shape[2])), struct((8, 128)), struct((share, 128))]
    return pl.pallas_call(
        functools.partial(class_weights_kernel, images),
        grid=(1,),
        in_specs=[whole(mine.shape), whole(factors.shape)],
        out_specs=[whole(out.shape) for out in outs],
        out_shape=outs,
        compiler_params=limit(KERNEL_MIB),
        cost_estimate=pl.CostEstimate(flops=1 << 29, bytes_accessed=3 << 20, transcendentals=0),
        name="class_weights",
    )(mine, factors)


def mm3_wide(left, right):
    width = right[0].shape[1]
    both = mm(left[0], jnp.concatenate(right, axis=1))
    return both[:, :width] + (both[:, width:] + mm(left[1], right[0]))


def backward_kernel(slots, images, dp_size, unroll, *refs):
    place_ref, lengths_ref = refs[:2]
    token_refs = refs[2 : 2 + slots]
    (
        e_high_ref, e_low_ref, pv_ref, inverse_ref, pv_bias_ref, cot_ref,
        kt_high, kt_low, v_high, v_low, query_ref, t1_ref, t2_ref, t1_rows, t2_rows,
        vec_rows_ref, vecs_ref, w_ref,
    ) = refs[2 + slots : 20 + slots]
    (
        even_ref, odd_ref, keep_ref, send_ref,
        d_keys, d_values, c1, c2, cot_t, qt, d_qt, v_three,
    ) = refs[20 + slots :]
    rows, width = cot_ref.shape
    step = pl.program_id(0)
    size = width // 8
    lanes = lax.broadcasted_iota(jnp.int32, (1, 128), 1)

    @pl.when(step == 0)
    def _():
        cot_t[...] = cot_ref[...].T
        qt[...] = query_ref[...].T
        d_qt[...] = jnp.zeros_like(d_qt)
        d_keys[...] = jnp.zeros_like(d_keys)
        c1[...] = jnp.zeros_like(c1)
        v_three[...] = jnp.concatenate([v_high[...], v_high[...], v_low[...]], axis=1)
        c2[...] = jnp.where(
            lanes == 8, jnp.sum(cot_t[...] * pv_bias_ref[...], axis=1, keepdims=True), 0.0
        )
        inside = jnp.concatenate(same_image(lengths_ref, images, place_ref[0], slots, rows), axis=0)
        inside = jnp.where(inside, 1.0, 0.0).astype(BF16)
        high, low = split(cot_ref[...] * t2_rows[8:9, :])
        d_values[...] = mm(inside, high) + mm(inside, low)

    found = []
    for u in range(unroll):
        head = step * unroll + u
        t2_column, inverse = column_of(t2_ref[...], head), inverse_ref[u]
        crossed = cot_t[...] * pv_ref[u]
        c2[...] += jnp.where(lanes == head, jnp.sum(crossed, axis=1, keepdims=True), 0.0)
        delta = jnp.sum(crossed * t2_column, axis=0, keepdims=True) * inverse
        high, low = split(cot_t[...] * (t2_column * inverse))
        found.append((mm(v_three[...], jnp.concatenate([high, low, high], axis=0)), delta))
    for u in range(unroll):
        head = step * unroll + u
        d_probs, delta = found[u]
        pair = (e_high_ref[u], e_low_ref[u])
        d_mixed = split((pair[0].astype(F32) + pair[1].astype(F32)) * (d_probs - delta))
        inverse_rows = jnp.broadcast_to(inverse_ref[u], (8, rows)).T[:, :1]
        cot = split(cot_ref[...] * inverse_rows * t2_rows[pl.ds(head, 1), :])
        d_values[...] += mm3_wide(pair, cot)
        d_keys[...] += mm3_wide(d_mixed, split(query_ref[...] * t1_rows[pl.ds(head, 1), :]))
        back = mm3((kt_high[...], kt_low[...]), d_mixed)
        d_qt[...] += back * column_of(t1_ref[...], head)
        c1[...] += jnp.where(lanes == head, jnp.sum(back * qt[...], axis=1, keepdims=True), 0.0)

    @pl.when(step == pl.num_programs(0) - 1)
    def _():
        d_query = d_qt[...].T * size ** (-0.5)
        w_q, w_k, w_v = (split(w_ref[:, i * width : (i + 1) * width]) for i in range(3))
        gain = shift = g_k = g_v = 0.0
        for slot in range(slots):
            here = pl.ds(slot * rows, rows)
            unit, _ = norm_rows(token_refs[slot][...])
            normed = split(unit * vecs_ref[0:1, :] + vecs_ref[1:2, :])
            dk, dv = split(d_keys[here, :]), split(d_values[here, :])
            piece = mm3(dk, w_k, NT) + mm3(dv, w_v, NT)
            if slot == 0:
                dq = split(d_query)
                piece = piece + mm3(dq, w_q, NT)
                g_q = mm3(normed, dq, TN)
            (odd_ref if slot % 2 else even_ref)[slot // 2] = piece
            gain, shift = gain + row_sum(piece * unit), shift + row_sum(piece)
            g_k, g_v = g_k + mm3(normed, dk, TN), g_v + mm3(normed, dv, TN)
        added = jnp.concatenate(
            [gain, shift, row_sum(d_query), row_sum(d_values[...]), jnp.zeros((4, width), F32)], axis=0
        )
        vec_rows = jnp.concatenate([vec_rows_ref[0:8, :] + added, vec_rows_ref[8:28, :]], axis=0)
        fold = lambda value: jnp.concatenate(
            [row_sum(value[i * size : (i + 1) * size]) for i in range(8)], axis=0
        )
        pre, post = fold(c1[...]).T[:8, :], fold(c2[...])
        count = vec_rows.shape[0]
        talk = jnp.concatenate([pre, post[:, :9], jnp.zeros((8, 128 - count - 17), F32)], axis=1)
        block = width // dp_size
        talk = jnp.concatenate([talk, jnp.zeros((block - 8, 128 - count), F32)], axis=0)
        talk = jnp.concatenate([talk] * dp_size, axis=0)
        small = jnp.concatenate([vec_rows.T, talk], axis=1)
        even = jnp.bitwise_and(place_ref[0], 1) == 0
        left = jnp.concatenate([g_q, g_k[:, :256]], axis=1)
        right = jnp.concatenate([g_k[:, 256:], g_v, small], axis=1)
        keep_ref[...] = jnp.where(even, left, right)
        send_ref[...] = jnp.where(even, right, left)


def backward(dp_size, place, lengths, token_slots, found, cot, keys_values, query, tables,
             vec_rows, vectors, matrices):
    rows, width = cot.shape
    heads, total, _ = found[0].shape
    slots, unroll = total // rows, 2 if total <= 1024 else 1
    operands = [*token_slots, *found, cot, *keys_values, query, *tables, vec_rows, vectors, matrices]
    specs = [whole(operand.shape) for operand in operands]
    specs[slots : slots + 4] = [by_head(unroll, operand.shape) for operand in found[:4]]
    specs[-1] = weight_block(0, 0, matrices.shape)
    outs = [struct((slots // 2, rows, width))] * 2 + [struct((width, 640))] * 2
    return pl.pallas_call(
        functools.partial(backward_kernel, slots, lengths.shape[1], dp_size, unroll),
        grid=(heads // unroll,),
        in_specs=[smem(), smem()] + specs,
        out_specs=[whole(out.shape) for out in outs],
        out_shape=outs,
        scratch_shapes=[pltpu.VMEM((total, width), F32)] * 2
        + [pltpu.VMEM((width, 128), F32)] * 2
        + [pltpu.VMEM((width, rows), F32)] * 3
        + [pltpu.VMEM((total, 3 * width), BF16)],
        compiler_params=limit(KERNEL_MIB),
        cost_estimate=pl.CostEstimate(
            flops=6 * (4 * heads + 6) * total * rows * width, bytes_accessed=24 << 20, transcendentals=0
        ),
        name="backward",
    )(place, lengths, *operands)


def token_grad_kernel(tokens_ref, vecs_ref, near_ref, far_ref, tail_ref, grad_ref):
    unit, scale = norm_rows(tokens_ref[...])
    d_normed = near_ref[...] + far_ref[...]
    grad_ref[...] = tail_ref[...] + norm_back(d_normed * vecs_ref[0:1, :], unit, scale)


def token_grad(*operands):
    tokens = operands[0]
    return pl.pallas_call(
        token_grad_kernel,
        out_shape=struct(tokens.shape),
        compiler_params=limit(KERNEL_MIB),
        cost_estimate=pl.CostEstimate(flops=1 << 21, bytes_accessed=2 << 20, transcendentals=0),
        name="token_grad",
    )(*operands)


def squares_kernel(dp_size, place_ref, early_ref, late_ref, added_ref, class_ref, out_ref):
    odd = jnp.bitwise_and(place_ref[0], 1) == 1
    late = late_ref[...]
    small = late[:, 512:] + jnp.where(odd, added_ref[...], 0.0)
    lane = lax.broadcasted_iota(jnp.int32, small.shape, 1)
    talk = jnp.logical_and(odd, jnp.logical_and(lane >= 28, lane < 45))
    small = small * small * jnp.where(talk, 1.0 / dp_size, 1.0)
    total = jnp.sum(small)
    for value in (late[:, :512], early_ref[...]):
        total = total + jnp.sum(value * value)
    out_ref[...] = 0.5 * class_ref[...] + total


def squares_of(dp_size, place, *operands):
    vmem = pl.BlockSpec(memory_space=pltpu.VMEM)
    return pl.pallas_call(
        functools.partial(squares_kernel, dp_size),
        in_specs=[smem()] + [vmem] * len(operands),
        out_shape=struct((8, 128)),
        compiler_params=limit(KERNEL_MIB),
        cost_estimate=pl.CostEstimate(flops=1 << 18, bytes_accessed=1 << 19, transcendentals=0),
        name="squares",
    )(place, *operands)


def adam_step(weight, gradient, moment1, moment2, rate, decay):
    first = BETA_ONE * moment1 + (1.0 - BETA_ONE) * gradient
    second = BETA_TWO * moment2 + (1.0 - BETA_TWO) * gradient * gradient
    first_hat = first * (1.0 / (1.0 - BETA_ONE**STEP))
    second_hat = second * (1.0 / (1.0 - BETA_TWO**STEP))
    updated = weight - rate * (first_hat / (jnp.sqrt(second_hat) + ADAM_EPS) + decay * weight)
    return (updated, first, second)


def adam_kernel(*refs):
    (
        place_ref, squares_ref, early_own, early_other, late_own, late_other, added_ref,
        class_ref, w_ref, m1_ref, m2_ref, ema_ref, v_ref, v1_ref, v2_ref, v_ema_ref,
        t_ref, t1_ref, t2_ref, t_ema_ref,
    ) = refs[:20]
    norm_ref, new_ref, first_ref, second_ref, average_ref = refs[20:25]
    v_outs, t_outs = refs[25:29], refs[29:33]
    grads = refs[33]
    step = pl.program_id(0)
    norm = jnp.sqrt(squares_ref[0:1, 0:1])
    factor = jnp.minimum(1.0, CLIP_NORM / norm)

    def store(outs, weight, gradient, moment1, moment2, ema, rate, decay):
        updated, first, second = adam_step(weight, gradient * factor, moment1, moment2, rate, decay)
        average = EMA_RATE * ema + (1.0 - EMA_RATE) * updated
        for out, value in zip(outs, (updated, first, second, average)):
            out[...] = value

    @pl.when(step == 0)
    def _():
        norm_ref[...] = norm
        even = jnp.bitwise_and(place_ref[0], 1) == 0
        pair = lambda own, other: (jnp.where(even, own[...], other[...]), jnp.where(even, other[...], own[...]))
        early_left, early_right = pair(early_own, early_other)
        late_left, late_right = pair(late_own, late_other)
        hidden = grads.shape[2]
        grads[0] = jnp.concatenate(
            [late_left, late_right[:, :512], early_left[:, hidden:], early_right[:, hidden : hidden + 128]],
            axis=1,
        )
        grads[1] = early_left[:, :hidden]
        grads[2] = early_right[:, :hidden]
        small = late_right[:, 512:] + added_ref[...]
        count = v_ref.shape[0]
        store(v_outs, v_ref[...], small.T[:count, :], v1_ref[...], v2_ref[...], v_ema_ref[...], LR_VECTOR, 0.0)
        talk = small[:8, count : count + 17]
        store(t_outs, t_ref[...], talk, t1_ref[...], t2_ref[...], t_ema_ref[...], LR_TALKING, 0.0)

    self_grad = grads[jnp.minimum(step, 2)]
    grad = jnp.where(step < 3, self_grad, class_ref[jnp.maximum(step - 3, 0)])
    store((new_ref, first_ref, second_ref, average_ref), w_ref[...], grad, m1_ref[...], m2_ref[...],
          ema_ref[...], LR_MATRIX, WEIGHT_DECAY)


def optimizer(place, squares, grads, class_share, mats, vecs, talks):
    shape = mats[1].shape
    block = pl.BlockSpec((None, None) + shape[2:], lambda i: (i // 3, i % 3, 0, 0))
    operands = [squares, *grads, class_share, *mats, *vecs, *talks]
    specs = [whole(operand.shape) for operand in operands]
    specs[7:11] = [block] * 4
    outs = [struct((1, 1))] + [struct(shape)] * 4
    outs += [struct(vecs[0].shape)] * 4 + [struct(talks[0].shape)] * 4
    out_specs = [whole(out.shape) for out in outs]
    out_specs[1:5] = [block] * 4
    return pl.pallas_call(
        adam_kernel,
        grid=(6,),
        in_specs=[smem()] + specs,
        out_specs=out_specs,
        out_shape=outs,
        scratch_shapes=[pltpu.VMEM((3,) + shape[2:], F32)],
        compiler_params=limit(KERNEL_MIB),
        cost_estimate=pl.CostEstimate(flops=1 << 23, bytes_accessed=14 << 20, transcendentals=0),
        name="optimizer",
    )(place, *operands)


def swap(value, axis, size, bit):
    return lax.ppermute(value, axis, [(place, place ^ bit) for place in range(size)])


def bits_of(axis, size, bit=1):
    return [(axis, bit << i) for i in range((size // bit).bit_length() - 1)]


class Reduce:
    def __init__(self, terms, dp_size, seq_size, order, y_first=False):
        self.sizes = {"dp": dp_size, "seq": seq_size}
        dp = bits_of("dp", dp_size)
        chips = bits_of("seq", seq_size, 2)
        order = [dp[i] for i in order] + dp[len(order) :]
        self.left = dp[::-1] + (chips[::-1] if y_first else [])
        self.steps = [(step, "half") for step in (chips if y_first else []) + order]
        self.steps += [(step, "join" if y_first else "sum") for step in chips]
        shape = (2,) * len(self.left) + (-1, terms[0].shape[1])
        self.terms = [term.reshape(shape) for term in terms]

    def start(self):
        step, kind = self.steps[0]
        if kind != "half":
            self.terms = [sum_of(self.terms)]
            return self.terms[0]
        dim = self.left.index(step)
        self.left.pop(dim)
        mine = lax.axis_index(step[0]) // step[1] % 2
        take = lambda term, index: lax.dynamic_index_in_dim(term, index, dim, keepdims=False)
        sent = sum_of([take(term, 1 - mine) for term in self.terms])
        self.terms = [take(term, mine) for term in self.terms]
        return sent

    def swap(self, sent):
        (axis, bit), kind = self.steps.pop(0)
        other = swap(sent, axis, self.sizes[axis], bit)
        if kind == "join":
            low = lax.axis_index(axis) // bit % 2 == 0
            pair = [jnp.where(low, sent, other), jnp.where(low, other, sent)]
            self.terms = [jnp.concatenate(pair, axis=0)]
        else:
            self.terms.append(other)

    def value(self):
        return sum_of(self.terms)


def sum_of(terms):
    total = terms[0]
    for term in terms[1:]:
        total = total + term
    return total


def tie(value, *others):
    return lax.optimization_barrier((value, *others))[0]


def together(*values):
    return lax.optimization_barrier(values)


class Gather:
    def __init__(self, value, dp_size, seq_size):
        self.sizes = {"dp": dp_size, "seq": seq_size}
        self.value = value[None]
        dp = bits_of("dp", dp_size)
        self.steps = dp[2:] + dp[1:2] + dp[:1] + bits_of("seq", seq_size, 2) + bits_of("seq", 2)

    def swap(self):
        axis, bit = self.steps[0]
        self.other = swap(self.value, axis, self.sizes[axis], bit)

    def join(self):
        axis, bit = self.steps.pop(0)
        if axis == "dp":
            self.value = jnp.concatenate([self.value, self.other], axis=0)
        else:
            low = lax.axis_index("seq") // bit % 2 == 0
            pair = [jnp.where(low, self.value, self.other), jnp.where(low, self.other, self.value)]
            self.value = jnp.concatenate(pair, axis=1)


def on_device(
    dp_size, seq_size,
    tokens, class_tokens, cot_patch, cot_class, lengths,
    matrices, matrices_moment1, matrices_moment2, matrices_ema,
    vectors, vectors_moment1, vectors_moment2, vectors_ema,
    talking, talking_moment1, talking_moment2, talking_ema,
):
    rows, width = tokens.shape
    images = class_tokens.shape[0]
    seq_index = lax.axis_index("seq")
    dp_index = lax.axis_index("dp")
    place = seq_index.astype(jnp.int32).reshape(1)
    row_share = width // dp_size

    slots = {0: tokens}
    slots[1] = swap(tokens, "seq", seq_size, 1)
    bit = 2
    while bit < seq_size:
        for slot in sorted(slot for slot in slots if slot % 2 == 0):
            slots[slot | bit] = swap(slots[slot], "seq", seq_size, bit)
        bit *= 2
    *prepared, t1, t2, t1_rows, t2_rows, query, k1, k2, v1, v2, kt1, kt2, vt1, vt2 = prepare(
        tokens, slots[1], class_tokens, matrices, vectors, talking
    )
    for slot in range(2, seq_size, 2):
        slots[slot + 1] = swap(tie(slots[slot], query), "seq", seq_size, 1)
    token_slots = [slots[slot] for slot in range(seq_size)]
    (
        e_high, e_low, pv, inverse, pv_bias, attended, kt_high, kt_low, v_high, v_low,
        patch_out, *kept, packed, scores,
    ) = forward(
        place, lengths, token_slots, matrices, vectors, t1, t2, prepared[3],
        [query, k1, k2, v1, v2, kt1, kt2, vt1, vt2],
    )
    parts = [packed] + [swap(packed, "seq", seq_size, bit) for bit in range(1, seq_size)]
    (
        class_out, d_attended, d_mixed, early_keep, early_send, partial, factors, vec_rows, class_terms,
    ) = middle(
        place, parts, vectors, prepared, class_tokens, cot_class, cot_patch,
        [patch_out, scores, attended, *kept], matrices,
    )

    early = Reduce([early_keep, swap(early_send, "seq", seq_size, 1)], dp_size, seq_size, (1, 0))
    partials = [partial] + [swap(partial, "seq", seq_size, bit) for bit in range(1, seq_size)]
    grad_class, factors = class_finish(partials, class_terms, class_tokens, vectors, matrices, factors)
    share = factors.shape[0] // seq_size
    at = (seq_index % 2 * (seq_size // 2) + seq_index // 2) * share
    gather = Gather(lax.dynamic_slice_in_dim(factors, at, share, 0), dp_size, seq_size)
    sent, gather.value, d_attended = together(early.start(), gather.value, d_attended)
    early.swap(sent)
    gather.swap()
    even, odd, late_keep, late_send = backward(
        dp_size, place, lengths, token_slots, [e_high, e_low, pv, inverse, pv_bias], d_attended,
        [kt_high, kt_low, v_high, v_low], query, [t1, t2, t1_rows, t2_rows], vec_rows, vectors, matrices,
    )

    late_send, odd, gather.other, early.terms[-1] = together(
        late_send, odd, gather.other, early.terms[-1]
    )
    late = Reduce([late_keep, swap(late_send, "seq", seq_size, 1)], dp_size, seq_size, (1, 0))
    odd = swap(odd, "seq", seq_size, 1)
    early.swap(early.start())
    gather.join()
    gather.swap()
    sent = late.start()
    late.swap(sent)
    even = tie(even, sent)
    chips = [even[i] + odd[i] for i in range(seq_size // 2)]
    bit = 1
    while 2 * bit < len(chips):
        for slot in range(0, len(chips), 2 * bit):
            chips[slot] = chips[slot] + swap(chips[slot + bit], "seq", seq_size, 2 * bit)
        bit *= 2
    far = swap(chips[bit], "seq", seq_size, 2 * bit)
    weight_rows, vector_columns = (
        lax.dynamic_slice_in_dim(tie(value, sent), dp_index * row_share, row_share, dim)
        for value, dim in ((matrices, 2), (vectors, 1))
    )
    late.terms[-1], weight_rows, vector_columns = together(late.terms[-1], weight_rows, vector_columns)
    class_share = None
    while late.steps or early.steps or gather.steps:
        after = []
        if late.steps:
            after = [late.start()]
            late.swap(after[0])
        if early.steps:
            early.terms[-1] = tie(early.terms[-1], *after)
            early.swap(early.start())
        if gather.steps:
            gather.join()
            gather.value = tie(gather.value, *after)
            if gather.steps:
                gather.swap()
                late.terms[-1], gather.other = together(late.terms[-1], gather.other)
        if far is not None:
            grad_tokens = token_grad(tokens, vectors, tie(chips[0], *after), far, d_mixed)
            far = None
            late.terms[-1], grad_tokens = together(late.terms[-1], grad_tokens)
    factors = gather.value
    mine = lax.dynamic_slice_in_dim(factors, dp_index * row_share, row_share, 2)
    class_share, class_squares, added = class_weights(images, mine, factors)
    late, early = late.value(), early.value()
    squares = squares_of(dp_size, place, early, late, added, class_squares)
    squares = squares + swap(squares, "seq", seq_size, 1)
    bit = 1
    while bit < dp_size:
        squares = squares + swap(squares, "dp", dp_size, bit)
        bit *= 2
    grads = []
    for value in (early, late):
        grads += [value, swap(value, "seq", seq_size, 1)]
    norm, *updated = optimizer(
        place, squares, [*grads, added], class_share,
        [weight_rows, matrices_moment1, matrices_moment2, matrices_ema],
        [vector_columns, vectors_moment1, vectors_moment2, vectors_ema],
        [talking, talking_moment1, talking_moment2, talking_ema],
    )
    return (patch_out, class_out, grad_tokens, grad_class, norm.reshape(()), *updated)


def solution(mesh):
    tokens = P(("dp", "seq"), None)
    by_group = P("dp", None)
    mats = P(None, None, "dp", None)
    vecs = P(None, "dp")
    body = functools.partial(on_device, mesh.shape["dp"], mesh.shape["seq"])
    return jax.shard_map(
        body,
        mesh=mesh,
        in_specs=(tokens, by_group, tokens, by_group, by_group, P(), mats, mats, mats,
                  P(), vecs, vecs, vecs, P(), P(), P(), P()),
        out_specs=(tokens, by_group, tokens, by_group, P(), mats, mats, mats, mats,
                   vecs, vecs, vecs, vecs, P(), P(), P(), P()),
        check_vma=False,
    )
```

```python
import functools

import jax
import jax.numpy as jnp
from jax import lax
from jax.experimental import pallas as pl
from jax.experimental.pallas import tpu as pltpu
from jax.sharding import PartitionSpec as P

STEP = 10
EPS_NORM = 1e-06
MASKED = -1e30
LR_MATRIX = 0.05
LR_VECTOR = 0.1
LR_TALKING = 0.2
BETA_ONE = 0.9
BETA_TWO = 0.999
ADAM_EPS = 1e-08
WEIGHT_DECAY = 0.05
EMA_RATE = 0.9
CLIP_NORM = 1.0
F32 = jnp.float32
BF16 = jnp.bfloat16
NN = (((1,), (0,)), ((), ()))
NT = (((1,), (1,)), ((), ()))
TN = (((0,), (0,)), ((), ()))
KERNEL_MIB, SMALL_MIB = 58, 24


def split(value):
    high = value.astype(BF16)
    return high, (value - high.astype(F32)).astype(BF16)


def mm(left, right, dims=NN):
    return lax.dot_general(left, right, dims, preferred_element_type=F32)


def mm3(left, right, dims=NN):
    return mm(left[0], right[0], dims) + (mm(left[0], right[1], dims) + mm(left[1], right[0], dims))


def mm3_tall(left, right, dims=NN):
    rows = left[0].shape[0]
    stacked = jnp.concatenate([part.astype(F32) for part in left], axis=0).astype(BF16)
    both = mm(stacked, right[0], dims)
    return both[:rows] + (both[rows:] + mm(left[0], right[1], dims))


def dot_tall(left, right, dims=NN):
    return mm3_tall(split(left), split(right), dims)


def dot3(left, right, dims=NN):
    return mm3(split(left), split(right), dims)


def norm_rows(values):
    average = jnp.mean(values, axis=-1, keepdims=True)
    centered = values - average
    variance = jnp.mean(centered * centered, axis=-1, keepdims=True)
    scale = lax.rsqrt(variance + EPS_NORM)
    return centered * scale, scale


def norm_back(grad, unit, scale):
    inner = jnp.mean(grad * unit, axis=-1, keepdims=True)
    return scale * (grad - jnp.mean(grad, axis=-1, keepdims=True) - unit * inner)


def gelu_both(values):
    half = 0.5 * (1.0 + lax.erf(values * 0.7071067811865476))
    slope = half + values * (0.3989422804014327 * jnp.exp(-0.5 * values * values))
    return values * half, slope


def row_sum(values):
    return jnp.sum(values, axis=0, keepdims=True)


def tail_forward(dot, inputs, attended, w_out, w_up, w_down, vecs):
    projected = dot(attended, w_out) + vecs[4:5]
    mixed = inputs + vecs[5:6] * projected
    unit, _ = norm_rows(mixed)
    normed = unit * vecs[6:7] + vecs[7:8]
    up_bias = jnp.concatenate([vecs[row : row + 1] for row in range(8, 12)], axis=1)
    hidden, slope = gelu_both(dot(normed, w_up) + up_bias)
    lowered = dot(hidden, w_down, NT) + vecs[12:13]
    return mixed + vecs[13:14] * lowered, (projected, mixed, hidden, slope, lowered)


def tail_backward(dot, cot, kept, w_out, w_up, w_down, vecs):
    projected, mixed, hidden, slope, lowered = kept
    width = cot.shape[1]
    unit, scale = norm_rows(mixed)
    normed = unit * vecs[6:7] + vecs[7:8]
    d_lowered = cot * vecs[13:14]
    d_hidden = dot(d_lowered, w_down) * slope
    d_normed = dot(d_hidden, w_up, NT)
    d_mixed = cot + norm_back(d_normed * vecs[6:7], unit, scale)
    d_projected = d_mixed * vecs[5:6]
    d_attended = dot(d_projected, w_out, NT)
    d_up = row_sum(d_hidden)
    rows = [
        row_sum(d_projected), row_sum(d_mixed * projected), row_sum(d_normed * unit), row_sum(d_normed),
        *[d_up[:, i * width : (i + 1) * width] for i in range(4)],
        row_sum(d_lowered), row_sum(cot * lowered),
    ]
    return d_mixed, d_attended, d_projected, d_hidden, d_lowered, normed, rows


def image_of(lengths_ref, images, positions):
    end = lengths_ref[0, 0]
    inside = (positions >= end).astype(jnp.int32)
    for image in range(1, images):
        end = end + lengths_ref[0, image]
        inside = inside + (positions >= end).astype(jnp.int32)
    return inside


def same_image(lengths_ref, images, place, slots, rows):
    queries = place * rows + lax.broadcasted_iota(jnp.int32, (1, rows), 1)
    query_image = image_of(lengths_ref, images, queries)
    parts = []
    for slot in range(slots):
        keys = jnp.bitwise_xor(place, slot) * rows + lax.broadcasted_iota(jnp.int32, (rows, 1), 0)
        parts.append(image_of(lengths_ref, images, keys) == query_image)
    return parts


def column_of(table, number):
    lanes = lax.broadcasted_iota(jnp.int32, (1, table.shape[1]), 1)
    return jnp.sum(jnp.where(lanes == number, table, 0.0), axis=1, keepdims=True)


def head_mask(heads, width):
    row = lax.broadcasted_iota(jnp.int32, (heads, width), 0)
    return jnp.where(lax.broadcasted_iota(jnp.int32, (heads, width), 1) // (width // heads) == row, 1.0, 0.0)


def spread(value, mask):
    return jnp.concatenate([value[i : i + 1] * mask for i in range(value.shape[0])], axis=0)


def repeat_rows(value, heads):
    shape = (heads, value.shape[1])
    return jnp.concatenate(
        [jnp.broadcast_to(value[i : i + 1], shape) for i in range(value.shape[0])], axis=0
    )


def fold_heads(value, mask):
    heads = mask.shape[0]
    return jnp.concatenate(
        [row_sum(value[i : i + heads] * mask) for i in range(0, value.shape[0], heads)], axis=0
    )


def head_sums(value, mask):
    return jnp.sum(spread(value, mask), axis=1, keepdims=True)


def rows_of(value, heads):
    return jnp.concatenate(
        [row_sum(value[i : i + heads]) for i in range(0, value.shape[0], heads)], axis=0
    )


def wide(column):
    return jnp.broadcast_to(column, (column.shape[0], 128))


def whole(shape):
    return pl.BlockSpec(shape, lambda *_: (0,) * len(shape))


def struct(shape, dtype=F32):
    return jax.ShapeDtypeStruct(shape, dtype)


def smem():
    return pl.BlockSpec(memory_space=pltpu.SMEM)


def anywhere():
    return pl.BlockSpec(memory_space=pl.ANY)


def weight_block(block, matrix, shape, columns=None):
    return pl.BlockSpec((None, None, shape[2], columns or shape[3]), lambda *_: (block, matrix, 0, 0))


def far_off(*operands):
    return [pltpu.with_memory_space_constraint(operand, pltpu.HBM) for operand in operands]


def copy_in(pairs, arrived):
    copies = [pltpu.make_async_copy(a, b, arrived.at[i]) for i, (a, b) in enumerate(pairs)]
    for copy in copies:
        copy.start()
    return copies


def limit(mebibytes):
    return pltpu.CompilerParams(vmem_limit_bytes=mebibytes << 20)


def prepare_kernel(
    own_ref, near_ref, class_ref, w_self_ref, w_class_ref, vecs_ref, talk_ref,
    normed_ref, query_c_ref, value_c_ref, key_rows_ref, score_ref, t1_ref, t2_ref, t1_rows_ref, t2_rows_ref,
    query_ref, k_high, k_low, v_high, v_low, kt_high, kt_low, vt_high, vt_low,
):
    rows, width = own_ref.shape
    heads = talk_ref.shape[0]
    size = width // heads
    scale = size ** (-0.5)
    vecs = vecs_ref[...]
    w_q, w_k, w_v = (split(w_self_ref[:, i * width : (i + 1) * width]) for i in range(3))
    tokens = jnp.concatenate([own_ref[...], near_ref[...]], axis=0)
    unit, _ = norm_rows(tokens)
    normed = split(unit * vecs[0:1] + vecs[1:2])
    query_ref[...] = (mm3((normed[0][:rows], normed[1][:rows]), w_q) + vecs[2:3]) * scale
    keys, values = mm3(normed, w_k), mm3(normed, w_v) + vecs[3:4]
    k_high[...], k_low[...] = split(keys)
    v_high[...], v_low[...] = split(values)
    kt_high[...], kt_low[...] = split(keys.T)
    vt_high[...], vt_low[...] = split(values.T)
    mask = head_mask(heads, width)
    unit, _ = norm_rows(class_ref[...])
    normed = unit * vecs[14:15] + vecs[15:16]
    both = dot_tall(normed, w_class_ref[...])
    query = both[:, :width] + vecs[16:17]
    normed_ref[...] = normed
    query_c_ref[...] = query
    value_c_ref[...] = both[:, 2 * width :] + vecs[17:18]
    key_rows_ref[...] = dot3(spread(query, mask), w_class_ref[:, width : 2 * width], NT) * scale
    score_ref[...] = wide(head_sums(query * both[:, width : 2 * width], mask) * scale)
    head_of = lax.broadcasted_iota(jnp.int32, (width, 1), 0) // size
    talk = talk_ref[...]
    talk_t = jnp.concatenate([talk, jnp.zeros((heads, 128 - talk.shape[1]), F32)], axis=1).T[: talk.shape[1], :]
    t1 = t2 = t1_rows = t2_rows = 0.0
    for head in range(heads):
        here = head_of == head
        t1 = t1 + jnp.where(here, talk_t[head : head + 1, :], 0.0)
        t2 = t2 + jnp.where(here, talk[head : head + 1, heads:], 0.0)
        t1_rows = t1_rows + mask[head : head + 1] * talk[:, head : head + 1]
        t2_rows = t2_rows + mask[head : head + 1] * talk_t[heads:, head : head + 1]
    t1_ref[...], t2_ref[...], t1_rows_ref[...], t2_rows_ref[...] = t1, t2, t1_rows, t2_rows


def prepare(own, near, class_tokens, matrices, vectors, talking):
    images, width = class_tokens.shape
    rows = own.shape[0]
    heads = talking.shape[0]
    pairs = images * heads
    outs = [struct((images, width))] * 3 + [
        struct((pairs, width)), struct((pairs, 128)),
        struct((width, heads)), struct((width, heads + 1)),
        struct((heads, width)), struct((heads + 1, width)),
        struct((rows, width)),
    ]
    outs += [struct((2 * rows, width), BF16)] * 4 + [struct((width, 2 * rows), BF16)] * 4
    own, class_tokens, matrices, vectors, talking = far_off(own, class_tokens, matrices, vectors, talking)
    operands = [own, near, class_tokens, matrices, matrices, vectors, talking]
    specs = [whole(operand.shape) for operand in operands]
    specs[3] = weight_block(0, 0, matrices.shape, 3 * width)
    specs[4] = weight_block(1, 0, matrices.shape, 3 * width)
    return pl.pallas_call(
        prepare_kernel,
        grid=(1,),
        in_specs=specs,
        out_specs=[whole(out.shape) for out in outs],
        out_shape=outs,
        compiler_params=limit(KERNEL_MIB),
        cost_estimate=pl.CostEstimate(flops=4 << 30, bytes_accessed=8 << 20, transcendentals=0),
        name="prepare",
    )(*operands)


def forward_kernel(slots, images, unroll, *refs):
    place_ref, lengths_ref = refs[:2]
    token_refs = refs[2 : 2 + slots]
    (
        vecs_ref, t1_ref, t2_ref, key_rows_ref, query_ref,
        k_high0, k_low0, v_high0, v_low0, kt_high0, kt_low0, vt_high0, vt_low0, mats_ref,
        e_high_hbm, e_low_hbm, pv_hbm, inverse_ref, pv_bias_ref, attended_ref,
        kt_high_hbm, kt_low_hbm, v_high_hbm, v_low_hbm,
        patch_ref, projected_ref, mixed_ref, hidden_hbm, slope_hbm, lowered_ref, packed_ref, scores_ref,
        k_three, vt_two, qt, bias, attended_t, w_kv, w_up, w_down, w_out, arrived,
        kt_high, kt_low, v_high, v_low, hidden_ref, slope_ref, e_high_ref, e_low_ref, pv_ref, leaving,
    ) = refs[2 + slots :]
    rows, width = token_refs[0].shape
    step = pl.program_id(0)
    place = place_ref[0]
    ready, columns = pl.ds(0, 2 * rows), lambda i: pl.ds(i * width, width)
    pairs = [
        (mats_ref.at[0, 0, :, pl.ds(width, 2 * width)], w_kv),
        (k_high0, k_three.at[ready, columns(0)]), (k_high0, k_three.at[ready, columns(1)]),
        (k_low0, k_three.at[ready, columns(2)]), (v_high0, v_high.at[ready, :]), (v_low0, v_low.at[ready, :]),
        (kt_high0, kt_high.at[:, ready]), (kt_low0, kt_low.at[:, ready]),
        (vt_high0, vt_two.at[columns(0), ready]), (vt_low0, vt_two.at[columns(1), ready]),
        (mats_ref.at[0, 0, :, pl.ds(3 * width, width)], w_out),
        (mats_ref.at[0, 1], w_up), (mats_ref.at[0, 2], w_down),
    ]
    fetches = [pltpu.make_async_copy(a, b, arrived.at[i]) for i, (a, b) in enumerate(pairs)]
    pairs = [(kt_high, kt_high_hbm), (kt_low, kt_low_hbm), (v_high, v_high_hbm), (v_low, v_low_hbm),
             (hidden_ref, hidden_hbm), (slope_ref, slope_hbm)]
    stores = [pltpu.make_async_copy(a, b, leaving.at[i]) for i, (a, b) in enumerate(pairs)]
    heads = inverse_ref.shape[0]
    groups = []
    for number in range(heads // unroll):
        here = pl.ds(number * unroll, unroll)
        groups.append([
            pltpu.make_async_copy(a.at[here], b.at[here], leaving.at[6 + 3 * number + i])
            for i, (a, b) in enumerate([(e_high_ref, e_high_hbm), (e_low_ref, e_low_hbm), (pv_ref, pv_hbm)])
        ])

    @pl.when(step == 0)
    def _():
        for fetch in fetches:
            fetch.start()
        vecs = vecs_ref[...]
        inside = same_image(lengths_ref, images, place, slots, rows)
        for slot in range(slots):
            bias[pl.ds(slot * rows, rows), :] = jnp.where(inside[slot], 0.0, MASKED)
        units = [norm_rows(ref[...])[0] for ref in token_refs[2:]]
        fetches[0].wait()
        w_k, w_v = split(w_kv[:, :width]), split(w_kv[:, width:])
        for slot in range(2, slots):
            here = pl.ds(slot * rows, rows)
            normed = split(units[slot - 2] * vecs[0:1] + vecs[1:2])
            keys, values = mm3(normed, w_k), mm3(normed, w_v) + vecs[3:4]
            high, low = split(keys)
            k_three[here, :] = jnp.concatenate([high, high, low], axis=1)
            v_high[here, :], v_low[here, :] = split(values)
            kt_high[:, here], kt_low[:, here] = split(keys.T)
            vt_two[:, here] = jnp.concatenate(split(values.T), axis=0)
        qt[...] = query_ref[...].T
        attended_t[...] = jnp.zeros_like(attended_t)
        for fetch in fetches[1:10]:
            fetch.wait()
        for store in stores[:4]:
            store.start()

    scores = []
    for u in range(unroll):
        high, low = split(qt[...] * column_of(t1_ref[...], step * unroll + u))
        scores.append(mm(k_three[...], jnp.concatenate([high, low, high], axis=0)) + bias[...])
    for u in range(unroll):
        exponentials = jnp.exp(scores[u] - jnp.max(scores[u], axis=0, keepdims=True))
        inverse = 1.0 / jnp.sum(exponentials, axis=0, keepdims=True)
        pair = split(exponentials)
        head = step * unroll + u
        e_high_ref[head], e_low_ref[head] = pair
        inverse_ref[head] = inverse
        both = mm(vt_two[...], pair[0])
        values = (both[:width] + (both[width:] + mm(vt_two[:width, :], pair[1]))) * inverse
        pv_ref[head] = values
        attended_t[...] += values * column_of(t2_ref[...], head)
    for number, group in enumerate(groups):

        @pl.when(step == number)
        def _(group=group):
            for copy in group:
                copy.start()

    @pl.when(step == pl.num_programs(0) - 1)
    def _():
        inside = jnp.where(bias[...] < 0.0, 0.0, 1.0).astype(BF16)
        both = mm(vt_two[...], inside)
        summed = both[:width] + both[width:]
        pv_bias_ref[...] = summed
        attended = (attended_t[...] + summed * t2_ref[:, 8:9]).T
        attended_ref[...] = attended
        for fetch in fetches[10:]:
            fetch.wait()
        vecs = vecs_ref[...]
        patch, kept = tail_forward(
            dot3, token_refs[0][...], attended, w_out[...], w_up[...], w_down[...], vecs
        )
        patch_ref[...] = patch
        for ref, value in zip((projected_ref, mixed_ref, hidden_ref, slope_ref, lowered_ref), kept):
            ref[...] = value
        for store in stores[4:]:
            store.start()
        unit, _ = norm_rows(patch)
        normed = split(unit * vecs[14:15] + vecs[15:16])
        pairs = images * 8
        image = lax.broadcasted_iota(jnp.int32, (pairs, 1), 0) // 8
        positions = place * rows + lax.broadcasted_iota(jnp.int32, (1, rows), 1)
        belong = image_of(lengths_ref, images, positions) == image
        class_scores = mm3(split(key_rows_ref[...]), normed, NT)
        class_scores = jnp.where(belong, class_scores, MASKED)
        scores_ref[...] = class_scores
        top = jnp.max(class_scores, axis=1, keepdims=True)
        weights = jnp.where(belong, jnp.exp(class_scores - top), 0.0)
        packed_ref[:, :width] = mm3(split(weights), normed)
        lane = lax.broadcasted_iota(jnp.int32, (1, 128), 1)
        total = jnp.sum(weights, axis=1, keepdims=True)
        packed_ref[:, width:] = jnp.where(lane < 64, top, total)
        for store in stores + [copy for group in groups for copy in group]:
            store.wait()


def by_head(unroll, shape):
    return pl.BlockSpec((unroll,) + shape[1:], lambda g: (g, 0, 0))


def forward(place, lengths, token_slots, matrices, vectors, t1, t2, key_rows, projected):
    slots, (rows, width) = len(token_slots), token_slots[0].shape
    total, heads = slots * rows, 8
    unroll = 4 if total <= 1024 else 1
    hidden = matrices.shape[3]
    pairs = key_rows.shape[0]
    outs = [
        struct((heads, total, rows), BF16), struct((heads, total, rows), BF16), struct((heads, width, rows)),
        struct((heads, 1, rows)), struct((width, rows)), struct((rows, width)),
        struct((width, total), BF16), struct((width, total), BF16),
        struct((total, width), BF16), struct((total, width), BF16),
        struct((rows, width)), struct((rows, width)), struct((rows, width)),
        struct((rows, hidden)), struct((rows, hidden)), struct((rows, width)),
        struct((pairs, width + 128)), struct((pairs, rows)),
    ]
    away = (0, 1, 2, 6, 7, 8, 9, 13, 14)
    out_specs = [anywhere() if i in away else whole(out.shape) for i, out in enumerate(outs)]
    operands = [*token_slots, vectors, t1, t2, key_rows, *projected, matrices]
    in_specs = [whole(operand.shape) for operand in operands]
    in_specs[-9:] = [anywhere()] * 9
    flops = 2 * 3 * ((2 * heads + 1) * total + 9 * width) * rows * width
    return pl.pallas_call(
        functools.partial(forward_kernel, slots, lengths.shape[1], unroll),
        grid=(heads // unroll,),
        in_specs=[smem(), smem()] + in_specs,
        out_specs=out_specs,
        out_shape=outs,
        scratch_shapes=[
            pltpu.VMEM((total, 3 * width), BF16),
            pltpu.VMEM((2 * width, total), BF16),
            pltpu.VMEM((width, rows), F32),
            pltpu.VMEM((total, rows), F32),
            pltpu.VMEM((width, rows), F32),
            pltpu.VMEM((width, 2 * width), F32),
            pltpu.VMEM((width, hidden), F32),
            pltpu.VMEM((width, hidden), F32),
            pltpu.VMEM((width, width), F32),
            pltpu.SemaphoreType.DMA((13,)),
            pltpu.VMEM((width, total), BF16),
            pltpu.VMEM((width, total), BF16),
            pltpu.VMEM((total, width), BF16),
            pltpu.VMEM((total, width), BF16),
            pltpu.VMEM((rows, hidden), F32),
            pltpu.VMEM((rows, hidden), F32),
            pltpu.VMEM((heads, total, rows), BF16),
            pltpu.VMEM((heads, total, rows), BF16),
            pltpu.VMEM((heads, width, rows), F32),
            pltpu.SemaphoreType.DMA((6 + 3 * heads // unroll,)),
        ],
        compiler_params=limit(KERNEL_MIB),
        cost_estimate=pl.CostEstimate(
            flops=flops, bytes_accessed=24 << 20, transcendentals=heads * total * rows
        ),
        name="forward",
    )(place, lengths, *operands)


def middle_kernel(images, slots, *refs):
    place_ref = refs[0]
    parts = [ref[...] for ref in refs[1 : 1 + slots]]
    (
        vecs_ref, normed_c_ref, query_c_ref, value_c_ref, key_rows_ref, own_ref,
        class_ref, cot_class_ref, cot_patch_ref, patch_ref, scores_ref,
        attended_hbm, projected_hbm, mixed_hbm, hidden_hbm, slope_hbm, lowered_hbm, mats_ref,
        class_out_ref, d_attended_ref, d_mixed_ref, keep_ref, send_ref, partial_ref,
        factors_ref, vec_rows_ref, class_terms_ref,
        wc0, wc1, wc2, ws0, ws1, ws2, attended_ref, projected_ref, mixed_ref, hidden_ref, slope_ref, lowered_ref,
        keep, send, arrived, stored,
    ) = refs[1 + slots :]
    width = class_ref.shape[1]
    heads = 8
    size = width // heads
    copies = copy_in(
        [(mats_ref.at[1, 0, :, pl.ds(2 * width, 2 * width)], wc0), (mats_ref.at[1, 1], wc1), (mats_ref.at[1, 2], wc2),
         (lowered_hbm, lowered_ref), (hidden_hbm, hidden_ref), (mats_ref.at[0, 2], ws2), (slope_hbm, slope_ref),
         (mixed_hbm, mixed_ref), (mats_ref.at[0, 1], ws1), (projected_hbm, projected_ref),
         (attended_hbm, attended_ref), (mats_ref.at[0, 0, :, pl.ds(3 * width, width)], ws0)], arrived)
    vecs = vecs_ref[...]
    vecs_s, vecs_c = vecs[:14], vecs[14:]
    mask = head_mask(heads, width)
    first = jnp.where(place_ref[0] == 0, 1.0, 0.0)
    own_score = own_ref[:, :1]
    normed_c = normed_c_ref[...]
    normed_rep = repeat_rows(normed_c, heads)
    top = own_score
    for part in parts:
        top = jnp.maximum(top, part[:, width : width + 1])
    own_weight = jnp.exp(own_score - top)
    total, summed = own_weight, own_weight * normed_rep
    for part in parts:
        rescale = jnp.exp(part[:, width : width + 1] - top)
        total = total + part[:, width + 64 : width + 65] * rescale
        summed = summed + part[:, :width] * rescale
    value_rows = summed / total
    own_prob = own_weight / total
    unit_p, scale_p = norm_rows(patch_ref[...])
    normed_p = split(unit_p * vecs_c[0:1] + vecs_c[1:2])
    scores = scores_ref[...]
    probs = jnp.where(scores > 0.5 * MASKED, jnp.exp(scores - top) * (1.0 / total), 0.0)
    for copy in copies[:3]:
        copy.wait()
    w_v = split(wc0[:, :width])
    class_attended = fold_heads(mm3_tall(split(value_rows), w_v), mask) + vecs_c[3:4]
    w_out_c = wc0[:, width:]
    class_out, kept_c = tail_forward(
        dot_tall, class_ref[...], class_attended, w_out_c, wc1[...], wc2[...], vecs_c
    )
    class_out_ref[...] = class_out
    d_mixed_c, d_attended_c, d_projected_c, d_hidden_c, d_lowered_c, normed2_c, tail_rows_c = (
        tail_backward(dot_tall, cot_class_ref[...], kept_c, w_out_c, wc1[...], wc2[...], vecs_c)
    )
    delta = head_sums(d_attended_c * class_attended, mask)
    cot_rows = mm3_tall(split(spread(d_attended_c, mask)), w_v, NT)
    cot_const = head_sums(d_attended_c * vecs_c[3:4], mask)
    cot_split = split(cot_rows)
    d_scores = probs * (mm3_tall(cot_split, normed_p, NT) + cot_const - delta)
    d_own = own_prob * (head_sums(d_attended_c * value_c_ref[...], mask) - delta)
    key_rows = key_rows_ref[...]
    d_split = split(d_scores)
    d_normed_p = mm3(d_split, split(key_rows), TN) + mm3(split(probs), cot_split, TN)
    partial_ref[...] = mm3_tall(d_split, normed_p)
    cot = cot_patch_ref[...] + norm_back(d_normed_p * vecs_c[0:1], unit_p, scale_p)
    class_terms_ref[...] = jnp.concatenate(
        [rows_of(d_own * key_rows + own_prob * cot_rows, heads), d_mixed_c], axis=0
    )
    query_c = query_c_ref[...]
    chunks = lambda value: [value[:, i * width : (i + 1) * width] for i in range(4)]
    factors_ref[...] = jnp.concatenate(
        [normed_c, class_attended, normed2_c, d_lowered_c, d_own * normed_rep, value_rows,
         jnp.zeros_like(query_c), query_c * size ** (-0.5), d_attended_c, d_projected_c,
         *chunks(d_hidden_c), *chunks(kept_c[2])], axis=0)
    for copy in copies[3:]:
        copy.wait()
    projected, mixed, hidden, lowered = projected_ref[...], mixed_ref[...], split(hidden_ref[...]), lowered_ref[...]
    unit, scale = norm_rows(mixed)
    normed = split(unit * vecs_s[6:7] + vecs_s[7:8])
    d_lowered = cot * vecs_s[13:14]
    d_low_split = split(d_lowered)
    d_hidden = mm3(d_low_split, split(ws2[...])) * slope_ref[...]
    d_hid_split = split(d_hidden)
    g_down = mm3(d_low_split, hidden, TN)
    g_up = mm3(normed, d_hid_split, TN)
    even = jnp.bitwise_and(place_ref[0], 1) == 0
    size_up = g_up.shape[1]
    send[:, :size_up] = jnp.where(even, g_down, g_up)
    keep[:, :size_up] = jnp.where(even, g_up, g_down)
    bulk = pl.ds(0, size_up)
    leaving = copy_in(
        [(send.at[:, bulk], send_ref.at[:, bulk]), (keep.at[:, bulk], keep_ref.at[:, bulk])], stored
    )
    d_normed = mm3(d_hid_split, split(ws1[...]), NT)
    d_mixed = cot + norm_back(d_normed * vecs_s[6:7], unit, scale)
    d_projected = d_mixed * vecs_s[5:6]
    d_proj_split = split(d_projected)
    g_out = mm3(split(attended_ref[...]), d_proj_split, TN)
    left = g_out[:, :256]
    right = jnp.concatenate([g_out[:, 256:], jnp.zeros((width, 512 - width), F32)], axis=1)
    send[:, size_up:] = jnp.where(even, right, left)
    keep[:, size_up:] = jnp.where(even, left, right)
    rest = pl.ds(size_up, 256)
    for i, (a, b) in enumerate([(send, send_ref), (keep, keep_ref)]):
        leaving.append(pltpu.make_async_copy(a.at[:, rest], b.at[:, rest], stored.at[2 + i]))
        leaving[-1].start()
    d_mixed_ref[...] = d_mixed
    d_attended_ref[...] = mm3(d_proj_split, split(ws0[...]), NT)
    d_up = row_sum(d_hidden)
    tail_rows = [
        row_sum(d_projected), row_sum(d_mixed * projected), row_sum(d_normed * unit), row_sum(d_normed),
        *[d_up[:, i * width : (i + 1) * width] for i in range(4)],
        row_sum(d_lowered), row_sum(cot * lowered),
    ]
    zero = jnp.zeros((1, width), F32)
    vec_rows_ref[...] = jnp.concatenate(
        [zero] * 4 + tail_rows
        + [row_sum(d_normed_p * unit_p), row_sum(d_normed_p), zero, row_sum(d_attended_c) * first]
        + [row * first for row in tail_rows_c], axis=0)
    for copy in leaving:
        copy.wait()


def middle(place, parts, vectors, prepared, class_tokens, cot_class, cot_patch, patch, scores, kept, matrices):
    images, width = class_tokens.shape
    rows = cot_patch.shape[0]
    hidden = matrices.shape[3]
    pairs = parts[0].shape[0]
    operands = [*parts, vectors, *prepared, class_tokens, cot_class, cot_patch, patch, scores, *kept, matrices]
    outs = [
        struct((images, width)), struct((rows, width)), struct((rows, width)),
        struct((width, hidden + 256)), struct((width, hidden + 256)), struct((pairs, width)),
        struct((16 * images + 2 * pairs, width)), struct((28, width)), struct((2 * images, width)),
    ]
    in_specs = [whole(operand.shape) for operand in operands]
    in_specs[-1 - len(kept) :] = [anywhere()] * (1 + len(kept))
    out_specs = [whole(out.shape) for out in outs]
    out_specs[3:5] = [anywhere()] * 2
    return pl.pallas_call(
        functools.partial(middle_kernel, images, len(parts)),
        grid=(1,),
        in_specs=[smem()] + in_specs,
        out_specs=out_specs,
        out_shape=outs,
        scratch_shapes=[pltpu.VMEM((width, 2 * width), F32)]
        + [pltpu.VMEM((width, hidden), F32)] * 2
        + [pltpu.VMEM((width, width), F32)]
        + [pltpu.VMEM((width, hidden), F32)] * 2
        + [pltpu.VMEM(value.shape, F32) for value in kept]
        + [pltpu.VMEM((width, hidden + 256), F32)] * 2
        + [pltpu.SemaphoreType.DMA((12,)), pltpu.SemaphoreType.DMA((4,))],
        compiler_params=limit(KERNEL_MIB),
        cost_estimate=pl.CostEstimate(flops=8 << 30, bytes_accessed=28 << 20, transcendentals=1 << 19),
        name="middle",
    )(place, *operands)


def class_kernel(slots, *refs):
    partial_refs = refs[:slots]
    terms_ref, class_ref, vecs_ref, w_ref, factors_ref, grad_ref, factors_out_ref = refs[slots:]
    images, width = class_ref.shape
    pairs = partial_refs[0].shape[0]
    heads = pairs // images
    mask = head_mask(heads, width)
    at = 4 * images
    query_rows = sum_of([factors_ref[at : at + pairs, :]] + [ref[...] for ref in partial_refs])
    w_k, w_q = w_ref[:, width : 2 * width], w_ref[:, :width]
    d_query = fold_heads(dot_tall(query_rows, w_k), mask) * (width // heads) ** (-0.5)
    d_normed = dot_tall(d_query, w_q, NT) + terms_ref[:images, :]
    unit, scale = norm_rows(class_ref[...])
    grad_ref[...] = terms_ref[images:, :] + norm_back(d_normed * vecs_ref[14:15, :], unit, scale)
    count = factors_ref.shape[0]
    factors_out_ref[:count, :] = factors_ref[...]
    factors_out_ref[at : at + pairs, :] = query_rows
    at = at + 2 * pairs
    factors_out_ref[at : at + images, :] = d_query
    added = [row_sum(d_normed * unit), row_sum(d_normed), row_sum(d_query), jnp.zeros((5, width), F32)]
    factors_out_ref[count:, :] = jnp.concatenate(added, axis=0)


def class_finish(partials, terms, class_tokens, vectors, matrices, factors):
    operands = [*partials, *far_off(terms, class_tokens, vectors, matrices, factors)]
    specs = [whole(operand.shape) for operand in operands]
    specs[-2] = weight_block(1, 0, matrices.shape, 2 * class_tokens.shape[1])
    outs = [struct(class_tokens.shape), struct((factors.shape[0] + 8, factors.shape[1]))]
    return pl.pallas_call(
        functools.partial(class_kernel, len(partials)),
        grid=(1,),
        in_specs=specs,
        out_specs=[whole(out.shape) for out in outs],
        out_shape=outs,
        compiler_params=limit(SMALL_MIB),
        cost_estimate=pl.CostEstimate(flops=1 << 29, bytes_accessed=3 << 20, transcendentals=0),
        name="class_finish",
    )(*operands)


def class_weights_kernel(images, mine_ref, factors_ref, grads_ref, squares_ref, small_ref):
    groups, count, width = factors_ref.shape
    heads = 8
    pairs = images * heads
    mask = head_mask(heads, width)
    at = 4 * images + 2 * pairs

    def rows(ref, begin, count=images):
        return jnp.concatenate([ref[g, begin : begin + count, :] for g in range(groups)], axis=0)

    def chunked(begin):
        return jnp.concatenate([rows(factors_ref, begin + i * images) for i in range(4)], axis=1)

    def headed(left, right):
        return dot3(rows(mine_ref, left, pairs), spread(rows(factors_ref, right), mask), TN)

    grads_ref[0, :, :width] = dot3(rows(mine_ref, 0), rows(factors_ref, at), TN)
    grads_ref[0, :, width : 2 * width] = headed(4 * images, at + images)
    grads_ref[0, :, 2 * width : 3 * width] = headed(4 * images + pairs, at + 2 * images)
    grads_ref[0, :, 3 * width :] = dot3(rows(mine_ref, images), rows(factors_ref, at + 3 * images), TN)
    grads_ref[1] = dot3(rows(mine_ref, 2 * images), chunked(at + 4 * images), TN)
    grads_ref[2] = dot3(rows(mine_ref, 3 * images), chunked(at + 8 * images), TN)
    grads = grads_ref[...]
    squares_ref[...] = jnp.broadcast_to(jnp.sum(grads * grads), squares_ref.shape)
    added = sum_of([mine_ref[g, count - 8 :, :] for g in range(groups)])
    lanes = 128 - 22
    share = added.shape[1]
    added = jnp.concatenate([jnp.zeros((14, share), F32), added, jnp.zeros((lanes, share), F32)], axis=0)
    small_ref[...] = added.T


def class_weights(images, mine, factors):
    share = mine.shape[2]
    outs = [struct((3, share, 4 * factors.shape[2])), struct((8, 128)), struct((share, 128))]
    return pl.pallas_call(
        functools.partial(class_weights_kernel, images),
        grid=(1,),
        in_specs=[whole(mine.shape), whole(factors.shape)],
        out_specs=[whole(out.shape) for out in outs],
        out_shape=outs,
        compiler_params=limit(KERNEL_MIB),
        cost_estimate=pl.CostEstimate(flops=1 << 29, bytes_accessed=3 << 20, transcendentals=0),
        name="class_weights",
    )(mine, factors)


def mm3_wide(left, right):
    width = right[0].shape[1]
    both = mm(left[0], jnp.concatenate(right, axis=1))
    return both[:, :width] + (both[:, width:] + mm(left[1], right[0]))


def backward_kernel(slots, images, dp_size, unroll, *refs):
    place_ref, lengths_ref = refs[:2]
    token_hbm = refs[2 : 2 + slots]
    (
        e_high_ref, e_low_ref, pv_ref, inverse_ref, pv_bias_ref, cot_ref,
        kt_high, kt_low, v_high, v_low, query_ref, t1_ref, t2_ref, t1_rows, t2_rows,
        vec_rows_ref, vecs_ref, mats_ref,
    ) = refs[2 + slots : 20 + slots]
    (
        even_ref, odd_ref, keep_ref, send_ref,
        d_keys, d_values, c1, c2, cot_t, qt, d_qt, v_three, w_ref, tokens, arrived,
    ) = refs[20 + slots :]
    rows, width = cot_ref.shape
    step = pl.program_id(0)
    size = width // 8
    lanes = lax.broadcasted_iota(jnp.int32, (1, 128), 1)
    pairs = [(mats_ref.at[0, 0, :, pl.ds(0, 3 * width)], w_ref)]
    pairs += [(ref, tokens.at[i]) for i, ref in enumerate(token_hbm)]
    copies = [pltpu.make_async_copy(a, b, arrived.at[i]) for i, (a, b) in enumerate(pairs)]

    @pl.when(step == 0)
    def _():
        for copy in copies:
            copy.start()
        cot_t[...] = cot_ref[...].T
        qt[...] = query_ref[...].T
        d_qt[...] = jnp.zeros_like(d_qt)
        d_keys[...] = jnp.zeros_like(d_keys)
        c1[...] = jnp.zeros_like(c1)
        v_three[...] = jnp.concatenate([v_high[...], v_high[...], v_low[...]], axis=1)
        c2[...] = jnp.where(
            lanes == 8, jnp.sum(cot_t[...] * pv_bias_ref[...], axis=1, keepdims=True), 0.0
        )
        inside = jnp.concatenate(same_image(lengths_ref, images, place_ref[0], slots, rows), axis=0)
        inside = jnp.where(inside, 1.0, 0.0).astype(BF16)
        high, low = split(cot_ref[...] * t2_rows[8:9, :])
        d_values[...] = mm(inside, high) + mm(inside, low)

    found = []
    for u in range(unroll):
        head = step * unroll + u
        t2_column, inverse = column_of(t2_ref[...], head), inverse_ref[u]
        crossed = cot_t[...] * pv_ref[u]
        c2[...] += jnp.where(lanes == head, jnp.sum(crossed, axis=1, keepdims=True), 0.0)
        delta = jnp.sum(crossed * t2_column, axis=0, keepdims=True) * inverse
        high, low = split(cot_t[...] * (t2_column * inverse))
        found.append((mm(v_three[...], jnp.concatenate([high, low, high], axis=0)), delta))
    for u in range(unroll):
        head = step * unroll + u
        d_probs, delta = found[u]
        pair = (e_high_ref[u], e_low_ref[u])
        d_mixed = split((pair[0].astype(F32) + pair[1].astype(F32)) * (d_probs - delta))
        inverse_rows = jnp.broadcast_to(inverse_ref[u], (8, rows)).T[:, :1]
        cot = split(cot_ref[...] * inverse_rows * t2_rows[pl.ds(head, 1), :])
        d_values[...] += mm3_wide(pair, cot)
        d_keys[...] += mm3_wide(d_mixed, split(query_ref[...] * t1_rows[pl.ds(head, 1), :]))
        back = mm3((kt_high[...], kt_low[...]), d_mixed)
        d_qt[...] += back * column_of(t1_ref[...], head)
        c1[...] += jnp.where(lanes == head, jnp.sum(back * qt[...], axis=1, keepdims=True), 0.0)

    @pl.when(step == pl.num_programs(0) - 1)
    def _():
        for copy in copies:
            copy.wait()
        d_query = d_qt[...].T * size ** (-0.5)
        w_q, w_k, w_v = (split(w_ref[:, i * width : (i + 1) * width]) for i in range(3))
        gain = shift = g_k = g_v = 0.0
        for slot in range(slots):
            here = pl.ds(slot * rows, rows)
            unit, _ = norm_rows(tokens[slot])
            normed = split(unit * vecs_ref[0:1, :] + vecs_ref[1:2, :])
            dk, dv = split(d_keys[here, :]), split(d_values[here, :])
            piece = mm3(dk, w_k, NT) + mm3(dv, w_v, NT)
            if slot == 0:
                dq = split(d_query)
                piece = piece + mm3(dq, w_q, NT)
                g_q = mm3(normed, dq, TN)
            (odd_ref if slot % 2 else even_ref)[slot // 2] = piece
            gain, shift = gain + row_sum(piece * unit), shift + row_sum(piece)
            g_k, g_v = g_k + mm3(normed, dk, TN), g_v + mm3(normed, dv, TN)
        added = jnp.concatenate(
            [gain, shift, row_sum(d_query), row_sum(d_values[...]), jnp.zeros((4, width), F32)], axis=0
        )
        vec_rows = jnp.concatenate([vec_rows_ref[0:8, :] + added, vec_rows_ref[8:28, :]], axis=0)
        fold = lambda value: jnp.concatenate(
            [row_sum(value[i * size : (i + 1) * size]) for i in range(8)], axis=0
        )
        pre, post = fold(c1[...]).T[:8, :], fold(c2[...])
        count = vec_rows.shape[0]
        talk = jnp.concatenate([pre, post[:, :9], jnp.zeros((8, 128 - count - 17), F32)], axis=1)
        block = width // dp_size
        talk = jnp.concatenate([talk, jnp.zeros((block - 8, 128 - count), F32)], axis=0)
        talk = jnp.concatenate([talk] * dp_size, axis=0)
        small = jnp.concatenate([vec_rows.T, talk], axis=1)
        even = jnp.bitwise_and(place_ref[0], 1) == 0
        left = jnp.concatenate([g_q, g_k[:, :256]], axis=1)
        right = jnp.concatenate([g_k[:, 256:], g_v, small], axis=1)
        keep_ref[...] = jnp.where(even, left, right)
        send_ref[...] = jnp.where(even, right, left)


def backward(dp_size, place, lengths, token_slots, found, cot, keys_values, query, tables,
             vec_rows, vectors, matrices):
    rows, width = cot.shape
    heads, total, _ = found[0].shape
    slots, unroll = total // rows, 2 if total <= 1024 else 1
    operands = [*token_slots, *found, cot, *keys_values, query, *tables, vec_rows, vectors, matrices]
    specs = [whole(operand.shape) for operand in operands]
    specs[:slots] = [anywhere()] * slots
    specs[slots : slots + 4] = [by_head(unroll, operand.shape) for operand in found[:4]]
    specs[-1] = anywhere()
    outs = [struct((slots // 2, rows, width))] * 2 + [struct((width, 640))] * 2
    return pl.pallas_call(
        functools.partial(backward_kernel, slots, lengths.shape[1], dp_size, unroll),
        grid=(heads // unroll,),
        in_specs=[smem(), smem()] + specs,
        out_specs=[whole(out.shape) for out in outs],
        out_shape=outs,
        scratch_shapes=[pltpu.VMEM((total, width), F32)] * 2
        + [pltpu.VMEM((width, 128), F32)] * 2
        + [pltpu.VMEM((width, rows), F32)] * 3
        + [
            pltpu.VMEM((total, 3 * width), BF16),
            pltpu.VMEM((width, 3 * width), F32),
            pltpu.VMEM((slots, rows, width), F32),
            pltpu.SemaphoreType.DMA((1 + slots,)),
        ],
        compiler_params=limit(KERNEL_MIB),
        cost_estimate=pl.CostEstimate(
            flops=6 * (4 * heads + 6) * total * rows * width, bytes_accessed=24 << 20, transcendentals=0
        ),
        name="backward",
    )(place, lengths, *operands)


def token_grad_kernel(tokens_ref, vecs_ref, own_ref, near_ref, far_ref, tail_ref, grad_ref):
    unit, scale = norm_rows(tokens_ref[...])
    d_normed = own_ref[...] + near_ref[...] + far_ref[...]
    grad_ref[...] = tail_ref[...] + norm_back(d_normed * vecs_ref[0:1, :], unit, scale)


def token_grad(tokens, vectors, own, near, far, tail):
    operands = [*far_off(tokens, vectors), own, near, far, *far_off(tail)]
    return pl.pallas_call(
        token_grad_kernel,
        out_shape=struct(tokens.shape),
        compiler_params=limit(SMALL_MIB),
        cost_estimate=pl.CostEstimate(flops=1 << 21, bytes_accessed=2 << 20, transcendentals=0),
        name="token_grad",
    )(*operands)


def squares_kernel(dp_size, counts, *refs):
    place_ref, added_ref, class_ref = refs[:3]
    early_refs = refs[3 : 3 + counts[0]]
    late_refs = refs[3 + counts[0] : 3 + sum(counts)]
    out_ref, early_ref, late_ref = refs[3 + sum(counts) :]
    odd = jnp.bitwise_and(place_ref[0], 1) == 1
    early = sum_of([ref[...] for ref in early_refs])
    late = sum_of([ref[...] for ref in late_refs])
    early_ref[...], late_ref[...] = early, late
    small = late[:, 512:] + jnp.where(odd, added_ref[...], 0.0)
    lane = lax.broadcasted_iota(jnp.int32, small.shape, 1)
    talk = jnp.logical_and(odd, jnp.logical_and(lane >= 28, lane < 45))
    small = small * small * jnp.where(talk, 1.0 / dp_size, 1.0)
    total = jnp.sum(small)
    for value in (late[:, :512], early):
        total = total + jnp.sum(value * value)
    out_ref[...] = 0.5 * class_ref[...] + total


def squares_of(dp_size, place, added, class_squares, early, late):
    operands = [added, class_squares, *early, *late]
    outs = [struct((8, 128)), struct(early[0].shape), struct(late[0].shape)]
    return pl.pallas_call(
        functools.partial(squares_kernel, dp_size, (len(early), len(late))),
        grid=(1,),
        in_specs=[smem()] + [whole(operand.shape) for operand in operands],
        out_specs=[whole(out.shape) for out in outs],
        out_shape=outs,
        compiler_params=limit(SMALL_MIB),
        cost_estimate=pl.CostEstimate(flops=1 << 18, bytes_accessed=1 << 20, transcendentals=0),
        name="squares",
    )(place, *operands)


def adam_step(weight, gradient, moment1, moment2, rate, decay):
    first = BETA_ONE * moment1 + (1.0 - BETA_ONE) * gradient
    second = BETA_TWO * moment2 + (1.0 - BETA_TWO) * gradient * gradient
    first_hat = first * (1.0 / (1.0 - BETA_ONE**STEP))
    second_hat = second * (1.0 / (1.0 - BETA_TWO**STEP))
    updated = weight - rate * (first_hat / (jnp.sqrt(second_hat) + ADAM_EPS) + decay * weight)
    return (updated, first, second)


def adam_kernel(sliced, *refs):
    (
        place_ref, squares_ref, early_own, early_other, late_own, late_other, added_ref,
        class_ref, w_ref, m1_ref, m2_ref, ema_ref, v_ref, v1_ref, v2_ref, v_ema_ref,
        t_ref, t1_ref, t2_ref, t_ema_ref,
    ) = refs[:20]
    norm_ref, new_ref, first_ref, second_ref, average_ref = refs[20:25]
    v_outs, t_outs = refs[25:29], refs[29:33]
    grads, columns = refs[33:35]
    step = pl.program_id(0)
    norm = jnp.sqrt(squares_ref[0:1, 0:1])
    factor = jnp.minimum(1.0, CLIP_NORM / norm)

    def store(outs, weight, gradient, moment1, moment2, ema, rate, decay):
        updated, first, second = adam_step(weight, gradient * factor, moment1, moment2, rate, decay)
        average = EMA_RATE * ema + (1.0 - EMA_RATE) * updated
        for out, value in zip(outs, (updated, first, second, average)):
            out[...] = value

    @pl.when(step == 0)
    def _():
        norm_ref[...] = norm
        even = jnp.bitwise_and(place_ref[0], 1) == 0
        pair = lambda own, other: (jnp.where(even, own[...], other[...]), jnp.where(even, other[...], own[...]))
        early_left, early_right = pair(early_own, early_other)
        late_left, late_right = pair(late_own, late_other)
        hidden = grads.shape[2]
        grads[0] = jnp.concatenate(
            [late_left, late_right[:, :512], early_left[:, hidden:], early_right[:, hidden : hidden + 128]],
            axis=1,
        )
        grads[1] = early_left[:, :hidden]
        grads[2] = early_right[:, :hidden]
        small = late_right[:, 512:] + added_ref[...]
        count = v_ref.shape[0]
        if sliced:
            columns[:, :count] = v_ref[...].T
            share = small.shape[0]
            begin = pl.multiple_of(place_ref[1] * share, share)
            weight = columns[pl.ds(begin, share), :].T[:count, :]
        else:
            weight = v_ref[...]
        store(v_outs, weight, small.T[:count, :], v1_ref[...], v2_ref[...], v_ema_ref[...], LR_VECTOR, 0.0)
        talk = small[:8, count : count + 17]
        store(t_outs, t_ref[...], talk, t1_ref[...], t2_ref[...], t_ema_ref[...], LR_TALKING, 0.0)

    self_grad = grads[jnp.minimum(step, 2)]
    grad = jnp.where(step < 3, self_grad, class_ref[jnp.maximum(step - 3, 0)])
    store((new_ref, first_ref, second_ref, average_ref), w_ref[...], grad, m1_ref[...], m2_ref[...],
          ema_ref[...], LR_MATRIX, WEIGHT_DECAY)


def optimizer(place, squares, grads, class_share, mats, vecs, talks):
    shape = mats[1].shape
    sliced = mats[0].shape != shape
    block = pl.BlockSpec((None, None) + shape[2:], lambda i, _: (i // 3, i % 3, 0, 0))
    operands = [squares, *grads, class_share, *far_off(*mats, *vecs, *talks)]
    specs = [whole(operand.shape) for operand in operands]
    at = 3 + len(grads) - 1
    specs[at : at + 4] = [block] * 4
    if sliced:
        specs[at] = pl.BlockSpec((None, None) + shape[2:], lambda i, ref: (i // 3, i % 3, ref[1], 0))
    outs = [struct((1, 1))] + [struct(shape)] * 4
    outs += [struct(vecs[1].shape)] * 4 + [struct(talks[0].shape)] * 4
    out_specs = [whole(out.shape) for out in outs]
    out_specs[1:5] = [block] * 4
    return pl.pallas_call(
        functools.partial(adam_kernel, sliced),
        grid_spec=pltpu.PrefetchScalarGridSpec(
            num_scalar_prefetch=1,
            grid=(6,),
            in_specs=specs,
            out_specs=out_specs,
            scratch_shapes=[pltpu.VMEM((3,) + shape[2:], F32), pltpu.VMEM((vecs[0].shape[1], 128), F32)],
        ),
        out_shape=outs,
        compiler_params=limit(SMALL_MIB),
        cost_estimate=pl.CostEstimate(flops=1 << 23, bytes_accessed=14 << 20, transcendentals=0),
        name="optimizer",
    )(place, *operands)


def swap(value, axis, size, bit):
    return lax.ppermute(value, axis, [(place, place ^ bit) for place in range(size)])


def bits_of(axis, size, bit=1):
    return [(axis, bit << i) for i in range((size // bit).bit_length() - 1)]


class Places:
    def __init__(self, dp_size, seq_size, row_share):
        seq, dp = lax.axis_index("seq"), lax.axis_index("dp")
        self.sizes = {"dp": dp_size, "seq": seq_size}
        steps = bits_of("dp", dp_size) + bits_of("seq", seq_size)
        names = {"dp": dp, "seq": seq}
        bits = {step: jnp.bitwise_and(lax.shift_right_logical(names[step[0]], step[1].bit_length() - 1), 1) for step in steps}
        self.found = {
            "seq": seq.astype(jnp.int32).reshape(1),
            "dp": dp.astype(jnp.int32).reshape(1),
            "rows": (dp * row_share).astype(jnp.uint32),
            "share": (bits["seq", 1] * (seq_size // 2) + lax.shift_right_logical(seq, 1)).astype(jnp.uint32),
        }
        for step, bit in bits.items():
            self.found[step, "mine"] = bit.astype(jnp.uint32)
            self.found[step, "other"] = (1 - bit).astype(jnp.uint32)
            self.found[step, "low"] = bit == 0

    def before(self, value):
        names = list(self.found)
        value, *found = together(value, *[self.found[name] for name in names])
        self.found = dict(zip(names, found))
        return value

    def take(self, value, picks):
        at = [jnp.uint32(0)] * value.ndim
        sizes = list(value.shape)
        for dim, (step, which) in picks.items():
            at[dim] = self.found[step, which]
            sizes[dim] = 1
        return lax.squeeze(lax.dynamic_slice(value, at, sizes), tuple(picks))

    def share(self, value, rows):
        at = self.found["share"] * jnp.uint32(rows)
        return lax.dynamic_slice(value, (at, jnp.uint32(0)), (rows, value.shape[1]))

    def rows(self, value, size, dim):
        at = [jnp.uint32(0)] * value.ndim
        at[dim] = self.found["rows"]
        sizes = list(value.shape)
        sizes[dim] = size
        return lax.dynamic_slice(value, at, sizes)

    def swap(self, value, steps):
        flip = sum(bit * (self.sizes["seq"] if axis == "dp" else 1) for axis, bit in steps)
        count = self.sizes["dp"] * self.sizes["seq"]
        return lax.ppermute(value, ("dp", "seq"), [(place, place ^ flip) for place in range(count)])

    def pair(self, value, other, step):
        low = self.found[step, "low"]
        return [jnp.where(low, value, other), jnp.where(low, other, value)]


def subsets(group):
    found = [()]
    for step in group:
        found += [one + (step,) for one in found]
    return found[1:]


class Reduce:
    def __init__(self, terms, places, groups):
        self.places, self.groups = places, list(groups)
        self.left = bits_of("dp", places.sizes["dp"])[::-1]
        shape = (2,) * len(self.left) + (-1, terms[0].shape[1])
        self.terms = [term.reshape(shape) for term in terms]
        self.got = 0

    def sends(self):
        group = self.groups[0]
        halves = [step for step in group if step[0] == "dp"]
        dims = {step: self.left.index(step) for step in halves}
        if not halves:
            self.terms = [sum_of(self.terms)]

        def taken(others):
            picks = {dims[step]: (step, "other" if step in others else "mine") for step in halves}
            return [self.places.take(term, picks) if picks else term for term in self.terms]

        sent = [sum_of(taken(others)) for others in subsets(group)]
        self.terms = taken(())
        self.left = [step for step in self.left if step not in halves]
        return sent

    def post(self, sent):
        group = self.groups.pop(0)
        self.got = len(sent)
        self.terms += [self.places.swap(value, steps) for value, steps in zip(sent, subsets(group))]

    def received(self):
        return self.terms[len(self.terms) - self.got :]

    def set_received(self, values):
        self.terms[len(self.terms) - self.got :] = values

    def value(self):
        return sum_of(self.terms)


class Gather:
    def __init__(self, value, places):
        self.places = places
        dp = bits_of("dp", places.sizes["dp"])
        self.value = value[None]
        self.groups = [(step,) for step in dp[2:]] + [tuple(dp[:2])]
        self.groups += [(step,) for step in bits_of("seq", places.sizes["seq"], 2) + bits_of("seq", 2)]

    def sends(self):
        return [self.value]

    def post(self, sent):
        self.value = sent[0]
        self.others = [self.places.swap(self.value, steps) for steps in subsets(self.groups[0])]

    def received(self):
        return list(self.others)

    def set_received(self, values):
        group = self.groups.pop(0)
        if group[0][0] == "dp":
            self.value = jnp.concatenate([self.value, *values], axis=0)
        else:
            self.value = jnp.concatenate(self.places.pair(self.value, values[0], group[0]), axis=1)
        self.others = []


def settle(streams, *work):
    streams = [stream for stream in streams if stream.received()]
    counts = [len(stream.received()) for stream in streams]
    found = together(*[value for stream in streams for value in stream.received()], *work)
    at = 0
    for stream, count in zip(streams, counts):
        stream.set_received(list(found[at : at + count]))
        at += count
    return found[at:]


def launch(streams, *after):
    streams = [stream for stream in streams if stream.groups]
    sent = [stream.sends() for stream in streams]
    found = together(*[value for one in sent for value in one], *after)
    at = 0
    for stream, one in zip(streams, sent):
        stream.post(list(found[at : at + len(one)]))
        at += len(one)
    return found[at:]


def sum_of(terms):
    total = terms[0]
    for term in terms[1:]:
        total = total + term
    return total


def tie(value, *others):
    return lax.optimization_barrier((value, *others))[0]


def together(*values):
    return lax.optimization_barrier(values)


def on_device(
    dp_size, seq_size,
    tokens, class_tokens, cot_patch, cot_class, lengths,
    matrices, matrices_moment1, matrices_moment2, matrices_ema,
    vectors, vectors_moment1, vectors_moment2, vectors_ema,
    talking, talking_moment1, talking_moment2, talking_ema,
):
    rows, width = tokens.shape
    images = class_tokens.shape[0]
    row_share = width // dp_size
    places = Places(dp_size, seq_size, row_share)
    tokens = places.before(tokens)
    place = places.found["seq"]

    slots = {0: tokens}
    slots[1] = swap(tokens, "seq", seq_size, 1)
    bit = 2
    while bit < seq_size:
        for slot in sorted(slot for slot in slots if slot % 2 == 0):
            slots[slot | bit] = swap(slots[slot], "seq", seq_size, bit)
        bit *= 2
    *prepared, t1, t2, t1_rows, t2_rows, query, k1, k2, v1, v2, kt1, kt2, vt1, vt2 = prepare(
        tokens, slots[1], class_tokens, matrices, vectors, talking
    )
    for slot in range(2, seq_size, 2):
        slots[slot + 1] = swap(tie(slots[slot], query), "seq", seq_size, 1)
    token_slots = [slots[slot] for slot in range(seq_size)]
    (
        e_high, e_low, pv, inverse, pv_bias, attended, kt_high, kt_low, v_high, v_low,
        patch_out, *kept, packed, scores,
    ) = forward(
        place, lengths, token_slots, matrices, vectors, t1, t2, prepared[3],
        [query, k1, k2, v1, v2, kt1, kt2, vt1, vt2],
    )
    parts = [packed] + [swap(packed, "seq", seq_size, bit) for bit in range(1, seq_size)]
    (
        class_out, d_attended, d_mixed, early_keep, early_send, partial, factors, vec_rows, class_terms,
    ) = middle(
        place, parts, vectors, prepared, class_tokens, cot_class, cot_patch,
        patch_out, scores, [attended, *kept], matrices,
    )

    core, chips, dp = ("seq", 1), bits_of("seq", seq_size, 2), bits_of("dp", dp_size)
    pairs = lambda steps: [tuple(steps[i : i + 2]) for i in range(0, len(steps), 2)]
    other = places.swap(early_send, [core])
    partials = [partial] + [swap(partial, "seq", seq_size, bit) for bit in range(1, seq_size)]
    grad_class, factors = class_finish(partials, class_terms, class_tokens, vectors, matrices, factors)
    gather = Gather(places.share(factors, factors.shape[0] // seq_size), places)
    other, gather.value = together(other, gather.value)
    early = Reduce(
        [early_keep, other], places, [tuple(dp[:2])] + [(step,) for step in dp[2:] + chips]
    )
    (later,) = launch([early, gather], place)
    even, odd, late_keep, late_send = backward(
        dp_size, later, lengths, token_slots, [e_high, e_low, pv, inverse, pv_bias], d_attended,
        [kt_high, kt_low, v_high, v_low], query, [t1, t2, t1_rows, t2_rows], vec_rows, vectors, matrices,
    )

    late_send, odd = settle([early, gather], late_send, odd)
    late_other, odd = places.swap(late_send, [core]), places.swap(odd, [core])
    late = Reduce([late_keep, late_other], places, pairs(dp + chips))
    (late.terms[1],) = launch([early], late.terms[1])
    (even,) = launch([late], even)
    own = [even[0]] + [even[i] + odd[i] for i in range(1, seq_size // 2)]
    near = odd[0]
    bit = 1
    while 2 * bit < len(own):
        for slot in range(0, len(own), 2 * bit):
            own[slot] = own[slot] + swap(own[slot + bit], "seq", seq_size, 2 * bit)
        bit *= 2
    far = swap(own[bit], "seq", seq_size, 2 * bit)
    (own[bit],) = launch([gather], own[bit])
    (own[bit],) = settle([gather], own[bit])
    while len(gather.groups) > len(chips) + 1:
        launch([gather])
        settle([gather])
    launch([gather], own[bit])
    (far,) = settle([late, early], far)
    (far,) = launch([late, early], far)
    (far,) = settle([gather], far)
    while gather.groups:
        launch([gather])
        settle([gather])
    mine = places.rows(gather.value, row_share, 2)
    class_share, class_squares, added = class_weights(images, mine, gather.value)
    class_share, class_squares, added = settle([late, early], class_share, class_squares, added)
    while late.groups or early.groups:
        launch([late, early])
        settle([late, early])
    last = [[term.reshape(row_share, -1) for term in stream.terms] for stream in (early, late)]
    squares, early, late = squares_of(dp_size, place, added, class_squares, *last)
    sliced = row_share % 8 == 0
    if not sliced:
        matrices_rows, vectors_columns = places.rows(matrices, row_share, 2), places.rows(vectors, row_share, 1)
    else:
        matrices_rows, vectors_columns = matrices, vectors
    far, squares = together(far, squares)
    for group in pairs([core] + dp):
        squares = sum_of([squares] + [places.swap(squares, steps) for steps in subsets(group)])
    grad_tokens = token_grad(tokens, vectors, own[0], near, far, d_mixed)
    grads = []
    for value in (early, late):
        grads += [value, places.swap(value, [core])]
    norm, *updated = optimizer(
        jnp.concatenate([place, places.found["dp"]]), squares, [*grads, added], class_share,
        [matrices_rows, matrices_moment1, matrices_moment2, matrices_ema],
        [vectors_columns, vectors_moment1, vectors_moment2, vectors_ema],
        [talking, talking_moment1, talking_moment2, talking_ema],
    )
    return (patch_out, class_out, grad_tokens, grad_class, norm.reshape(()), *updated)


def solution(mesh):
    tokens = P(("dp", "seq"), None)
    by_group = P("dp", None)
    mats = P(None, None, "dp", None)
    vecs = P(None, "dp")
    body = functools.partial(on_device, mesh.shape["dp"], mesh.shape["seq"])
    return jax.shard_map(
        body,
        mesh=mesh,
        in_specs=(tokens, by_group, tokens, by_group, by_group, P(), mats, mats, mats,
                  P(), vecs, vecs, vecs, P(), P(), P(), P()),
        out_specs=(tokens, by_group, tokens, by_group, P(), mats, mats, mats, mats,
                   vecs, vecs, vecs, vecs, P(), P(), P(), P()),
        check_vma=False,
    )
```

```python
import functools

import jax
import jax.numpy as jnp
from jax import lax
from jax.experimental import pallas as pl
from jax.experimental.pallas import tpu as pltpu
from jax.sharding import PartitionSpec as P

STEP = 10
EPS_NORM = 1e-06
MASKED = -1e30
LR_MATRIX = 0.05
LR_VECTOR = 0.1
LR_TALKING = 0.2
BETA_ONE = 0.9
BETA_TWO = 0.999
ADAM_EPS = 1e-08
WEIGHT_DECAY = 0.05
EMA_RATE = 0.9
CLIP_NORM = 1.0
F32 = jnp.float32
BF16 = jnp.bfloat16
NN = (((1,), (0,)), ((), ()))
NT = (((1,), (1,)), ((), ()))
TN = (((0,), (0,)), ((), ()))
KERNEL_MIB, NEAR_MIB, SMALL_MIB = 58, 52, 24


def split(value):
    high = value.astype(BF16)
    return high, (value - high.astype(F32)).astype(BF16)


def mm(left, right, dims=NN):
    return lax.dot_general(left, right, dims, preferred_element_type=F32)


def mm3(left, right, dims=NN):
    return mm(left[0], right[0], dims) + (mm(left[0], right[1], dims) + mm(left[1], right[0], dims))


def mm3_tall(left, right, dims=NN):
    rows = left[0].shape[0]
    stacked = jnp.concatenate([part.astype(F32) for part in left], axis=0).astype(BF16)
    both = mm(stacked, right[0], dims)
    return both[:rows] + (both[rows:] + mm(left[0], right[1], dims))


def dot_tall(left, right, dims=NN):
    return mm3_tall(split(left), split(right), dims)


def dot3(left, right, dims=NN):
    return mm3(split(left), split(right), dims)


def norm_rows(values):
    average = jnp.mean(values, axis=-1, keepdims=True)
    centered = values - average
    variance = jnp.mean(centered * centered, axis=-1, keepdims=True)
    scale = lax.rsqrt(variance + EPS_NORM)
    return centered * scale, scale


def norm_back(grad, unit, scale):
    inner = jnp.mean(grad * unit, axis=-1, keepdims=True)
    return scale * (grad - jnp.mean(grad, axis=-1, keepdims=True) - unit * inner)


def gelu_both(values):
    half = 0.5 * (1.0 + lax.erf(values * 0.7071067811865476))
    slope = half + values * (0.3989422804014327 * jnp.exp(-0.5 * values * values))
    return values * half, slope


def row_sum(values):
    return jnp.sum(values, axis=0, keepdims=True)


def tail_forward(dot, inputs, attended, w_out, w_up, w_down, vecs):
    projected = dot(attended, w_out) + vecs[4:5]
    mixed = inputs + vecs[5:6] * projected
    unit, _ = norm_rows(mixed)
    normed = unit * vecs[6:7] + vecs[7:8]
    up_bias = jnp.concatenate([vecs[row : row + 1] for row in range(8, 12)], axis=1)
    hidden, slope = gelu_both(dot(normed, w_up) + up_bias)
    lowered = dot(hidden, w_down, NT) + vecs[12:13]
    return mixed + vecs[13:14] * lowered, (projected, mixed, hidden, slope, lowered)


def tail_backward(dot, cot, kept, w_out, w_up, w_down, vecs):
    projected, mixed, hidden, slope, lowered = kept
    width = cot.shape[1]
    unit, scale = norm_rows(mixed)
    normed = unit * vecs[6:7] + vecs[7:8]
    d_lowered = cot * vecs[13:14]
    d_hidden = dot(d_lowered, w_down) * slope
    d_normed = dot(d_hidden, w_up, NT)
    d_mixed = cot + norm_back(d_normed * vecs[6:7], unit, scale)
    d_projected = d_mixed * vecs[5:6]
    d_attended = dot(d_projected, w_out, NT)
    d_up = row_sum(d_hidden)
    rows = [
        row_sum(d_projected), row_sum(d_mixed * projected), row_sum(d_normed * unit), row_sum(d_normed),
        *[d_up[:, i * width : (i + 1) * width] for i in range(4)],
        row_sum(d_lowered), row_sum(cot * lowered),
    ]
    return d_mixed, d_attended, d_projected, d_hidden, d_lowered, normed, rows


def image_of(lengths_ref, images, positions):
    end = lengths_ref[0, 0]
    inside = (positions >= end).astype(jnp.int32)
    for image in range(1, images):
        end = end + lengths_ref[0, image]
        inside = inside + (positions >= end).astype(jnp.int32)
    return inside


def same_image(lengths_ref, images, place, slots, rows):
    queries = place * rows + lax.broadcasted_iota(jnp.int32, (1, rows), 1)
    query_image = image_of(lengths_ref, images, queries)
    parts = []
    for slot in range(slots):
        keys = jnp.bitwise_xor(place, slot) * rows + lax.broadcasted_iota(jnp.int32, (rows, 1), 0)
        parts.append(image_of(lengths_ref, images, keys) == query_image)
    return parts


def column_of(table, number):
    lanes = lax.broadcasted_iota(jnp.int32, (1, table.shape[1]), 1)
    return jnp.sum(jnp.where(lanes == number, table, 0.0), axis=1, keepdims=True)


def head_mask(heads, width):
    row = lax.broadcasted_iota(jnp.int32, (heads, width), 0)
    return jnp.where(lax.broadcasted_iota(jnp.int32, (heads, width), 1) // (width // heads) == row, 1.0, 0.0)


def spread(value, mask):
    return jnp.concatenate([value[i : i + 1] * mask for i in range(value.shape[0])], axis=0)


def repeat_rows(value, heads):
    shape = (heads, value.shape[1])
    return jnp.concatenate(
        [jnp.broadcast_to(value[i : i + 1], shape) for i in range(value.shape[0])], axis=0
    )


def fold_heads(value, mask):
    heads = mask.shape[0]
    return jnp.concatenate(
        [row_sum(value[i : i + heads] * mask) for i in range(0, value.shape[0], heads)], axis=0
    )


def head_sums(value, mask):
    return jnp.sum(spread(value, mask), axis=1, keepdims=True)


def rows_of(value, heads):
    return jnp.concatenate(
        [row_sum(value[i : i + heads]) for i in range(0, value.shape[0], heads)], axis=0
    )


def wide(column):
    return jnp.broadcast_to(column, (column.shape[0], 128))


def whole(shape):
    return pl.BlockSpec(shape, lambda *_: (0,) * len(shape))


def struct(shape, dtype=F32):
    return jax.ShapeDtypeStruct(shape, dtype)


def far_struct(shape, dtype=F32):
    return pltpu.HBM(shape, dtype)


def smem():
    return pl.BlockSpec(memory_space=pltpu.SMEM)


def anywhere():
    return pl.BlockSpec(memory_space=pl.ANY)


def weight_block(block, matrix, shape, columns=None):
    return pl.BlockSpec((None, None, shape[2], columns or shape[3]), lambda *_: (block, matrix, 0, 0))


def far_off(*operands):
    return [pltpu.with_memory_space_constraint(operand, pltpu.HBM) for operand in operands]


def copy_in(pairs, arrived):
    copies = [pltpu.make_async_copy(a, b, arrived.at[i]) for i, (a, b) in enumerate(pairs)]
    for copy in copies:
        copy.start()
    return copies


def limit(mebibytes):
    return pltpu.CompilerParams(vmem_limit_bytes=mebibytes << 20)


def prepare_kernel(
    own_ref, near_ref, class_ref, w_self_ref, w_class_ref, vecs_ref, talk_ref,
    normed_ref, query_c_ref, value_c_ref, key_rows_ref, score_ref, t1_ref, t2_ref, t1_rows_ref, t2_rows_ref,
    query_ref, k_high, k_low, v_high, v_low, kt_high, kt_low, vt_high, vt_low,
):
    rows, width = own_ref.shape
    heads = talk_ref.shape[0]
    size = width // heads
    scale = size ** (-0.5)
    vecs = vecs_ref[...]
    w_q, w_kv = split(w_self_ref[:, :width]), split(w_self_ref[:, width:])
    tokens = jnp.concatenate([own_ref[...], near_ref[...]], axis=0)
    unit, _ = norm_rows(tokens)
    normed = split(unit * vecs[0:1] + vecs[1:2])
    query_ref[...] = (mm3((normed[0][:rows], normed[1][:rows]), w_q) + vecs[2:3]) * scale
    both = mm3(normed, w_kv)
    keys, values = both[:, :width], both[:, width:] + vecs[3:4]
    k_high[...], k_low[...] = split(keys)
    v_high[...], v_low[...] = split(values)
    kt_high[...], kt_low[...] = split(keys.T)
    vt_high[...], vt_low[...] = split(values.T)
    mask = head_mask(heads, width)
    unit, _ = norm_rows(class_ref[...])
    normed = unit * vecs[14:15] + vecs[15:16]
    both = dot_tall(normed, w_class_ref[...])
    query = both[:, :width] + vecs[16:17]
    normed_ref[...] = normed
    query_c_ref[...] = query
    value_c_ref[...] = both[:, 2 * width :] + vecs[17:18]
    key_rows_ref[...] = dot3(spread(query, mask), w_class_ref[:, width : 2 * width], NT) * scale
    score_ref[...] = wide(head_sums(query * both[:, width : 2 * width], mask) * scale)
    head_of = lax.broadcasted_iota(jnp.int32, (width, 1), 0) // size
    talk = talk_ref[...]
    talk_t = jnp.concatenate([talk, jnp.zeros((heads, 128 - talk.shape[1]), F32)], axis=1).T[: talk.shape[1], :]
    t1 = t2 = t1_rows = t2_rows = 0.0
    for head in range(heads):
        here = head_of == head
        t1 = t1 + jnp.where(here, talk_t[head : head + 1, :], 0.0)
        t2 = t2 + jnp.where(here, talk[head : head + 1, heads:], 0.0)
        t1_rows = t1_rows + mask[head : head + 1] * talk[:, head : head + 1]
        t2_rows = t2_rows + mask[head : head + 1] * talk_t[heads:, head : head + 1]
    t1_ref[...], t2_ref[...], t1_rows_ref[...], t2_rows_ref[...] = t1, t2, t1_rows, t2_rows


def prepare(own, near, class_tokens, matrices, vectors, talking):
    images, width = class_tokens.shape
    rows = own.shape[0]
    heads = talking.shape[0]
    pairs = images * heads
    outs = [far_struct((images, width))] * 3 + [
        far_struct((pairs, width)), far_struct((pairs, 128)),
        far_struct((width, heads)), far_struct((width, heads + 1)),
        far_struct((heads, width)), far_struct((heads + 1, width)),
        far_struct((rows, width)),
    ]
    outs += [far_struct((2 * rows, width), BF16)] * 4 + [far_struct((width, 2 * rows), BF16)] * 4
    own, class_tokens, matrices, vectors, talking = far_off(own, class_tokens, matrices, vectors, talking)
    operands = [own, near, class_tokens, matrices, matrices, vectors, talking]
    specs = [whole(operand.shape) for operand in operands]
    specs[3] = weight_block(0, 0, matrices.shape, 3 * width)
    specs[4] = weight_block(1, 0, matrices.shape, 3 * width)
    return pl.pallas_call(
        prepare_kernel,
        grid=(1,),
        in_specs=specs,
        out_specs=[whole(out.shape) for out in outs],
        out_shape=outs,
        compiler_params=limit(NEAR_MIB),
        cost_estimate=pl.CostEstimate(flops=4 << 30, bytes_accessed=8 << 20, transcendentals=0),
        name="prepare",
    )(*operands)


def forward_kernel(slots, images, unroll, *refs):
    place_ref, lengths_ref = refs[:2]
    token_refs = refs[2 : 1 + slots]
    (
        vecs_ref, t1_ref, t2_ref, key_rows_ref, query_ref,
        k_high0, k_low0, v_high0, v_low0, kt_high0, kt_low0, vt_high0, vt_low0, mats_ref,
        e_high_hbm, e_low_hbm, pv_hbm, inverse_ref, pv_bias_ref, attended_ref,
        kt_high_hbm, kt_low_hbm, v_high_hbm, v_low_hbm,
        patch_ref, projected_ref, mixed_ref, hidden_hbm, slope_hbm, lowered_ref, packed_ref, scores_ref,
        k_three, vt_two, qt, bias, attended_t, w_kv, w_up, w_down, w_out, arrived,
        kt_high, kt_low, v_high, v_low, hidden_ref, slope_ref, e_high_ref, e_low_ref, pv_ref, leaving,
    ) = refs[1 + slots :]
    rows, width = token_refs[0].shape
    step = pl.program_id(0)
    place = place_ref[0]
    ready, columns = pl.ds(0, 2 * rows), lambda i: pl.ds(i * width, width)
    pairs = [
        (mats_ref.at[0, 0, :, pl.ds(width, 2 * width)], w_kv),
        (k_high0, k_three.at[ready, columns(0)]), (k_high0, k_three.at[ready, columns(1)]),
        (k_low0, k_three.at[ready, columns(2)]), (v_high0, v_high.at[ready, :]), (v_low0, v_low.at[ready, :]),
        (kt_high0, kt_high.at[:, ready]), (kt_low0, kt_low.at[:, ready]),
        (vt_high0, vt_two.at[columns(0), ready]), (vt_low0, vt_two.at[columns(1), ready]),
        (mats_ref.at[0, 0, :, pl.ds(3 * width, width)], w_out),
        (mats_ref.at[0, 1], w_up), (mats_ref.at[0, 2], w_down),
    ]
    fetches = [pltpu.make_async_copy(a, b, arrived.at[i]) for i, (a, b) in enumerate(pairs)]
    pairs = [(kt_high, kt_high_hbm), (kt_low, kt_low_hbm), (v_high, v_high_hbm), (v_low, v_low_hbm),
             (hidden_ref, hidden_hbm), (slope_ref, slope_hbm)]
    stores = [pltpu.make_async_copy(a, b, leaving.at[i]) for i, (a, b) in enumerate(pairs)]
    heads = inverse_ref.shape[0]
    groups = []
    for number in range(heads // unroll):
        here = pl.ds(number * unroll, unroll)
        groups.append([
            pltpu.make_async_copy(a.at[here], b.at[here], leaving.at[6 + 3 * number + i])
            for i, (a, b) in enumerate([(e_high_ref, e_high_hbm), (e_low_ref, e_low_hbm), (pv_ref, pv_hbm)])
        ])

    @pl.when(step == 0)
    def _():
        for fetch in fetches:
            fetch.start()
        vecs = vecs_ref[...]
        inside = same_image(lengths_ref, images, place, slots, rows)
        for slot in range(slots):
            bias[pl.ds(slot * rows, rows), :] = jnp.where(inside[slot], 0.0, MASKED)
        units = [norm_rows(ref[...])[0] for ref in token_refs[1:]]
        fetches[0].wait()
        w_both = split(w_kv[...])
        for slot in range(2, slots):
            here = pl.ds(slot * rows, rows)
            normed = split(units[slot - 2] * vecs[0:1] + vecs[1:2])
            both = mm3(normed, w_both)
            keys, values = both[:, :width], both[:, width:] + vecs[3:4]
            high, low = split(keys)
            k_three[here, :] = jnp.concatenate([high, high, low], axis=1)
            v_high[here, :], v_low[here, :] = split(values)
            kt_high[:, here], kt_low[:, here] = split(keys.T)
            vt_two[:, here] = jnp.concatenate(split(values.T), axis=0)
        qt[...] = query_ref[...].T
        attended_t[...] = jnp.zeros_like(attended_t)
        for fetch in fetches[1:10]:
            fetch.wait()
        for store in stores[:4]:
            store.start()

    scores = []
    for u in range(unroll):
        high, low = split(qt[...] * column_of(t1_ref[...], step * unroll + u))
        scores.append(mm(k_three[...], jnp.concatenate([high, low, high], axis=0)) + bias[...])
    for u in range(unroll):
        exponentials = jnp.exp(scores[u] - jnp.max(scores[u], axis=0, keepdims=True))
        inverse = 1.0 / jnp.sum(exponentials, axis=0, keepdims=True)
        pair = split(exponentials)
        head = step * unroll + u
        e_high_ref[head], e_low_ref[head] = pair
        inverse_ref[head] = inverse
        both = mm(vt_two[...], pair[0])
        values = (both[:width] + (both[width:] + mm(vt_two[:width, :], pair[1]))) * inverse
        pv_ref[head] = values
        attended_t[...] += values * column_of(t2_ref[...], head)
    for number, group in enumerate(groups):

        @pl.when(step == number)
        def _(group=group):
            for copy in group:
                copy.start()

    @pl.when(step == pl.num_programs(0) - 1)
    def _():
        inside = jnp.where(bias[...] < 0.0, 0.0, 1.0).astype(BF16)
        both = mm(vt_two[...], inside)
        summed = both[:width] + both[width:]
        pv_bias_ref[...] = summed
        attended = (attended_t[...] + summed * t2_ref[:, 8:9]).T
        attended_ref[...] = attended
        for fetch in fetches[10:]:
            fetch.wait()
        vecs = vecs_ref[...]
        patch, kept = tail_forward(
            dot3, token_refs[0][...], attended, w_out[...], w_up[...], w_down[...], vecs
        )
        patch_ref[...] = patch
        for ref, value in zip((projected_ref, mixed_ref, hidden_ref, slope_ref, lowered_ref), kept):
            ref[...] = value
        for store in stores[4:]:
            store.start()
        unit, _ = norm_rows(patch)
        normed = split(unit * vecs[14:15] + vecs[15:16])
        pairs = images * 8
        image = lax.broadcasted_iota(jnp.int32, (pairs, 1), 0) // 8
        positions = place * rows + lax.broadcasted_iota(jnp.int32, (1, rows), 1)
        belong = image_of(lengths_ref, images, positions) == image
        class_scores = mm3(split(key_rows_ref[...]), normed, NT)
        class_scores = jnp.where(belong, class_scores, MASKED)
        scores_ref[...] = class_scores
        top = jnp.max(class_scores, axis=1, keepdims=True)
        weights = jnp.where(belong, jnp.exp(class_scores - top), 0.0)
        packed_ref[:, :width] = mm3(split(weights), normed)
        lane = lax.broadcasted_iota(jnp.int32, (1, 128), 1)
        total = jnp.sum(weights, axis=1, keepdims=True)
        packed_ref[:, width:] = jnp.where(lane < 64, top, total)
        for store in stores + [copy for group in groups for copy in group]:
            store.wait()


def by_head(unroll, shape):
    return pl.BlockSpec((unroll,) + shape[1:], lambda g: (g, 0, 0))


def forward(place, lengths, token_slots, matrices, vectors, t1, t2, key_rows, projected):
    slots, (rows, width) = len(token_slots), token_slots[0].shape
    total, heads = slots * rows, 8
    unroll = 4 if total <= 1024 else 1
    hidden = matrices.shape[3]
    pairs = key_rows.shape[0]
    outs = [
        far_struct((heads, total, rows), BF16), far_struct((heads, total, rows), BF16), far_struct((heads, width, rows)),
        far_struct((heads, 1, rows)), far_struct((width, rows)), far_struct((rows, width)),
        far_struct((width, total), BF16), far_struct((width, total), BF16),
        far_struct((total, width), BF16), far_struct((total, width), BF16),
        far_struct((rows, width)), far_struct((rows, width)), far_struct((rows, width)),
        far_struct((rows, hidden)), far_struct((rows, hidden)), far_struct((rows, width)),
        far_struct((pairs, width + 128)), far_struct((pairs, rows)),
    ]
    away = (0, 1, 2, 6, 7, 8, 9, 13, 14)
    out_specs = [anywhere() if i in away else whole(out.shape) for i, out in enumerate(outs)]
    operands = [token_slots[0], *token_slots[2:], *far_off(vectors, t1, t2, key_rows, *projected, matrices)]
    in_specs = [whole(operand.shape) for operand in operands]
    in_specs[-9:] = [anywhere()] * 9
    flops = 2 * 3 * ((2 * heads + 1) * total + 9 * width) * rows * width
    return pl.pallas_call(
        functools.partial(forward_kernel, slots, lengths.shape[1], unroll),
        grid=(heads // unroll,),
        in_specs=[smem(), smem()] + in_specs,
        out_specs=out_specs,
        out_shape=outs,
        scratch_shapes=[
            pltpu.VMEM((total, 3 * width), BF16),
            pltpu.VMEM((2 * width, total), BF16),
            pltpu.VMEM((width, rows), F32),
            pltpu.VMEM((total, rows), F32),
            pltpu.VMEM((width, rows), F32),
            pltpu.VMEM((width, 2 * width), F32),
            pltpu.VMEM((width, hidden), F32),
            pltpu.VMEM((width, hidden), F32),
            pltpu.VMEM((width, width), F32),
            pltpu.SemaphoreType.DMA((13,)),
            pltpu.VMEM((width, total), BF16),
            pltpu.VMEM((width, total), BF16),
            pltpu.VMEM((total, width), BF16),
            pltpu.VMEM((total, width), BF16),
            pltpu.VMEM((rows, hidden), F32),
            pltpu.VMEM((rows, hidden), F32),
            pltpu.VMEM((heads, total, rows), BF16),
            pltpu.VMEM((heads, total, rows), BF16),
            pltpu.VMEM((heads, width, rows), F32),
            pltpu.SemaphoreType.DMA((6 + 3 * heads // unroll,)),
        ],
        compiler_params=limit(NEAR_MIB if total <= 1024 else KERNEL_MIB),
        cost_estimate=pl.CostEstimate(
            flops=flops, bytes_accessed=24 << 20, transcendentals=heads * total * rows
        ),
        name="forward",
    )(place, lengths, *operands)


def middle_kernel(images, slots, *refs):
    place_ref = refs[0]
    parts = [ref[...] for ref in refs[1 : 1 + slots]]
    (
        vecs_ref, normed_c_ref, query_c_ref, value_c_ref, key_rows_ref, own_ref,
        class_ref, cot_class_ref, cot_patch_ref, patch_ref, scores_ref,
        attended_hbm, projected_hbm, mixed_hbm, hidden_hbm, slope_hbm, lowered_hbm, mats_ref,
        class_out_ref, d_attended_ref, d_mixed_ref, keep_ref, send_ref, partial_ref,
        factors_ref, vec_rows_ref, class_terms_ref,
        wc0, wc1, wc2, ws0, ws1, ws2, attended_ref, projected_ref, mixed_ref, hidden_ref, slope_ref, lowered_ref,
        keep, send, arrived, stored,
    ) = refs[1 + slots :]
    width = class_ref.shape[1]
    heads = 8
    size = width // heads
    copies = copy_in(
        [(mats_ref.at[1, 0, :, pl.ds(2 * width, 2 * width)], wc0), (mats_ref.at[1, 1], wc1), (mats_ref.at[1, 2], wc2),
         (lowered_hbm, lowered_ref), (hidden_hbm, hidden_ref), (mats_ref.at[0, 2], ws2), (slope_hbm, slope_ref),
         (mixed_hbm, mixed_ref), (mats_ref.at[0, 1], ws1), (projected_hbm, projected_ref),
         (attended_hbm, attended_ref), (mats_ref.at[0, 0, :, pl.ds(3 * width, width)], ws0)], arrived)
    vecs = vecs_ref[...]
    vecs_s, vecs_c = vecs[:14], vecs[14:]
    mask = head_mask(heads, width)
    first = jnp.where(place_ref[0] == 0, 1.0, 0.0)
    own_score = own_ref[:, :1]
    normed_c = normed_c_ref[...]
    normed_rep = repeat_rows(normed_c, heads)
    top = own_score
    for part in parts:
        top = jnp.maximum(top, part[:, width : width + 1])
    own_weight = jnp.exp(own_score - top)
    total, summed = own_weight, own_weight * normed_rep
    for part in parts:
        rescale = jnp.exp(part[:, width : width + 1] - top)
        total = total + part[:, width + 64 : width + 65] * rescale
        summed = summed + part[:, :width] * rescale
    value_rows = summed / total
    own_prob = own_weight / total
    unit_p, scale_p = norm_rows(patch_ref[...])
    normed_p = split(unit_p * vecs_c[0:1] + vecs_c[1:2])
    scores = scores_ref[...]
    probs = jnp.where(scores > 0.5 * MASKED, jnp.exp(scores - top) * (1.0 / total), 0.0)
    for copy in copies[:3]:
        copy.wait()
    w_v = split(wc0[:, :width])
    class_attended = fold_heads(mm3_tall(split(value_rows), w_v), mask) + vecs_c[3:4]
    w_out_c = wc0[:, width:]
    class_out, kept_c = tail_forward(
        dot_tall, class_ref[...], class_attended, w_out_c, wc1[...], wc2[...], vecs_c
    )
    class_out_ref[...] = class_out
    d_mixed_c, d_attended_c, d_projected_c, d_hidden_c, d_lowered_c, normed2_c, tail_rows_c = (
        tail_backward(dot_tall, cot_class_ref[...], kept_c, w_out_c, wc1[...], wc2[...], vecs_c)
    )
    delta = head_sums(d_attended_c * class_attended, mask)
    cot_rows = mm3_tall(split(spread(d_attended_c, mask)), w_v, NT)
    cot_const = head_sums(d_attended_c * vecs_c[3:4], mask)
    cot_split = split(cot_rows)
    d_scores = probs * (mm3_tall(cot_split, normed_p, NT) + cot_const - delta)
    d_own = own_prob * (head_sums(d_attended_c * value_c_ref[...], mask) - delta)
    key_rows = key_rows_ref[...]
    d_split = split(d_scores)
    d_normed_p = mm3(d_split, split(key_rows), TN) + mm3(split(probs), cot_split, TN)
    partial_ref[...] = mm3_tall(d_split, normed_p)
    cot = cot_patch_ref[...] + norm_back(d_normed_p * vecs_c[0:1], unit_p, scale_p)
    class_terms_ref[...] = jnp.concatenate(
        [rows_of(d_own * key_rows + own_prob * cot_rows, heads), d_mixed_c], axis=0
    )
    query_c = query_c_ref[...]
    chunks = lambda value: [value[:, i * width : (i + 1) * width] for i in range(4)]
    factors_ref[...] = jnp.concatenate(
        [normed_c, class_attended, normed2_c, d_lowered_c, d_own * normed_rep, value_rows,
         jnp.zeros_like(query_c), query_c * size ** (-0.5), d_attended_c, d_projected_c,
         *chunks(d_hidden_c), *chunks(kept_c[2])], axis=0)
    for copy in copies[3:]:
        copy.wait()
    projected, mixed, hidden, lowered = projected_ref[...], mixed_ref[...], split(hidden_ref[...]), lowered_ref[...]
    unit, scale = norm_rows(mixed)
    normed = split(unit * vecs_s[6:7] + vecs_s[7:8])
    d_lowered = cot * vecs_s[13:14]
    d_low_split = split(d_lowered)
    d_hidden = mm3(d_low_split, split(ws2[...])) * slope_ref[...]
    d_hid_split = split(d_hidden)
    g_down = mm3(d_low_split, hidden, TN)
    g_up = mm3(normed, d_hid_split, TN)
    even = jnp.bitwise_and(place_ref[0], 1) == 0
    size_up = g_up.shape[1]
    send[:, :size_up] = jnp.where(even, g_down, g_up)
    keep[:, :size_up] = jnp.where(even, g_up, g_down)
    bulk = pl.ds(0, size_up)
    leaving = copy_in(
        [(send.at[:, bulk], send_ref.at[:, bulk]), (keep.at[:, bulk], keep_ref.at[:, bulk])], stored
    )
    d_normed = mm3(d_hid_split, split(ws1[...]), NT)
    d_mixed = cot + norm_back(d_normed * vecs_s[6:7], unit, scale)
    d_projected = d_mixed * vecs_s[5:6]
    d_proj_split = split(d_projected)
    g_out = mm3(split(attended_ref[...]), d_proj_split, TN)
    left = g_out[:, :256]
    right = jnp.concatenate([g_out[:, 256:], jnp.zeros((width, 512 - width), F32)], axis=1)
    send[:, size_up:] = jnp.where(even, right, left)
    keep[:, size_up:] = jnp.where(even, left, right)
    rest = pl.ds(size_up, 256)
    for i, (a, b) in enumerate([(send, send_ref), (keep, keep_ref)]):
        leaving.append(pltpu.make_async_copy(a.at[:, rest], b.at[:, rest], stored.at[2 + i]))
        leaving[-1].start()
    d_mixed_ref[...] = d_mixed
    d_attended_ref[...] = mm3(d_proj_split, split(ws0[...]), NT)
    d_up = row_sum(d_hidden)
    tail_rows = [
        row_sum(d_projected), row_sum(d_mixed * projected), row_sum(d_normed * unit), row_sum(d_normed),
        *[d_up[:, i * width : (i + 1) * width] for i in range(4)],
        row_sum(d_lowered), row_sum(cot * lowered),
    ]
    zero = jnp.zeros((1, width), F32)
    vec_rows_ref[...] = jnp.concatenate(
        [zero] * 4 + tail_rows
        + [row_sum(d_normed_p * unit_p), row_sum(d_normed_p), zero, row_sum(d_attended_c) * first]
        + [row * first for row in tail_rows_c], axis=0)
    for copy in leaving:
        copy.wait()


def middle(place, parts, vectors, prepared, class_tokens, cot_class, cot_patch, patch, scores, kept, matrices):
    images, width = class_tokens.shape
    rows = cot_patch.shape[0]
    hidden = matrices.shape[3]
    pairs = parts[0].shape[0]
    rest = [vectors, *prepared, class_tokens, cot_class, cot_patch, patch, scores, *kept, matrices]
    operands = [*parts, *far_off(*rest)]
    outs = [
        far_struct((images, width)), far_struct((rows, width)), far_struct((rows, width)),
        far_struct((width, hidden + 256)), far_struct((width, hidden + 256)), far_struct((pairs, width)),
        far_struct((16 * images + 2 * pairs, width)), far_struct((28, width)), far_struct((2 * images, width)),
    ]
    in_specs = [whole(operand.shape) for operand in operands]
    in_specs[-1 - len(kept) :] = [anywhere()] * (1 + len(kept))
    out_specs = [whole(out.shape) for out in outs]
    out_specs[3:5] = [anywhere()] * 2
    return pl.pallas_call(
        functools.partial(middle_kernel, images, len(parts)),
        grid=(1,),
        in_specs=[smem()] + in_specs,
        out_specs=out_specs,
        out_shape=outs,
        scratch_shapes=[pltpu.VMEM((width, 2 * width), F32)]
        + [pltpu.VMEM((width, hidden), F32)] * 2
        + [pltpu.VMEM((width, width), F32)]
        + [pltpu.VMEM((width, hidden), F32)] * 2
        + [pltpu.VMEM(value.shape, F32) for value in kept]
        + [pltpu.VMEM((width, hidden + 256), F32)] * 2
        + [pltpu.SemaphoreType.DMA((12,)), pltpu.SemaphoreType.DMA((4,))],
        compiler_params=limit(NEAR_MIB),
        cost_estimate=pl.CostEstimate(flops=8 << 30, bytes_accessed=28 << 20, transcendentals=1 << 19),
        name="middle",
    )(place, *operands)


def class_kernel(slots, *refs):
    partial_refs = refs[:slots]
    terms_ref, class_ref, vecs_ref, w_ref, factors_ref, grad_ref, factors_out_ref = refs[slots:]
    images, width = class_ref.shape
    pairs = partial_refs[0].shape[0]
    heads = pairs // images
    mask = head_mask(heads, width)
    at = 4 * images
    query_rows = sum_of([factors_ref[at : at + pairs, :]] + [ref[...] for ref in partial_refs])
    w_k, w_q = w_ref[:, width : 2 * width], w_ref[:, :width]
    d_query = fold_heads(dot_tall(query_rows, w_k), mask) * (width // heads) ** (-0.5)
    d_normed = dot_tall(d_query, w_q, NT) + terms_ref[:images, :]
    unit, scale = norm_rows(class_ref[...])
    grad_ref[...] = terms_ref[images:, :] + norm_back(d_normed * vecs_ref[14:15, :], unit, scale)
    count = factors_ref.shape[0]
    factors_out_ref[:count, :] = factors_ref[...]
    factors_out_ref[at : at + pairs, :] = query_rows
    at = at + 2 * pairs
    factors_out_ref[at : at + images, :] = d_query
    added = [row_sum(d_normed * unit), row_sum(d_normed), row_sum(d_query), jnp.zeros((5, width), F32)]
    factors_out_ref[count:, :] = jnp.concatenate(added, axis=0)


def class_finish(partials, terms, class_tokens, vectors, matrices, factors):
    operands = [*partials, *far_off(terms, class_tokens, vectors, matrices, factors)]
    specs = [whole(operand.shape) for operand in operands]
    specs[-2] = weight_block(1, 0, matrices.shape, 2 * class_tokens.shape[1])
    outs = [struct(class_tokens.shape), struct((factors.shape[0] + 8, factors.shape[1]))]
    return pl.pallas_call(
        functools.partial(class_kernel, len(partials)),
        grid=(1,),
        in_specs=specs,
        out_specs=[whole(out.shape) for out in outs],
        out_shape=outs,
        compiler_params=limit(SMALL_MIB),
        cost_estimate=pl.CostEstimate(flops=1 << 29, bytes_accessed=3 << 20, transcendentals=0),
        name="class_finish",
    )(*operands)


def class_weights_kernel(images, mine_ref, factors_ref, grads_ref, squares_ref, small_ref):
    groups, count, width = factors_ref.shape
    heads = 8
    pairs = images * heads
    mask = head_mask(heads, width)
    at = 4 * images + 2 * pairs

    def rows(ref, begin, count=images):
        return jnp.concatenate([ref[g, begin : begin + count, :] for g in range(groups)], axis=0)

    def chunked(begin):
        return jnp.concatenate([rows(factors_ref, begin + i * images) for i in range(4)], axis=1)

    def headed(left, right):
        return dot3(rows(mine_ref, left, pairs), spread(rows(factors_ref, right), mask), TN)

    grads_ref[0, :, :width] = dot3(rows(mine_ref, 0), rows(factors_ref, at), TN)
    grads_ref[0, :, width : 2 * width] = headed(4 * images, at + images)
    grads_ref[0, :, 2 * width : 3 * width] = headed(4 * images + pairs, at + 2 * images)
    grads_ref[0, :, 3 * width :] = dot3(rows(mine_ref, images), rows(factors_ref, at + 3 * images), TN)
    grads_ref[1] = dot3(rows(mine_ref, 2 * images), chunked(at + 4 * images), TN)
    grads_ref[2] = dot3(rows(mine_ref, 3 * images), chunked(at + 8 * images), TN)
    grads = grads_ref[...]
    squares_ref[...] = jnp.broadcast_to(jnp.sum(grads * grads), squares_ref.shape)
    added = sum_of([mine_ref[g, count - 8 :, :] for g in range(groups)])
    lanes = 128 - 22
    share = added.shape[1]
    added = jnp.concatenate([jnp.zeros((14, share), F32), added, jnp.zeros((lanes, share), F32)], axis=0)
    small_ref[...] = added.T


def class_weights(images, mine, factors):
    share = mine.shape[2]
    outs = [struct((3, share, 4 * factors.shape[2])), struct((8, 128)), struct((share, 128))]
    return pl.pallas_call(
        functools.partial(class_weights_kernel, images),
        grid=(1,),
        in_specs=[whole(mine.shape), whole(factors.shape)],
        out_specs=[whole(out.shape) for out in outs],
        out_shape=outs,
        compiler_params=limit(SMALL_MIB),
        cost_estimate=pl.CostEstimate(flops=1 << 29, bytes_accessed=3 << 20, transcendentals=0),
        name="class_weights",
    )(mine, factors)


def mm3_wide(left, right):
    width = right[0].shape[1]
    both = mm(left[0], jnp.concatenate(right, axis=1))
    return both[:, :width] + (both[:, width:] + mm(left[1], right[0]))


def backward_kernel(slots, images, dp_size, unroll, *refs):
    place_ref, lengths_ref = refs[:2]
    token_hbm = refs[2 : 2 + slots]
    (
        e_high_ref, e_low_ref, pv_ref, inverse_ref, pv_bias_ref, cot_ref,
        kt_high, kt_low, v_high, v_low, query_ref, t1_ref, t2_ref, t1_rows, t2_rows,
        vec_rows_ref, vecs_ref, mats_ref,
    ) = refs[2 + slots : 20 + slots]
    (
        even_ref, odd_ref, keep_ref, send_ref,
        d_keys, d_values, c1, c2, cot_t, qt, d_qt, v_three, w_ref, tokens, arrived,
    ) = refs[20 + slots :]
    rows, width = cot_ref.shape
    step = pl.program_id(0)
    size = width // 8
    lanes = lax.broadcasted_iota(jnp.int32, (1, 128), 1)
    pairs = [(mats_ref.at[0, 0, :, pl.ds(0, 3 * width)], w_ref)]
    pairs += [(ref, tokens.at[i]) for i, ref in enumerate(token_hbm)]
    copies = [pltpu.make_async_copy(a, b, arrived.at[i]) for i, (a, b) in enumerate(pairs)]

    @pl.when(step == 0)
    def _():
        for copy in copies:
            copy.start()
        cot_t[...] = cot_ref[...].T
        qt[...] = query_ref[...].T
        d_qt[...] = jnp.zeros_like(d_qt)
        d_keys[...] = jnp.zeros_like(d_keys)
        c1[...] = jnp.zeros_like(c1)
        v_three[...] = jnp.concatenate([v_high[...], v_high[...], v_low[...]], axis=1)
        c2[...] = jnp.where(
            lanes == 8, jnp.sum(cot_t[...] * pv_bias_ref[...], axis=1, keepdims=True), 0.0
        )
        inside = jnp.concatenate(same_image(lengths_ref, images, place_ref[0], slots, rows), axis=0)
        inside = jnp.where(inside, 1.0, 0.0).astype(BF16)
        high, low = split(cot_ref[...] * t2_rows[8:9, :])
        d_values[...] = mm(inside, high) + mm(inside, low)

    found = []
    for u in range(unroll):
        head = step * unroll + u
        t2_column, inverse = column_of(t2_ref[...], head), inverse_ref[u]
        crossed = cot_t[...] * pv_ref[u]
        c2[...] += jnp.where(lanes == head, jnp.sum(crossed, axis=1, keepdims=True), 0.0)
        delta = jnp.sum(crossed * t2_column, axis=0, keepdims=True) * inverse
        high, low = split(cot_t[...] * (t2_column * inverse))
        found.append((mm(v_three[...], jnp.concatenate([high, low, high], axis=0)), delta))
    for u in range(unroll):
        head = step * unroll + u
        d_probs, delta = found[u]
        pair = (e_high_ref[u], e_low_ref[u])
        d_mixed = split((pair[0].astype(F32) + pair[1].astype(F32)) * (d_probs - delta))
        inverse_rows = jnp.broadcast_to(inverse_ref[u], (8, rows)).T[:, :1]
        cot = split(cot_ref[...] * inverse_rows * t2_rows[pl.ds(head, 1), :])
        d_values[...] += mm3_wide(pair, cot)
        d_keys[...] += mm3_wide(d_mixed, split(query_ref[...] * t1_rows[pl.ds(head, 1), :]))
        back = mm3((kt_high[...], kt_low[...]), d_mixed)
        d_qt[...] += back * column_of(t1_ref[...], head)
        c1[...] += jnp.where(lanes == head, jnp.sum(back * qt[...], axis=1, keepdims=True), 0.0)

    @pl.when(step == pl.num_programs(0) - 1)
    def _():
        for copy in copies:
            copy.wait()
        d_query = d_qt[...].T * size ** (-0.5)
        w_q, w_kv = split(w_ref[:, :width]), split(w_ref[:, width:])
        gain = shift = g_kv = 0.0
        for slot in range(slots):
            here = pl.ds(slot * rows, rows)
            unit, _ = norm_rows(tokens[slot])
            normed = split(unit * vecs_ref[0:1, :] + vecs_ref[1:2, :])
            d_kv = split(jnp.concatenate([d_keys[here, :], d_values[here, :]], axis=1))
            piece = mm3(d_kv, w_kv, NT)
            if slot == 0:
                dq = split(d_query)
                piece = piece + mm3(dq, w_q, NT)
                g_q = mm3(normed, dq, TN)
            (odd_ref if slot % 2 else even_ref)[slot // 2] = piece
            gain, shift = gain + row_sum(piece * unit), shift + row_sum(piece)
            g_kv = g_kv + mm3(normed, d_kv, TN)
        g_k, g_v = g_kv[:, :width], g_kv[:, width:]
        added = jnp.concatenate(
            [gain, shift, row_sum(d_query), row_sum(d_values[...]), jnp.zeros((4, width), F32)], axis=0
        )
        vec_rows = jnp.concatenate([vec_rows_ref[0:8, :] + added, vec_rows_ref[8:28, :]], axis=0)
        fold = lambda value: jnp.concatenate(
            [row_sum(value[i * size : (i + 1) * size]) for i in range(8)], axis=0
        )
        pre, post = fold(c1[...]).T[:8, :], fold(c2[...])
        count = vec_rows.shape[0]
        talk = jnp.concatenate([pre, post[:, :9], jnp.zeros((8, 128 - count - 17), F32)], axis=1)
        block = width // dp_size
        talk = jnp.concatenate([talk, jnp.zeros((block - 8, 128 - count), F32)], axis=0)
        talk = jnp.concatenate([talk] * dp_size, axis=0)
        small = jnp.concatenate([vec_rows.T, talk], axis=1)
        even = jnp.bitwise_and(place_ref[0], 1) == 0
        left = jnp.concatenate([g_q, g_k[:, :256]], axis=1)
        right = jnp.concatenate([g_k[:, 256:], g_v, small], axis=1)
        keep_ref[...] = jnp.where(even, left, right)
        send_ref[...] = jnp.where(even, right, left)


def backward(dp_size, place, lengths, token_slots, found, cot, keys_values, query, tables,
             vec_rows, vectors, matrices):
    rows, width = cot.shape
    heads, total, _ = found[0].shape
    slots, unroll = total // rows, 2 if total <= 1024 else 1
    operands = far_off(*token_slots, *found, cot, *keys_values, query, *tables, vec_rows, vectors, matrices)
    specs = [whole(operand.shape) for operand in operands]
    specs[:slots] = [anywhere()] * slots
    specs[slots : slots + 4] = [by_head(unroll, operand.shape) for operand in found[:4]]
    specs[-1] = anywhere()
    outs = [far_struct((slots // 2, rows, width))] * 2 + [far_struct((width, 640))] * 2
    return pl.pallas_call(
        functools.partial(backward_kernel, slots, lengths.shape[1], dp_size, unroll),
        grid=(heads // unroll,),
        in_specs=[smem(), smem()] + specs,
        out_specs=[whole(out.shape) for out in outs],
        out_shape=outs,
        scratch_shapes=[pltpu.VMEM((total, width), F32)] * 2
        + [pltpu.VMEM((width, 128), F32)] * 2
        + [pltpu.VMEM((width, rows), F32)] * 3
        + [
            pltpu.VMEM((total, 3 * width), BF16),
            pltpu.VMEM((width, 3 * width), F32),
            pltpu.VMEM((slots, rows, width), F32),
            pltpu.SemaphoreType.DMA((1 + slots,)),
        ],
        compiler_params=limit(NEAR_MIB if total <= 1024 else KERNEL_MIB),
        cost_estimate=pl.CostEstimate(
            flops=6 * (4 * heads + 6) * total * rows * width, bytes_accessed=24 << 20, transcendentals=0
        ),
        name="backward",
    )(place, lengths, *operands)


def token_grad_kernel(tokens_ref, vecs_ref, own_ref, near_ref, far_ref, tail_ref, grad_ref):
    unit, scale = norm_rows(tokens_ref[...])
    d_normed = own_ref[...] + near_ref[...] + far_ref[...]
    grad_ref[...] = tail_ref[...] + norm_back(d_normed * vecs_ref[0:1, :], unit, scale)


def token_grad(tokens, vectors, own, near, far, tail):
    operands = [*far_off(tokens, vectors), own, near, far, *far_off(tail)]
    return pl.pallas_call(
        token_grad_kernel,
        out_shape=struct(tokens.shape),
        compiler_params=limit(SMALL_MIB),
        cost_estimate=pl.CostEstimate(flops=1 << 21, bytes_accessed=2 << 20, transcendentals=0),
        name="token_grad",
    )(*operands)


def squares_kernel(dp_size, counts, *refs):
    place_ref, added_ref, class_ref = refs[:3]
    early_refs = refs[3 : 3 + counts[0]]
    late_refs = refs[3 + counts[0] : 3 + sum(counts)]
    out_ref, early_ref, late_ref = refs[3 + sum(counts) :]
    odd = jnp.bitwise_and(place_ref[0], 1) == 1
    early = sum_of([ref[...] for ref in early_refs])
    late = sum_of([ref[...] for ref in late_refs])
    early_ref[...], late_ref[...] = early, late
    small = late[:, 512:] + jnp.where(odd, added_ref[...], 0.0)
    lane = lax.broadcasted_iota(jnp.int32, small.shape, 1)
    talk = jnp.logical_and(odd, jnp.logical_and(lane >= 28, lane < 45))
    small = small * small * jnp.where(talk, 1.0 / dp_size, 1.0)
    total = jnp.sum(small)
    for value in (late[:, :512], early):
        total = total + jnp.sum(value * value)
    out_ref[...] = 0.5 * class_ref[...] + total


def squares_of(dp_size, place, added, class_squares, early, late):
    operands = [added, class_squares, *early, *late]
    outs = [struct((8, 128)), struct(early[0].shape), struct(late[0].shape)]
    return pl.pallas_call(
        functools.partial(squares_kernel, dp_size, (len(early), len(late))),
        grid=(1,),
        in_specs=[smem()] + [whole(operand.shape) for operand in operands],
        out_specs=[whole(out.shape) for out in outs],
        out_shape=outs,
        compiler_params=limit(SMALL_MIB),
        cost_estimate=pl.CostEstimate(flops=1 << 18, bytes_accessed=1 << 20, transcendentals=0),
        name="squares",
    )(place, *operands)


def adam_step(weight, gradient, moment1, moment2, rate, decay):
    first = BETA_ONE * moment1 + (1.0 - BETA_ONE) * gradient
    second = BETA_TWO * moment2 + (1.0 - BETA_TWO) * gradient * gradient
    first_hat = first * (1.0 / (1.0 - BETA_ONE**STEP))
    second_hat = second * (1.0 / (1.0 - BETA_TWO**STEP))
    updated = weight - rate * (first_hat / (jnp.sqrt(second_hat) + ADAM_EPS) + decay * weight)
    return (updated, first, second)


def stage_kernel(sliced, place_ref, w_ref, m1_ref, m2_ref, ema_ref, w_out, m1_out, m2_out, ema_out, arrived):
    rows = w_out.shape[2]
    if sliced:
        w_ref = w_ref.at[:, :, pl.ds(pl.multiple_of(place_ref[1] * rows, rows), rows), :]
    pairs = [(w_ref, w_out), (m1_ref, m1_out), (m2_ref, m2_out), (ema_ref, ema_out)]
    for copy in copy_in(pairs, arrived):
        copy.wait()


def stage(place, mats):
    shape = mats[1].shape
    return pl.pallas_call(
        functools.partial(stage_kernel, mats[0].shape != shape),
        in_specs=[smem()] + [anywhere()] * 4,
        out_specs=[pl.BlockSpec(memory_space=pltpu.VMEM)] * 4,
        out_shape=[pltpu.VMEM(shape, F32)] * 4,
        scratch_shapes=[pltpu.SemaphoreType.DMA((4,))],
        compiler_params=limit(8),
        cost_estimate=pl.CostEstimate(flops=1, bytes_accessed=1, transcendentals=0),
        name="stage",
    )(place, *far_off(*mats))


def adam_kernel(sliced, *refs):
    (
        place_ref, squares_ref, early_own, early_other, late_own, late_other, added_ref,
        class_ref, w_ref, m1_ref, m2_ref, ema_ref, v_ref, v1_ref, v2_ref, v_ema_ref,
        t_ref, t1_ref, t2_ref, t_ema_ref,
    ) = refs[:20]
    norm_ref, mat_outs, v_outs, t_outs = refs[20], refs[21:25], refs[25:29], refs[29:33]
    stored, leaving, columns = refs[33:37], refs[37], refs[38]
    norm = jnp.sqrt(squares_ref[0:1, 0:1])
    factor = jnp.minimum(1.0, CLIP_NORM / norm)
    norm_ref[...] = norm

    def updates(weight, gradient, moment1, moment2, ema, rate, decay):
        updated, first, second = adam_step(weight, gradient * factor, moment1, moment2, rate, decay)
        return updated, first, second, EMA_RATE * ema + (1.0 - EMA_RATE) * updated

    even = jnp.bitwise_and(place_ref[0], 1) == 0
    pair = lambda own, other: (jnp.where(even, own[...], other[...]), jnp.where(even, other[...], own[...]))
    early_left, early_right = pair(early_own, early_other)
    late_left, late_right = pair(late_own, late_other)
    hidden = w_ref.shape[3]
    first = jnp.concatenate(
        [late_left, late_right[:, :512], early_left[:, hidden:], early_right[:, hidden : hidden + 128]], axis=1
    )
    grads = [first, early_left[:, :hidden], early_right[:, :hidden], *[class_ref[i] for i in range(3)]]
    copies = []
    for number in (3, 4, 5, 1, 2, 0):
        at = (number // 3, number % 3)
        values = updates(w_ref[at], grads[number], m1_ref[at], m2_ref[at], ema_ref[at], LR_MATRIX, WEIGHT_DECAY)
        for i, value in enumerate(values):
            stored[i][at] = value
            copies.append(pltpu.make_async_copy(stored[i].at[at], mat_outs[i].at[at], leaving.at[i, number]))
            copies[-1].start()
    small = late_right[:, 512:] + added_ref[...]
    count = v1_ref.shape[0]
    if sliced:
        columns[:, :count] = v_ref[...].T
        share = small.shape[0]
        begin = pl.multiple_of(place_ref[1] * share, share)
        weight = columns[pl.ds(begin, share), :].T[:count, :]
    else:
        weight = v_ref[...]
    values = updates(weight, small.T[:count, :], v1_ref[...], v2_ref[...], v_ema_ref[...], LR_VECTOR, 0.0)
    for ref, value in zip(v_outs, values):
        ref[...] = value
    talk = small[:8, count : count + 17]
    values = updates(t_ref[...], talk, t1_ref[...], t2_ref[...], t_ema_ref[...], LR_TALKING, 0.0)
    for ref, value in zip(t_outs, values):
        ref[...] = value
    for copy in copies:
        copy.wait()


def optimizer(place, squares, grads, class_share, mats, vecs, talks):
    shape = mats[0].shape
    sliced = vecs[0].shape != vecs[1].shape
    operands = [squares, *grads, class_share, *mats, *far_off(*vecs, *talks)]
    vmem = pl.BlockSpec(memory_space=pltpu.VMEM)
    outs = [struct((1, 1))] + [struct(shape)] * 4
    outs += [struct(vecs[1].shape)] * 4 + [struct(talks[0].shape)] * 4
    return pl.pallas_call(
        functools.partial(adam_kernel, sliced),
        in_specs=[smem()] + [vmem] * len(operands),
        out_specs=[vmem] + [anywhere()] * 4 + [vmem] * 8,
        out_shape=outs,
        scratch_shapes=[pltpu.VMEM(shape, F32)] * 4
        + [pltpu.SemaphoreType.DMA((4, 6)), pltpu.VMEM((vecs[0].shape[1], 128), F32)],
        compiler_params=limit(SMALL_MIB),
        cost_estimate=pl.CostEstimate(flops=1 << 23, bytes_accessed=14 << 20, transcendentals=0),
        name="optimizer",
    )(place, *operands)


def swap(value, axis, size, bit):
    return lax.ppermute(value, axis, [(place, place ^ bit) for place in range(size)])


def bits_of(axis, size, bit=1):
    return [(axis, bit << i) for i in range((size // bit).bit_length() - 1)]


class Places:
    def __init__(self, dp_size, seq_size, row_share):
        seq, dp = lax.axis_index("seq"), lax.axis_index("dp")
        self.sizes = {"dp": dp_size, "seq": seq_size}
        steps = bits_of("dp", dp_size) + bits_of("seq", seq_size)
        names = {"dp": dp, "seq": seq}
        bits = {step: jnp.bitwise_and(lax.shift_right_logical(names[step[0]], step[1].bit_length() - 1), 1) for step in steps}
        self.found = {
            "seq": seq.astype(jnp.int32).reshape(1),
            "dp": dp.astype(jnp.int32).reshape(1),
            "rows": (dp * row_share).astype(jnp.uint32),
            "share": (bits["seq", 1] * (seq_size // 2) + lax.shift_right_logical(seq, 1)).astype(jnp.uint32),
        }
        for step, bit in bits.items():
            self.found[step, "mine"] = bit.astype(jnp.uint32)
            self.found[step, "other"] = (1 - bit).astype(jnp.uint32)
            self.found[step, "low"] = bit == 0

    def before(self, value):
        names = list(self.found)
        value, *found = together(value, *[self.found[name] for name in names])
        self.found = dict(zip(names, found))
        return value

    def take(self, value, picks):
        at = [jnp.uint32(0)] * value.ndim
        sizes = list(value.shape)
        for dim, (step, which) in picks.items():
            at[dim] = self.found[step, which]
            sizes[dim] = 1
        return lax.squeeze(lax.dynamic_slice(value, at, sizes), tuple(picks))

    def share(self, value, rows):
        at = self.found["share"] * jnp.uint32(rows)
        return lax.dynamic_slice(value, (at, jnp.uint32(0)), (rows, value.shape[1]))

    def rows(self, value, size, dim):
        at = [jnp.uint32(0)] * value.ndim
        at[dim] = self.found["rows"]
        sizes = list(value.shape)
        sizes[dim] = size
        return lax.dynamic_slice(value, at, sizes)

    def swap(self, value, steps):
        flip = sum(bit * (self.sizes["seq"] if axis == "dp" else 1) for axis, bit in steps)
        count = self.sizes["dp"] * self.sizes["seq"]
        return lax.ppermute(value, ("dp", "seq"), [(place, place ^ flip) for place in range(count)])

    def pair(self, value, other, step):
        low = self.found[step, "low"]
        return [jnp.where(low, value, other), jnp.where(low, other, value)]


def subsets(group):
    found = [()]
    for step in group:
        found += [one + (step,) for one in found]
    return found[1:]


class Reduce:
    def __init__(self, terms, places, groups):
        self.places, self.groups = places, list(groups)
        self.left = bits_of("dp", places.sizes["dp"])[::-1]
        shape = (2,) * len(self.left) + (-1, terms[0].shape[1])
        self.terms = [term.reshape(shape) for term in terms]
        self.got = 0

    def sends(self):
        group = self.groups[0]
        halves = [step for step in group if step[0] == "dp"]
        dims = {step: self.left.index(step) for step in halves}
        if not halves:
            self.terms = [sum_of(self.terms)]

        def taken(others):
            picks = {dims[step]: (step, "other" if step in others else "mine") for step in halves}
            return [self.places.take(term, picks) if picks else term for term in self.terms]

        sent = [sum_of(taken(others)) for others in subsets(group)]
        self.terms = taken(())
        self.left = [step for step in self.left if step not in halves]
        return sent

    def post(self, sent):
        group = self.groups.pop(0)
        self.got = len(sent)
        self.terms += [self.places.swap(value, steps) for value, steps in zip(sent, subsets(group))]

    def received(self):
        return self.terms[len(self.terms) - self.got :]

    def set_received(self, values):
        self.terms[len(self.terms) - self.got :] = values

    def value(self):
        return sum_of(self.terms)


class Gather:
    def __init__(self, value, places):
        self.places = places
        dp = bits_of("dp", places.sizes["dp"])
        self.value = value[None]
        self.groups = [(step,) for step in dp[2:]] + [tuple(dp[:2])]
        self.groups += [(step,) for step in bits_of("seq", places.sizes["seq"], 2) + bits_of("seq", 2)]

    def sends(self):
        return [self.value]

    def post(self, sent):
        self.value = sent[0]
        self.others = [self.places.swap(self.value, steps) for steps in subsets(self.groups[0])]

    def received(self):
        return list(self.others)

    def set_received(self, values):
        group = self.groups.pop(0)
        if group[0][0] == "dp":
            self.value = jnp.concatenate([self.value, *values], axis=0)
        else:
            self.value = jnp.concatenate(self.places.pair(self.value, values[0], group[0]), axis=1)
        self.others = []


def settle(streams, *work):
    streams = [stream for stream in streams if stream.received()]
    counts = [len(stream.received()) for stream in streams]
    found = together(*[value for stream in streams for value in stream.received()], *work)
    at = 0
    for stream, count in zip(streams, counts):
        stream.set_received(list(found[at : at + count]))
        at += count
    return found[at:]


def launch(streams, *after):
    streams = [stream for stream in streams if stream.groups]
    sent = [stream.sends() for stream in streams]
    found = together(*[value for one in sent for value in one], *after)
    at = 0
    for stream, one in zip(streams, sent):
        stream.post(list(found[at : at + len(one)]))
        at += len(one)
    return found[at:]


def sum_of(terms):
    total = terms[0]
    for term in terms[1:]:
        total = total + term
    return total


def tie(value, *others):
    return lax.optimization_barrier((value, *others))[0]


def together(*values):
    return lax.optimization_barrier(values)


def on_device(
    dp_size, seq_size,
    tokens, class_tokens, cot_patch, cot_class, lengths,
    matrices, matrices_moment1, matrices_moment2, matrices_ema,
    vectors, vectors_moment1, vectors_moment2, vectors_ema,
    talking, talking_moment1, talking_moment2, talking_ema,
):
    rows, width = tokens.shape
    images = class_tokens.shape[0]
    row_share = width // dp_size
    places = Places(dp_size, seq_size, row_share)
    tokens = places.before(tokens)
    place = places.found["seq"]

    slots = {0: tokens}
    slots[1] = swap(tokens, "seq", seq_size, 1)
    bit = 2
    while bit < seq_size:
        for slot in sorted(slot for slot in slots if slot % 2 == 0):
            slots[slot | bit] = swap(slots[slot], "seq", seq_size, bit)
        bit *= 2
    *prepared, t1, t2, t1_rows, t2_rows, query, k1, k2, v1, v2, kt1, kt2, vt1, vt2 = prepare(
        tokens, slots[1], class_tokens, matrices, vectors, talking
    )
    for slot in range(2, seq_size, 2):
        slots[slot + 1] = swap(tie(slots[slot], query), "seq", seq_size, 1)
    token_slots = [slots[slot] for slot in range(seq_size)]
    (
        e_high, e_low, pv, inverse, pv_bias, attended, kt_high, kt_low, v_high, v_low,
        patch_out, *kept, packed, scores,
    ) = forward(
        place, lengths, token_slots, matrices, vectors, t1, t2, prepared[3],
        [query, k1, k2, v1, v2, kt1, kt2, vt1, vt2],
    )
    parts = [packed] + [swap(packed, "seq", seq_size, bit) for bit in range(1, seq_size)]
    (
        class_out, d_attended, d_mixed, early_keep, early_send, partial, factors, vec_rows, class_terms,
    ) = middle(
        place, parts, vectors, prepared, class_tokens, cot_class, cot_patch,
        patch_out, scores, [attended, *kept], matrices,
    )

    core, chips, dp = ("seq", 1), bits_of("seq", seq_size, 2), bits_of("dp", dp_size)
    pairs = lambda steps: [tuple(steps[i : i + 2]) for i in range(0, len(steps), 2)]
    other = places.swap(early_send, [core])
    partials = [partial] + [swap(partial, "seq", seq_size, bit) for bit in range(1, seq_size)]
    grad_class, factors = class_finish(partials, class_terms, class_tokens, vectors, matrices, factors)
    gather = Gather(places.share(factors, factors.shape[0] // seq_size), places)
    other, gather.value = together(other, gather.value)
    early = Reduce(
        [early_keep, other], places, [tuple(dp[:2])] + [(step,) for step in dp[2:] + chips]
    )
    (later,) = launch([early, gather], place)
    even, odd, late_keep, late_send = backward(
        dp_size, later, lengths, token_slots, [e_high, e_low, pv, inverse, pv_bias], d_attended,
        [kt_high, kt_low, v_high, v_low], query, [t1, t2, t1_rows, t2_rows], vec_rows, vectors, matrices,
    )

    late_send, odd = settle([early, gather], late_send, odd)
    late_other, odd = places.swap(late_send, [core]), places.swap(odd, [core])
    late = Reduce([late_keep, late_other], places, [tuple(dp[:2])] + [(step,) for step in dp[2:] + chips])
    (late.terms[1],) = launch([early], late.terms[1])
    (even,) = launch([late], even)
    own = [even[0]] + [even[i] + odd[i] for i in range(1, seq_size // 2)]
    near = odd[0]
    bit = 1
    while 2 * bit < len(own):
        for slot in range(0, len(own), 2 * bit):
            own[slot] = own[slot] + swap(own[slot + bit], "seq", seq_size, 2 * bit)
        bit *= 2
    far = swap(own[bit], "seq", seq_size, 2 * bit)
    (own[bit],) = launch([gather], own[bit])
    (own[bit],) = settle([gather], own[bit])
    while len(gather.groups) > len(chips) + 1:
        launch([gather])
        settle([gather])
    launch([gather], own[bit])
    (far,) = settle([late, early], far)
    (far,) = launch([late, early], far)
    (far,) = settle([gather], far)
    while gather.groups:
        launch([gather])
        settle([gather])
    sliced = row_share % 8 == 0
    if not sliced:
        matrices_rows, vectors_columns = places.rows(matrices, row_share, 2), places.rows(vectors, row_share, 1)
    else:
        matrices_rows, vectors_columns = matrices, vectors
    both_places = tie(jnp.concatenate([place, places.found["dp"]]), gather.value)
    staged = stage(both_places, [matrices_rows, matrices_moment1, matrices_moment2, matrices_ema])
    gather.value, *staged = settle([late], gather.value, *staged)
    while late.groups[1:]:
        launch([late])
        settle([late])
    (gather.value,) = launch([late], gather.value)
    mine = places.rows(gather.value, row_share, 2)
    class_share, class_squares, added = class_weights(images, mine, gather.value)
    while early.groups:
        settle([early])
        launch([early])
    class_share, class_squares, added = settle([late, early], class_share, class_squares, added)
    last = [[term.reshape(row_share, -1) for term in stream.terms] for stream in (early, late)]
    squares, early, late = squares_of(dp_size, place, added, class_squares, *last)
    far, squares = together(far, squares)
    for group in pairs([core] + dp):
        squares = sum_of([squares] + [places.swap(squares, steps) for steps in subsets(group)])
    grad_tokens = token_grad(tokens, vectors, own[0], near, far, d_mixed)
    grads = []
    for value in (early, late):
        grads += [value, places.swap(value, [core])]
    norm, *updated = optimizer(
        both_places, squares, [*grads, added], class_share, staged,
        [vectors_columns, vectors_moment1, vectors_moment2, vectors_ema],
        [talking, talking_moment1, talking_moment2, talking_ema],
    )
    return (patch_out, class_out, grad_tokens, grad_class, norm.reshape(()), *updated)


def solution(mesh):
    tokens = P(("dp", "seq"), None)
    by_group = P("dp", None)
    mats = P(None, None, "dp", None)
    vecs = P(None, "dp")
    body = functools.partial(on_device, mesh.shape["dp"], mesh.shape["seq"])
    return jax.shard_map(
        body,
        mesh=mesh,
        in_specs=(tokens, by_group, tokens, by_group, by_group, P(), mats, mats, mats,
                  P(), vecs, vecs, vecs, P(), P(), P(), P()),
        out_specs=(tokens, by_group, tokens, by_group, P(), mats, mats, mats, mats,
                   vecs, vecs, vecs, vecs, P(), P(), P(), P()),
        check_vma=False,
    )
```

```python
import functools

import jax
import jax.numpy as jnp
from jax import lax
from jax.experimental import pallas as pl
from jax.experimental.pallas import tpu as pltpu
from jax.sharding import PartitionSpec as P

STEP = 10
EPS_NORM = 1e-06
MASKED = -1e30
LR_MATRIX = 0.05
LR_VECTOR = 0.1
LR_TALKING = 0.2
BETA_ONE = 0.9
BETA_TWO = 0.999
ADAM_EPS = 1e-08
WEIGHT_DECAY = 0.05
EMA_RATE = 0.9
CLIP_NORM = 1.0
F32 = jnp.float32
BF16 = jnp.bfloat16
NN = (((1,), (0,)), ((), ()))
NT = (((1,), (1,)), ((), ()))
TN = (((0,), (0,)), ((), ()))
KERNEL_MIB, NEAR_MIB, SMALL_MIB = 58, 52, 24


def split(value):
    high = value.astype(BF16)
    return high, (value - high.astype(F32)).astype(BF16)


def mm(left, right, dims=NN):
    return lax.dot_general(left, right, dims, preferred_element_type=F32)


def mm3(left, right, dims=NN):
    return mm(left[0], right[0], dims) + (mm(left[0], right[1], dims) + mm(left[1], right[0], dims))


def mm3_tall(left, right, dims=NN):
    rows = left[0].shape[0]
    stacked = jnp.concatenate([part.astype(F32) for part in left], axis=0).astype(BF16)
    both = mm(stacked, right[0], dims)
    return both[:rows] + (both[rows:] + mm(left[0], right[1], dims))


def dot_tall(left, right, dims=NN):
    return mm3_tall(split(left), split(right), dims)


def dot3(left, right, dims=NN):
    return mm3(split(left), split(right), dims)


def norm_rows(values):
    average = jnp.mean(values, axis=-1, keepdims=True)
    centered = values - average
    variance = jnp.mean(centered * centered, axis=-1, keepdims=True)
    scale = lax.rsqrt(variance + EPS_NORM)
    return centered * scale, scale


def norm_back(grad, unit, scale):
    inner = jnp.mean(grad * unit, axis=-1, keepdims=True)
    return scale * (grad - jnp.mean(grad, axis=-1, keepdims=True) - unit * inner)


def gelu_both(values):
    half = 0.5 * (1.0 + lax.erf(values * 0.7071067811865476))
    slope = half + values * (0.3989422804014327 * jnp.exp(-0.5 * values * values))
    return values * half, slope


def row_sum(values):
    return jnp.sum(values, axis=0, keepdims=True)


def tail_forward(dot, inputs, attended, w_out, w_up, w_down, vecs):
    projected = dot(attended, w_out) + vecs[4:5]
    mixed = inputs + vecs[5:6] * projected
    unit, _ = norm_rows(mixed)
    normed = unit * vecs[6:7] + vecs[7:8]
    up_bias = jnp.concatenate([vecs[row : row + 1] for row in range(8, 12)], axis=1)
    hidden, slope = gelu_both(dot(normed, w_up) + up_bias)
    lowered = dot(hidden, w_down, NT) + vecs[12:13]
    return mixed + vecs[13:14] * lowered, (projected, mixed, hidden, slope, lowered)


def tail_backward(dot, cot, kept, w_out, w_up, w_down, vecs):
    projected, mixed, hidden, slope, lowered = kept
    width = cot.shape[1]
    unit, scale = norm_rows(mixed)
    normed = unit * vecs[6:7] + vecs[7:8]
    d_lowered = cot * vecs[13:14]
    d_hidden = dot(d_lowered, w_down) * slope
    d_normed = dot(d_hidden, w_up, NT)
    d_mixed = cot + norm_back(d_normed * vecs[6:7], unit, scale)
    d_projected = d_mixed * vecs[5:6]
    d_attended = dot(d_projected, w_out, NT)
    d_up = row_sum(d_hidden)
    rows = [
        row_sum(d_projected), row_sum(d_mixed * projected), row_sum(d_normed * unit), row_sum(d_normed),
        *[d_up[:, i * width : (i + 1) * width] for i in range(4)],
        row_sum(d_lowered), row_sum(cot * lowered),
    ]
    return d_mixed, d_attended, d_projected, d_hidden, d_lowered, normed, rows


def image_of(lengths_ref, images, positions):
    end = lengths_ref[0, 0]
    inside = (positions >= end).astype(jnp.int32)
    for image in range(1, images):
        end = end + lengths_ref[0, image]
        inside = inside + (positions >= end).astype(jnp.int32)
    return inside


def same_image(lengths_ref, images, place, slots, rows):
    queries = place * rows + lax.broadcasted_iota(jnp.int32, (1, rows), 1)
    query_image = image_of(lengths_ref, images, queries)
    parts = []
    for slot in range(slots):
        keys = jnp.bitwise_xor(place, slot) * rows + lax.broadcasted_iota(jnp.int32, (rows, 1), 0)
        parts.append(image_of(lengths_ref, images, keys) == query_image)
    return parts


def column_of(table, number):
    lanes = lax.broadcasted_iota(jnp.int32, (1, table.shape[1]), 1)
    return jnp.sum(jnp.where(lanes == number, table, 0.0), axis=1, keepdims=True)


def head_mask(heads, width):
    row = lax.broadcasted_iota(jnp.int32, (heads, width), 0)
    return jnp.where(lax.broadcasted_iota(jnp.int32, (heads, width), 1) // (width // heads) == row, 1.0, 0.0)


def spread(value, mask):
    return jnp.concatenate([value[i : i + 1] * mask for i in range(value.shape[0])], axis=0)


def repeat_rows(value, heads):
    shape = (heads, value.shape[1])
    return jnp.concatenate(
        [jnp.broadcast_to(value[i : i + 1], shape) for i in range(value.shape[0])], axis=0
    )


def fold_heads(value, mask):
    heads = mask.shape[0]
    return jnp.concatenate(
        [row_sum(value[i : i + heads] * mask) for i in range(0, value.shape[0], heads)], axis=0
    )


def head_sums(value, mask):
    return jnp.sum(spread(value, mask), axis=1, keepdims=True)


def rows_of(value, heads):
    return jnp.concatenate(
        [row_sum(value[i : i + heads]) for i in range(0, value.shape[0], heads)], axis=0
    )


def wide(column):
    return jnp.broadcast_to(column, (column.shape[0], 128))


def whole(shape):
    return pl.BlockSpec(shape, lambda *_: (0,) * len(shape))


def struct(shape, dtype=F32):
    return jax.ShapeDtypeStruct(shape, dtype)


def far_struct(shape, dtype=F32):
    return pltpu.HBM(shape, dtype)


def smem():
    return pl.BlockSpec(memory_space=pltpu.SMEM)


def anywhere():
    return pl.BlockSpec(memory_space=pl.ANY)


def weight_block(block, matrix, shape, columns=None):
    return pl.BlockSpec((None, None, shape[2], columns or shape[3]), lambda *_: (block, matrix, 0, 0))


def far_off(*operands):
    return [pltpu.with_memory_space_constraint(operand, pltpu.HBM) for operand in operands]


def copy_in(pairs, arrived):
    copies = [pltpu.make_async_copy(a, b, arrived.at[i]) for i, (a, b) in enumerate(pairs)]
    for copy in copies:
        copy.start()
    return copies


def limit(mebibytes):
    return pltpu.CompilerParams(vmem_limit_bytes=mebibytes << 20)


def prepare_kernel(
    own_ref, near_ref, class_ref, w_self_ref, w_class_ref, vecs_ref, talk_ref,
    normed_ref, query_c_ref, value_c_ref, key_rows_ref, score_ref, t1_ref, t2_ref, t1_rows_ref, t2_rows_ref,
    query_ref, k_high, k_low, v_high, v_low, kt_high, kt_low, vt_high, vt_low,
):
    rows, width = own_ref.shape
    heads = talk_ref.shape[0]
    size = width // heads
    scale = size ** (-0.5)
    vecs = vecs_ref[...]
    w_q, w_kv = split(w_self_ref[:, :width]), split(w_self_ref[:, width:])
    tokens = jnp.concatenate([own_ref[...], near_ref[...]], axis=0)
    unit, _ = norm_rows(tokens)
    normed = split(unit * vecs[0:1] + vecs[1:2])
    query_ref[...] = (mm3((normed[0][:rows], normed[1][:rows]), w_q) + vecs[2:3]) * scale
    both = mm3(normed, w_kv)
    keys, values = both[:, :width], both[:, width:] + vecs[3:4]
    k_high[...], k_low[...] = split(keys)
    v_high[...], v_low[...] = split(values)
    kt_high[...], kt_low[...] = split(keys.T)
    vt_high[...], vt_low[...] = split(values.T)
    mask = head_mask(heads, width)
    unit, _ = norm_rows(class_ref[...])
    normed = unit * vecs[14:15] + vecs[15:16]
    both = dot_tall(normed, w_class_ref[...])
    query = both[:, :width] + vecs[16:17]
    normed_ref[...] = normed
    query_c_ref[...] = query
    value_c_ref[...] = both[:, 2 * width :] + vecs[17:18]
    key_rows_ref[...] = dot3(spread(query, mask), w_class_ref[:, width : 2 * width], NT) * scale
    score_ref[...] = wide(head_sums(query * both[:, width : 2 * width], mask) * scale)
    head_of = lax.broadcasted_iota(jnp.int32, (width, 1), 0) // size
    talk = talk_ref[...]
    talk_t = jnp.concatenate([talk, jnp.zeros((heads, 128 - talk.shape[1]), F32)], axis=1).T[: talk.shape[1], :]
    t1 = t2 = t1_rows = t2_rows = 0.0
    for head in range(heads):
        here = head_of == head
        t1 = t1 + jnp.where(here, talk_t[head : head + 1, :], 0.0)
        t2 = t2 + jnp.where(here, talk[head : head + 1, heads:], 0.0)
        t1_rows = t1_rows + mask[head : head + 1] * talk[:, head : head + 1]
        t2_rows = t2_rows + mask[head : head + 1] * talk_t[heads:, head : head + 1]
    t1_ref[...], t2_ref[...], t1_rows_ref[...], t2_rows_ref[...] = t1, t2, t1_rows, t2_rows


def prepare(own, near, class_tokens, matrices, vectors, talking):
    images, width = class_tokens.shape
    rows = own.shape[0]
    heads = talking.shape[0]
    pairs = images * heads
    outs = [far_struct((images, width))] * 3 + [
        far_struct((pairs, width)), far_struct((pairs, 128)),
        far_struct((width, heads)), far_struct((width, heads + 1)),
        far_struct((heads, width)), far_struct((heads + 1, width)),
        far_struct((rows, width)),
    ]
    outs += [far_struct((2 * rows, width), BF16)] * 4 + [far_struct((width, 2 * rows), BF16)] * 4
    own, class_tokens, matrices, vectors, talking = far_off(own, class_tokens, matrices, vectors, talking)
    operands = [own, near, class_tokens, matrices, matrices, vectors, talking]
    specs = [whole(operand.shape) for operand in operands]
    specs[3] = weight_block(0, 0, matrices.shape, 3 * width)
    specs[4] = weight_block(1, 0, matrices.shape, 3 * width)
    return pl.pallas_call(
        prepare_kernel,
        grid=(1,),
        in_specs=specs,
        out_specs=[whole(out.shape) for out in outs],
        out_shape=outs,
        compiler_params=limit(NEAR_MIB),
        cost_estimate=pl.CostEstimate(flops=4 << 30, bytes_accessed=8 << 20, transcendentals=0),
        name="prepare",
    )(*operands)


def forward_kernel(slots, images, unroll, *refs):
    place_ref, lengths_ref = refs[:2]
    token_refs = refs[2 : 1 + slots]
    (
        vecs_ref, t1_ref, t2_ref, key_rows_ref, query_ref,
        k_high0, k_low0, v_high0, v_low0, kt_high0, kt_low0, vt_high0, vt_low0, mats_ref,
        e_high_hbm, e_low_hbm, pv_hbm, inverse_ref, pv_bias_ref, attended_ref,
        kt_high_hbm, kt_low_hbm, v_high_hbm, v_low_hbm,
        patch_ref, projected_ref, mixed_ref, hidden_hbm, slope_hbm, lowered_ref, packed_ref, scores_ref,
        k_three, vt_two, qt, bias, attended_t, w_kv, w_up, w_down, w_out, arrived,
        kt_high, kt_low, v_high, v_low, hidden_ref, slope_ref, e_high_ref, e_low_ref, pv_ref, leaving,
    ) = refs[1 + slots :]
    rows, width = token_refs[0].shape
    step = pl.program_id(0)
    place = place_ref[0]
    ready, columns = pl.ds(0, 2 * rows), lambda i: pl.ds(i * width, width)
    pairs = [
        (mats_ref.at[0, 0, :, pl.ds(width, 2 * width)], w_kv),
        (k_high0, k_three.at[ready, columns(0)]), (k_high0, k_three.at[ready, columns(1)]),
        (k_low0, k_three.at[ready, columns(2)]), (v_high0, v_high.at[ready, :]), (v_low0, v_low.at[ready, :]),
        (kt_high0, kt_high.at[:, ready]), (kt_low0, kt_low.at[:, ready]),
        (vt_high0, vt_two.at[columns(0), ready]), (vt_low0, vt_two.at[columns(1), ready]),
        (mats_ref.at[0, 0, :, pl.ds(3 * width, width)], w_out),
        (mats_ref.at[0, 1], w_up), (mats_ref.at[0, 2], w_down),
    ]
    fetches = [pltpu.make_async_copy(a, b, arrived.at[i]) for i, (a, b) in enumerate(pairs)]
    pairs = [(kt_high, kt_high_hbm), (kt_low, kt_low_hbm), (v_high, v_high_hbm), (v_low, v_low_hbm),
             (hidden_ref, hidden_hbm), (slope_ref, slope_hbm)]
    stores = [pltpu.make_async_copy(a, b, leaving.at[i]) for i, (a, b) in enumerate(pairs)]
    heads = inverse_ref.shape[0]
    groups = []
    for number in range(heads // unroll):
        here = pl.ds(number * unroll, unroll)
        groups.append([
            pltpu.make_async_copy(a.at[here], b.at[here], leaving.at[6 + 3 * number + i])
            for i, (a, b) in enumerate([(e_high_ref, e_high_hbm), (e_low_ref, e_low_hbm), (pv_ref, pv_hbm)])
        ])

    @pl.when(step == 0)
    def _():
        for fetch in fetches:
            fetch.start()
        vecs = vecs_ref[...]
        inside = same_image(lengths_ref, images, place, slots, rows)
        for slot in range(slots):
            bias[pl.ds(slot * rows, rows), :] = jnp.where(inside[slot], 0.0, MASKED)
        units = [norm_rows(ref[...])[0] for ref in token_refs[1:]]
        fetches[0].wait()
        w_both = split(w_kv[...])
        for slot in range(2, slots):
            here = pl.ds(slot * rows, rows)
            normed = split(units[slot - 2] * vecs[0:1] + vecs[1:2])
            both = mm3(normed, w_both)
            keys, values = both[:, :width], both[:, width:] + vecs[3:4]
            high, low = split(keys)
            k_three[here, :] = jnp.concatenate([high, high, low], axis=1)
            v_high[here, :], v_low[here, :] = split(values)
            kt_high[:, here], kt_low[:, here] = split(keys.T)
            vt_two[:, here] = jnp.concatenate(split(values.T), axis=0)
        qt[...] = query_ref[...].T
        attended_t[...] = jnp.zeros_like(attended_t)
        for fetch in fetches[1:10]:
            fetch.wait()
        for store in stores[:4]:
            store.start()

    scores = []
    for u in range(unroll):
        high, low = split(qt[...] * column_of(t1_ref[...], step * unroll + u))
        scores.append(mm(k_three[...], jnp.concatenate([high, low, high], axis=0)) + bias[...])
    for u in range(unroll):
        exponentials = jnp.exp(scores[u] - jnp.max(scores[u], axis=0, keepdims=True))
        inverse = 1.0 / jnp.sum(exponentials, axis=0, keepdims=True)
        pair = split(exponentials)
        head = step * unroll + u
        e_high_ref[head], e_low_ref[head] = pair
        inverse_ref[head] = inverse
        both = mm(vt_two[...], pair[0])
        values = (both[:width] + (both[width:] + mm(vt_two[:width, :], pair[1]))) * inverse
        pv_ref[head] = values
        attended_t[...] += values * column_of(t2_ref[...], head)
    for number, group in enumerate(groups):

        @pl.when(step == number)
        def _(group=group):
            for copy in group:
                copy.start()

    @pl.when(step == pl.num_programs(0) - 1)
    def _():
        inside = jnp.where(bias[...] < 0.0, 0.0, 1.0).astype(BF16)
        both = mm(vt_two[...], inside)
        summed = both[:width] + both[width:]
        pv_bias_ref[...] = summed
        attended = (attended_t[...] + summed * t2_ref[:, 8:9]).T
        attended_ref[...] = attended
        for fetch in fetches[10:]:
            fetch.wait()
        vecs = vecs_ref[...]
        patch, kept = tail_forward(
            dot3, token_refs[0][...], attended, w_out[...], w_up[...], w_down[...], vecs
        )
        patch_ref[...] = patch
        for ref, value in zip((projected_ref, mixed_ref, hidden_ref, slope_ref, lowered_ref), kept):
            ref[...] = value
        for store in stores[4:]:
            store.start()
        unit, _ = norm_rows(patch)
        normed = split(unit * vecs[14:15] + vecs[15:16])
        pairs = images * 8
        image = lax.broadcasted_iota(jnp.int32, (pairs, 1), 0) // 8
        positions = place * rows + lax.broadcasted_iota(jnp.int32, (1, rows), 1)
        belong = image_of(lengths_ref, images, positions) == image
        class_scores = mm3(split(key_rows_ref[...]), normed, NT)
        class_scores = jnp.where(belong, class_scores, MASKED)
        scores_ref[...] = class_scores
        top = jnp.max(class_scores, axis=1, keepdims=True)
        weights = jnp.where(belong, jnp.exp(class_scores - top), 0.0)
        packed_ref[:, :width] = mm3(split(weights), normed)
        lane = lax.broadcasted_iota(jnp.int32, (1, 128), 1)
        total = jnp.sum(weights, axis=1, keepdims=True)
        packed_ref[:, width:] = jnp.where(lane < 64, top, total)
        for store in stores + [copy for group in groups for copy in group]:
            store.wait()


def by_head(unroll, shape):
    return pl.BlockSpec((unroll,) + shape[1:], lambda g: (g, 0, 0))


def forward(place, lengths, token_slots, matrices, vectors, t1, t2, key_rows, projected):
    slots, (rows, width) = len(token_slots), token_slots[0].shape
    total, heads = slots * rows, 8
    unroll = 4 if total <= 1024 else 1
    hidden = matrices.shape[3]
    pairs = key_rows.shape[0]
    outs = [
        far_struct((heads, total, rows), BF16), far_struct((heads, total, rows), BF16), far_struct((heads, width, rows)),
        far_struct((heads, 1, rows)), far_struct((width, rows)), far_struct((rows, width)),
        far_struct((width, total), BF16), far_struct((width, total), BF16),
        far_struct((total, width), BF16), far_struct((total, width), BF16),
        far_struct((rows, width)), far_struct((rows, width)), far_struct((rows, width)),
        far_struct((rows, hidden)), far_struct((rows, hidden)), far_struct((rows, width)),
        far_struct((pairs, width + 128)), far_struct((pairs, rows)),
    ]
    away = (0, 1, 2, 6, 7, 8, 9, 13, 14)
    out_specs = [anywhere() if i in away else whole(out.shape) for i, out in enumerate(outs)]
    operands = [token_slots[0], *token_slots[2:], *far_off(vectors, t1, t2, key_rows, *projected, matrices)]
    in_specs = [whole(operand.shape) for operand in operands]
    in_specs[-9:] = [anywhere()] * 9
    flops = 2 * 3 * ((2 * heads + 1) * total + 9 * width) * rows * width
    return pl.pallas_call(
        functools.partial(forward_kernel, slots, lengths.shape[1], unroll),
        grid=(heads // unroll,),
        in_specs=[smem(), smem()] + in_specs,
        out_specs=out_specs,
        out_shape=outs,
        scratch_shapes=[
            pltpu.VMEM((total, 3 * width), BF16),
            pltpu.VMEM((2 * width, total), BF16),
            pltpu.VMEM((width, rows), F32),
            pltpu.VMEM((total, rows), F32),
            pltpu.VMEM((width, rows), F32),
            pltpu.VMEM((width, 2 * width), F32),
            pltpu.VMEM((width, hidden), F32),
            pltpu.VMEM((width, hidden), F32),
            pltpu.VMEM((width, width), F32),
            pltpu.SemaphoreType.DMA((13,)),
            pltpu.VMEM((width, total), BF16),
            pltpu.VMEM((width, total), BF16),
            pltpu.VMEM((total, width), BF16),
            pltpu.VMEM((total, width), BF16),
            pltpu.VMEM((rows, hidden), F32),
            pltpu.VMEM((rows, hidden), F32),
            pltpu.VMEM((heads, total, rows), BF16),
            pltpu.VMEM((heads, total, rows), BF16),
            pltpu.VMEM((heads, width, rows), F32),
            pltpu.SemaphoreType.DMA((6 + 3 * heads // unroll,)),
        ],
        compiler_params=limit(NEAR_MIB if total <= 1024 else KERNEL_MIB),
        cost_estimate=pl.CostEstimate(
            flops=flops, bytes_accessed=24 << 20, transcendentals=heads * total * rows
        ),
        name="forward",
    )(place, lengths, *operands)


def class_stage_kernel(place_ref, mats_ref, last_out, up_out, down_out, first_out, arrived):
    width = first_out.shape[1]
    pairs = [(mats_ref.at[1, 0, :, pl.ds(width, width)], last_out), (mats_ref.at[1, 1], up_out),
             (mats_ref.at[1, 2], down_out), (mats_ref.at[1, 0, :, pl.ds(0, width)], first_out)]
    for copy in copy_in(pairs, arrived):
        copy.wait()


def class_stage(place, matrices):
    rows, columns = matrices.shape[2:]
    half, whole_matrix = (rows, columns // 2), (rows, columns)
    return pl.pallas_call(
        class_stage_kernel,
        in_specs=[smem(), anywhere()],
        out_specs=[pl.BlockSpec(memory_space=pltpu.VMEM)] * 4,
        out_shape=[pltpu.VMEM(shape, F32) for shape in (half, whole_matrix, whole_matrix, half)],
        scratch_shapes=[pltpu.SemaphoreType.DMA((4,))],
        compiler_params=limit(8),
        cost_estimate=pl.CostEstimate(flops=1, bytes_accessed=1, transcendentals=0),
        name="class_stage",
    )(place, *far_off(matrices))


def middle_kernel(images, slots, *refs):
    place_ref = refs[0]
    parts = [ref[...] for ref in refs[1 : 1 + slots]]
    (
        vecs_ref, normed_c_ref, query_c_ref, value_c_ref, key_rows_ref, own_ref,
        class_ref, cot_class_ref, cot_patch_ref, patch_ref, scores_ref, wc0, wc1, wc2,
        attended_hbm, projected_hbm, mixed_hbm, hidden_hbm, slope_hbm, lowered_hbm, mats_ref,
        class_out_ref, d_attended_ref, d_mixed_ref, keep_ref, send_ref, partial_ref,
        factors_ref, vec_rows_ref, class_terms_ref,
        ws0, ws1, ws2, attended_ref, projected_ref, mixed_ref, hidden_ref, slope_ref, lowered_ref,
        keep, send, arrived, stored,
    ) = refs[1 + slots :]
    width = class_ref.shape[1]
    heads = 8
    size = width // heads
    copies = copy_in(
        [(lowered_hbm, lowered_ref), (hidden_hbm, hidden_ref), (mats_ref.at[0, 2], ws2), (slope_hbm, slope_ref),
         (mixed_hbm, mixed_ref), (mats_ref.at[0, 1], ws1), (projected_hbm, projected_ref),
         (attended_hbm, attended_ref), (mats_ref.at[0, 0, :, pl.ds(3 * width, width)], ws0)], arrived)
    vecs = vecs_ref[...]
    vecs_s, vecs_c = vecs[:14], vecs[14:]
    mask = head_mask(heads, width)
    first = jnp.where(place_ref[0] == 0, 1.0, 0.0)
    own_score = own_ref[:, :1]
    normed_c = normed_c_ref[...]
    normed_rep = repeat_rows(normed_c, heads)
    top = own_score
    for part in parts:
        top = jnp.maximum(top, part[:, width : width + 1])
    own_weight = jnp.exp(own_score - top)
    total, summed = own_weight, own_weight * normed_rep
    for part in parts:
        rescale = jnp.exp(part[:, width : width + 1] - top)
        total = total + part[:, width + 64 : width + 65] * rescale
        summed = summed + part[:, :width] * rescale
    value_rows = summed / total
    own_prob = own_weight / total
    unit_p, scale_p = norm_rows(patch_ref[...])
    normed_p = split(unit_p * vecs_c[0:1] + vecs_c[1:2])
    scores = scores_ref[...]
    probs = jnp.where(scores > 0.5 * MASKED, jnp.exp(scores - top) * (1.0 / total), 0.0)
    w_v = split(wc0[:, :width])
    class_attended = fold_heads(mm3_tall(split(value_rows), w_v), mask) + vecs_c[3:4]
    w_out_c = wc0[:, width:]
    class_out, kept_c = tail_forward(
        dot_tall, class_ref[...], class_attended, w_out_c, wc1[...], wc2[...], vecs_c
    )
    class_out_ref[...] = class_out
    d_mixed_c, d_attended_c, d_projected_c, d_hidden_c, d_lowered_c, normed2_c, tail_rows_c = (
        tail_backward(dot_tall, cot_class_ref[...], kept_c, w_out_c, wc1[...], wc2[...], vecs_c)
    )
    for copy in copies:
        copy.wait()
    delta = head_sums(d_attended_c * class_attended, mask)
    cot_rows = mm3_tall(split(spread(d_attended_c, mask)), w_v, NT)
    cot_const = head_sums(d_attended_c * vecs_c[3:4], mask)
    cot_split = split(cot_rows)
    d_scores = probs * (mm3_tall(cot_split, normed_p, NT) + cot_const - delta)
    d_own = own_prob * (head_sums(d_attended_c * value_c_ref[...], mask) - delta)
    key_rows = key_rows_ref[...]
    d_split = split(d_scores)
    d_normed_p = mm3(d_split, split(key_rows), TN) + mm3(split(probs), cot_split, TN)
    partial_ref[...] = mm3_tall(d_split, normed_p)
    cot = cot_patch_ref[...] + norm_back(d_normed_p * vecs_c[0:1], unit_p, scale_p)
    class_terms_ref[...] = jnp.concatenate(
        [rows_of(d_own * key_rows + own_prob * cot_rows, heads), d_mixed_c], axis=0
    )
    query_c = query_c_ref[...]
    chunks = lambda value: [value[:, i * width : (i + 1) * width] for i in range(4)]
    factors_ref[...] = jnp.concatenate(
        [normed_c, class_attended, normed2_c, d_lowered_c, d_own * normed_rep, value_rows,
         jnp.zeros_like(query_c), query_c * size ** (-0.5), d_attended_c, d_projected_c,
         *chunks(d_hidden_c), *chunks(kept_c[2])], axis=0)
    projected, mixed, hidden, lowered = projected_ref[...], mixed_ref[...], split(hidden_ref[...]), lowered_ref[...]
    unit, scale = norm_rows(mixed)
    normed = split(unit * vecs_s[6:7] + vecs_s[7:8])
    d_lowered = cot * vecs_s[13:14]
    d_low_split = split(d_lowered)
    d_hidden = mm3(d_low_split, split(ws2[...])) * slope_ref[...]
    d_hid_split = split(d_hidden)
    g_down = mm3(d_low_split, hidden, TN)
    g_up = mm3(normed, d_hid_split, TN)
    even = jnp.bitwise_and(place_ref[0], 1) == 0
    size_up = g_up.shape[1]
    send[:, :size_up] = jnp.where(even, g_down, g_up)
    keep[:, :size_up] = jnp.where(even, g_up, g_down)
    bulk = pl.ds(0, size_up)
    leaving = copy_in(
        [(send.at[:, bulk], send_ref.at[:, bulk]), (keep.at[:, bulk], keep_ref.at[:, bulk])], stored
    )
    d_normed = mm3(d_hid_split, split(ws1[...]), NT)
    d_mixed = cot + norm_back(d_normed * vecs_s[6:7], unit, scale)
    d_projected = d_mixed * vecs_s[5:6]
    d_proj_split = split(d_projected)
    g_out = mm3(split(attended_ref[...]), d_proj_split, TN)
    left = g_out[:, :256]
    right = jnp.concatenate([g_out[:, 256:], jnp.zeros((width, 512 - width), F32)], axis=1)
    send[:, size_up:] = jnp.where(even, right, left)
    keep[:, size_up:] = jnp.where(even, left, right)
    rest = pl.ds(size_up, 256)
    for i, (a, b) in enumerate([(send, send_ref), (keep, keep_ref)]):
        leaving.append(pltpu.make_async_copy(a.at[:, rest], b.at[:, rest], stored.at[2 + i]))
        leaving[-1].start()
    d_mixed_ref[...] = d_mixed
    d_attended_ref[...] = mm3(d_proj_split, split(ws0[...]), NT)
    d_up = row_sum(d_hidden)
    tail_rows = [
        row_sum(d_projected), row_sum(d_mixed * projected), row_sum(d_normed * unit), row_sum(d_normed),
        *[d_up[:, i * width : (i + 1) * width] for i in range(4)],
        row_sum(d_lowered), row_sum(cot * lowered),
    ]
    zero = jnp.zeros((1, width), F32)
    vec_rows_ref[...] = jnp.concatenate(
        [zero] * 4 + tail_rows
        + [row_sum(d_normed_p * unit_p), row_sum(d_normed_p), zero, row_sum(d_attended_c) * first]
        + [row * first for row in tail_rows_c], axis=0)
    for copy in leaving:
        copy.wait()


def middle(
    place, parts, vectors, prepared, class_tokens, cot_class, cot_patch, patch, scores, staged, kept, matrices
):
    images, width = class_tokens.shape
    rows = cot_patch.shape[0]
    hidden = matrices.shape[3]
    pairs = parts[0].shape[0]
    rest = [vectors, *prepared, class_tokens, cot_class, cot_patch, patch, scores]
    operands = [*parts, *far_off(*rest), *staged, *far_off(*kept, matrices)]
    outs = [
        far_struct((images, width)), far_struct((rows, width)), far_struct((rows, width)),
        far_struct((width, hidden + 256)), far_struct((width, hidden + 256)), far_struct((pairs, width)),
        far_struct((16 * images + 2 * pairs, width)), far_struct((28, width)), far_struct((2 * images, width)),
    ]
    vmem = pl.BlockSpec(memory_space=pltpu.VMEM)
    in_specs = [vmem] * len(operands)
    in_specs[-1 - len(kept) :] = [anywhere()] * (1 + len(kept))
    out_specs = [vmem] * len(outs)
    out_specs[3:5] = [anywhere()] * 2
    return pl.pallas_call(
        functools.partial(middle_kernel, images, len(parts)),
        in_specs=[smem()] + in_specs,
        out_specs=out_specs,
        out_shape=outs,
        scratch_shapes=[pltpu.VMEM((width, width), F32)]
        + [pltpu.VMEM((width, hidden), F32)] * 2
        + [pltpu.VMEM(value.shape, F32) for value in kept]
        + [pltpu.VMEM((width, hidden + 256), F32)] * 2
        + [pltpu.SemaphoreType.DMA((9,)), pltpu.SemaphoreType.DMA((4,))],
        compiler_params=limit(44),
        cost_estimate=pl.CostEstimate(flops=8 << 30, bytes_accessed=28 << 20, transcendentals=1 << 19),
        name="middle",
    )(place, *operands)


def class_kernel(slots, *refs):
    partial_refs = refs[:slots]
    terms_ref, class_ref, vecs_ref, w_ref, factors_ref, grad_ref, factors_out_ref = refs[slots:]
    images, width = class_ref.shape
    pairs = partial_refs[0].shape[0]
    heads = pairs // images
    mask = head_mask(heads, width)
    at = 4 * images
    query_rows = sum_of([factors_ref[at : at + pairs, :]] + [ref[...] for ref in partial_refs])
    w_k, w_q = w_ref[:, width : 2 * width], w_ref[:, :width]
    d_query = fold_heads(dot_tall(query_rows, w_k), mask) * (width // heads) ** (-0.5)
    d_normed = dot_tall(d_query, w_q, NT) + terms_ref[:images, :]
    unit, scale = norm_rows(class_ref[...])
    grad_ref[...] = terms_ref[images:, :] + norm_back(d_normed * vecs_ref[14:15, :], unit, scale)
    count = factors_ref.shape[0]
    factors_out_ref[:count, :] = factors_ref[...]
    factors_out_ref[at : at + pairs, :] = query_rows
    at = at + 2 * pairs
    factors_out_ref[at : at + images, :] = d_query
    added = [row_sum(d_normed * unit), row_sum(d_normed), row_sum(d_query), jnp.zeros((5, width), F32)]
    factors_out_ref[count:, :] = jnp.concatenate(added, axis=0)


def class_finish(partials, terms, class_tokens, vectors, w_first, factors):
    operands = [*partials, *far_off(terms, class_tokens, vectors), w_first, *far_off(factors)]
    vmem = pl.BlockSpec(memory_space=pltpu.VMEM)
    outs = [struct(class_tokens.shape), struct((factors.shape[0] + 8, factors.shape[1]))]
    return pl.pallas_call(
        functools.partial(class_kernel, len(partials)),
        in_specs=[vmem] * len(operands),
        out_specs=[vmem] * len(outs),
        out_shape=outs,
        compiler_params=limit(12),
        cost_estimate=pl.CostEstimate(flops=1, bytes_accessed=1, transcendentals=0),
        name="class_finish",
    )(*operands)


def class_weights_kernel(images, mine_ref, factors_ref, grads_ref, squares_ref, small_ref):
    groups, count, width = factors_ref.shape
    heads = 8
    pairs = images * heads
    mask = head_mask(heads, width)
    at = 4 * images + 2 * pairs

    def rows(ref, begin, count=images):
        return jnp.concatenate([ref[g, begin : begin + count, :] for g in range(groups)], axis=0)

    def chunked(begin):
        return jnp.concatenate([rows(factors_ref, begin + i * images) for i in range(4)], axis=1)

    def headed(left, right):
        return dot3(rows(mine_ref, left, pairs), spread(rows(factors_ref, right), mask), TN)

    grads_ref[0, :, :width] = dot3(rows(mine_ref, 0), rows(factors_ref, at), TN)
    grads_ref[0, :, width : 2 * width] = headed(4 * images, at + images)
    grads_ref[0, :, 2 * width : 3 * width] = headed(4 * images + pairs, at + 2 * images)
    grads_ref[0, :, 3 * width :] = dot3(rows(mine_ref, images), rows(factors_ref, at + 3 * images), TN)
    grads_ref[1] = dot3(rows(mine_ref, 2 * images), chunked(at + 4 * images), TN)
    grads_ref[2] = dot3(rows(mine_ref, 3 * images), chunked(at + 8 * images), TN)
    grads = grads_ref[...]
    squares_ref[...] = jnp.broadcast_to(jnp.sum(grads * grads), squares_ref.shape)
    added = sum_of([mine_ref[g, count - 8 :, :] for g in range(groups)])
    lanes = 128 - 22
    share = added.shape[1]
    added = jnp.concatenate([jnp.zeros((14, share), F32), added, jnp.zeros((lanes, share), F32)], axis=0)
    small_ref[...] = added.T


def class_weights(images, mine, factors):
    share = mine.shape[2]
    outs = [struct((3, share, 4 * factors.shape[2])), struct((8, 128)), struct((share, 128))]
    return pl.pallas_call(
        functools.partial(class_weights_kernel, images),
        grid=(1,),
        in_specs=[whole(mine.shape), whole(factors.shape)],
        out_specs=[whole(out.shape) for out in outs],
        out_shape=outs,
        compiler_params=limit(SMALL_MIB),
        cost_estimate=pl.CostEstimate(flops=1 << 29, bytes_accessed=3 << 20, transcendentals=0),
        name="class_weights",
    )(mine, factors)


def mm3_wide(left, right):
    width = right[0].shape[1]
    both = mm(left[0], jnp.concatenate(right, axis=1))
    return both[:, :width] + (both[:, width:] + mm(left[1], right[0]))


def backward_kernel(slots, images, dp_size, unroll, *refs):
    place_ref, lengths_ref = refs[:2]
    token_hbm = refs[2 : 2 + slots]
    (
        e_high_ref, e_low_ref, pv_ref, inverse_ref, pv_bias_ref, cot_ref,
        kt_high, kt_low, v_high, v_low, query_ref, t1_ref, t2_ref, t1_rows, t2_rows,
        vec_rows_ref, vecs_ref, mats_ref,
    ) = refs[2 + slots : 20 + slots]
    (
        even_ref, odd_ref, keep_ref, send_ref,
        d_keys, d_values, c1, c2, cot_t, qt, d_qt, v_three, w_ref, tokens, arrived,
    ) = refs[20 + slots :]
    rows, width = cot_ref.shape
    step = pl.program_id(0)
    size = width // 8
    lanes = lax.broadcasted_iota(jnp.int32, (1, 128), 1)
    pairs = [(mats_ref.at[0, 0, :, pl.ds(0, 3 * width)], w_ref)]
    pairs += [(ref, tokens.at[i]) for i, ref in enumerate(token_hbm)]
    copies = [pltpu.make_async_copy(a, b, arrived.at[i]) for i, (a, b) in enumerate(pairs)]

    @pl.when(step == 0)
    def _():
        for copy in copies:
            copy.start()
        cot_t[...] = cot_ref[...].T
        qt[...] = query_ref[...].T
        d_qt[...] = jnp.zeros_like(d_qt)
        d_keys[...] = jnp.zeros_like(d_keys)
        c1[...] = jnp.zeros_like(c1)
        v_three[...] = jnp.concatenate([v_high[...], v_high[...], v_low[...]], axis=1)
        c2[...] = jnp.where(
            lanes == 8, jnp.sum(cot_t[...] * pv_bias_ref[...], axis=1, keepdims=True), 0.0
        )
        inside = jnp.concatenate(same_image(lengths_ref, images, place_ref[0], slots, rows), axis=0)
        inside = jnp.where(inside, 1.0, 0.0).astype(BF16)
        high, low = split(cot_ref[...] * t2_rows[8:9, :])
        d_values[...] = mm(inside, high) + mm(inside, low)

    found = []
    for u in range(unroll):
        head = step * unroll + u
        t2_column, inverse = column_of(t2_ref[...], head), inverse_ref[u]
        crossed = cot_t[...] * pv_ref[u]
        c2[...] += jnp.where(lanes == head, jnp.sum(crossed, axis=1, keepdims=True), 0.0)
        delta = jnp.sum(crossed * t2_column, axis=0, keepdims=True) * inverse
        high, low = split(cot_t[...] * (t2_column * inverse))
        found.append((mm(v_three[...], jnp.concatenate([high, low, high], axis=0)), delta))
    for u in range(unroll):
        head = step * unroll + u
        d_probs, delta = found[u]
        pair = (e_high_ref[u], e_low_ref[u])
        d_mixed = split((pair[0].astype(F32) + pair[1].astype(F32)) * (d_probs - delta))
        inverse_rows = jnp.broadcast_to(inverse_ref[u], (8, rows)).T[:, :1]
        cot = split(cot_ref[...] * inverse_rows * t2_rows[pl.ds(head, 1), :])
        d_values[...] += mm3_wide(pair, cot)
        d_keys[...] += mm3_wide(d_mixed, split(query_ref[...] * t1_rows[pl.ds(head, 1), :]))
        back = mm3((kt_high[...], kt_low[...]), d_mixed)
        d_qt[...] += back * column_of(t1_ref[...], head)
        c1[...] += jnp.where(lanes == head, jnp.sum(back * qt[...], axis=1, keepdims=True), 0.0)

    @pl.when(step == pl.num_programs(0) - 1)
    def _():
        for copy in copies:
            copy.wait()
        d_query = d_qt[...].T * size ** (-0.5)
        w_q, w_kv = split(w_ref[:, :width]), split(w_ref[:, width:])
        gain = shift = g_kv = 0.0
        for slot in range(slots):
            here = pl.ds(slot * rows, rows)
            unit, _ = norm_rows(tokens[slot])
            normed = split(unit * vecs_ref[0:1, :] + vecs_ref[1:2, :])
            d_kv = split(jnp.concatenate([d_keys[here, :], d_values[here, :]], axis=1))
            piece = mm3(d_kv, w_kv, NT)
            if slot == 0:
                dq = split(d_query)
                piece = piece + mm3(dq, w_q, NT)
                g_q = mm3(normed, dq, TN)
            (odd_ref if slot % 2 else even_ref)[slot // 2] = piece
            gain, shift = gain + row_sum(piece * unit), shift + row_sum(piece)
            g_kv = g_kv + mm3(normed, d_kv, TN)
        g_k, g_v = g_kv[:, :width], g_kv[:, width:]
        added = jnp.concatenate(
            [gain, shift, row_sum(d_query), row_sum(d_values[...]), jnp.zeros((4, width), F32)], axis=0
        )
        vec_rows = jnp.concatenate([vec_rows_ref[0:8, :] + added, vec_rows_ref[8:28, :]], axis=0)
        fold = lambda value: jnp.concatenate(
            [row_sum(value[i * size : (i + 1) * size]) for i in range(8)], axis=0
        )
        pre, post = fold(c1[...]).T[:8, :], fold(c2[...])
        count = vec_rows.shape[0]
        talk = jnp.concatenate([pre, post[:, :9], jnp.zeros((8, 128 - count - 17), F32)], axis=1)
        block = width // dp_size
        talk = jnp.concatenate([talk, jnp.zeros((block - 8, 128 - count), F32)], axis=0)
        talk = jnp.concatenate([talk] * dp_size, axis=0)
        small = jnp.concatenate([vec_rows.T, talk], axis=1)
        even = jnp.bitwise_and(place_ref[0], 1) == 0
        left = jnp.concatenate([g_q, g_k[:, :256]], axis=1)
        right = jnp.concatenate([g_k[:, 256:], g_v, small], axis=1)
        keep_ref[...] = jnp.where(even, left, right)
        send_ref[...] = jnp.where(even, right, left)


def backward(dp_size, place, lengths, token_slots, found, cot, keys_values, query, tables,
             vec_rows, vectors, matrices):
    rows, width = cot.shape
    heads, total, _ = found[0].shape
    slots, unroll = total // rows, 2 if total <= 1024 else 1
    operands = far_off(*token_slots, *found, cot, *keys_values, query, *tables, vec_rows, vectors, matrices)
    specs = [whole(operand.shape) for operand in operands]
    specs[:slots] = [anywhere()] * slots
    specs[slots : slots + 4] = [by_head(unroll, operand.shape) for operand in found[:4]]
    specs[-1] = anywhere()
    outs = [far_struct((slots // 2, rows, width))] * 2 + [far_struct((width, 640))] * 2
    return pl.pallas_call(
        functools.partial(backward_kernel, slots, lengths.shape[1], dp_size, unroll),
        grid=(heads // unroll,),
        in_specs=[smem(), smem()] + specs,
        out_specs=[whole(out.shape) for out in outs],
        out_shape=outs,
        scratch_shapes=[pltpu.VMEM((total, width), F32)] * 2
        + [pltpu.VMEM((width, 128), F32)] * 2
        + [pltpu.VMEM((width, rows), F32)] * 3
        + [
            pltpu.VMEM((total, 3 * width), BF16),
            pltpu.VMEM((width, 3 * width), F32),
            pltpu.VMEM((slots, rows, width), F32),
            pltpu.SemaphoreType.DMA((1 + slots,)),
        ],
        compiler_params=limit(NEAR_MIB if total <= 1024 else KERNEL_MIB),
        cost_estimate=pl.CostEstimate(
            flops=6 * (4 * heads + 6) * total * rows * width, bytes_accessed=24 << 20, transcendentals=0
        ),
        name="backward",
    )(place, lengths, *operands)


def token_grad_kernel(tokens_ref, vecs_ref, own_ref, near_ref, far_ref, tail_ref, grad_ref):
    unit, scale = norm_rows(tokens_ref[...])
    d_normed = own_ref[...] + near_ref[...] + far_ref[...]
    grad_ref[...] = tail_ref[...] + norm_back(d_normed * vecs_ref[0:1, :], unit, scale)


def token_grad(tokens, vectors, own, near, far, tail):
    operands = [*far_off(tokens, vectors), own, near, far, *far_off(tail)]
    return pl.pallas_call(
        token_grad_kernel,
        out_shape=struct(tokens.shape),
        compiler_params=limit(SMALL_MIB),
        cost_estimate=pl.CostEstimate(flops=1 << 21, bytes_accessed=2 << 20, transcendentals=0),
        name="token_grad",
    )(*operands)


def squares_kernel(dp_size, counts, *refs):
    place_ref, added_ref, class_ref = refs[:3]
    early_refs = refs[3 : 3 + counts[0]]
    late_refs = refs[3 + counts[0] : 3 + sum(counts)]
    out_ref, early_ref, late_ref = refs[3 + sum(counts) :]
    odd = jnp.bitwise_and(place_ref[0], 1) == 1
    early = sum_of([ref[...] for ref in early_refs])
    late = sum_of([ref[...] for ref in late_refs])
    early_ref[...], late_ref[...] = early, late
    small = late[:, 512:] + jnp.where(odd, added_ref[...], 0.0)
    lane = lax.broadcasted_iota(jnp.int32, small.shape, 1)
    talk = jnp.logical_and(odd, jnp.logical_and(lane >= 28, lane < 45))
    small = small * small * jnp.where(talk, 1.0 / dp_size, 1.0)
    total = jnp.sum(small)
    for value in (late[:, :512], early):
        total = total + jnp.sum(value * value)
    out_ref[...] = 0.5 * class_ref[...] + total


def squares_of(dp_size, place, added, class_squares, early, late):
    operands = [added, class_squares, *early, *late]
    outs = [struct((8, 128)), struct(early[0].shape), struct(late[0].shape)]
    return pl.pallas_call(
        functools.partial(squares_kernel, dp_size, (len(early), len(late))),
        grid=(1,),
        in_specs=[smem()] + [whole(operand.shape) for operand in operands],
        out_specs=[whole(out.shape) for out in outs],
        out_shape=outs,
        compiler_params=limit(SMALL_MIB),
        cost_estimate=pl.CostEstimate(flops=1 << 18, bytes_accessed=1 << 20, transcendentals=0),
        name="squares",
    )(place, *operands)


def adam_step(weight, gradient, moment1, moment2, rate, decay):
    first = BETA_ONE * moment1 + (1.0 - BETA_ONE) * gradient
    second = BETA_TWO * moment2 + (1.0 - BETA_TWO) * gradient * gradient
    first_hat = first * (1.0 / (1.0 - BETA_ONE**STEP))
    second_hat = second * (1.0 / (1.0 - BETA_TWO**STEP))
    updated = weight - rate * (first_hat / (jnp.sqrt(second_hat) + ADAM_EPS) + decay * weight)
    return (updated, first, second)


def stage_kernel(sliced, place_ref, w_ref, m1_ref, m2_ref, ema_ref, w_out, m1_out, m2_out, ema_out, arrived):
    rows = w_out.shape[2]
    if sliced:
        w_ref = w_ref.at[:, :, pl.ds(pl.multiple_of(place_ref[1] * rows, rows), rows), :]
    pairs = [(w_ref, w_out), (m1_ref, m1_out), (m2_ref, m2_out), (ema_ref, ema_out)]
    for copy in copy_in(pairs, arrived):
        copy.wait()


def stage(place, mats):
    shape = mats[1].shape
    return pl.pallas_call(
        functools.partial(stage_kernel, mats[0].shape != shape),
        in_specs=[smem()] + [anywhere()] * 4,
        out_specs=[pl.BlockSpec(memory_space=pltpu.VMEM)] * 4,
        out_shape=[pltpu.VMEM(shape, F32)] * 4,
        scratch_shapes=[pltpu.SemaphoreType.DMA((4,))],
        compiler_params=limit(8),
        cost_estimate=pl.CostEstimate(flops=1, bytes_accessed=1, transcendentals=0),
        name="stage",
    )(place, *far_off(*mats))


def adam_kernel(sliced, *refs):
    (
        place_ref, squares_ref, early_own, early_other, late_own, late_other, added_ref,
        class_ref, w_ref, m1_ref, m2_ref, ema_ref, v_ref, v1_ref, v2_ref, v_ema_ref,
        t_ref, t1_ref, t2_ref, t_ema_ref,
    ) = refs[:20]
    norm_ref, mat_outs, v_outs, t_outs = refs[20], refs[21:25], refs[25:29], refs[29:33]
    stored, leaving, columns = refs[33:37], refs[37], refs[38]
    norm = jnp.sqrt(squares_ref[0:1, 0:1])
    factor = jnp.minimum(1.0, CLIP_NORM / norm)
    norm_ref[...] = norm

    def updates(weight, gradient, moment1, moment2, ema, rate, decay):
        updated, first, second = adam_step(weight, gradient * factor, moment1, moment2, rate, decay)
        return updated, first, second, EMA_RATE * ema + (1.0 - EMA_RATE) * updated

    even = jnp.bitwise_and(place_ref[0], 1) == 0
    pair = lambda own, other: (jnp.where(even, own[...], other[...]), jnp.where(even, other[...], own[...]))
    early_left, early_right = pair(early_own, early_other)
    late_left, late_right = pair(late_own, late_other)
    hidden = w_ref.shape[3]
    first = jnp.concatenate(
        [late_left, late_right[:, :512], early_left[:, hidden:], early_right[:, hidden : hidden + 128]], axis=1
    )
    grads = [first, early_left[:, :hidden], early_right[:, :hidden], *[class_ref[i] for i in range(3)]]
    copies = []
    for number in (3, 4, 5, 1, 2, 0):
        at = (number // 3, number % 3)
        values = updates(w_ref[at], grads[number], m1_ref[at], m2_ref[at], ema_ref[at], LR_MATRIX, WEIGHT_DECAY)
        for i, value in enumerate(values):
            stored[i][at] = value
            copies.append(pltpu.make_async_copy(stored[i].at[at], mat_outs[i].at[at], leaving.at[i, number]))
            copies[-1].start()
    small = late_right[:, 512:] + added_ref[...]
    count = v1_ref.shape[0]
    if sliced:
        columns[:, :count] = v_ref[...].T
        share = small.shape[0]
        begin = pl.multiple_of(place_ref[1] * share, share)
        weight = columns[pl.ds(begin, share), :].T[:count, :]
    else:
        weight = v_ref[...]
    values = updates(weight, small.T[:count, :], v1_ref[...], v2_ref[...], v_ema_ref[...], LR_VECTOR, 0.0)
    for ref, value in zip(v_outs, values):
        ref[...] = value
    talk = small[:8, count : count + 17]
    values = updates(t_ref[...], talk, t1_ref[...], t2_ref[...], t_ema_ref[...], LR_TALKING, 0.0)
    for ref, value in zip(t_outs, values):
        ref[...] = value
    for copy in copies:
        copy.wait()


def optimizer(place, squares, grads, class_share, mats, vecs, talks):
    shape = mats[0].shape
    sliced = vecs[0].shape != vecs[1].shape
    operands = [squares, *grads, class_share, *mats, *far_off(*vecs, *talks)]
    vmem = pl.BlockSpec(memory_space=pltpu.VMEM)
    outs = [struct((1, 1))] + [struct(shape)] * 4
    outs += [struct(vecs[1].shape)] * 4 + [struct(talks[0].shape)] * 4
    return pl.pallas_call(
        functools.partial(adam_kernel, sliced),
        in_specs=[smem()] + [vmem] * len(operands),
        out_specs=[vmem] + [anywhere()] * 4 + [vmem] * 8,
        out_shape=outs,
        scratch_shapes=[pltpu.VMEM(shape, F32)] * 4
        + [pltpu.SemaphoreType.DMA((4, 6)), pltpu.VMEM((vecs[0].shape[1], 128), F32)],
        compiler_params=limit(SMALL_MIB),
        cost_estimate=pl.CostEstimate(flops=1 << 23, bytes_accessed=14 << 20, transcendentals=0),
        name="optimizer",
    )(place, *operands)


def swap(value, axis, size, bit):
    return lax.ppermute(value, axis, [(place, place ^ bit) for place in range(size)])


def bits_of(axis, size, bit=1):
    return [(axis, bit << i) for i in range((size // bit).bit_length() - 1)]


class Places:
    def __init__(self, dp_size, seq_size, row_share):
        seq, dp = lax.axis_index("seq"), lax.axis_index("dp")
        self.sizes = {"dp": dp_size, "seq": seq_size}
        steps = bits_of("dp", dp_size) + bits_of("seq", seq_size)
        names = {"dp": dp, "seq": seq}
        bits = {step: jnp.bitwise_and(lax.shift_right_logical(names[step[0]], step[1].bit_length() - 1), 1) for step in steps}
        self.found = {
            "seq": seq.astype(jnp.int32).reshape(1),
            "dp": dp.astype(jnp.int32).reshape(1),
            "rows": (dp * row_share).astype(jnp.uint32),
            "share": (bits["seq", 1] * (seq_size // 2) + lax.shift_right_logical(seq, 1)).astype(jnp.uint32),
        }
        for step, bit in bits.items():
            self.found[step, "mine"] = bit.astype(jnp.uint32)
            self.found[step, "other"] = (1 - bit).astype(jnp.uint32)
            self.found[step, "low"] = bit == 0

    def before(self, value):
        names = list(self.found)
        value, *found = together(value, *[self.found[name] for name in names])
        self.found = dict(zip(names, found))
        return value

    def take(self, value, picks):
        at = [jnp.uint32(0)] * value.ndim
        sizes = list(value.shape)
        for dim, (step, which) in picks.items():
            at[dim] = self.found[step, which]
            sizes[dim] = 1
        return lax.squeeze(lax.dynamic_slice(value, at, sizes), tuple(picks))

    def share(self, value, rows):
        at = self.found["share"] * jnp.uint32(rows)
        return lax.dynamic_slice(value, (at, jnp.uint32(0)), (rows, value.shape[1]))

    def rows(self, value, size, dim):
        at = [jnp.uint32(0)] * value.ndim
        at[dim] = self.found["rows"]
        sizes = list(value.shape)
        sizes[dim] = size
        return lax.dynamic_slice(value, at, sizes)

    def swap(self, value, steps):
        flip = sum(bit * (self.sizes["seq"] if axis == "dp" else 1) for axis, bit in steps)
        count = self.sizes["dp"] * self.sizes["seq"]
        return lax.ppermute(value, ("dp", "seq"), [(place, place ^ flip) for place in range(count)])

    def pair(self, value, other, step):
        low = self.found[step, "low"]
        return [jnp.where(low, value, other), jnp.where(low, other, value)]


def subsets(group):
    found = [()]
    for step in group:
        found += [one + (step,) for one in found]
    return found[1:]


class Reduce:
    def __init__(self, terms, places, groups):
        self.places, self.groups = places, list(groups)
        self.left = bits_of("dp", places.sizes["dp"])[::-1]
        shape = (2,) * len(self.left) + (-1, terms[0].shape[1])
        self.terms = [term.reshape(shape) for term in terms]
        self.got = 0

    def sends(self):
        group = self.groups[0]
        halves = [step for step in group if step[0] == "dp"]
        dims = {step: self.left.index(step) for step in halves}
        if not halves:
            self.terms = [sum_of(self.terms)]

        def taken(others):
            picks = {dims[step]: (step, "other" if step in others else "mine") for step in halves}
            return [self.places.take(term, picks) if picks else term for term in self.terms]

        sent = [sum_of(taken(others)) for others in subsets(group)]
        self.terms = taken(())
        self.left = [step for step in self.left if step not in halves]
        return sent

    def post(self, sent):
        group = self.groups.pop(0)
        self.got = len(sent)
        self.terms += [self.places.swap(value, steps) for value, steps in zip(sent, subsets(group))]

    def received(self):
        return self.terms[len(self.terms) - self.got :]

    def set_received(self, values):
        self.terms[len(self.terms) - self.got :] = values

    def value(self):
        return sum_of(self.terms)


def join_kernel(*refs):
    out_ref, at = refs[-1], 0
    for ref in refs[:-1]:
        out_ref[at : at + ref.shape[0]] = ref[...]
        at += ref.shape[0]


def join(parts):
    shape = (sum(part.shape[0] for part in parts),) + parts[0].shape[1:]
    return pl.pallas_call(
        join_kernel,
        in_specs=[pl.BlockSpec(memory_space=pltpu.VMEM)] * len(parts),
        out_specs=pl.BlockSpec(memory_space=pltpu.VMEM),
        out_shape=struct(shape),
        compiler_params=limit(SMALL_MIB),
        cost_estimate=pl.CostEstimate(flops=1, bytes_accessed=1, transcendentals=0),
        name="join",
    )(*parts)


class Gather:
    def __init__(self, value, places):
        self.places = places
        dp = bits_of("dp", places.sizes["dp"])
        self.value = value[None]
        self.groups = [(step,) for step in dp[2:]] + [tuple(dp[:2])]
        self.groups += [(step,) for step in bits_of("seq", places.sizes["seq"], 2) + bits_of("seq", 2)]

    def sends(self):
        return [self.value]

    def post(self, sent):
        self.value = sent[0]
        self.others = [self.places.swap(self.value, steps) for steps in subsets(self.groups[0])]

    def received(self):
        return list(self.others)

    def set_received(self, values):
        group = self.groups.pop(0)
        if group[0][0] == "dp":
            self.value = join([self.value, *values])
        else:
            self.value = jnp.concatenate(self.places.pair(self.value, values[0], group[0]), axis=1)
        self.others = []


def settle(streams, *work):
    streams = [stream for stream in streams if stream.received()]
    counts = [len(stream.received()) for stream in streams]
    found = together(*[value for stream in streams for value in stream.received()], *work)
    at = 0
    for stream, count in zip(streams, counts):
        stream.set_received(list(found[at : at + count]))
        at += count
    return found[at:]


def launch(streams, *after):
    streams = [stream for stream in streams if stream.groups]
    sent = [stream.sends() for stream in streams]
    found = together(*[value for one in sent for value in one], *after)
    at = 0
    for stream, one in zip(streams, sent):
        stream.post(list(found[at : at + len(one)]))
        at += len(one)
    return found[at:]


def sum_of(terms):
    total = terms[0]
    for term in terms[1:]:
        total = total + term
    return total


def tie(value, *others):
    return lax.optimization_barrier((value, *others))[0]


def together(*values):
    return lax.optimization_barrier(values)


def on_device(
    dp_size, seq_size,
    tokens, class_tokens, cot_patch, cot_class, lengths,
    matrices, matrices_moment1, matrices_moment2, matrices_ema,
    vectors, vectors_moment1, vectors_moment2, vectors_ema,
    talking, talking_moment1, talking_moment2, talking_ema,
):
    rows, width = tokens.shape
    images = class_tokens.shape[0]
    row_share = width // dp_size
    places = Places(dp_size, seq_size, row_share)
    tokens = places.before(tokens)
    place = places.found["seq"]

    slots = {0: tokens}
    slots[1] = swap(tokens, "seq", seq_size, 1)
    bit = 2
    while bit < seq_size:
        for slot in sorted(slot for slot in slots if slot % 2 == 0):
            slots[slot | bit] = swap(slots[slot], "seq", seq_size, bit)
        bit *= 2
    *prepared, t1, t2, t1_rows, t2_rows, query, k1, k2, v1, v2, kt1, kt2, vt1, vt2 = prepare(
        tokens, slots[1], class_tokens, matrices, vectors, talking
    )
    for slot in range(2, seq_size, 2):
        slots[slot + 1] = swap(tie(slots[slot], query), "seq", seq_size, 1)
    token_slots = [slots[slot] for slot in range(seq_size)]
    (
        e_high, e_low, pv, inverse, pv_bias, attended, kt_high, kt_low, v_high, v_low,
        patch_out, *kept, packed, scores,
    ) = forward(
        place, lengths, token_slots, matrices, vectors, t1, t2, prepared[3],
        [query, k1, k2, v1, v2, kt1, kt2, vt1, vt2],
    )
    parts = [packed] + [swap(packed, "seq", seq_size, bit) for bit in range(1, seq_size)]
    *staged, w_first = class_stage(tie(place, packed), matrices)
    (
        class_out, d_attended, d_mixed, early_keep, early_send, partial, factors, vec_rows, class_terms,
    ) = middle(
        place, parts, vectors, prepared, class_tokens, cot_class, cot_patch,
        patch_out, scores, staged, [attended, *kept], matrices,
    )

    core, chips, dp = ("seq", 1), bits_of("seq", seq_size, 2), bits_of("dp", dp_size)
    pairs = lambda steps: [tuple(steps[i : i + 2]) for i in range(0, len(steps), 2)]
    other = places.swap(early_send, [core])
    partials = [partial] + [swap(partial, "seq", seq_size, bit) for bit in range(1, seq_size)]
    grad_class, factors = class_finish(partials, class_terms, class_tokens, vectors, w_first, factors)
    gather = Gather(places.share(factors, factors.shape[0] // seq_size), places)
    other, gather.value = together(other, gather.value)
    early = Reduce(
        [early_keep, other], places, [tuple(dp[:2])] + [(step,) for step in dp[2:] + chips]
    )
    (later,) = launch([early, gather], place)
    even, odd, late_keep, late_send = backward(
        dp_size, later, lengths, token_slots, [e_high, e_low, pv, inverse, pv_bias], d_attended,
        [kt_high, kt_low, v_high, v_low], query, [t1, t2, t1_rows, t2_rows], vec_rows, vectors, matrices,
    )

    late_send, odd = settle([early, gather], late_send, odd)
    late_other, odd = places.swap(late_send, [core]), places.swap(odd, [core])
    late = Reduce([late_keep, late_other], places, [tuple(dp[:2])] + [(step,) for step in dp[2:] + chips])
    (late.terms[1],) = launch([early], late.terms[1])
    (even,) = launch([late], even)
    own = [even[0]] + [even[i] + odd[i] for i in range(1, seq_size // 2)]
    near = odd[0]
    bit = 1
    while 2 * bit < len(own):
        for slot in range(0, len(own), 2 * bit):
            own[slot] = own[slot] + swap(own[slot + bit], "seq", seq_size, 2 * bit)
        bit *= 2
    far = swap(own[bit], "seq", seq_size, 2 * bit)
    (own[bit],) = launch([gather], own[bit])
    (own[bit],) = settle([gather], own[bit])
    while len(gather.groups) > len(chips) + 1:
        launch([gather])
        settle([gather])
    launch([gather], own[bit])
    (far,) = settle([late, early], far)
    (far,) = launch([late, early], far)
    (far,) = settle([gather], far)
    while gather.groups:
        launch([gather])
        settle([gather])
    sliced = row_share % 8 == 0
    if not sliced:
        matrices_rows, vectors_columns = places.rows(matrices, row_share, 2), places.rows(vectors, row_share, 1)
    else:
        matrices_rows, vectors_columns = matrices, vectors
    both_places = tie(jnp.concatenate([place, places.found["dp"]]), gather.value)
    staged = stage(both_places, [matrices_rows, matrices_moment1, matrices_moment2, matrices_ema])
    gather.value, *staged = settle([late], gather.value, *staged)
    while late.groups[1:]:
        launch([late])
        settle([late])
    (gather.value,) = launch([late], gather.value)
    mine = places.rows(gather.value, row_share, 2)
    class_share, class_squares, added = class_weights(images, mine, gather.value)
    while early.groups:
        settle([early])
        launch([early])
    class_share, class_squares, added = settle([late, early], class_share, class_squares, added)
    last = [[term.reshape(row_share, -1) for term in stream.terms] for stream in (early, late)]
    squares, early, late = squares_of(dp_size, place, added, class_squares, *last)
    far, squares = together(far, squares)
    for group in pairs([core] + dp):
        squares = sum_of([squares] + [places.swap(squares, steps) for steps in subsets(group)])
    grad_tokens = token_grad(tokens, vectors, own[0], near, far, d_mixed)
    grads = []
    for value in (early, late):
        grads += [value, places.swap(value, [core])]
    norm, *updated = optimizer(
        both_places, squares, [*grads, added], class_share, staged,
        [vectors_columns, vectors_moment1, vectors_moment2, vectors_ema],
        [talking, talking_moment1, talking_moment2, talking_ema],
    )
    return (patch_out, class_out, grad_tokens, grad_class, norm.reshape(()), *updated)


def solution(mesh):
    tokens = P(("dp", "seq"), None)
    by_group = P("dp", None)
    mats = P(None, None, "dp", None)
    vecs = P(None, "dp")
    body = functools.partial(on_device, mesh.shape["dp"], mesh.shape["seq"])
    return jax.shard_map(
        body,
        mesh=mesh,
        in_specs=(tokens, by_group, tokens, by_group, by_group, P(), mats, mats, mats,
                  P(), vecs, vecs, vecs, P(), P(), P(), P()),
        out_specs=(tokens, by_group, tokens, by_group, P(), mats, mats, mats, mats,
                   vecs, vecs, vecs, vecs, P(), P(), P(), P()),
        check_vma=False,
    )
```

```python
import functools

import jax
import jax.numpy as jnp
from jax import lax
from jax.experimental import pallas as pl
from jax.experimental.pallas import tpu as pltpu
from jax.sharding import PartitionSpec as P

STEP = 10
EPS_NORM = 1e-06
MASKED = -1e30
LR_MATRIX = 0.05
LR_VECTOR = 0.1
LR_TALKING = 0.2
BETA_ONE = 0.9
BETA_TWO = 0.999
ADAM_EPS = 1e-08
WEIGHT_DECAY = 0.05
EMA_RATE = 0.9
CLIP_NORM = 1.0
F32 = jnp.float32
BF16 = jnp.bfloat16
NN = (((1,), (0,)), ((), ()))
NT = (((1,), (1,)), ((), ()))
TN = (((0,), (0,)), ((), ()))
KERNEL_MIB, NEAR_MIB, SMALL_MIB = 58, 52, 24


def split(value):
    high = value.astype(BF16)
    return high, (value - high.astype(F32)).astype(BF16)


def mm(left, right, dims=NN):
    return lax.dot_general(left, right, dims, preferred_element_type=F32)


def mm3(left, right, dims=NN):
    return mm(left[0], right[0], dims) + (mm(left[0], right[1], dims) + mm(left[1], right[0], dims))


def mm3_tall(left, right, dims=NN):
    rows = left[0].shape[0]
    stacked = jnp.concatenate([part.astype(F32) for part in left], axis=0).astype(BF16)
    both = mm(stacked, right[0], dims)
    return both[:rows] + (both[rows:] + mm(left[0], right[1], dims))


def dot_tall(left, right, dims=NN):
    return mm3_tall(split(left), split(right), dims)


def dot3(left, right, dims=NN):
    return mm3(split(left), split(right), dims)


def norm_rows(values):
    average = jnp.mean(values, axis=-1, keepdims=True)
    centered = values - average
    variance = jnp.mean(centered * centered, axis=-1, keepdims=True)
    scale = lax.rsqrt(variance + EPS_NORM)
    return centered * scale, scale


def norm_back(grad, unit, scale):
    inner = jnp.mean(grad * unit, axis=-1, keepdims=True)
    return scale * (grad - jnp.mean(grad, axis=-1, keepdims=True) - unit * inner)


def gelu_both(values):
    half = 0.5 * (1.0 + lax.erf(values * 0.7071067811865476))
    slope = half + values * (0.3989422804014327 * jnp.exp(-0.5 * values * values))
    return values * half, slope


def row_sum(values):
    return jnp.sum(values, axis=0, keepdims=True)


def tail_forward(dot, inputs, attended, w_out, w_up, w_down, vecs):
    projected = dot(attended, w_out) + vecs[4:5]
    mixed = inputs + vecs[5:6] * projected
    unit, _ = norm_rows(mixed)
    normed = unit * vecs[6:7] + vecs[7:8]
    up_bias = jnp.concatenate([vecs[row : row + 1] for row in range(8, 12)], axis=1)
    hidden, slope = gelu_both(dot(normed, w_up) + up_bias)
    lowered = dot(hidden, w_down, NT) + vecs[12:13]
    return mixed + vecs[13:14] * lowered, (projected, mixed, hidden, slope, lowered)


def tail_backward(dot, cot, kept, w_out, w_up, w_down, vecs):
    projected, mixed, hidden, slope, lowered = kept
    width = cot.shape[1]
    unit, scale = norm_rows(mixed)
    normed = unit * vecs[6:7] + vecs[7:8]
    d_lowered = cot * vecs[13:14]
    d_hidden = dot(d_lowered, w_down) * slope
    d_normed = dot(d_hidden, w_up, NT)
    d_mixed = cot + norm_back(d_normed * vecs[6:7], unit, scale)
    d_projected = d_mixed * vecs[5:6]
    d_attended = dot(d_projected, w_out, NT)
    d_up = row_sum(d_hidden)
    rows = [
        row_sum(d_projected), row_sum(d_mixed * projected), row_sum(d_normed * unit), row_sum(d_normed),
        *[d_up[:, i * width : (i + 1) * width] for i in range(4)],
        row_sum(d_lowered), row_sum(cot * lowered),
    ]
    return d_mixed, d_attended, d_projected, d_hidden, d_lowered, normed, rows


def image_of(lengths_ref, images, positions):
    end = lengths_ref[0, 0]
    inside = (positions >= end).astype(jnp.int32)
    for image in range(1, images):
        end = end + lengths_ref[0, image]
        inside = inside + (positions >= end).astype(jnp.int32)
    return inside


def same_image(lengths_ref, images, place, slots, rows):
    queries = place * rows + lax.broadcasted_iota(jnp.int32, (1, rows), 1)
    query_image = image_of(lengths_ref, images, queries)
    parts = []
    for slot in range(slots):
        keys = jnp.bitwise_xor(place, slot) * rows + lax.broadcasted_iota(jnp.int32, (rows, 1), 0)
        parts.append(image_of(lengths_ref, images, keys) == query_image)
    return parts


def column_of(table, number):
    lanes = lax.broadcasted_iota(jnp.int32, (1, table.shape[1]), 1)
    return jnp.sum(jnp.where(lanes == number, table, 0.0), axis=1, keepdims=True)


def head_mask(heads, width):
    row = lax.broadcasted_iota(jnp.int32, (heads, width), 0)
    return jnp.where(lax.broadcasted_iota(jnp.int32, (heads, width), 1) // (width // heads) == row, 1.0, 0.0)


def spread(value, mask):
    return jnp.concatenate([value[i : i + 1] * mask for i in range(value.shape[0])], axis=0)


def repeat_rows(value, heads):
    shape = (heads, value.shape[1])
    return jnp.concatenate(
        [jnp.broadcast_to(value[i : i + 1], shape) for i in range(value.shape[0])], axis=0
    )


def fold_heads(value, mask):
    heads = mask.shape[0]
    return jnp.concatenate(
        [row_sum(value[i : i + heads] * mask) for i in range(0, value.shape[0], heads)], axis=0
    )


def head_sums(value, mask):
    return jnp.sum(spread(value, mask), axis=1, keepdims=True)


def rows_of(value, heads):
    return jnp.concatenate(
        [row_sum(value[i : i + heads]) for i in range(0, value.shape[0], heads)], axis=0
    )


def wide(column):
    return jnp.broadcast_to(column, (column.shape[0], 128))


def whole(shape):
    return pl.BlockSpec(shape, lambda *_: (0,) * len(shape))


def struct(shape, dtype=F32):
    return jax.ShapeDtypeStruct(shape, dtype)


def far_struct(shape, dtype=F32):
    return pltpu.HBM(shape, dtype)


def smem():
    return pl.BlockSpec(memory_space=pltpu.SMEM)


def anywhere():
    return pl.BlockSpec(memory_space=pl.ANY)


def weight_block(block, matrix, shape, columns=None):
    return pl.BlockSpec((None, None, shape[2], columns or shape[3]), lambda *_: (block, matrix, 0, 0))


def far_off(*operands):
    return [pltpu.with_memory_space_constraint(operand, pltpu.HBM) for operand in operands]


def copy_in(pairs, arrived):
    copies = [pltpu.make_async_copy(a, b, arrived.at[i]) for i, (a, b) in enumerate(pairs)]
    for copy in copies:
        copy.start()
    return copies


def limit(mebibytes):
    return pltpu.CompilerParams(vmem_limit_bytes=mebibytes << 20)


def prepare_kernel(
    own_ref, near_ref, class_ref, w_self_ref, w_class_ref, vecs_ref, talk_ref,
    normed_ref, query_c_ref, value_c_ref, key_rows_ref, score_ref, t1_ref, t2_ref, t1_rows_ref, t2_rows_ref,
    query_ref, k_high, k_low, v_high, v_low, kt_high, kt_low, vt_high, vt_low,
):
    rows, width = own_ref.shape
    heads = talk_ref.shape[0]
    size = width // heads
    scale = size ** (-0.5)
    vecs = vecs_ref[...]
    w_q, w_kv = split(w_self_ref[:, :width]), split(w_self_ref[:, width:])
    tokens = jnp.concatenate([own_ref[...], near_ref[...]], axis=0)
    unit, _ = norm_rows(tokens)
    normed = split(unit * vecs[0:1] + vecs[1:2])
    query_ref[...] = (mm3((normed[0][:rows], normed[1][:rows]), w_q) + vecs[2:3]) * scale
    both = mm3(normed, w_kv)
    keys, values = both[:, :width], both[:, width:] + vecs[3:4]
    k_high[...], k_low[...] = split(keys)
    v_high[...], v_low[...] = split(values)
    kt_high[...], kt_low[...] = split(keys.T)
    vt_high[...], vt_low[...] = split(values.T)
    mask = head_mask(heads, width)
    unit, _ = norm_rows(class_ref[...])
    normed = unit * vecs[14:15] + vecs[15:16]
    both = dot_tall(normed, w_class_ref[...])
    query = both[:, :width] + vecs[16:17]
    normed_ref[...] = normed
    query_c_ref[...] = query
    value_c_ref[...] = both[:, 2 * width :] + vecs[17:18]
    key_rows_ref[...] = dot3(spread(query, mask), w_class_ref[:, width : 2 * width], NT) * scale
    score_ref[...] = wide(head_sums(query * both[:, width : 2 * width], mask) * scale)
    head_of = lax.broadcasted_iota(jnp.int32, (width, 1), 0) // size
    talk = talk_ref[...]
    talk_t = jnp.concatenate([talk, jnp.zeros((heads, 128 - talk.shape[1]), F32)], axis=1).T[: talk.shape[1], :]
    t1 = t2 = t1_rows = t2_rows = 0.0
    for head in range(heads):
        here = head_of == head
        t1 = t1 + jnp.where(here, talk_t[head : head + 1, :], 0.0)
        t2 = t2 + jnp.where(here, talk[head : head + 1, heads:], 0.0)
        t1_rows = t1_rows + mask[head : head + 1] * talk[:, head : head + 1]
        t2_rows = t2_rows + mask[head : head + 1] * talk_t[heads:, head : head + 1]
    t1_ref[...], t2_ref[...], t1_rows_ref[...], t2_rows_ref[...] = t1, t2, t1_rows, t2_rows


def prepare(own, near, class_tokens, matrices, vectors, talking):
    images, width = class_tokens.shape
    rows = own.shape[0]
    heads = talking.shape[0]
    pairs = images * heads
    outs = [far_struct((images, width))] * 3 + [
        far_struct((pairs, width)), far_struct((pairs, 128)),
        far_struct((width, heads)), far_struct((width, heads + 1)),
        far_struct((heads, width)), far_struct((heads + 1, width)),
        far_struct((rows, width)),
    ]
    outs += [far_struct((2 * rows, width), BF16)] * 4 + [far_struct((width, 2 * rows), BF16)] * 4
    own, class_tokens, matrices, vectors, talking = far_off(own, class_tokens, matrices, vectors, talking)
    operands = [own, near, class_tokens, matrices, matrices, vectors, talking]
    specs = [whole(operand.shape) for operand in operands]
    specs[3] = weight_block(0, 0, matrices.shape, 3 * width)
    specs[4] = weight_block(1, 0, matrices.shape, 3 * width)
    return pl.pallas_call(
        prepare_kernel,
        grid=(1,),
        in_specs=specs,
        out_specs=[whole(out.shape) for out in outs],
        out_shape=outs,
        compiler_params=limit(NEAR_MIB),
        cost_estimate=pl.CostEstimate(flops=4 << 30, bytes_accessed=8 << 20, transcendentals=0),
        name="prepare",
    )(*operands)


def forward_kernel(slots, images, unroll, *refs):
    place_ref, lengths_ref = refs[:2]
    token_refs = refs[2 : 1 + slots]
    (
        vecs_ref, t1_ref, t2_ref, key_rows_ref, query_ref,
        k_high0, k_low0, v_high0, v_low0, kt_high0, kt_low0, vt_high0, vt_low0, mats_ref,
        e_high_hbm, e_low_hbm, pv_hbm, inverse_ref, pv_bias_ref, attended_ref,
        kt_high_hbm, kt_low_hbm, v_high_hbm, v_low_hbm,
        patch_ref, projected_ref, mixed_ref, hidden_hbm, slope_hbm, lowered_ref, packed_ref, scores_ref,
        k_three, vt_two, qt, bias, attended_t, w_kv, w_up, w_down, w_out, arrived,
        kt_high, kt_low, v_high, v_low, hidden_ref, slope_ref, e_high_ref, e_low_ref, pv_ref, leaving,
    ) = refs[1 + slots :]
    rows, width = token_refs[0].shape
    step = pl.program_id(0)
    place = place_ref[0]
    ready, columns = pl.ds(0, 2 * rows), lambda i: pl.ds(i * width, width)
    pairs = [
        (mats_ref.at[0, 0, :, pl.ds(width, 2 * width)], w_kv),
        (k_high0, k_three.at[ready, columns(0)]), (k_high0, k_three.at[ready, columns(1)]),
        (k_low0, k_three.at[ready, columns(2)]), (v_high0, v_high.at[ready, :]), (v_low0, v_low.at[ready, :]),
        (kt_high0, kt_high.at[:, ready]), (kt_low0, kt_low.at[:, ready]),
        (vt_high0, vt_two.at[columns(0), ready]), (vt_low0, vt_two.at[columns(1), ready]),
        (mats_ref.at[0, 0, :, pl.ds(3 * width, width)], w_out),
        (mats_ref.at[0, 1], w_up), (mats_ref.at[0, 2], w_down),
    ]
    fetches = [pltpu.make_async_copy(a, b, arrived.at[i]) for i, (a, b) in enumerate(pairs)]
    pairs = [(kt_high, kt_high_hbm), (kt_low, kt_low_hbm), (v_high, v_high_hbm), (v_low, v_low_hbm),
             (hidden_ref, hidden_hbm), (slope_ref, slope_hbm)]
    stores = [pltpu.make_async_copy(a, b, leaving.at[i]) for i, (a, b) in enumerate(pairs)]
    heads = inverse_ref.shape[0]
    groups = []
    for number in range(heads // unroll):
        here = pl.ds(number * unroll, unroll)
        groups.append([
            pltpu.make_async_copy(a.at[here], b.at[here], leaving.at[6 + 3 * number + i])
            for i, (a, b) in enumerate([(e_high_ref, e_high_hbm), (e_low_ref, e_low_hbm), (pv_ref, pv_hbm)])
        ])

    @pl.when(step == 0)
    def _():
        for fetch in fetches:
            fetch.start()
        vecs = vecs_ref[...]
        inside = same_image(lengths_ref, images, place, slots, rows)
        for slot in range(slots):
            bias[pl.ds(slot * rows, rows), :] = jnp.where(inside[slot], 0.0, MASKED)
        units = [norm_rows(ref[...])[0] for ref in token_refs[1:]]
        fetches[0].wait()
        w_both = split(w_kv[...])
        for slot in range(2, slots):
            here = pl.ds(slot * rows, rows)
            normed = split(units[slot - 2] * vecs[0:1] + vecs[1:2])
            both = mm3(normed, w_both)
            keys, values = both[:, :width], both[:, width:] + vecs[3:4]
            high, low = split(keys)
            k_three[here, :] = jnp.concatenate([high, high, low], axis=1)
            v_high[here, :], v_low[here, :] = split(values)
            kt_high[:, here], kt_low[:, here] = split(keys.T)
            vt_two[:, here] = jnp.concatenate(split(values.T), axis=0)
        qt[...] = query_ref[...].T
        attended_t[...] = jnp.zeros_like(attended_t)
        for fetch in fetches[1:10]:
            fetch.wait()
        for store in stores[:4]:
            store.start()

    scores = []
    for u in range(unroll):
        high, low = split(qt[...] * column_of(t1_ref[...], step * unroll + u))
        scores.append(mm(k_three[...], jnp.concatenate([high, low, high], axis=0)) + bias[...])
    for u in range(unroll):
        exponentials = jnp.exp(scores[u] - jnp.max(scores[u], axis=0, keepdims=True))
        inverse = 1.0 / jnp.sum(exponentials, axis=0, keepdims=True)
        pair = split(exponentials)
        head = step * unroll + u
        e_high_ref[head], e_low_ref[head] = pair
        inverse_ref[head] = inverse
        both = mm(vt_two[...], pair[0])
        values = (both[:width] + (both[width:] + mm(vt_two[:width, :], pair[1]))) * inverse
        pv_ref[head] = values
        attended_t[...] += values * column_of(t2_ref[...], head)
    for number, group in enumerate(groups):

        @pl.when(step == number)
        def _(group=group):
            for copy in group:
                copy.start()

    @pl.when(step == pl.num_programs(0) - 1)
    def _():
        inside = jnp.where(bias[...] < 0.0, 0.0, 1.0).astype(BF16)
        both = mm(vt_two[...], inside)
        summed = both[:width] + both[width:]
        pv_bias_ref[...] = summed
        attended = (attended_t[...] + summed * t2_ref[:, 8:9]).T
        attended_ref[...] = attended
        for fetch in fetches[10:]:
            fetch.wait()
        vecs = vecs_ref[...]
        patch, kept = tail_forward(
            dot3, token_refs[0][...], attended, w_out[...], w_up[...], w_down[...], vecs
        )
        patch_ref[...] = patch
        for ref, value in zip((projected_ref, mixed_ref, hidden_ref, slope_ref, lowered_ref), kept):
            ref[...] = value
        for store in stores[4:]:
            store.start()
        unit, _ = norm_rows(patch)
        normed = split(unit * vecs[14:15] + vecs[15:16])
        pairs = images * 8
        image = lax.broadcasted_iota(jnp.int32, (pairs, 1), 0) // 8
        positions = place * rows + lax.broadcasted_iota(jnp.int32, (1, rows), 1)
        belong = image_of(lengths_ref, images, positions) == image
        class_scores = mm3(split(key_rows_ref[...]), normed, NT)
        class_scores = jnp.where(belong, class_scores, MASKED)
        scores_ref[...] = class_scores
        top = jnp.max(class_scores, axis=1, keepdims=True)
        weights = jnp.where(belong, jnp.exp(class_scores - top), 0.0)
        packed_ref[:, :width] = mm3(split(weights), normed)
        lane = lax.broadcasted_iota(jnp.int32, (1, 128), 1)
        total = jnp.sum(weights, axis=1, keepdims=True)
        packed_ref[:, width:] = jnp.where(lane < 64, top, total)
        for store in stores + [copy for group in groups for copy in group]:
            store.wait()


def by_head(unroll, shape):
    return pl.BlockSpec((unroll,) + shape[1:], lambda g: (g, 0, 0))


def forward(place, lengths, token_slots, matrices, vectors, t1, t2, key_rows, projected):
    slots, (rows, width) = len(token_slots), token_slots[0].shape
    total, heads = slots * rows, 8
    unroll = 4 if total <= 1024 else 1
    hidden = matrices.shape[3]
    pairs = key_rows.shape[0]
    outs = [
        far_struct((heads, total, rows), BF16), far_struct((heads, total, rows), BF16), far_struct((heads, width, rows)),
        far_struct((heads, 1, rows)), far_struct((width, rows)), far_struct((rows, width)),
        far_struct((width, total), BF16), far_struct((width, total), BF16),
        far_struct((total, width), BF16), far_struct((total, width), BF16),
        far_struct((rows, width)), far_struct((rows, width)), far_struct((rows, width)),
        far_struct((rows, hidden)), far_struct((rows, hidden)), far_struct((rows, width)),
        far_struct((pairs, width + 128)), far_struct((pairs, rows)),
    ]
    away = (0, 1, 2, 6, 7, 8, 9, 13, 14)
    out_specs = [anywhere() if i in away else whole(out.shape) for i, out in enumerate(outs)]
    operands = [token_slots[0], *token_slots[2:], *far_off(vectors, t1, t2, key_rows, *projected, matrices)]
    in_specs = [whole(operand.shape) for operand in operands]
    in_specs[-9:] = [anywhere()] * 9
    flops = 2 * 3 * ((2 * heads + 1) * total + 9 * width) * rows * width
    return pl.pallas_call(
        functools.partial(forward_kernel, slots, lengths.shape[1], unroll),
        grid=(heads // unroll,),
        in_specs=[smem(), smem()] + in_specs,
        out_specs=out_specs,
        out_shape=outs,
        scratch_shapes=[
            pltpu.VMEM((total, 3 * width), BF16),
            pltpu.VMEM((2 * width, total), BF16),
            pltpu.VMEM((width, rows), F32),
            pltpu.VMEM((total, rows), F32),
            pltpu.VMEM((width, rows), F32),
            pltpu.VMEM((width, 2 * width), F32),
            pltpu.VMEM((width, hidden), F32),
            pltpu.VMEM((width, hidden), F32),
            pltpu.VMEM((width, width), F32),
            pltpu.SemaphoreType.DMA((13,)),
            pltpu.VMEM((width, total), BF16),
            pltpu.VMEM((width, total), BF16),
            pltpu.VMEM((total, width), BF16),
            pltpu.VMEM((total, width), BF16),
            pltpu.VMEM((rows, hidden), F32),
            pltpu.VMEM((rows, hidden), F32),
            pltpu.VMEM((heads, total, rows), BF16),
            pltpu.VMEM((heads, total, rows), BF16),
            pltpu.VMEM((heads, width, rows), F32),
            pltpu.SemaphoreType.DMA((6 + 3 * heads // unroll,)),
        ],
        compiler_params=limit(NEAR_MIB if total <= 1024 else KERNEL_MIB),
        cost_estimate=pl.CostEstimate(
            flops=flops, bytes_accessed=24 << 20, transcendentals=heads * total * rows
        ),
        name="forward",
    )(place, lengths, *operands)


def class_stage_kernel(place_ref, mats_ref, last_out, up_out, down_out, first_out, arrived):
    width = first_out.shape[1]
    pairs = [(mats_ref.at[1, 0, :, pl.ds(width, width)], last_out), (mats_ref.at[1, 1], up_out),
             (mats_ref.at[1, 2], down_out), (mats_ref.at[1, 0, :, pl.ds(0, width)], first_out)]
    for copy in copy_in(pairs, arrived):
        copy.wait()


def class_stage(place, matrices):
    rows, columns = matrices.shape[2:]
    half, whole_matrix = (rows, columns // 2), (rows, columns)
    return pl.pallas_call(
        class_stage_kernel,
        in_specs=[smem(), anywhere()],
        out_specs=[pl.BlockSpec(memory_space=pltpu.VMEM)] * 4,
        out_shape=[pltpu.VMEM(shape, F32) for shape in (half, whole_matrix, whole_matrix, half)],
        scratch_shapes=[pltpu.SemaphoreType.DMA((4,))],
        compiler_params=limit(8),
        cost_estimate=pl.CostEstimate(flops=1, bytes_accessed=1, transcendentals=0),
        name="class_stage",
    )(place, *far_off(matrices))


def middle_kernel(images, slots, *refs):
    place_ref = refs[0]
    parts = [ref[...] for ref in refs[1 : 1 + slots]]
    (
        vecs_ref, normed_c_ref, query_c_ref, value_c_ref, key_rows_ref, own_ref,
        class_ref, cot_class_ref, cot_patch_ref, patch_ref, scores_ref, wc0, wc1, wc2,
        attended_hbm, projected_hbm, mixed_hbm, hidden_hbm, slope_hbm, lowered_hbm, mats_ref,
        class_out_ref, d_attended_ref, d_mixed_ref, keep_ref, send_ref, partial_ref,
        factors_ref, vec_rows_ref, class_terms_ref,
        ws0, ws1, ws2, attended_ref, projected_ref, mixed_ref, hidden_ref, slope_ref, lowered_ref,
        keep, send, arrived, stored,
    ) = refs[1 + slots :]
    width = class_ref.shape[1]
    heads = 8
    size = width // heads
    copies = copy_in(
        [(lowered_hbm, lowered_ref), (hidden_hbm, hidden_ref), (mats_ref.at[0, 2], ws2), (slope_hbm, slope_ref),
         (mixed_hbm, mixed_ref), (mats_ref.at[0, 1], ws1), (projected_hbm, projected_ref),
         (attended_hbm, attended_ref), (mats_ref.at[0, 0, :, pl.ds(3 * width, width)], ws0)], arrived)
    vecs = vecs_ref[...]
    vecs_s, vecs_c = vecs[:14], vecs[14:]
    mask = head_mask(heads, width)
    first = jnp.where(place_ref[0] == 0, 1.0, 0.0)
    own_score = own_ref[:, :1]
    normed_c = normed_c_ref[...]
    normed_rep = repeat_rows(normed_c, heads)
    top = own_score
    for part in parts:
        top = jnp.maximum(top, part[:, width : width + 1])
    own_weight = jnp.exp(own_score - top)
    total, summed = own_weight, own_weight * normed_rep
    for part in parts:
        rescale = jnp.exp(part[:, width : width + 1] - top)
        total = total + part[:, width + 64 : width + 65] * rescale
        summed = summed + part[:, :width] * rescale
    value_rows = summed / total
    own_prob = own_weight / total
    unit_p, scale_p = norm_rows(patch_ref[...])
    normed_p = split(unit_p * vecs_c[0:1] + vecs_c[1:2])
    scores = scores_ref[...]
    probs = jnp.where(scores > 0.5 * MASKED, jnp.exp(scores - top) * (1.0 / total), 0.0)
    w_v = split(wc0[:, :width])
    class_attended = fold_heads(mm3_tall(split(value_rows), w_v), mask) + vecs_c[3:4]
    w_out_c = wc0[:, width:]
    class_out, kept_c = tail_forward(
        dot_tall, class_ref[...], class_attended, w_out_c, wc1[...], wc2[...], vecs_c
    )
    class_out_ref[...] = class_out
    d_mixed_c, d_attended_c, d_projected_c, d_hidden_c, d_lowered_c, normed2_c, tail_rows_c = (
        tail_backward(dot_tall, cot_class_ref[...], kept_c, w_out_c, wc1[...], wc2[...], vecs_c)
    )
    for copy in copies:
        copy.wait()
    delta = head_sums(d_attended_c * class_attended, mask)
    cot_rows = mm3_tall(split(spread(d_attended_c, mask)), w_v, NT)
    cot_const = head_sums(d_attended_c * vecs_c[3:4], mask)
    cot_split = split(cot_rows)
    d_scores = probs * (mm3_tall(cot_split, normed_p, NT) + cot_const - delta)
    d_own = own_prob * (head_sums(d_attended_c * value_c_ref[...], mask) - delta)
    key_rows = key_rows_ref[...]
    d_split = split(d_scores)
    d_normed_p = mm3(d_split, split(key_rows), TN) + mm3(split(probs), cot_split, TN)
    partial_ref[...] = mm3_tall(d_split, normed_p)
    cot = cot_patch_ref[...] + norm_back(d_normed_p * vecs_c[0:1], unit_p, scale_p)
    class_terms_ref[...] = jnp.concatenate(
        [rows_of(d_own * key_rows + own_prob * cot_rows, heads), d_mixed_c], axis=0
    )
    query_c = query_c_ref[...]
    chunks = lambda value: [value[:, i * width : (i + 1) * width] for i in range(4)]
    factors_ref[...] = jnp.concatenate(
        [normed_c, class_attended, normed2_c, d_lowered_c, d_own * normed_rep, value_rows,
         jnp.zeros_like(query_c), query_c * size ** (-0.5), d_attended_c, d_projected_c,
         *chunks(d_hidden_c), *chunks(kept_c[2])], axis=0)
    projected, mixed, hidden, lowered = projected_ref[...], mixed_ref[...], split(hidden_ref[...]), lowered_ref[...]
    unit, scale = norm_rows(mixed)
    normed = split(unit * vecs_s[6:7] + vecs_s[7:8])
    d_lowered = cot * vecs_s[13:14]
    d_low_split = split(d_lowered)
    d_hidden = mm3(d_low_split, split(ws2[...])) * slope_ref[...]
    d_hid_split = split(d_hidden)
    g_down = mm3(d_low_split, hidden, TN)
    g_up = mm3(normed, d_hid_split, TN)
    even = jnp.bitwise_and(place_ref[0], 1) == 0
    size_up = g_up.shape[1]
    send[:, :size_up] = jnp.where(even, g_down, g_up)
    keep[:, :size_up] = jnp.where(even, g_up, g_down)
    bulk = pl.ds(0, size_up)
    leaving = copy_in(
        [(send.at[:, bulk], send_ref.at[:, bulk]), (keep.at[:, bulk], keep_ref.at[:, bulk])], stored
    )
    d_normed = mm3(d_hid_split, split(ws1[...]), NT)
    d_mixed = cot + norm_back(d_normed * vecs_s[6:7], unit, scale)
    d_projected = d_mixed * vecs_s[5:6]
    d_proj_split = split(d_projected)
    g_out = mm3(split(attended_ref[...]), d_proj_split, TN)
    left = g_out[:, :256]
    right = jnp.concatenate([g_out[:, 256:], jnp.zeros((width, 512 - width), F32)], axis=1)
    send[:, size_up:] = jnp.where(even, right, left)
    keep[:, size_up:] = jnp.where(even, left, right)
    rest = pl.ds(size_up, 256)
    for i, (a, b) in enumerate([(send, send_ref), (keep, keep_ref)]):
        leaving.append(pltpu.make_async_copy(a.at[:, rest], b.at[:, rest], stored.at[2 + i]))
        leaving[-1].start()
    d_mixed_ref[...] = d_mixed
    d_attended_ref[...] = mm3(d_proj_split, split(ws0[...]), NT)
    d_up = row_sum(d_hidden)
    tail_rows = [
        row_sum(d_projected), row_sum(d_mixed * projected), row_sum(d_normed * unit), row_sum(d_normed),
        *[d_up[:, i * width : (i + 1) * width] for i in range(4)],
        row_sum(d_lowered), row_sum(cot * lowered),
    ]
    zero = jnp.zeros((1, width), F32)
    vec_rows_ref[...] = jnp.concatenate(
        [zero] * 4 + tail_rows
        + [row_sum(d_normed_p * unit_p), row_sum(d_normed_p), zero, row_sum(d_attended_c) * first]
        + [row * first for row in tail_rows_c], axis=0)
    for copy in leaving:
        copy.wait()


def middle(
    place, parts, vectors, prepared, class_tokens, cot_class, cot_patch, patch, scores, staged, kept, matrices
):
    images, width = class_tokens.shape
    rows = cot_patch.shape[0]
    hidden = matrices.shape[3]
    pairs = parts[0].shape[0]
    rest = [vectors, *prepared, class_tokens, cot_class, cot_patch, patch, scores]
    operands = [*parts, *far_off(*rest), *staged, *far_off(*kept, matrices)]
    outs = [
        far_struct((images, width)), far_struct((rows, width)), far_struct((rows, width)),
        far_struct((width, hidden + 256)), far_struct((width, hidden + 256)), far_struct((pairs, width)),
        far_struct((16 * images + 2 * pairs, width)), far_struct((28, width)), far_struct((2 * images, width)),
    ]
    vmem = pl.BlockSpec(memory_space=pltpu.VMEM)
    in_specs = [vmem] * len(operands)
    in_specs[-1 - len(kept) :] = [anywhere()] * (1 + len(kept))
    out_specs = [vmem] * len(outs)
    out_specs[3:5] = [anywhere()] * 2
    return pl.pallas_call(
        functools.partial(middle_kernel, images, len(parts)),
        in_specs=[smem()] + in_specs,
        out_specs=out_specs,
        out_shape=outs,
        scratch_shapes=[pltpu.VMEM((width, width), F32)]
        + [pltpu.VMEM((width, hidden), F32)] * 2
        + [pltpu.VMEM(value.shape, F32) for value in kept]
        + [pltpu.VMEM((width, hidden + 256), F32)] * 2
        + [pltpu.SemaphoreType.DMA((9,)), pltpu.SemaphoreType.DMA((4,))],
        compiler_params=limit(44),
        cost_estimate=pl.CostEstimate(flops=8 << 30, bytes_accessed=28 << 20, transcendentals=1 << 19),
        name="middle",
    )(place, *operands)


def class_kernel(slots, *refs):
    partial_refs = refs[:slots]
    terms_ref, class_ref, vecs_ref, w_ref, factors_ref, grad_ref, factors_out_ref = refs[slots:]
    images, width = class_ref.shape
    pairs = partial_refs[0].shape[0]
    heads = pairs // images
    mask = head_mask(heads, width)
    at = 4 * images
    query_rows = sum_of([factors_ref[at : at + pairs, :]] + [ref[...] for ref in partial_refs])
    w_k, w_q = w_ref[:, width : 2 * width], w_ref[:, :width]
    d_query = fold_heads(dot_tall(query_rows, w_k), mask) * (width // heads) ** (-0.5)
    d_normed = dot_tall(d_query, w_q, NT) + terms_ref[:images, :]
    unit, scale = norm_rows(class_ref[...])
    grad_ref[...] = terms_ref[images:, :] + norm_back(d_normed * vecs_ref[14:15, :], unit, scale)
    count = factors_ref.shape[0]
    factors_out_ref[:count, :] = factors_ref[...]
    factors_out_ref[at : at + pairs, :] = query_rows
    at = at + 2 * pairs
    factors_out_ref[at : at + images, :] = d_query
    added = [row_sum(d_normed * unit), row_sum(d_normed), row_sum(d_query), jnp.zeros((5, width), F32)]
    factors_out_ref[count:, :] = jnp.concatenate(added, axis=0)


def class_finish(partials, terms, class_tokens, vectors, w_first, factors):
    operands = [*far_off(partials[0]), *partials[1:], *far_off(terms, class_tokens, vectors), w_first]
    operands += far_off(factors)
    vmem = pl.BlockSpec(memory_space=pltpu.VMEM)
    outs = [struct(class_tokens.shape), struct((factors.shape[0] + 8, factors.shape[1]))]
    return pl.pallas_call(
        functools.partial(class_kernel, len(partials)),
        in_specs=[vmem] * len(operands),
        out_specs=[vmem] * len(outs),
        out_shape=outs,
        compiler_params=limit(12),
        cost_estimate=pl.CostEstimate(flops=1, bytes_accessed=1, transcendentals=0),
        name="class_finish",
    )(*operands)


def class_weights_kernel(images, mine_ref, factors_ref, grads_ref, squares_ref, small_ref):
    groups, count, width = factors_ref.shape
    heads = 8
    pairs = images * heads
    mask = head_mask(heads, width)
    at = 4 * images + 2 * pairs

    def rows(ref, begin, count=images):
        return jnp.concatenate([ref[g, begin : begin + count, :] for g in range(groups)], axis=0)

    def chunked(begin):
        return jnp.concatenate([rows(factors_ref, begin + i * images) for i in range(4)], axis=1)

    def headed(left, right):
        return dot3(rows(mine_ref, left, pairs), spread(rows(factors_ref, right), mask), TN)

    grads_ref[0, :, :width] = dot3(rows(mine_ref, 0), rows(factors_ref, at), TN)
    grads_ref[0, :, width : 2 * width] = headed(4 * images, at + images)
    grads_ref[0, :, 2 * width : 3 * width] = headed(4 * images + pairs, at + 2 * images)
    grads_ref[0, :, 3 * width :] = dot3(rows(mine_ref, images), rows(factors_ref, at + 3 * images), TN)
    grads_ref[1] = dot3(rows(mine_ref, 2 * images), chunked(at + 4 * images), TN)
    grads_ref[2] = dot3(rows(mine_ref, 3 * images), chunked(at + 8 * images), TN)
    grads = grads_ref[...]
    squares_ref[...] = jnp.broadcast_to(jnp.sum(grads * grads), squares_ref.shape)
    added = sum_of([mine_ref[g, count - 8 :, :] for g in range(groups)])
    lanes = 128 - 22
    share = added.shape[1]
    added = jnp.concatenate([jnp.zeros((14, share), F32), added, jnp.zeros((lanes, share), F32)], axis=0)
    small_ref[...] = added.T


def class_weights(images, mine, factors):
    share = mine.shape[2]
    outs = [struct((3, share, 4 * factors.shape[2])), struct((8, 128)), struct((share, 128))]
    return pl.pallas_call(
        functools.partial(class_weights_kernel, images),
        grid=(1,),
        in_specs=[whole(mine.shape), whole(factors.shape)],
        out_specs=[whole(out.shape) for out in outs],
        out_shape=outs,
        compiler_params=limit(SMALL_MIB),
        cost_estimate=pl.CostEstimate(flops=1 << 29, bytes_accessed=3 << 20, transcendentals=0),
        name="class_weights",
    )(mine, factors)


def mm3_wide(left, right):
    width = right[0].shape[1]
    both = mm(left[0], jnp.concatenate(right, axis=1))
    return both[:, :width] + (both[:, width:] + mm(left[1], right[0]))


def backward_kernel(slots, images, dp_size, unroll, *refs):
    place_ref, lengths_ref = refs[:2]
    token_hbm = refs[2 : 2 + slots]
    (
        e_high_ref, e_low_ref, pv_ref, inverse_ref, pv_bias_ref, cot_ref,
        kt_high, kt_low, v_high, v_low, query_ref, t1_ref, t2_ref, t1_rows, t2_rows,
        vec_rows_ref, vecs_ref, mats_ref,
    ) = refs[2 + slots : 20 + slots]
    (
        even_ref, odd_ref, keep_ref, send_ref,
        d_keys, d_values, c1, c2, cot_t, qt, d_qt, v_three, w_ref, tokens, arrived,
    ) = refs[20 + slots :]
    rows, width = cot_ref.shape
    step = pl.program_id(0)
    size = width // 8
    lanes = lax.broadcasted_iota(jnp.int32, (1, 128), 1)
    pairs = [(mats_ref.at[0, 0, :, pl.ds(0, 3 * width)], w_ref)]
    pairs += [(ref, tokens.at[i]) for i, ref in enumerate(token_hbm)]
    copies = [pltpu.make_async_copy(a, b, arrived.at[i]) for i, (a, b) in enumerate(pairs)]

    @pl.when(step == 0)
    def _():
        for copy in copies:
            copy.start()
        cot_t[...] = cot_ref[...].T
        qt[...] = query_ref[...].T
        d_qt[...] = jnp.zeros_like(d_qt)
        d_keys[...] = jnp.zeros_like(d_keys)
        c1[...] = jnp.zeros_like(c1)
        v_three[...] = jnp.concatenate([v_high[...], v_high[...], v_low[...]], axis=1)
        c2[...] = jnp.where(
            lanes == 8, jnp.sum(cot_t[...] * pv_bias_ref[...], axis=1, keepdims=True), 0.0
        )
        inside = jnp.concatenate(same_image(lengths_ref, images, place_ref[0], slots, rows), axis=0)
        inside = jnp.where(inside, 1.0, 0.0).astype(BF16)
        high, low = split(cot_ref[...] * t2_rows[8:9, :])
        d_values[...] = mm(inside, high) + mm(inside, low)

    found = []
    for u in range(unroll):
        head = step * unroll + u
        t2_column, inverse = column_of(t2_ref[...], head), inverse_ref[u]
        crossed = cot_t[...] * pv_ref[u]
        c2[...] += jnp.where(lanes == head, jnp.sum(crossed, axis=1, keepdims=True), 0.0)
        delta = jnp.sum(crossed * t2_column, axis=0, keepdims=True) * inverse
        high, low = split(cot_t[...] * (t2_column * inverse))
        found.append((mm(v_three[...], jnp.concatenate([high, low, high], axis=0)), delta))
    for u in range(unroll):
        head = step * unroll + u
        d_probs, delta = found[u]
        pair = (e_high_ref[u], e_low_ref[u])
        d_mixed = split((pair[0].astype(F32) + pair[1].astype(F32)) * (d_probs - delta))
        inverse_rows = jnp.broadcast_to(inverse_ref[u], (8, rows)).T[:, :1]
        cot = split(cot_ref[...] * inverse_rows * t2_rows[pl.ds(head, 1), :])
        d_values[...] += mm3_wide(pair, cot)
        d_keys[...] += mm3_wide(d_mixed, split(query_ref[...] * t1_rows[pl.ds(head, 1), :]))
        back = mm3((kt_high[...], kt_low[...]), d_mixed)
        d_qt[...] += back * column_of(t1_ref[...], head)
        c1[...] += jnp.where(lanes == head, jnp.sum(back * qt[...], axis=1, keepdims=True), 0.0)

    @pl.when(step == pl.num_programs(0) - 1)
    def _():
        for copy in copies:
            copy.wait()
        d_query = d_qt[...].T * size ** (-0.5)
        w_q, w_kv = split(w_ref[:, :width]), split(w_ref[:, width:])
        gain = shift = g_kv = 0.0
        for slot in range(slots):
            here = pl.ds(slot * rows, rows)
            unit, _ = norm_rows(tokens[slot])
            normed = split(unit * vecs_ref[0:1, :] + vecs_ref[1:2, :])
            d_kv = split(jnp.concatenate([d_keys[here, :], d_values[here, :]], axis=1))
            piece = mm3(d_kv, w_kv, NT)
            if slot == 0:
                dq = split(d_query)
                piece = piece + mm3(dq, w_q, NT)
                g_q = mm3(normed, dq, TN)
            (odd_ref if slot % 2 else even_ref)[slot // 2] = piece
            gain, shift = gain + row_sum(piece * unit), shift + row_sum(piece)
            g_kv = g_kv + mm3(normed, d_kv, TN)
        g_k, g_v = g_kv[:, :width], g_kv[:, width:]
        added = jnp.concatenate(
            [gain, shift, row_sum(d_query), row_sum(d_values[...]), jnp.zeros((4, width), F32)], axis=0
        )
        vec_rows = jnp.concatenate([vec_rows_ref[0:8, :] + added, vec_rows_ref[8:28, :]], axis=0)
        fold = lambda value: jnp.concatenate(
            [row_sum(value[i * size : (i + 1) * size]) for i in range(8)], axis=0
        )
        pre, post = fold(c1[...]).T[:8, :], fold(c2[...])
        count = vec_rows.shape[0]
        talk = jnp.concatenate([pre, post[:, :9], jnp.zeros((8, 128 - count - 17), F32)], axis=1)
        block = width // dp_size
        talk = jnp.concatenate([talk, jnp.zeros((block - 8, 128 - count), F32)], axis=0)
        talk = jnp.concatenate([talk] * dp_size, axis=0)
        small = jnp.concatenate([vec_rows.T, talk], axis=1)
        even = jnp.bitwise_and(place_ref[0], 1) == 0
        left = jnp.concatenate([g_q, g_k[:, :256]], axis=1)
        right = jnp.concatenate([g_k[:, 256:], g_v, small], axis=1)
        keep_ref[...] = jnp.where(even, left, right)
        send_ref[...] = jnp.where(even, right, left)


def backward(dp_size, place, lengths, token_slots, found, cot, keys_values, query, tables,
             vec_rows, vectors, matrices):
    rows, width = cot.shape
    heads, total, _ = found[0].shape
    slots, unroll = total // rows, 2 if total <= 1024 else 1
    operands = far_off(*token_slots, *found, cot, *keys_values, query, *tables, vec_rows, vectors, matrices)
    specs = [whole(operand.shape) for operand in operands]
    specs[:slots] = [anywhere()] * slots
    specs[slots : slots + 4] = [by_head(unroll, operand.shape) for operand in found[:4]]
    specs[-1] = anywhere()
    outs = [far_struct((slots // 2, rows, width))] * 2 + [far_struct((width, 640))] * 2
    return pl.pallas_call(
        functools.partial(backward_kernel, slots, lengths.shape[1], dp_size, unroll),
        grid=(heads // unroll,),
        in_specs=[smem(), smem()] + specs,
        out_specs=[whole(out.shape) for out in outs],
        out_shape=outs,
        scratch_shapes=[pltpu.VMEM((total, width), F32)] * 2
        + [pltpu.VMEM((width, 128), F32)] * 2
        + [pltpu.VMEM((width, rows), F32)] * 3
        + [
            pltpu.VMEM((total, 3 * width), BF16),
            pltpu.VMEM((width, 3 * width), F32),
            pltpu.VMEM((slots, rows, width), F32),
            pltpu.SemaphoreType.DMA((1 + slots,)),
        ],
        compiler_params=limit(46 if total <= 1024 else KERNEL_MIB),
        cost_estimate=pl.CostEstimate(
            flops=6 * (4 * heads + 6) * total * rows * width, bytes_accessed=24 << 20, transcendentals=0
        ),
        name="backward",
    )(place, lengths, *operands)


def token_grad_kernel(tokens_ref, vecs_ref, own_ref, near_ref, far_ref, tail_ref, grad_ref):
    unit, scale = norm_rows(tokens_ref[...])
    d_normed = own_ref[...] + near_ref[...] + far_ref[...]
    grad_ref[...] = tail_ref[...] + norm_back(d_normed * vecs_ref[0:1, :], unit, scale)


def token_grad(tokens, vectors, own, near, far, tail):
    operands = [*far_off(tokens, vectors), own, near, far, *far_off(tail)]
    return pl.pallas_call(
        token_grad_kernel,
        out_shape=struct(tokens.shape),
        compiler_params=limit(SMALL_MIB),
        cost_estimate=pl.CostEstimate(flops=1 << 21, bytes_accessed=2 << 20, transcendentals=0),
        name="token_grad",
    )(*operands)


def squares_kernel(dp_size, counts, *refs):
    place_ref, added_ref, class_ref = refs[:3]
    early_refs = refs[3 : 3 + counts[0]]
    late_refs = refs[3 + counts[0] : 3 + sum(counts)]
    out_ref, early_ref, late_ref = refs[3 + sum(counts) :]
    odd = jnp.bitwise_and(place_ref[0], 1) == 1
    early = sum_of([ref[...] for ref in early_refs])
    late = sum_of([ref[...] for ref in late_refs])
    early_ref[...], late_ref[...] = early, late
    small = late[:, 512:] + jnp.where(odd, added_ref[...], 0.0)
    lane = lax.broadcasted_iota(jnp.int32, small.shape, 1)
    talk = jnp.logical_and(odd, jnp.logical_and(lane >= 28, lane < 45))
    small = small * small * jnp.where(talk, 1.0 / dp_size, 1.0)
    total = jnp.sum(small)
    for value in (late[:, :512], early):
        total = total + jnp.sum(value * value)
    out_ref[...] = 0.5 * class_ref[...] + total


def squares_of(dp_size, place, added, class_squares, early, late):
    operands = [added, class_squares, *early, *late]
    outs = [struct((8, 128)), struct(early[0].shape), struct(late[0].shape)]
    return pl.pallas_call(
        functools.partial(squares_kernel, dp_size, (len(early), len(late))),
        grid=(1,),
        in_specs=[smem()] + [whole(operand.shape) for operand in operands],
        out_specs=[whole(out.shape) for out in outs],
        out_shape=outs,
        compiler_params=limit(SMALL_MIB),
        cost_estimate=pl.CostEstimate(flops=1 << 18, bytes_accessed=1 << 20, transcendentals=0),
        name="squares",
    )(place, *operands)


def adam_step(weight, gradient, moment1, moment2, rate, decay):
    first = BETA_ONE * moment1 + (1.0 - BETA_ONE) * gradient
    second = BETA_TWO * moment2 + (1.0 - BETA_TWO) * gradient * gradient
    first_hat = first * (1.0 / (1.0 - BETA_ONE**STEP))
    second_hat = second * (1.0 / (1.0 - BETA_TWO**STEP))
    updated = weight - rate * (first_hat / (jnp.sqrt(second_hat) + ADAM_EPS) + decay * weight)
    return (updated, first, second)


def stage_kernel(sliced, place_ref, w_ref, m1_ref, m2_ref, ema_ref, w_out, m1_out, m2_out, ema_out, arrived):
    rows = w_out.shape[2]
    if sliced:
        w_ref = w_ref.at[:, :, pl.ds(pl.multiple_of(place_ref[1] * rows, rows), rows), :]
    pairs = [(w_ref, w_out), (m1_ref, m1_out), (m2_ref, m2_out), (ema_ref, ema_out)]
    for copy in copy_in(pairs, arrived):
        copy.wait()


def stage(place, mats):
    shape = mats[1].shape
    return pl.pallas_call(
        functools.partial(stage_kernel, mats[0].shape != shape),
        in_specs=[smem()] + [anywhere()] * 4,
        out_specs=[pl.BlockSpec(memory_space=pltpu.VMEM)] * 4,
        out_shape=[pltpu.VMEM(shape, F32)] * 4,
        scratch_shapes=[pltpu.SemaphoreType.DMA((4,))],
        compiler_params=limit(8),
        cost_estimate=pl.CostEstimate(flops=1, bytes_accessed=1, transcendentals=0),
        name="stage",
    )(place, *far_off(*mats))


def adam_kernel(sliced, *refs):
    (
        place_ref, squares_ref, early_own, early_other, late_own, late_other, added_ref,
        class_ref, w_ref, m1_ref, m2_ref, ema_ref, v_ref, v1_ref, v2_ref, v_ema_ref,
        t_ref, t1_ref, t2_ref, t_ema_ref,
    ) = refs[:20]
    norm_ref, mat_outs, v_outs, t_outs = refs[20], refs[21:25], refs[25:29], refs[29:33]
    stored, leaving, columns = refs[33:37], refs[37], refs[38]
    norm = jnp.sqrt(squares_ref[0:1, 0:1])
    factor = jnp.minimum(1.0, CLIP_NORM / norm)
    norm_ref[...] = norm

    def updates(weight, gradient, moment1, moment2, ema, rate, decay):
        updated, first, second = adam_step(weight, gradient * factor, moment1, moment2, rate, decay)
        return updated, first, second, EMA_RATE * ema + (1.0 - EMA_RATE) * updated

    even = jnp.bitwise_and(place_ref[0], 1) == 0
    pair = lambda own, other: (jnp.where(even, own[...], other[...]), jnp.where(even, other[...], own[...]))
    early_left, early_right = pair(early_own, early_other)
    late_left, late_right = pair(late_own, late_other)
    hidden = w_ref.shape[3]
    first = jnp.concatenate(
        [late_left, late_right[:, :512], early_left[:, hidden:], early_right[:, hidden : hidden + 128]], axis=1
    )
    grads = [first, early_left[:, :hidden], early_right[:, :hidden], *[class_ref[i] for i in range(3)]]
    copies = []
    for number in (3, 4, 5, 1, 2, 0):
        at = (number // 3, number % 3)
        values = updates(w_ref[at], grads[number], m1_ref[at], m2_ref[at], ema_ref[at], LR_MATRIX, WEIGHT_DECAY)
        for i, value in enumerate(values):
            stored[i][at] = value
            copies.append(pltpu.make_async_copy(stored[i].at[at], mat_outs[i].at[at], leaving.at[i, number]))
            copies[-1].start()
    small = late_right[:, 512:] + added_ref[...]
    count = v1_ref.shape[0]
    if sliced:
        columns[:, :count] = v_ref[...].T
        share = small.shape[0]
        begin = pl.multiple_of(place_ref[1] * share, share)
        weight = columns[pl.ds(begin, share), :].T[:count, :]
    else:
        weight = v_ref[...]
    values = updates(weight, small.T[:count, :], v1_ref[...], v2_ref[...], v_ema_ref[...], LR_VECTOR, 0.0)
    for ref, value in zip(v_outs, values):
        ref[...] = value
    talk = small[:8, count : count + 17]
    values = updates(t_ref[...], talk, t1_ref[...], t2_ref[...], t_ema_ref[...], LR_TALKING, 0.0)
    for ref, value in zip(t_outs, values):
        ref[...] = value
    for copy in copies:
        copy.wait()


def optimizer(place, squares, grads, class_share, mats, vecs, talks):
    shape = mats[0].shape
    sliced = vecs[0].shape != vecs[1].shape
    operands = [squares, *grads, class_share, *mats, *far_off(*vecs, *talks)]
    vmem = pl.BlockSpec(memory_space=pltpu.VMEM)
    outs = [struct((1, 1))] + [struct(shape)] * 4
    outs += [struct(vecs[1].shape)] * 4 + [struct(talks[0].shape)] * 4
    return pl.pallas_call(
        functools.partial(adam_kernel, sliced),
        in_specs=[smem()] + [vmem] * len(operands),
        out_specs=[vmem] + [anywhere()] * 4 + [vmem] * 8,
        out_shape=outs,
        scratch_shapes=[pltpu.VMEM(shape, F32)] * 4
        + [pltpu.SemaphoreType.DMA((4, 6)), pltpu.VMEM((vecs[0].shape[1], 128), F32)],
        compiler_params=limit(SMALL_MIB),
        cost_estimate=pl.CostEstimate(flops=1 << 23, bytes_accessed=14 << 20, transcendentals=0),
        name="optimizer",
    )(place, *operands)


def swap(value, axis, size, bit):
    return lax.ppermute(value, axis, [(place, place ^ bit) for place in range(size)])


def bits_of(axis, size, bit=1):
    return [(axis, bit << i) for i in range((size // bit).bit_length() - 1)]


class Places:
    def __init__(self, dp_size, seq_size, row_share):
        seq, dp = lax.axis_index("seq"), lax.axis_index("dp")
        self.sizes = {"dp": dp_size, "seq": seq_size}
        steps = bits_of("dp", dp_size) + bits_of("seq", seq_size)
        names = {"dp": dp, "seq": seq}
        bits = {step: jnp.bitwise_and(lax.shift_right_logical(names[step[0]], step[1].bit_length() - 1), 1) for step in steps}
        self.found = {
            "seq": seq.astype(jnp.int32).reshape(1),
            "dp": dp.astype(jnp.int32).reshape(1),
            "rows": (dp * row_share).astype(jnp.uint32),
            "share": (bits["seq", 1] * (seq_size // 2) + lax.shift_right_logical(seq, 1)).astype(jnp.uint32),
        }
        for step, bit in bits.items():
            self.found[step, "mine"] = bit.astype(jnp.uint32)
            self.found[step, "other"] = (1 - bit).astype(jnp.uint32)
            self.found[step, "low"] = bit == 0

    def before(self, value):
        names = list(self.found)
        value, *found = together(value, *[self.found[name] for name in names])
        self.found = dict(zip(names, found))
        return value

    def take(self, value, picks):
        at = [jnp.uint32(0)] * value.ndim
        sizes = list(value.shape)
        for dim, (step, which) in picks.items():
            at[dim] = self.found[step, which]
            sizes[dim] = 1
        return lax.squeeze(lax.dynamic_slice(value, at, sizes), tuple(picks))

    def share(self, value, rows):
        at = self.found["share"] * jnp.uint32(rows)
        return lax.dynamic_slice(value, (at, jnp.uint32(0)), (rows, value.shape[1]))

    def rows(self, value, size, dim):
        at = [jnp.uint32(0)] * value.ndim
        at[dim] = self.found["rows"]
        sizes = list(value.shape)
        sizes[dim] = size
        return lax.dynamic_slice(value, at, sizes)

    def swap(self, value, steps):
        flip = sum(bit * (self.sizes["seq"] if axis == "dp" else 1) for axis, bit in steps)
        count = self.sizes["dp"] * self.sizes["seq"]
        return lax.ppermute(value, ("dp", "seq"), [(place, place ^ flip) for place in range(count)])

    def pair(self, value, other, step):
        low = self.found[step, "low"]
        return [jnp.where(low, value, other), jnp.where(low, other, value)]


def subsets(group):
    found = [()]
    for step in group:
        found += [one + (step,) for one in found]
    return found[1:]


class Reduce:
    def __init__(self, terms, places, groups):
        self.places, self.groups = places, list(groups)
        self.left = bits_of("dp", places.sizes["dp"])[::-1]
        shape = (2,) * len(self.left) + (-1, terms[0].shape[1])
        self.terms = [term.reshape(shape) for term in terms]
        self.got = 0

    def sends(self):
        group = self.groups[0]
        halves = [step for step in group if step[0] == "dp"]
        dims = {step: self.left.index(step) for step in halves}
        if not halves:
            self.terms = [sum_of(self.terms)]

        def taken(others):
            picks = {dims[step]: (step, "other" if step in others else "mine") for step in halves}
            return [self.places.take(term, picks) if picks else term for term in self.terms]

        sent = [sum_of(taken(others)) for others in subsets(group)]
        self.terms = taken(())
        self.left = [step for step in self.left if step not in halves]
        return sent

    def post(self, sent):
        group = self.groups.pop(0)
        self.got = len(sent)
        self.terms += [self.places.swap(value, steps) for value, steps in zip(sent, subsets(group))]

    def received(self):
        return self.terms[len(self.terms) - self.got :]

    def set_received(self, values):
        self.terms[len(self.terms) - self.got :] = values

    def value(self):
        return sum_of(self.terms)


def join_kernel(*refs):
    out_ref, at = refs[-1], 0
    for ref in refs[:-1]:
        out_ref[at : at + ref.shape[0]] = ref[...]
        at += ref.shape[0]


def join(parts):
    shape = (sum(part.shape[0] for part in parts),) + parts[0].shape[1:]
    return pl.pallas_call(
        join_kernel,
        in_specs=[pl.BlockSpec(memory_space=pltpu.VMEM)] * len(parts),
        out_specs=pl.BlockSpec(memory_space=pltpu.VMEM),
        out_shape=struct(shape),
        compiler_params=limit(SMALL_MIB),
        cost_estimate=pl.CostEstimate(flops=1, bytes_accessed=1, transcendentals=0),
        name="join",
    )(*parts)


class Gather:
    def __init__(self, value, places):
        self.places = places
        dp = bits_of("dp", places.sizes["dp"])
        self.value = value[None]
        self.groups = [(step,) for step in dp[2:]] + [tuple(dp[:2])]
        self.groups += [(step,) for step in bits_of("seq", places.sizes["seq"], 2) + bits_of("seq", 2)]

    def sends(self):
        return [self.value]

    def post(self, sent):
        self.value = sent[0]
        self.others = [self.places.swap(self.value, steps) for steps in subsets(self.groups[0])]

    def received(self):
        return list(self.others)

    def set_received(self, values):
        group = self.groups.pop(0)
        if group[0][0] == "dp":
            self.value = join([self.value, *values])
        else:
            self.value = jnp.concatenate(self.places.pair(self.value, values[0], group[0]), axis=1)
        self.others = []


def settle(streams, *work):
    streams = [stream for stream in streams if stream.received()]
    counts = [len(stream.received()) for stream in streams]
    found = together(*[value for stream in streams for value in stream.received()], *work)
    at = 0
    for stream, count in zip(streams, counts):
        stream.set_received(list(found[at : at + count]))
        at += count
    return found[at:]


def launch(streams, *after):
    streams = [stream for stream in streams if stream.groups]
    sent = [stream.sends() for stream in streams]
    found = together(*[value for one in sent for value in one], *after)
    at = 0
    for stream, one in zip(streams, sent):
        stream.post(list(found[at : at + len(one)]))
        at += len(one)
    return found[at:]


def sum_of(terms):
    total = terms[0]
    for term in terms[1:]:
        total = total + term
    return total


def tie(value, *others):
    return lax.optimization_barrier((value, *others))[0]


def together(*values):
    return lax.optimization_barrier(values)


def on_device(
    dp_size, seq_size,
    tokens, class_tokens, cot_patch, cot_class, lengths,
    matrices, matrices_moment1, matrices_moment2, matrices_ema,
    vectors, vectors_moment1, vectors_moment2, vectors_ema,
    talking, talking_moment1, talking_moment2, talking_ema,
):
    rows, width = tokens.shape
    images = class_tokens.shape[0]
    row_share = width // dp_size
    places = Places(dp_size, seq_size, row_share)
    tokens = places.before(tokens)
    place = places.found["seq"]

    slots = {0: tokens}
    slots[1] = swap(tokens, "seq", seq_size, 1)
    bit = 2
    while bit < seq_size:
        for slot in sorted(slot for slot in slots if slot % 2 == 0):
            slots[slot | bit] = swap(slots[slot], "seq", seq_size, bit)
        bit *= 2
    *prepared, t1, t2, t1_rows, t2_rows, query, k1, k2, v1, v2, kt1, kt2, vt1, vt2 = prepare(
        tokens, slots[1], class_tokens, matrices, vectors, talking
    )
    for slot in range(2, seq_size, 2):
        slots[slot + 1] = swap(tie(slots[slot], query), "seq", seq_size, 1)
    token_slots = [slots[slot] for slot in range(seq_size)]
    (
        e_high, e_low, pv, inverse, pv_bias, attended, kt_high, kt_low, v_high, v_low,
        patch_out, *kept, packed, scores,
    ) = forward(
        place, lengths, token_slots, matrices, vectors, t1, t2, prepared[3],
        [query, k1, k2, v1, v2, kt1, kt2, vt1, vt2],
    )
    parts = [packed] + [swap(packed, "seq", seq_size, bit) for bit in range(1, seq_size)]
    *staged, w_first = class_stage(tie(place, packed), matrices)
    (
        class_out, d_attended, d_mixed, early_keep, early_send, partial, factors, vec_rows, class_terms,
    ) = middle(
        place, parts, vectors, prepared, class_tokens, cot_class, cot_patch,
        patch_out, scores, staged, [attended, *kept], matrices,
    )

    core, chips, dp = ("seq", 1), bits_of("seq", seq_size, 2), bits_of("dp", dp_size)
    pairs = lambda steps: [tuple(steps[i : i + 2]) for i in range(0, len(steps), 2)]
    other = places.swap(early_send, [core])
    partials = [partial] + [swap(partial, "seq", seq_size, bit) for bit in range(1, seq_size)]
    grad_class, factors = class_finish(partials, class_terms, class_tokens, vectors, w_first, factors)
    gather = Gather(places.share(factors, factors.shape[0] // seq_size), places)
    other, gather.value = together(other, gather.value)
    early = Reduce(
        [early_keep, other], places, [tuple(dp[:2])] + [(step,) for step in dp[2:] + chips]
    )
    (later,) = launch([early, gather], place)
    even, odd, late_keep, late_send = backward(
        dp_size, later, lengths, token_slots, [e_high, e_low, pv, inverse, pv_bias], d_attended,
        [kt_high, kt_low, v_high, v_low], query, [t1, t2, t1_rows, t2_rows], vec_rows, vectors, matrices,
    )

    late_send, odd = settle([early, gather], late_send, odd)
    late_other, odd = places.swap(late_send, [core]), places.swap(odd, [core])
    late = Reduce([late_keep, late_other], places, [tuple(dp[:2])] + [(step,) for step in dp[2:] + chips])
    (late.terms[1],) = launch([early], late.terms[1])
    (even,) = launch([late], even)
    own = [even[0]] + [even[i] + odd[i] for i in range(1, seq_size // 2)]
    near = odd[0]
    bit = 1
    while 2 * bit < len(own):
        for slot in range(0, len(own), 2 * bit):
            own[slot] = own[slot] + swap(own[slot + bit], "seq", seq_size, 2 * bit)
        bit *= 2
    far = swap(own[bit], "seq", seq_size, 2 * bit)
    (own[bit],) = launch([gather], own[bit])
    (own[bit],) = settle([gather], own[bit])
    while len(gather.groups) > len(chips) + 1:
        launch([gather])
        settle([gather])
    launch([gather], own[bit])
    (far,) = settle([late, early], far)
    (far,) = launch([late, early], far)
    (far,) = settle([gather], far)
    while gather.groups:
        launch([gather])
        settle([gather])
    sliced = row_share % 8 == 0
    if not sliced:
        matrices_rows, vectors_columns = places.rows(matrices, row_share, 2), places.rows(vectors, row_share, 1)
    else:
        matrices_rows, vectors_columns = matrices, vectors
    both_places = tie(jnp.concatenate([place, places.found["dp"]]), gather.value)
    staged = stage(both_places, [matrices_rows, matrices_moment1, matrices_moment2, matrices_ema])
    gather.value, *staged = settle([late], gather.value, *staged)
    while late.groups[1:]:
        launch([late])
        settle([late])
    (gather.value,) = launch([late], gather.value)
    mine = places.rows(gather.value, row_share, 2)
    class_share, class_squares, added = class_weights(images, mine, gather.value)
    while early.groups:
        settle([early])
        launch([early])
    class_share, class_squares, added = settle([late, early], class_share, class_squares, added)
    last = [[term.reshape(row_share, -1) for term in stream.terms] for stream in (early, late)]
    squares, early, late = squares_of(dp_size, place, added, class_squares, *last)
    far, squares = together(far, squares)
    for group in pairs([core] + dp):
        squares = sum_of([squares] + [places.swap(squares, steps) for steps in subsets(group)])
    grad_tokens = token_grad(tokens, vectors, own[0], near, far, d_mixed)
    grads = []
    for value in (early, late):
        grads += [value, places.swap(value, [core])]
    norm, *updated = optimizer(
        both_places, squares, [*grads, added], class_share, staged,
        [vectors_columns, vectors_moment1, vectors_moment2, vectors_ema],
        [talking, talking_moment1, talking_moment2, talking_ema],
    )
    return (patch_out, class_out, grad_tokens, grad_class, norm.reshape(()), *updated)


def solution(mesh):
    tokens = P(("dp", "seq"), None)
    by_group = P("dp", None)
    mats = P(None, None, "dp", None)
    vecs = P(None, "dp")
    body = functools.partial(on_device, mesh.shape["dp"], mesh.shape["seq"])
    return jax.shard_map(
        body,
        mesh=mesh,
        in_specs=(tokens, by_group, tokens, by_group, by_group, P(), mats, mats, mats,
                  P(), vecs, vecs, vecs, P(), P(), P(), P()),
        out_specs=(tokens, by_group, tokens, by_group, P(), mats, mats, mats, mats,
                   vecs, vecs, vecs, vecs, P(), P(), P(), P()),
        check_vma=False,
    )
```

```python
import functools

import jax
import jax.numpy as jnp
from jax import lax
from jax.experimental import pallas as pl
from jax.experimental.pallas import tpu as pltpu
from jax.sharding import PartitionSpec as P

STEP = 10
EPS_NORM = 1e-06
MASKED = -1e30
LR_MATRIX = 0.05
LR_VECTOR = 0.1
LR_TALKING = 0.2
BETA_ONE = 0.9
BETA_TWO = 0.999
ADAM_EPS = 1e-08
WEIGHT_DECAY = 0.05
EMA_RATE = 0.9
CLIP_NORM = 1.0
F32 = jnp.float32
BF16 = jnp.bfloat16
NN = (((1,), (0,)), ((), ()))
NT = (((1,), (1,)), ((), ()))
TN = (((0,), (0,)), ((), ()))
KERNEL_MIB, NEAR_MIB, SMALL_MIB = 58, 52, 24


def split(value):
    high = value.astype(BF16)
    return high, (value - high.astype(F32)).astype(BF16)


def mm(left, right, dims=NN):
    return lax.dot_general(left, right, dims, preferred_element_type=F32)


def mm3(left, right, dims=NN):
    return mm(left[0], right[0], dims) + (mm(left[0], right[1], dims) + mm(left[1], right[0], dims))


def mm3_tall(left, right, dims=NN):
    rows = left[0].shape[0]
    stacked = jnp.concatenate([part.astype(F32) for part in left], axis=0).astype(BF16)
    both = mm(stacked, right[0], dims)
    return both[:rows] + (both[rows:] + mm(left[0], right[1], dims))


def dot_tall(left, right, dims=NN):
    return mm3_tall(split(left), split(right), dims)


def dot3(left, right, dims=NN):
    return mm3(split(left), split(right), dims)


def norm_rows(values):
    average = jnp.mean(values, axis=-1, keepdims=True)
    centered = values - average
    variance = jnp.mean(centered * centered, axis=-1, keepdims=True)
    scale = lax.rsqrt(variance + EPS_NORM)
    return centered * scale, scale


def norm_back(grad, unit, scale):
    inner = jnp.mean(grad * unit, axis=-1, keepdims=True)
    return scale * (grad - jnp.mean(grad, axis=-1, keepdims=True) - unit * inner)


def gelu_both(values):
    half = 0.5 * (1.0 + lax.erf(values * 0.7071067811865476))
    slope = half + values * (0.3989422804014327 * jnp.exp(-0.5 * values * values))
    return values * half, slope


def row_sum(values):
    return jnp.sum(values, axis=0, keepdims=True)


def tail_forward(dot, inputs, attended, w_out, w_up, w_down, vecs):
    projected = dot(attended, w_out) + vecs[4:5]
    mixed = inputs + vecs[5:6] * projected
    unit, _ = norm_rows(mixed)
    normed = unit * vecs[6:7] + vecs[7:8]
    up_bias = jnp.concatenate([vecs[row : row + 1] for row in range(8, 12)], axis=1)
    hidden, slope = gelu_both(dot(normed, w_up) + up_bias)
    lowered = dot(hidden, w_down, NT) + vecs[12:13]
    return mixed + vecs[13:14] * lowered, (projected, mixed, hidden, slope, lowered)


def tail_backward(dot, cot, kept, w_out, w_up, w_down, vecs):
    projected, mixed, hidden, slope, lowered = kept
    width = cot.shape[1]
    unit, scale = norm_rows(mixed)
    normed = unit * vecs[6:7] + vecs[7:8]
    d_lowered = cot * vecs[13:14]
    d_hidden = dot(d_lowered, w_down) * slope
    d_normed = dot(d_hidden, w_up, NT)
    d_mixed = cot + norm_back(d_normed * vecs[6:7], unit, scale)
    d_projected = d_mixed * vecs[5:6]
    d_attended = dot(d_projected, w_out, NT)
    d_up = row_sum(d_hidden)
    rows = [
        row_sum(d_projected), row_sum(d_mixed * projected), row_sum(d_normed * unit), row_sum(d_normed),
        *[d_up[:, i * width : (i + 1) * width] for i in range(4)],
        row_sum(d_lowered), row_sum(cot * lowered),
    ]
    return d_mixed, d_attended, d_projected, d_hidden, d_lowered, normed, rows


def image_of(lengths_ref, images, positions):
    end = lengths_ref[0, 0]
    inside = (positions >= end).astype(jnp.int32)
    for image in range(1, images):
        end = end + lengths_ref[0, image]
        inside = inside + (positions >= end).astype(jnp.int32)
    return inside


def same_image(lengths_ref, images, place, slots, rows):
    queries = place * rows + lax.broadcasted_iota(jnp.int32, (1, rows), 1)
    query_image = image_of(lengths_ref, images, queries)
    parts = []
    for slot in range(slots):
        keys = jnp.bitwise_xor(place, slot) * rows + lax.broadcasted_iota(jnp.int32, (rows, 1), 0)
        parts.append(image_of(lengths_ref, images, keys) == query_image)
    return parts


def column_of(table, number):
    lanes = lax.broadcasted_iota(jnp.int32, (1, table.shape[1]), 1)
    return jnp.sum(jnp.where(lanes == number, table, 0.0), axis=1, keepdims=True)


def head_mask(heads, width):
    row = lax.broadcasted_iota(jnp.int32, (heads, width), 0)
    return jnp.where(lax.broadcasted_iota(jnp.int32, (heads, width), 1) // (width // heads) == row, 1.0, 0.0)


def spread(value, mask):
    return jnp.concatenate([value[i : i + 1] * mask for i in range(value.shape[0])], axis=0)


def repeat_rows(value, heads):
    shape = (heads, value.shape[1])
    return jnp.concatenate(
        [jnp.broadcast_to(value[i : i + 1], shape) for i in range(value.shape[0])], axis=0
    )


def fold_heads(value, mask):
    heads = mask.shape[0]
    return jnp.concatenate(
        [row_sum(value[i : i + heads] * mask) for i in range(0, value.shape[0], heads)], axis=0
    )


def head_sums(value, mask):
    return jnp.sum(spread(value, mask), axis=1, keepdims=True)


def rows_of(value, heads):
    return jnp.concatenate(
        [row_sum(value[i : i + heads]) for i in range(0, value.shape[0], heads)], axis=0
    )


def wide(column):
    return jnp.broadcast_to(column, (column.shape[0], 128))


def whole(shape):
    return pl.BlockSpec(shape, lambda *_: (0,) * len(shape))


def struct(shape, dtype=F32):
    return jax.ShapeDtypeStruct(shape, dtype)


def far_struct(shape, dtype=F32):
    return pltpu.HBM(shape, dtype)


def smem():
    return pl.BlockSpec(memory_space=pltpu.SMEM)


def anywhere():
    return pl.BlockSpec(memory_space=pl.ANY)


def weight_block(block, matrix, shape, columns=None):
    return pl.BlockSpec((None, None, shape[2], columns or shape[3]), lambda *_: (block, matrix, 0, 0))


def far_off(*operands):
    return [pltpu.with_memory_space_constraint(operand, pltpu.HBM) for operand in operands]


def copy_in(pairs, arrived):
    copies = [pltpu.make_async_copy(a, b, arrived.at[i]) for i, (a, b) in enumerate(pairs)]
    for copy in copies:
        copy.start()
    return copies


def limit(mebibytes):
    return pltpu.CompilerParams(vmem_limit_bytes=mebibytes << 20)


def prepare_kernel(
    own_ref, near_ref, class_ref, w_self_ref, w_class_ref, vecs_ref, talk_ref,
    normed_ref, query_c_ref, value_c_ref, key_rows_ref, score_ref, t1_ref, t2_ref, t1_rows_ref, t2_rows_ref,
    query_ref, k_high, k_low, v_high, v_low, kt_high, kt_low, vt_high, vt_low,
):
    rows, width = own_ref.shape
    heads = talk_ref.shape[0]
    size = width // heads
    scale = size ** (-0.5)
    vecs = vecs_ref[...]
    w_q, w_kv = split(w_self_ref[:, :width]), split(w_self_ref[:, width:])
    tokens = jnp.concatenate([own_ref[...], near_ref[...]], axis=0)
    unit, _ = norm_rows(tokens)
    normed = split(unit * vecs[0:1] + vecs[1:2])
    query_ref[...] = (mm3((normed[0][:rows], normed[1][:rows]), w_q) + vecs[2:3]) * scale
    both = mm3(normed, w_kv)
    keys, values = both[:, :width], both[:, width:] + vecs[3:4]
    k_high[...], k_low[...] = split(keys)
    v_high[...], v_low[...] = split(values)
    kt_high[...], kt_low[...] = split(keys.T)
    vt_high[...], vt_low[...] = split(values.T)
    mask = head_mask(heads, width)
    unit, _ = norm_rows(class_ref[...])
    normed = unit * vecs[14:15] + vecs[15:16]
    both = dot_tall(normed, w_class_ref[...])
    query = both[:, :width] + vecs[16:17]
    normed_ref[...] = normed
    query_c_ref[...] = query
    value_c_ref[...] = both[:, 2 * width :] + vecs[17:18]
    key_rows_ref[...] = dot3(spread(query, mask), w_class_ref[:, width : 2 * width], NT) * scale
    score_ref[...] = wide(head_sums(query * both[:, width : 2 * width], mask) * scale)
    head_of = lax.broadcasted_iota(jnp.int32, (width, 1), 0) // size
    talk = talk_ref[...]
    talk_t = jnp.concatenate([talk, jnp.zeros((heads, 128 - talk.shape[1]), F32)], axis=1).T[: talk.shape[1], :]
    t1 = t2 = t1_rows = t2_rows = 0.0
    for head in range(heads):
        here = head_of == head
        t1 = t1 + jnp.where(here, talk_t[head : head + 1, :], 0.0)
        t2 = t2 + jnp.where(here, talk[head : head + 1, heads:], 0.0)
        t1_rows = t1_rows + mask[head : head + 1] * talk[:, head : head + 1]
        t2_rows = t2_rows + mask[head : head + 1] * talk_t[heads:, head : head + 1]
    t1_ref[...], t2_ref[...], t1_rows_ref[...], t2_rows_ref[...] = t1, t2, t1_rows, t2_rows


def prepare(own, near, class_tokens, matrices, vectors, talking):
    images, width = class_tokens.shape
    rows = own.shape[0]
    heads = talking.shape[0]
    pairs = images * heads
    outs = [far_struct((images, width))] * 3 + [
        far_struct((pairs, width)), far_struct((pairs, 128)),
        far_struct((width, heads)), far_struct((width, heads + 1)),
        far_struct((heads, width)), far_struct((heads + 1, width)),
        far_struct((rows, width)),
    ]
    outs += [far_struct((2 * rows, width), BF16)] * 4 + [far_struct((width, 2 * rows), BF16)] * 4
    own, class_tokens, matrices, vectors, talking = far_off(own, class_tokens, matrices, vectors, talking)
    operands = [own, near, class_tokens, matrices, matrices, vectors, talking]
    specs = [whole(operand.shape) for operand in operands]
    specs[3] = weight_block(0, 0, matrices.shape, 3 * width)
    specs[4] = weight_block(1, 0, matrices.shape, 3 * width)
    return pl.pallas_call(
        prepare_kernel,
        grid=(1,),
        in_specs=specs,
        out_specs=[whole(out.shape) for out in outs],
        out_shape=outs,
        compiler_params=limit(NEAR_MIB),
        cost_estimate=pl.CostEstimate(flops=4 << 30, bytes_accessed=8 << 20, transcendentals=0),
        name="prepare",
    )(*operands)


def forward_kernel(slots, images, unroll, *refs):
    place_ref, lengths_ref = refs[:2]
    token_refs = refs[2 : 1 + slots]
    (
        vecs_ref, t1_ref, t2_ref, key_rows_ref, query_ref,
        k_high0, k_low0, v_high0, v_low0, kt_high0, kt_low0, vt_high0, vt_low0, mats_ref,
        e_high_hbm, e_low_hbm, pv_hbm, inverse_ref, pv_bias_ref, attended_ref,
        kt_high_hbm, kt_low_hbm, v_high_hbm, v_low_hbm,
        patch_ref, projected_ref, mixed_ref, hidden_hbm, slope_hbm, lowered_ref, packed_ref, scores_ref,
        k_three, vt_two, qt, bias, attended_t, w_kv, w_up, w_down, w_out, arrived,
        kt_high, kt_low, v_high, v_low, hidden_ref, slope_ref, e_high_ref, e_low_ref, pv_ref, leaving,
    ) = refs[1 + slots :]
    rows, width = token_refs[0].shape
    step = pl.program_id(0)
    place = place_ref[0]
    ready, columns = pl.ds(0, 2 * rows), lambda i: pl.ds(i * width, width)
    pairs = [
        (mats_ref.at[0, 0, :, pl.ds(width, 2 * width)], w_kv),
        (k_high0, k_three.at[ready, columns(0)]), (k_high0, k_three.at[ready, columns(1)]),
        (k_low0, k_three.at[ready, columns(2)]), (v_high0, v_high.at[ready, :]), (v_low0, v_low.at[ready, :]),
        (kt_high0, kt_high.at[:, ready]), (kt_low0, kt_low.at[:, ready]),
        (vt_high0, vt_two.at[columns(0), ready]), (vt_low0, vt_two.at[columns(1), ready]),
        (mats_ref.at[0, 0, :, pl.ds(3 * width, width)], w_out),
        (mats_ref.at[0, 1], w_up), (mats_ref.at[0, 2], w_down),
    ]
    fetches = [pltpu.make_async_copy(a, b, arrived.at[i]) for i, (a, b) in enumerate(pairs)]
    pairs = [(kt_high, kt_high_hbm), (kt_low, kt_low_hbm), (v_high, v_high_hbm), (v_low, v_low_hbm),
             (hidden_ref, hidden_hbm), (slope_ref, slope_hbm)]
    stores = [pltpu.make_async_copy(a, b, leaving.at[i]) for i, (a, b) in enumerate(pairs)]
    heads = inverse_ref.shape[0]
    groups = []
    for number in range(heads // unroll):
        here = pl.ds(number * unroll, unroll)
        groups.append([
            pltpu.make_async_copy(a.at[here], b.at[here], leaving.at[6 + 3 * number + i])
            for i, (a, b) in enumerate([(e_high_ref, e_high_hbm), (e_low_ref, e_low_hbm), (pv_ref, pv_hbm)])
        ])

    @pl.when(step == 0)
    def _():
        for fetch in fetches:
            fetch.start()
        vecs = vecs_ref[...]
        inside = same_image(lengths_ref, images, place, slots, rows)
        for slot in range(slots):
            bias[pl.ds(slot * rows, rows), :] = jnp.where(inside[slot], 0.0, MASKED)
        units = [norm_rows(ref[...])[0] for ref in token_refs[1:]]
        fetches[0].wait()
        w_both = split(w_kv[...])
        for slot in range(2, slots):
            here = pl.ds(slot * rows, rows)
            normed = split(units[slot - 2] * vecs[0:1] + vecs[1:2])
            both = mm3(normed, w_both)
            keys, values = both[:, :width], both[:, width:] + vecs[3:4]
            high, low = split(keys)
            k_three[here, :] = jnp.concatenate([high, high, low], axis=1)
            v_high[here, :], v_low[here, :] = split(values)
            kt_high[:, here], kt_low[:, here] = split(keys.T)
            vt_two[:, here] = jnp.concatenate(split(values.T), axis=0)
        qt[...] = query_ref[...].T
        attended_t[...] = jnp.zeros_like(attended_t)
        for fetch in fetches[1:10]:
            fetch.wait()
        for store in stores[:4]:
            store.start()

    scores = []
    for u in range(unroll):
        high, low = split(qt[...] * column_of(t1_ref[...], step * unroll + u))
        scores.append(mm(k_three[...], jnp.concatenate([high, low, high], axis=0)) + bias[...])
    for u in range(unroll):
        exponentials = jnp.exp(scores[u] - jnp.max(scores[u], axis=0, keepdims=True))
        inverse = 1.0 / jnp.sum(exponentials, axis=0, keepdims=True)
        pair = split(exponentials)
        head = step * unroll + u
        e_high_ref[head], e_low_ref[head] = pair
        inverse_ref[head] = inverse
        both = mm(vt_two[...], pair[0])
        values = (both[:width] + (both[width:] + mm(vt_two[:width, :], pair[1]))) * inverse
        pv_ref[head] = values
        attended_t[...] += values * column_of(t2_ref[...], head)
    for number, group in enumerate(groups):

        @pl.when(step == number)
        def _(group=group):
            for copy in group:
                copy.start()

    @pl.when(step == pl.num_programs(0) - 1)
    def _():
        inside = jnp.where(bias[...] < 0.0, 0.0, 1.0).astype(BF16)
        both = mm(vt_two[...], inside)
        summed = both[:width] + both[width:]
        pv_bias_ref[...] = summed
        attended = (attended_t[...] + summed * t2_ref[:, 8:9]).T
        attended_ref[...] = attended
        for fetch in fetches[10:]:
            fetch.wait()
        vecs = vecs_ref[...]
        patch, kept = tail_forward(
            dot3, token_refs[0][...], attended, w_out[...], w_up[...], w_down[...], vecs
        )
        patch_ref[...] = patch
        for ref, value in zip((projected_ref, mixed_ref, hidden_ref, slope_ref, lowered_ref), kept):
            ref[...] = value
        for store in stores[4:]:
            store.start()
        unit, _ = norm_rows(patch)
        normed = split(unit * vecs[14:15] + vecs[15:16])
        pairs = images * 8
        image = lax.broadcasted_iota(jnp.int32, (pairs, 1), 0) // 8
        positions = place * rows + lax.broadcasted_iota(jnp.int32, (1, rows), 1)
        belong = image_of(lengths_ref, images, positions) == image
        class_scores = mm3(split(key_rows_ref[...]), normed, NT)
        class_scores = jnp.where(belong, class_scores, MASKED)
        scores_ref[...] = class_scores
        top = jnp.max(class_scores, axis=1, keepdims=True)
        weights = jnp.where(belong, jnp.exp(class_scores - top), 0.0)
        packed_ref[:, :width] = mm3(split(weights), normed)
        lane = lax.broadcasted_iota(jnp.int32, (1, 128), 1)
        total = jnp.sum(weights, axis=1, keepdims=True)
        packed_ref[:, width:] = jnp.where(lane < 64, top, total)
        for store in stores + [copy for group in groups for copy in group]:
            store.wait()


def by_head(unroll, shape):
    return pl.BlockSpec((unroll,) + shape[1:], lambda g: (g, 0, 0))


def forward(place, lengths, token_slots, matrices, vectors, t1, t2, key_rows, projected):
    slots, (rows, width) = len(token_slots), token_slots[0].shape
    total, heads = slots * rows, 8
    unroll = 4 if total <= 1024 else 1
    hidden = matrices.shape[3]
    pairs = key_rows.shape[0]
    outs = [
        far_struct((heads, total, rows), BF16), far_struct((heads, total, rows), BF16), far_struct((heads, width, rows)),
        far_struct((heads, 1, rows)), far_struct((width, rows)), far_struct((rows, width)),
        far_struct((width, total), BF16), far_struct((width, total), BF16),
        far_struct((total, width), BF16), far_struct((total, width), BF16),
        far_struct((rows, width)), far_struct((rows, width)), far_struct((rows, width)),
        far_struct((rows, hidden)), far_struct((rows, hidden)), far_struct((rows, width)),
        far_struct((pairs, width + 128)), far_struct((pairs, rows)),
    ]
    away = (0, 1, 2, 6, 7, 8, 9, 13, 14)
    out_specs = [anywhere() if i in away else whole(out.shape) for i, out in enumerate(outs)]
    operands = [token_slots[0], *token_slots[2:], *far_off(vectors, t1, t2, key_rows, *projected, matrices)]
    in_specs = [whole(operand.shape) for operand in operands]
    in_specs[-9:] = [anywhere()] * 9
    flops = 2 * 3 * ((2 * heads + 1) * total + 9 * width) * rows * width
    return pl.pallas_call(
        functools.partial(forward_kernel, slots, lengths.shape[1], unroll),
        grid=(heads // unroll,),
        in_specs=[smem(), smem()] + in_specs,
        out_specs=out_specs,
        out_shape=outs,
        scratch_shapes=[
            pltpu.VMEM((total, 3 * width), BF16),
            pltpu.VMEM((2 * width, total), BF16),
            pltpu.VMEM((width, rows), F32),
            pltpu.VMEM((total, rows), F32),
            pltpu.VMEM((width, rows), F32),
            pltpu.VMEM((width, 2 * width), F32),
            pltpu.VMEM((width, hidden), F32),
            pltpu.VMEM((width, hidden), F32),
            pltpu.VMEM((width, width), F32),
            pltpu.SemaphoreType.DMA((13,)),
            pltpu.VMEM((width, total), BF16),
            pltpu.VMEM((width, total), BF16),
            pltpu.VMEM((total, width), BF16),
            pltpu.VMEM((total, width), BF16),
            pltpu.VMEM((rows, hidden), F32),
            pltpu.VMEM((rows, hidden), F32),
            pltpu.VMEM((heads, total, rows), BF16),
            pltpu.VMEM((heads, total, rows), BF16),
            pltpu.VMEM((heads, width, rows), F32),
            pltpu.SemaphoreType.DMA((6 + 3 * heads // unroll,)),
        ],
        compiler_params=limit(NEAR_MIB if total <= 1024 else KERNEL_MIB),
        cost_estimate=pl.CostEstimate(
            flops=flops, bytes_accessed=24 << 20, transcendentals=heads * total * rows
        ),
        name="forward",
    )(place, lengths, *operands)


def class_stage_kernel(place_ref, mats_ref, last_out, up_out, down_out, first_out, arrived):
    width = first_out.shape[1]
    pairs = [(mats_ref.at[1, 0, :, pl.ds(width, width)], last_out), (mats_ref.at[1, 1], up_out),
             (mats_ref.at[1, 2], down_out), (mats_ref.at[1, 0, :, pl.ds(0, width)], first_out)]
    for copy in copy_in(pairs, arrived):
        copy.wait()


def class_stage(place, matrices):
    rows, columns = matrices.shape[2:]
    half, whole_matrix = (rows, columns // 2), (rows, columns)
    return pl.pallas_call(
        class_stage_kernel,
        in_specs=[smem(), anywhere()],
        out_specs=[pl.BlockSpec(memory_space=pltpu.VMEM)] * 4,
        out_shape=[pltpu.VMEM(shape, F32) for shape in (half, whole_matrix, whole_matrix, half)],
        scratch_shapes=[pltpu.SemaphoreType.DMA((4,))],
        compiler_params=limit(8),
        cost_estimate=pl.CostEstimate(flops=1, bytes_accessed=1, transcendentals=0),
        name="class_stage",
    )(place, *far_off(matrices))


def middle_kernel(images, slots, *refs):
    place_ref = refs[0]
    parts = [ref[...] for ref in refs[1 : 1 + slots]]
    (
        vecs_ref, normed_c_ref, query_c_ref, value_c_ref, key_rows_ref, own_ref,
        class_ref, cot_class_ref, cot_patch_ref, patch_ref, scores_ref, wc0, wc1, wc2,
        attended_hbm, projected_hbm, mixed_hbm, hidden_hbm, slope_hbm, lowered_hbm, mats_ref,
        class_out_ref, d_attended_ref, d_mixed_ref, keep_ref, send_ref, partial_ref,
        factors_ref, vec_rows_ref, class_terms_ref,
        ws0, ws1, ws2, attended_ref, projected_ref, mixed_ref, hidden_ref, slope_ref, lowered_ref,
        keep, send, arrived, stored,
    ) = refs[1 + slots :]
    width = class_ref.shape[1]
    heads = 8
    size = width // heads
    copies = copy_in(
        [(lowered_hbm, lowered_ref), (hidden_hbm, hidden_ref), (mats_ref.at[0, 2], ws2), (slope_hbm, slope_ref),
         (mixed_hbm, mixed_ref), (mats_ref.at[0, 1], ws1), (projected_hbm, projected_ref),
         (attended_hbm, attended_ref), (mats_ref.at[0, 0, :, pl.ds(3 * width, width)], ws0)], arrived)
    vecs = vecs_ref[...]
    vecs_s, vecs_c = vecs[:14], vecs[14:]
    mask = head_mask(heads, width)
    first = jnp.where(place_ref[0] == 0, 1.0, 0.0)
    own_score = own_ref[:, :1]
    normed_c = normed_c_ref[...]
    normed_rep = repeat_rows(normed_c, heads)
    top = own_score
    for part in parts:
        top = jnp.maximum(top, part[:, width : width + 1])
    own_weight = jnp.exp(own_score - top)
    total, summed = own_weight, own_weight * normed_rep
    for part in parts:
        rescale = jnp.exp(part[:, width : width + 1] - top)
        total = total + part[:, width + 64 : width + 65] * rescale
        summed = summed + part[:, :width] * rescale
    value_rows = summed / total
    own_prob = own_weight / total
    unit_p, scale_p = norm_rows(patch_ref[...])
    normed_p = split(unit_p * vecs_c[0:1] + vecs_c[1:2])
    scores = scores_ref[...]
    probs = jnp.where(scores > 0.5 * MASKED, jnp.exp(scores - top) * (1.0 / total), 0.0)
    w_v = split(wc0[:, :width])
    class_attended = fold_heads(mm3_tall(split(value_rows), w_v), mask) + vecs_c[3:4]
    w_out_c = wc0[:, width:]
    class_out, kept_c = tail_forward(
        dot_tall, class_ref[...], class_attended, w_out_c, wc1[...], wc2[...], vecs_c
    )
    class_out_ref[...] = class_out
    d_mixed_c, d_attended_c, d_projected_c, d_hidden_c, d_lowered_c, normed2_c, tail_rows_c = (
        tail_backward(dot_tall, cot_class_ref[...], kept_c, w_out_c, wc1[...], wc2[...], vecs_c)
    )
    for copy in copies:
        copy.wait()
    delta = head_sums(d_attended_c * class_attended, mask)
    cot_rows = mm3_tall(split(spread(d_attended_c, mask)), w_v, NT)
    cot_const = head_sums(d_attended_c * vecs_c[3:4], mask)
    cot_split = split(cot_rows)
    d_scores = probs * (mm3_tall(cot_split, normed_p, NT) + cot_const - delta)
    d_own = own_prob * (head_sums(d_attended_c * value_c_ref[...], mask) - delta)
    key_rows = key_rows_ref[...]
    d_split = split(d_scores)
    d_normed_p = mm3(d_split, split(key_rows), TN) + mm3(split(probs), cot_split, TN)
    partial_ref[...] = mm3_tall(d_split, normed_p)
    cot = cot_patch_ref[...] + norm_back(d_normed_p * vecs_c[0:1], unit_p, scale_p)
    class_terms_ref[...] = jnp.concatenate(
        [rows_of(d_own * key_rows + own_prob * cot_rows, heads), d_mixed_c], axis=0
    )
    query_c = query_c_ref[...]
    chunks = lambda value: [value[:, i * width : (i + 1) * width] for i in range(4)]
    factors_ref[...] = jnp.concatenate(
        [normed_c, class_attended, normed2_c, d_lowered_c, d_own * normed_rep, value_rows,
         jnp.zeros_like(query_c), query_c * size ** (-0.5), d_attended_c, d_projected_c,
         *chunks(d_hidden_c), *chunks(kept_c[2])], axis=0)
    projected, mixed, hidden, lowered = projected_ref[...], mixed_ref[...], split(hidden_ref[...]), lowered_ref[...]
    unit, scale = norm_rows(mixed)
    normed = split(unit * vecs_s[6:7] + vecs_s[7:8])
    d_lowered = cot * vecs_s[13:14]
    d_low_split = split(d_lowered)
    d_hidden = mm3(d_low_split, split(ws2[...])) * slope_ref[...]
    d_hid_split = split(d_hidden)
    g_down = mm3(d_low_split, hidden, TN)
    g_up = mm3(normed, d_hid_split, TN)
    even = jnp.bitwise_and(place_ref[0], 1) == 0
    size_up = g_up.shape[1]
    send[:, :size_up] = jnp.where(even, g_down, g_up)
    keep[:, :size_up] = jnp.where(even, g_up, g_down)
    bulk = pl.ds(0, size_up)
    leaving = copy_in(
        [(send.at[:, bulk], send_ref.at[:, bulk]), (keep.at[:, bulk], keep_ref.at[:, bulk])], stored
    )
    d_normed = mm3(d_hid_split, split(ws1[...]), NT)
    d_mixed = cot + norm_back(d_normed * vecs_s[6:7], unit, scale)
    d_projected = d_mixed * vecs_s[5:6]
    d_proj_split = split(d_projected)
    g_out = mm3(split(attended_ref[...]), d_proj_split, TN)
    left = g_out[:, :256]
    right = jnp.concatenate([g_out[:, 256:], jnp.zeros((width, 512 - width), F32)], axis=1)
    send[:, size_up:] = jnp.where(even, right, left)
    keep[:, size_up:] = jnp.where(even, left, right)
    rest = pl.ds(size_up, 256)
    for i, (a, b) in enumerate([(send, send_ref), (keep, keep_ref)]):
        leaving.append(pltpu.make_async_copy(a.at[:, rest], b.at[:, rest], stored.at[2 + i]))
        leaving[-1].start()
    d_mixed_ref[...] = d_mixed
    d_attended_ref[...] = mm3(d_proj_split, split(ws0[...]), NT)
    d_up = row_sum(d_hidden)
    tail_rows = [
        row_sum(d_projected), row_sum(d_mixed * projected), row_sum(d_normed * unit), row_sum(d_normed),
        *[d_up[:, i * width : (i + 1) * width] for i in range(4)],
        row_sum(d_lowered), row_sum(cot * lowered),
    ]
    zero = jnp.zeros((1, width), F32)
    vec_rows_ref[...] = jnp.concatenate(
        [zero] * 4 + tail_rows
        + [row_sum(d_normed_p * unit_p), row_sum(d_normed_p), zero, row_sum(d_attended_c) * first]
        + [row * first for row in tail_rows_c], axis=0)
    for copy in leaving:
        copy.wait()


def middle(
    place, parts, vectors, prepared, class_tokens, cot_class, cot_patch, patch, scores, staged, kept, matrices
):
    images, width = class_tokens.shape
    rows = cot_patch.shape[0]
    hidden = matrices.shape[3]
    pairs = parts[0].shape[0]
    rest = [vectors, *prepared, class_tokens, cot_class, cot_patch, patch, scores]
    operands = [*parts, *far_off(*rest), *staged, *far_off(*kept, matrices)]
    outs = [
        far_struct((images, width)), far_struct((rows, width)), far_struct((rows, width)),
        far_struct((width, hidden + 256)), far_struct((width, hidden + 256)), far_struct((pairs, width)),
        far_struct((16 * images + 2 * pairs, width)), far_struct((28, width)), far_struct((2 * images, width)),
    ]
    vmem = pl.BlockSpec(memory_space=pltpu.VMEM)
    in_specs = [vmem] * len(operands)
    in_specs[-1 - len(kept) :] = [anywhere()] * (1 + len(kept))
    out_specs = [vmem] * len(outs)
    out_specs[3:5] = [anywhere()] * 2
    return pl.pallas_call(
        functools.partial(middle_kernel, images, len(parts)),
        in_specs=[smem()] + in_specs,
        out_specs=out_specs,
        out_shape=outs,
        scratch_shapes=[pltpu.VMEM((width, width), F32)]
        + [pltpu.VMEM((width, hidden), F32)] * 2
        + [pltpu.VMEM(value.shape, F32) for value in kept]
        + [pltpu.VMEM((width, hidden + 256), F32)] * 2
        + [pltpu.SemaphoreType.DMA((9,)), pltpu.SemaphoreType.DMA((4,))],
        compiler_params=limit(44),
        cost_estimate=pl.CostEstimate(flops=8 << 30, bytes_accessed=28 << 20, transcendentals=1 << 19),
        name="middle",
    )(place, *operands)


def class_kernel(slots, *refs):
    partial_refs = refs[:slots]
    terms_ref, class_ref, vecs_ref, w_ref, factors_ref, grad_ref, factors_out_ref = refs[slots:]
    images, width = class_ref.shape
    pairs = partial_refs[0].shape[0]
    heads = pairs // images
    mask = head_mask(heads, width)
    at = 4 * images
    query_rows = sum_of([factors_ref[at : at + pairs, :]] + [ref[...] for ref in partial_refs])
    w_k, w_q = w_ref[:, width : 2 * width], w_ref[:, :width]
    d_query = fold_heads(dot_tall(query_rows, w_k), mask) * (width // heads) ** (-0.5)
    d_normed = dot_tall(d_query, w_q, NT) + terms_ref[:images, :]
    unit, scale = norm_rows(class_ref[...])
    grad_ref[...] = terms_ref[images:, :] + norm_back(d_normed * vecs_ref[14:15, :], unit, scale)
    count = factors_ref.shape[0]
    factors_out_ref[:count, :] = factors_ref[...]
    factors_out_ref[at : at + pairs, :] = query_rows
    at = at + 2 * pairs
    factors_out_ref[at : at + images, :] = d_query
    added = [row_sum(d_normed * unit), row_sum(d_normed), row_sum(d_query), jnp.zeros((5, width), F32)]
    factors_out_ref[count:, :] = jnp.concatenate(added, axis=0)


def class_finish(partials, terms, class_tokens, vectors, w_first, factors):
    operands = [*far_off(partials[0]), *partials[1:], *far_off(terms, class_tokens, vectors), w_first]
    operands += far_off(factors)
    vmem = pl.BlockSpec(memory_space=pltpu.VMEM)
    outs = [struct(class_tokens.shape), struct((factors.shape[0] + 8, factors.shape[1]))]
    return pl.pallas_call(
        functools.partial(class_kernel, len(partials)),
        in_specs=[vmem] * len(operands),
        out_specs=[vmem] * len(outs),
        out_shape=outs,
        compiler_params=limit(12),
        cost_estimate=pl.CostEstimate(flops=1, bytes_accessed=1, transcendentals=0),
        name="class_finish",
    )(*operands)


def class_weights_kernel(images, mine_ref, factors_ref, grads_ref, squares_ref, small_ref):
    groups, count, width = factors_ref.shape
    heads = 8
    pairs = images * heads
    mask = head_mask(heads, width)
    at = 4 * images + 2 * pairs

    def rows(ref, begin, count=images):
        return jnp.concatenate([ref[g, begin : begin + count, :] for g in range(groups)], axis=0)

    def chunked(begin):
        return jnp.concatenate([rows(factors_ref, begin + i * images) for i in range(4)], axis=1)

    def headed(left, right):
        return dot3(rows(mine_ref, left, pairs), spread(rows(factors_ref, right), mask), TN)

    grads_ref[0, :, :width] = dot3(rows(mine_ref, 0), rows(factors_ref, at), TN)
    grads_ref[0, :, width : 2 * width] = headed(4 * images, at + images)
    grads_ref[0, :, 2 * width : 3 * width] = headed(4 * images + pairs, at + 2 * images)
    grads_ref[0, :, 3 * width :] = dot3(rows(mine_ref, images), rows(factors_ref, at + 3 * images), TN)
    grads_ref[1] = dot3(rows(mine_ref, 2 * images), chunked(at + 4 * images), TN)
    grads_ref[2] = dot3(rows(mine_ref, 3 * images), chunked(at + 8 * images), TN)
    grads = grads_ref[...]
    squares_ref[...] = jnp.broadcast_to(jnp.sum(grads * grads), squares_ref.shape)
    added = sum_of([mine_ref[g, count - 8 :, :] for g in range(groups)])
    lanes = 128 - 22
    share = added.shape[1]
    added = jnp.concatenate([jnp.zeros((14, share), F32), added, jnp.zeros((lanes, share), F32)], axis=0)
    small_ref[...] = added.T


def class_weights(images, mine, factors):
    share = mine.shape[2]
    outs = [struct((3, share, 4 * factors.shape[2])), struct((8, 128)), struct((share, 128))]
    return pl.pallas_call(
        functools.partial(class_weights_kernel, images),
        grid=(1,),
        in_specs=[whole(mine.shape), whole(factors.shape)],
        out_specs=[whole(out.shape) for out in outs],
        out_shape=outs,
        compiler_params=limit(SMALL_MIB),
        cost_estimate=pl.CostEstimate(flops=1 << 29, bytes_accessed=3 << 20, transcendentals=0),
        name="class_weights",
    )(mine, factors)


def mm3_wide(left, right):
    width = right[0].shape[1]
    both = mm(left[0], jnp.concatenate(right, axis=1))
    return both[:, :width] + (both[:, width:] + mm(left[1], right[0]))


def backward_kernel(slots, images, dp_size, unroll, *refs):
    place_ref, lengths_ref = refs[:2]
    token_hbm = refs[2 : 2 + slots]
    (
        e_high_ref, e_low_ref, pv_ref, inverse_ref, pv_bias_ref, cot_ref,
        kt_high, kt_low, v_high, v_low, query_ref, t1_ref, t2_ref, t1_rows, t2_rows,
        vec_rows_ref, vecs_ref, mats_ref,
    ) = refs[2 + slots : 20 + slots]
    (
        even_ref, odd_ref, keep_ref, send_ref,
        d_keys, d_values, c1, c2, cot_t, qt, d_qt, v_three, w_ref, tokens, arrived,
    ) = refs[20 + slots :]
    rows, width = cot_ref.shape
    step = pl.program_id(0)
    size = width // 8
    lanes = lax.broadcasted_iota(jnp.int32, (1, 128), 1)
    pairs = [(mats_ref.at[0, 0, :, pl.ds(0, 3 * width)], w_ref)]
    pairs += [(ref, tokens.at[i]) for i, ref in enumerate(token_hbm)]
    copies = [pltpu.make_async_copy(a, b, arrived.at[i]) for i, (a, b) in enumerate(pairs)]

    @pl.when(step == 0)
    def _():
        for copy in copies:
            copy.start()
        cot_t[...] = cot_ref[...].T
        qt[...] = query_ref[...].T
        d_qt[...] = jnp.zeros_like(d_qt)
        d_keys[...] = jnp.zeros_like(d_keys)
        c1[...] = jnp.zeros_like(c1)
        v_three[...] = jnp.concatenate([v_high[...], v_high[...], v_low[...]], axis=1)
        c2[...] = jnp.where(
            lanes == 8, jnp.sum(cot_t[...] * pv_bias_ref[...], axis=1, keepdims=True), 0.0
        )
        inside = jnp.concatenate(same_image(lengths_ref, images, place_ref[0], slots, rows), axis=0)
        inside = jnp.where(inside, 1.0, 0.0).astype(BF16)
        high, low = split(cot_ref[...] * t2_rows[8:9, :])
        d_values[...] = mm(inside, high) + mm(inside, low)

    found = []
    for u in range(unroll):
        head = step * unroll + u
        t2_column, inverse = column_of(t2_ref[...], head), inverse_ref[u]
        crossed = cot_t[...] * pv_ref[u]
        c2[...] += jnp.where(lanes == head, jnp.sum(crossed, axis=1, keepdims=True), 0.0)
        delta = jnp.sum(crossed * t2_column, axis=0, keepdims=True) * inverse
        high, low = split(cot_t[...] * (t2_column * inverse))
        found.append((mm(v_three[...], jnp.concatenate([high, low, high], axis=0)), delta))
    for u in range(unroll):
        head = step * unroll + u
        d_probs, delta = found[u]
        pair = (e_high_ref[u], e_low_ref[u])
        d_mixed = split((pair[0].astype(F32) + pair[1].astype(F32)) * (d_probs - delta))
        inverse_rows = jnp.broadcast_to(inverse_ref[u], (8, rows)).T[:, :1]
        cot = split(cot_ref[...] * inverse_rows * t2_rows[pl.ds(head, 1), :])
        d_values[...] += mm3_wide(pair, cot)
        d_keys[...] += mm3_wide(d_mixed, split(query_ref[...] * t1_rows[pl.ds(head, 1), :]))
        back = mm3((kt_high[...], kt_low[...]), d_mixed)
        d_qt[...] += back * column_of(t1_ref[...], head)
        c1[...] += jnp.where(lanes == head, jnp.sum(back * qt[...], axis=1, keepdims=True), 0.0)

    @pl.when(step == pl.num_programs(0) - 1)
    def _():
        for copy in copies:
            copy.wait()
        d_query = d_qt[...].T * size ** (-0.5)
        w_q, w_kv = split(w_ref[:, :width]), split(w_ref[:, width:])
        gain = shift = g_kv = 0.0
        for slot in range(slots):
            here = pl.ds(slot * rows, rows)
            unit, _ = norm_rows(tokens[slot])
            normed = split(unit * vecs_ref[0:1, :] + vecs_ref[1:2, :])
            d_kv = split(jnp.concatenate([d_keys[here, :], d_values[here, :]], axis=1))
            piece = mm3(d_kv, w_kv, NT)
            if slot == 0:
                dq = split(d_query)
                piece = piece + mm3(dq, w_q, NT)
                g_q = mm3(normed, dq, TN)
            (odd_ref if slot % 2 else even_ref)[slot // 2] = piece
            gain, shift = gain + row_sum(piece * unit), shift + row_sum(piece)
            g_kv = g_kv + mm3(normed, d_kv, TN)
        g_k, g_v = g_kv[:, :width], g_kv[:, width:]
        added = jnp.concatenate(
            [gain, shift, row_sum(d_query), row_sum(d_values[...]), jnp.zeros((4, width), F32)], axis=0
        )
        vec_rows = jnp.concatenate([vec_rows_ref[0:8, :] + added, vec_rows_ref[8:28, :]], axis=0)
        fold = lambda value: jnp.concatenate(
            [row_sum(value[i * size : (i + 1) * size]) for i in range(8)], axis=0
        )
        pre, post = fold(c1[...]).T[:8, :], fold(c2[...])
        count = vec_rows.shape[0]
        talk = jnp.concatenate([pre, post[:, :9], jnp.zeros((8, 128 - count - 17), F32)], axis=1)
        block = width // dp_size
        talk = jnp.concatenate([talk, jnp.zeros((block - 8, 128 - count), F32)], axis=0)
        talk = jnp.concatenate([talk] * dp_size, axis=0)
        small = jnp.concatenate([vec_rows.T, talk], axis=1)
        even = jnp.bitwise_and(place_ref[0], 1) == 0
        left = jnp.concatenate([g_q, g_k[:, :256]], axis=1)
        right = jnp.concatenate([g_k[:, 256:], g_v, small], axis=1)
        keep_ref[...] = jnp.where(even, left, right)
        send_ref[...] = jnp.where(even, right, left)


def backward(dp_size, place, lengths, token_slots, found, cot, keys_values, query, tables,
             vec_rows, vectors, matrices):
    rows, width = cot.shape
    heads, total, _ = found[0].shape
    slots, unroll = total // rows, 2 if total <= 1024 else 1
    operands = far_off(*token_slots, *found, cot, *keys_values, query, *tables, vec_rows, vectors, matrices)
    specs = [whole(operand.shape) for operand in operands]
    specs[:slots] = [anywhere()] * slots
    specs[slots : slots + 4] = [by_head(unroll, operand.shape) for operand in found[:4]]
    specs[-1] = anywhere()
    outs = [far_struct((slots // 2, rows, width))] * 2 + [far_struct((width, 640))] * 2
    return pl.pallas_call(
        functools.partial(backward_kernel, slots, lengths.shape[1], dp_size, unroll),
        grid=(heads // unroll,),
        in_specs=[smem(), smem()] + specs,
        out_specs=[whole(out.shape) for out in outs],
        out_shape=outs,
        scratch_shapes=[pltpu.VMEM((total, width), F32)] * 2
        + [pltpu.VMEM((width, 128), F32)] * 2
        + [pltpu.VMEM((width, rows), F32)] * 3
        + [
            pltpu.VMEM((total, 3 * width), BF16),
            pltpu.VMEM((width, 3 * width), F32),
            pltpu.VMEM((slots, rows, width), F32),
            pltpu.SemaphoreType.DMA((1 + slots,)),
        ],
        compiler_params=limit(46 if total <= 1024 else KERNEL_MIB),
        cost_estimate=pl.CostEstimate(
            flops=6 * (4 * heads + 6) * total * rows * width, bytes_accessed=24 << 20, transcendentals=0
        ),
        name="backward",
    )(place, lengths, *operands)


def token_grad_kernel(tokens_ref, vecs_ref, own_ref, near_ref, far_ref, tail_ref, grad_ref):
    unit, scale = norm_rows(tokens_ref[...])
    d_normed = own_ref[...] + near_ref[...] + far_ref[...]
    grad_ref[...] = tail_ref[...] + norm_back(d_normed * vecs_ref[0:1, :], unit, scale)


def token_grad(tokens, vectors, own, near, far, tail):
    operands = [*far_off(tokens, vectors), own, near, far, *far_off(tail)]
    return pl.pallas_call(
        token_grad_kernel,
        out_shape=struct(tokens.shape),
        compiler_params=limit(SMALL_MIB),
        cost_estimate=pl.CostEstimate(flops=1 << 21, bytes_accessed=2 << 20, transcendentals=0),
        name="token_grad",
    )(*operands)


def squares_kernel(dp_size, counts, *refs):
    place_ref, added_ref, class_ref = refs[:3]
    early_refs = refs[3 : 3 + counts[0]]
    late_refs = refs[3 + counts[0] : 3 + sum(counts)]
    out_ref, early_ref, late_ref = refs[3 + sum(counts) :]
    odd = jnp.bitwise_and(place_ref[0], 1) == 1
    early = sum_of([ref[...] for ref in early_refs])
    late = sum_of([ref[...] for ref in late_refs])
    early_ref[...], late_ref[...] = early, late
    small = late[:, 512:] + jnp.where(odd, added_ref[...], 0.0)
    lane = lax.broadcasted_iota(jnp.int32, small.shape, 1)
    talk = jnp.logical_and(odd, jnp.logical_and(lane >= 28, lane < 45))
    small = small * small * jnp.where(talk, 1.0 / dp_size, 1.0)
    total = jnp.sum(small)
    for value in (late[:, :512], early):
        total = total + jnp.sum(value * value)
    out_ref[...] = 0.5 * class_ref[...] + total


def squares_of(dp_size, place, added, class_squares, early, late):
    operands = [added, class_squares, *early, *late]
    outs = [struct((8, 128)), struct(early[0].shape), struct(late[0].shape)]
    return pl.pallas_call(
        functools.partial(squares_kernel, dp_size, (len(early), len(late))),
        grid=(1,),
        in_specs=[smem()] + [whole(operand.shape) for operand in operands],
        out_specs=[whole(out.shape) for out in outs],
        out_shape=outs,
        compiler_params=limit(SMALL_MIB),
        cost_estimate=pl.CostEstimate(flops=1 << 18, bytes_accessed=1 << 20, transcendentals=0),
        name="squares",
    )(place, *operands)


def adam_step(weight, gradient, moment1, moment2, rate, decay):
    first = BETA_ONE * moment1 + (1.0 - BETA_ONE) * gradient
    second = BETA_TWO * moment2 + (1.0 - BETA_TWO) * gradient * gradient
    first_hat = first * (1.0 / (1.0 - BETA_ONE**STEP))
    second_hat = second * (1.0 / (1.0 - BETA_TWO**STEP))
    updated = weight - rate * (first_hat / (jnp.sqrt(second_hat) + ADAM_EPS) + decay * weight)
    return (updated, first, second)


def stage_kernel(sliced, place_ref, w_ref, m1_ref, m2_ref, ema_ref, w_out, m1_out, m2_out, ema_out, arrived):
    rows = w_out.shape[2]
    if sliced:
        w_ref = w_ref.at[:, :, pl.ds(pl.multiple_of(place_ref[1] * rows, rows), rows), :]
    pairs = [(w_ref, w_out), (m1_ref, m1_out), (m2_ref, m2_out), (ema_ref, ema_out)]
    for copy in copy_in(pairs, arrived):
        copy.wait()


def stage(place, mats):
    shape = mats[1].shape
    return pl.pallas_call(
        functools.partial(stage_kernel, mats[0].shape != shape),
        in_specs=[smem()] + [anywhere()] * 4,
        out_specs=[pl.BlockSpec(memory_space=pltpu.VMEM)] * 4,
        out_shape=[pltpu.VMEM(shape, F32)] * 4,
        scratch_shapes=[pltpu.SemaphoreType.DMA((4,))],
        compiler_params=limit(8),
        cost_estimate=pl.CostEstimate(flops=1, bytes_accessed=1, transcendentals=0),
        name="stage",
    )(place, *far_off(*mats))


def adam_kernel(sliced, *refs):
    (
        place_ref, squares_ref, early_own, early_other, late_own, late_other, added_ref,
        class_ref, w_ref, m1_ref, m2_ref, ema_ref, v_ref, v1_ref, v2_ref, v_ema_ref,
        t_ref, t1_ref, t2_ref, t_ema_ref,
    ) = refs[:20]
    norm_ref, mat_outs, v_outs, t_outs = refs[20], refs[21:25], refs[25:29], refs[29:33]
    stored, leaving, columns = refs[33:37], refs[37], refs[38]
    norm = jnp.sqrt(squares_ref[0:1, 0:1])
    factor = jnp.minimum(1.0, CLIP_NORM / norm)
    norm_ref[...] = norm

    def updates(weight, gradient, moment1, moment2, ema, rate, decay):
        updated, first, second = adam_step(weight, gradient * factor, moment1, moment2, rate, decay)
        return updated, first, second, EMA_RATE * ema + (1.0 - EMA_RATE) * updated

    even = jnp.bitwise_and(place_ref[0], 1) == 0
    pair = lambda own, other: (jnp.where(even, own[...], other[...]), jnp.where(even, other[...], own[...]))
    early_left, early_right = pair(early_own, early_other)
    late_left, late_right = pair(late_own, late_other)
    hidden = w_ref.shape[3]
    first = jnp.concatenate(
        [late_left, late_right[:, :512], early_left[:, hidden:], early_right[:, hidden : hidden + 128]], axis=1
    )
    grads = [first, early_left[:, :hidden], early_right[:, :hidden], *[class_ref[i] for i in range(3)]]
    copies = []
    for number in (3, 4, 5, 1, 2, 0):
        at = (number // 3, number % 3)
        values = updates(w_ref[at], grads[number], m1_ref[at], m2_ref[at], ema_ref[at], LR_MATRIX, WEIGHT_DECAY)
        for i, value in enumerate(values):
            stored[i][at] = value
            copies.append(pltpu.make_async_copy(stored[i].at[at], mat_outs[i].at[at], leaving.at[i, number]))
            copies[-1].start()
    small = late_right[:, 512:] + added_ref[...]
    count = v1_ref.shape[0]
    if sliced:
        columns[:, :count] = v_ref[...].T
        share = small.shape[0]
        begin = pl.multiple_of(place_ref[1] * share, share)
        weight = columns[pl.ds(begin, share), :].T[:count, :]
    else:
        weight = v_ref[...]
    values = updates(weight, small.T[:count, :], v1_ref[...], v2_ref[...], v_ema_ref[...], LR_VECTOR, 0.0)
    for ref, value in zip(v_outs, values):
        ref[...] = value
    talk = small[:8, count : count + 17]
    values = updates(t_ref[...], talk, t1_ref[...], t2_ref[...], t_ema_ref[...], LR_TALKING, 0.0)
    for ref, value in zip(t_outs, values):
        ref[...] = value
    for copy in copies:
        copy.wait()


def optimizer(place, squares, grads, class_share, mats, vecs, talks):
    shape = mats[0].shape
    sliced = vecs[0].shape != vecs[1].shape
    operands = [squares, *grads, class_share, *mats, *far_off(*vecs, *talks)]
    vmem = pl.BlockSpec(memory_space=pltpu.VMEM)
    outs = [struct((1, 1))] + [struct(shape)] * 4
    outs += [struct(vecs[1].shape)] * 4 + [struct(talks[0].shape)] * 4
    return pl.pallas_call(
        functools.partial(adam_kernel, sliced),
        in_specs=[smem()] + [vmem] * len(operands),
        out_specs=[vmem] + [anywhere()] * 4 + [vmem] * 8,
        out_shape=outs,
        scratch_shapes=[pltpu.VMEM(shape, F32)] * 4
        + [pltpu.SemaphoreType.DMA((4, 6)), pltpu.VMEM((vecs[0].shape[1], 128), F32)],
        compiler_params=limit(SMALL_MIB),
        cost_estimate=pl.CostEstimate(flops=1 << 23, bytes_accessed=14 << 20, transcendentals=0),
        name="optimizer",
    )(place, *operands)


def swap(value, axis, size, bit):
    return lax.ppermute(value, axis, [(place, place ^ bit) for place in range(size)])


def bits_of(axis, size, bit=1):
    return [(axis, bit << i) for i in range((size // bit).bit_length() - 1)]


class Places:
    def __init__(self, dp_size, seq_size, row_share):
        seq, dp = lax.axis_index("seq"), lax.axis_index("dp")
        self.sizes = {"dp": dp_size, "seq": seq_size}
        steps = bits_of("dp", dp_size) + bits_of("seq", seq_size)
        names = {"dp": dp, "seq": seq}
        bits = {step: jnp.bitwise_and(lax.shift_right_logical(names[step[0]], step[1].bit_length() - 1), 1) for step in steps}
        self.found = {
            "seq": seq.astype(jnp.int32).reshape(1),
            "dp": dp.astype(jnp.int32).reshape(1),
            "rows": (dp * row_share).astype(jnp.uint32),
            "share": (bits["seq", 1] * (seq_size // 2) + lax.shift_right_logical(seq, 1)).astype(jnp.uint32),
        }
        for step, bit in bits.items():
            self.found[step, "mine"] = bit.astype(jnp.uint32)
            self.found[step, "other"] = (1 - bit).astype(jnp.uint32)
            self.found[step, "low"] = bit == 0

    def before(self, value):
        names = list(self.found)
        value, *found = together(value, *[self.found[name] for name in names])
        self.found = dict(zip(names, found))
        return value

    def take(self, value, picks):
        at = [jnp.uint32(0)] * value.ndim
        sizes = list(value.shape)
        for dim, (step, which) in picks.items():
            at[dim] = self.found[step, which]
            sizes[dim] = 1
        return lax.squeeze(lax.dynamic_slice(value, at, sizes), tuple(picks))

    def share(self, value, rows):
        at = self.found["share"] * jnp.uint32(rows)
        return lax.dynamic_slice(value, (at, jnp.uint32(0)), (rows, value.shape[1]))

    def rows(self, value, size, dim):
        at = [jnp.uint32(0)] * value.ndim
        at[dim] = self.found["rows"]
        sizes = list(value.shape)
        sizes[dim] = size
        return lax.dynamic_slice(value, at, sizes)

    def swap(self, value, steps):
        flip = sum(bit * (self.sizes["seq"] if axis == "dp" else 1) for axis, bit in steps)
        count = self.sizes["dp"] * self.sizes["seq"]
        return lax.ppermute(value, ("dp", "seq"), [(place, place ^ flip) for place in range(count)])

    def pair(self, value, other, step):
        low = self.found[step, "low"]
        return [jnp.where(low, value, other), jnp.where(low, other, value)]


def subsets(group):
    found = [()]
    for step in group:
        found += [one + (step,) for one in found]
    return found[1:]


class Reduce:
    def __init__(self, terms, places, groups):
        self.places, self.groups = places, list(groups)
        self.left = bits_of("dp", places.sizes["dp"])[::-1]
        shape = (2,) * len(self.left) + (-1, terms[0].shape[1])
        self.terms = [term.reshape(shape) for term in terms]
        self.got = 0

    def sends(self):
        group = self.groups[0]
        halves = [step for step in group if step[0] == "dp"]
        dims = {step: self.left.index(step) for step in halves}
        if not halves:
            self.terms = [sum_of(self.terms)]

        def taken(others):
            picks = {dims[step]: (step, "other" if step in others else "mine") for step in halves}
            return [self.places.take(term, picks) if picks else term for term in self.terms]

        sent = [sum_of(taken(others)) for others in subsets(group)]
        self.terms = taken(())
        self.left = [step for step in self.left if step not in halves]
        return sent

    def post(self, sent):
        group = self.groups.pop(0)
        self.got = len(sent)
        self.terms += [self.places.swap(value, steps) for value, steps in zip(sent, subsets(group))]

    def received(self):
        return self.terms[len(self.terms) - self.got :]

    def set_received(self, values):
        self.terms[len(self.terms) - self.got :] = values

    def value(self):
        return sum_of(self.terms)


def join_kernel(*refs):
    out_ref, at = refs[-1], 0
    for ref in refs[:-1]:
        out_ref[at : at + ref.shape[0]] = ref[...]
        at += ref.shape[0]


def join(parts):
    shape = (sum(part.shape[0] for part in parts),) + parts[0].shape[1:]
    return pl.pallas_call(
        join_kernel,
        in_specs=[pl.BlockSpec(memory_space=pltpu.VMEM)] * len(parts),
        out_specs=pl.BlockSpec(memory_space=pltpu.VMEM),
        out_shape=struct(shape),
        compiler_params=limit(SMALL_MIB),
        cost_estimate=pl.CostEstimate(flops=1, bytes_accessed=1, transcendentals=0),
        name="join",
    )(*parts)


class Gather:
    def __init__(self, value, places):
        self.places = places
        dp = bits_of("dp", places.sizes["dp"])
        self.value = value[None]
        self.groups = [(step,) for step in dp[2:]] + [tuple(dp[:2])]
        self.groups += [(step,) for step in bits_of("seq", places.sizes["seq"], 2) + bits_of("seq", 2)]

    def sends(self):
        return [self.value]

    def post(self, sent):
        self.value = sent[0]
        self.others = [self.places.swap(self.value, steps) for steps in subsets(self.groups[0])]

    def received(self):
        return list(self.others)

    def set_received(self, values):
        group = self.groups.pop(0)
        if group[0][0] == "dp":
            self.value = join([self.value, *values])
        else:
            self.value = jnp.concatenate(self.places.pair(self.value, values[0], group[0]), axis=1)
        self.others = []


def settle(streams, *work):
    streams = [stream for stream in streams if stream.received()]
    counts = [len(stream.received()) for stream in streams]
    found = together(*[value for stream in streams for value in stream.received()], *work)
    at = 0
    for stream, count in zip(streams, counts):
        stream.set_received(list(found[at : at + count]))
        at += count
    return found[at:]


def launch(streams, *after):
    streams = [stream for stream in streams if stream.groups]
    sent = [stream.sends() for stream in streams]
    found = together(*[value for one in sent for value in one], *after)
    at = 0
    for stream, one in zip(streams, sent):
        stream.post(list(found[at : at + len(one)]))
        at += len(one)
    return found[at:]


def sum_of(terms):
    total = terms[0]
    for term in terms[1:]:
        total = total + term
    return total


def tie(value, *others):
    return lax.optimization_barrier((value, *others))[0]


def together(*values):
    return lax.optimization_barrier(values)


def on_device(
    dp_size, seq_size,
    tokens, class_tokens, cot_patch, cot_class, lengths,
    matrices, matrices_moment1, matrices_moment2, matrices_ema,
    vectors, vectors_moment1, vectors_moment2, vectors_ema,
    talking, talking_moment1, talking_moment2, talking_ema,
):
    rows, width = tokens.shape
    images = class_tokens.shape[0]
    row_share = width // dp_size
    places = Places(dp_size, seq_size, row_share)
    tokens = places.before(tokens)
    place = places.found["seq"]

    slots = {0: tokens}
    slots[1] = swap(tokens, "seq", seq_size, 1)
    bit = 2
    while bit < seq_size:
        for slot in sorted(slot for slot in slots if slot % 2 == 0):
            slots[slot | bit] = swap(slots[slot], "seq", seq_size, bit)
        bit *= 2
    *prepared, t1, t2, t1_rows, t2_rows, query, k1, k2, v1, v2, kt1, kt2, vt1, vt2 = prepare(
        tokens, slots[1], class_tokens, matrices, vectors, talking
    )
    for slot in range(2, seq_size, 2):
        slots[slot + 1] = swap(tie(slots[slot], query), "seq", seq_size, 1)
    token_slots = [slots[slot] for slot in range(seq_size)]
    (
        e_high, e_low, pv, inverse, pv_bias, attended, kt_high, kt_low, v_high, v_low,
        patch_out, *kept, packed, scores,
    ) = forward(
        place, lengths, token_slots, matrices, vectors, t1, t2, prepared[3],
        [query, k1, k2, v1, v2, kt1, kt2, vt1, vt2],
    )
    parts = [packed] + [swap(packed, "seq", seq_size, bit) for bit in range(1, seq_size)]
    *staged, w_first = class_stage(tie(place, packed), matrices)
    (
        class_out, d_attended, d_mixed, early_keep, early_send, partial, factors, vec_rows, class_terms,
    ) = middle(
        place, parts, vectors, prepared, class_tokens, cot_class, cot_patch,
        patch_out, scores, staged, [attended, *kept], matrices,
    )

    core, chips, dp = ("seq", 1), bits_of("seq", seq_size, 2), bits_of("dp", dp_size)
    pairs = lambda steps: [tuple(steps[i : i + 2]) for i in range(0, len(steps), 2)]
    other = places.swap(early_send, [core])
    partials = [partial] + [swap(partial, "seq", seq_size, bit) for bit in range(1, seq_size)]
    grad_class, factors = class_finish(partials, class_terms, class_tokens, vectors, w_first, factors)
    gather = Gather(places.share(factors, factors.shape[0] // seq_size), places)
    other, gather.value = together(other, gather.value)
    early = Reduce(
        [early_keep, other], places, [tuple(dp[:2])] + [(step,) for step in dp[2:] + chips]
    )
    (later,) = launch([early, gather], place)
    even, odd, late_keep, late_send = backward(
        dp_size, later, lengths, token_slots, [e_high, e_low, pv, inverse, pv_bias], d_attended,
        [kt_high, kt_low, v_high, v_low], query, [t1, t2, t1_rows, t2_rows], vec_rows, vectors, matrices,
    )

    late_send, odd = settle([early, gather], late_send, odd)
    late_other, odd = places.swap(late_send, [core]), places.swap(odd, [core])
    late = Reduce([late_keep, late_other], places, [tuple(dp[:2])] + [(step,) for step in dp[2:] + chips])
    (late.terms[1],) = launch([early], late.terms[1])
    (even,) = launch([late], even)
    own = [even[0]] + [even[i] + odd[i] for i in range(1, seq_size // 2)]
    near = odd[0]
    bit = 1
    while 2 * bit < len(own):
        for slot in range(0, len(own), 2 * bit):
            own[slot] = own[slot] + swap(own[slot + bit], "seq", seq_size, 2 * bit)
        bit *= 2
    far = swap(own[bit], "seq", seq_size, 2 * bit)
    (own[bit],) = launch([gather], own[bit])
    (own[bit],) = settle([gather], own[bit])
    while len(gather.groups) > len(chips) + 1:
        launch([gather])
        settle([gather])
    launch([gather], own[bit])
    (far,) = settle([late, early], far)
    (far,) = launch([late, early], far)
    (far,) = settle([gather], far)
    while gather.groups:
        launch([gather])
        settle([gather])
    sliced = row_share % 8 == 0
    if not sliced:
        matrices_rows, vectors_columns = places.rows(matrices, row_share, 2), places.rows(vectors, row_share, 1)
    else:
        matrices_rows, vectors_columns = matrices, vectors
    both_places = tie(jnp.concatenate([place, places.found["dp"]]), gather.value)
    staged = stage(both_places, [matrices_rows, matrices_moment1, matrices_moment2, matrices_ema])
    gather.value, *staged = settle([late], gather.value, *staged)
    while late.groups[1:]:
        launch([late])
        settle([late])
    (gather.value,) = launch([late], gather.value)
    mine = places.rows(gather.value, row_share, 2)
    class_share, class_squares, added = class_weights(images, mine, gather.value)
    while early.groups:
        settle([early])
        launch([early])
    class_share, class_squares, added = settle([late, early], class_share, class_squares, added)
    last = [[term.reshape(row_share, -1) for term in stream.terms] for stream in (early, late)]
    squares, early, late = squares_of(dp_size, place, added, class_squares, *last)
    far, squares = together(far, squares)
    for group in pairs(dp + [core]):
        squares = sum_of([squares] + [places.swap(squares, steps) for steps in subsets(group)])
    grad_tokens = token_grad(tokens, vectors, own[0], near, far, d_mixed)
    grads = []
    for value in (early, late):
        grads += [value, places.swap(value, [core])]
    norm, *updated = optimizer(
        both_places, squares, [*grads, added], class_share, staged,
        [vectors_columns, vectors_moment1, vectors_moment2, vectors_ema],
        [talking, talking_moment1, talking_moment2, talking_ema],
    )
    return (patch_out, class_out, grad_tokens, grad_class, norm.reshape(()), *updated)


def solution(mesh):
    tokens = P(("dp", "seq"), None)
    by_group = P("dp", None)
    mats = P(None, None, "dp", None)
    vecs = P(None, "dp")
    body = functools.partial(on_device, mesh.shape["dp"], mesh.shape["seq"])
    return jax.shard_map(
        body,
        mesh=mesh,
        in_specs=(tokens, by_group, tokens, by_group, by_group, P(), mats, mats, mats,
                  P(), vecs, vecs, vecs, P(), P(), P(), P()),
        out_specs=(tokens, by_group, tokens, by_group, P(), mats, mats, mats, mats,
                   vecs, vecs, vecs, vecs, P(), P(), P(), P()),
        check_vma=False,
    )
```
